32 devices in a mesh: dp: 8 (over z, y), blk: 4 (over x, core).
Axes of the slice: x: 2, y: 2, z: 4, core: 2. Of those that a mesh axis runs over, the one named last changes fastest.
Arguments:
- tokens: bfloat16 [2, 8, 3072, 512], P(None, 'dp', 'blk'), may hold values from -6 to 6
- cotangent: bfloat16 [2, 8, 3072, 512], P(None, 'dp', 'blk'), may hold values from -6 to 6
- segments: int32 [2, 8, 3072], P(None, 'dp', 'blk'), may hold values from 0 to 766, as said below
- padding: int32 [2, 8, 3072], P(None, 'dp', 'blk'), may hold values from 0 to 1, as said below
- known: int32 [2, 8, 3072], P(None, 'dp', 'blk'), may hold values from 0 to 1, as said below
- w_qkv: bfloat16 [512, 1536], P(('dp', 'blk')), may hold values from -0.25 to 0.25
- w_out: bfloat16 [512, 512], P(('dp', 'blk')), may hold values from -2 to 2
- w_up: bfloat16 [512, 512], P(('dp', 'blk')), may hold values from -0.25 to 0.25
- w_down: bfloat16 [512, 512], P(('dp', 'blk')), may hold values from -0.25 to 0.25
- norm_gains: bfloat16 [2, 512], P(None, ('dp', 'blk')), may hold values from 0.25 to 1.75
- norm_shifts: bfloat16 [2, 512], P(None, ('dp', 'blk')), may hold values from -3 to 3
Outputs:
- layer_out: bfloat16 [2, 8, 3072, 512], P(None, 'dp', 'blk')
- token_grad: bfloat16 [2, 8, 3072, 512], P(None, 'dp', 'blk')
- grad_qkv: float32 [512, 1536], P(('dp', 'blk'))
- grad_out: float32 [512, 512], P(('dp', 'blk'))
- grad_up: float32 [512, 512], P(('dp', 'blk'))
- grad_down: float32 [512, 512], P(('dp', 'blk'))
- grad_gains: float32 [2, 512], P(None, ('dp', 'blk'))
- grad_shifts: float32 [2, 512], P(None, ('dp', 'blk'))
The draws below stay inside these ranges and needn't reach their ends.
Inputs may be any that keep to these rules, and one draw needn't show every extreme that they name: `segments`: within a row the ids start at 0 and never fall; one segment of every row covers positions 384 to 2687. `padding`: 0 at the first position of every segment. `known`: 1 at the first position of every segment.
All inputs are finite; a program needn't handle non-finite values.
Results may differ from the reference program's by a relative error of at most 0.018.
Values may be sent and summed in bfloat16 or wider, within the bound.
A program may use at most 384 MiB of HBM per device.

```python
import jax
import jax.numpy as jnp
from jax import lax

D = 512
FF = 512
HEADS = 8
ROW_LEN = 3072
MICRO = 2
BLOCK = 768
ROWS = 8


def segment_cuts(key):
    where_at = jnp.arange(ROW_LEN, dtype=jnp.int32)
    upper = max(BLOCK // 2, 3)
    micro_at = jnp.arange(MICRO, dtype=jnp.int32)[:, None, None]
    row_at = jnp.arange(ROWS, dtype=jnp.int32)[None, :, None]
    forced = (micro_at == 0) & (row_at == 0)
    first_cut = jax.random.randint(jax.random.fold_in(key, 101), (MICRO, ROWS, 1), 1, upper, dtype=jnp.int32)
    last_cut = ROW_LEN - jax.random.randint(jax.random.fold_in(key, 102), (MICRO, ROWS, 1), 1, upper, dtype=jnp.int32)
    first_cut = jnp.where(forced, upper - 1, first_cut)
    last_cut = jnp.where(forced, ROW_LEN - upper + 1, last_cut)
    extra = jax.random.randint(jax.random.fold_in(key, 103), (MICRO, ROWS, ROW_LEN), 0, 12, dtype=jnp.int32) == 0
    extra = extra | forced
    outside = (where_at < first_cut) | (where_at > last_cut)
    cuts = (where_at == first_cut) | (where_at == last_cut) | extra & outside
    return cuts & (where_at > 0)


def segment_starts(key):
    where_at = jnp.arange(ROW_LEN, dtype=jnp.int32)
    return segment_cuts(key) | (where_at == 0)


def draw_segments(key, part):
    cuts = segment_cuts(key)
    return jnp.cumsum(cuts.astype(jnp.int32), axis=-1).astype(jnp.int32)


def draw_padding(key, part):
    starts = segment_starts(key)
    key = jax.random.fold_in(key, 2)
    flagged = jax.random.randint(key, (MICRO, ROWS, ROW_LEN), 0, 8, dtype=jnp.int32) == 0
    return (flagged & jnp.logical_not(starts)).astype(jnp.int32)


def draw_known(key, part):
    starts = segment_starts(key)
    key = jax.random.fold_in(key, 3)
    flagged = jax.random.randint(key, (MICRO, ROWS, ROW_LEN), 0, 2, dtype=jnp.int32) == 1
    return (flagged | starts).astype(jnp.int32)


def block_levels(key, shape, shards, least, largest):
    level = 1.0
    for axis_at, shards_of in shards:
        steps = jax.random.uniform(jax.random.fold_in(jax.random.fold_in(key, 6), axis_at), (shards_of,), jnp.float32, least / len(shards), largest / len(shards))
        level = level * jnp.repeat(jnp.exp(steps), shape[axis_at] // shards_of).reshape((-1,) + (1,) * (len(shape) - 1 - axis_at))
    return level


def gaussian(key, dims, scale, limit, split=(), kind=jnp.bfloat16):
    drawn = jax.random.normal(key, dims, jnp.float32) * scale
    if len(split) > 0:
        drawn = block_levels(key, dims, split, -0.22, 0.18) * drawn
    return jnp.clip(drawn, min=-limit, max=limit).astype(kind)


def setup_inputs(seed: int = 0) -> dict:
    key_of = jax.random.split(jax.random.key(seed), 12)
    tokens = gaussian(key_of[0], (MICRO, ROWS, ROW_LEN, D), 1.0, 6.0, ((1, 8), (2, 4)))
    cotangent = gaussian(key_of[1], (MICRO, ROWS, ROW_LEN, D), 1.0, 6.0, ((1, 8), (2, 4)))
    segments = draw_segments(jax.random.fold_in(key_of[11], 71), 0)
    padding = draw_padding(jax.random.fold_in(key_of[11], 71), 0)
    known = draw_known(jax.random.fold_in(key_of[11], 71), 0)
    w_qkv = gaussian(key_of[5], (D, 3 * D), D ** -0.5, 0.25, ((0, 32),))
    w_out = gaussian(key_of[6], (D, D), (D // 64) ** -0.5, 2.0, ((0, 32),))
    w_up = gaussian(key_of[7], (D, FF), D ** -0.5, 0.25, ((0, 32),))
    w_down = gaussian(key_of[8], (FF, D), FF ** -0.5, 0.25, ((0, 32),))
    norm_gains = jnp.clip(1.0 + 0.15 * jax.random.normal(key_of[9], (2, D), jnp.float32), 0.25, 1.75).astype(jnp.bfloat16)
    norm_shifts = gaussian(key_of[10], (2, D), 0.5, 3.0, ((1, 32),))
    return dict(tokens=tokens, cotangent=cotangent, segments=segments, padding=padding, known=known, w_qkv=w_qkv, w_out=w_out, w_up=w_up, w_down=w_down, norm_gains=norm_gains, norm_shifts=norm_shifts)


EPSILON = 1e-05
MASKED_SCORE = -1e+30

@jax.custom_vjp
def low(v):
    return lax.optimization_barrier(v.astype(jnp.bfloat16)).astype(jnp.float32)

@jax.custom_vjp
def low_back(v):
    return v

def low_keep(v):
    return (low(v), None)

def low_pass(kept, grad):
    return (grad,)

def back_keep(v):
    return (v, None)

def back_low(kept, grad):
    return (low(grad),)
low.defvjp(low_keep, low_pass)
low_back.defvjp(back_keep, back_low)

def matmul(left, right):
    return jnp.dot(left, right, precision=lax.Precision.HIGHEST, preferred_element_type=jnp.float32)

def normalize(rows_in, gain, shift):
    center = rows_in - lax.optimization_barrier(jnp.mean(rows_in, axis=-1, keepdims=True))
    inverse = lax.rsqrt(lax.optimization_barrier(jnp.mean(center * center, axis=-1, keepdims=True)) + EPSILON)
    return center * inverse * gain + shift

def query_block_len():
    divisor = 1
    for candidate in range(1, min(ROW_LEN, 512) + 1):
        if ROW_LEN % candidate == 0:
            divisor = candidate
    return divisor

def row_forward(params, row_in, seg_row, pad_row, known_row):
    w_qkv, w_out, w_up, w_down, gain_rows, shifts = params
    model_width = w_out.shape[0]
    head_size = model_width // HEADS
    factor = head_size ** (-0.5)
    qkv = low_back(low(matmul(row_in, w_qkv)))
    queries = qkv[:, :model_width].reshape(ROW_LEN, HEADS, head_size)
    keys = qkv[:, model_width:2 * model_width].reshape(ROW_LEN, HEADS, head_size)
    values = qkv[:, 2 * model_width:].reshape(ROW_LEN, HEADS, head_size)
    positions = jnp.arange(ROW_LEN, dtype=jnp.int32)
    sub_len = query_block_len()
    block_count = ROW_LEN // sub_len

    def attend_block(block_in):
        query_part, seg_part, pos_part = block_in
        scores = low_back(jnp.einsum('qhd,khd->qhk', query_part, keys, precision=lax.Precision.HIGHEST) * factor)
        allow_mask = (seg_part[:, None] == seg_row[None, :]) & (pad_row[None, :] == 0) & ((known_row[None, :] == 1) | (pos_part[:, None] == positions[None, :]))
        scores = jnp.where(allow_mask[:, None, :], scores, MASKED_SCORE)
        probabilities = jax.nn.softmax(scores, axis=-1)
        return jnp.einsum('qhk,khd->qhd', low(probabilities), values, precision=lax.Precision.HIGHEST)
    blocks = (queries.reshape(block_count, sub_len, HEADS, head_size), seg_row.reshape(block_count, sub_len), positions.reshape(block_count, sub_len))
    attended = lax.map(jax.checkpoint(attend_block), blocks).reshape(ROW_LEN, model_width)
    attended = low_back(low(attended))
    branch = low_back(matmul(attended, w_out))
    first = low(normalize(row_in + branch, gain_rows[0], shifts[0]))
    hidden = low_back(matmul(first, w_up))
    activated = low(jax.nn.gelu(hidden, approximate=False))
    feed = low_back(matmul(activated, w_down))
    return normalize(first + feed, gain_rows[1], shifts[1])

def reference(tokens, cotangent, segments, padding, known, w_qkv, w_out, w_up, w_down, norm_gains, norm_shifts):
    params = tuple((weight.astype(jnp.float32) for weight in (w_qkv, w_out, w_up, w_down, norm_gains, norm_shifts)))
    row_total = MICRO * ROWS

    def flatten(array):
        return array.reshape((row_total,) + array.shape[2:])
    inputs = (flatten(tokens).astype(jnp.float32), flatten(cotangent).astype(jnp.float32), flatten(segments), flatten(padding), flatten(known))
    zeros = jax.tree.map(jnp.zeros_like, params)

    def one_row(summed, item):
        row_in, row_cot, seg_row, pad_row, known_row = item

        def forward(weights, activations):
            return row_forward(weights, activations, seg_row, pad_row, known_row)
        out_row, backward = jax.vjp(forward, params, row_in)
        grad_params, grad_row = backward(row_cot)
        summed = jax.tree.map(jnp.add, summed, grad_params)
        return (summed, (out_row.astype(jnp.bfloat16), grad_row.astype(jnp.bfloat16)))
    summed, (outputs, grads) = lax.scan(one_row, zeros, inputs)
    layer_out = outputs.reshape(tokens.shape)
    token_grad = grads.reshape(tokens.shape)
    return (layer_out, token_grad, summed[0], summed[1], summed[2], summed[3], summed[4], summed[5])
```

```python
import functools, math
import jax, jax.numpy as jnp
from jax import lax
from jax.experimental import pallas as pl
from jax.experimental.pallas import tpu as pltpu
from jax.sharding import PartitionSpec as P

HEADS = 8
bf=jnp.bfloat16; f32=jnp.float32
HEAD=64
QB=512
KB=512
SRC=512
SAFE=60.0
CODE=16
SLOTS=3
def dot(a,b,ca,cb): return lax.dot_general(a,b,(((ca,),(cb,)),((),())),preferred_element_type=f32)
def al(x,n): return pl.multiple_of(x,n)
def iota(shape,axis): return lax.broadcasted_iota(jnp.int32,shape,axis)

class Counts:
    def __init__(self,L):
        self.nd=L//256; self.ns=L//SRC; self.nq=L//QB
        self.total=0; self.src=1; self.start=self.src+2*self.nd; self.size=self.start+self.nq; self.begin=self.size+self.nq
        self.length=self.begin+self.nd

def window(cnt_ref,at,i):
    groups=cnt_ref[at.size+i]
    full=(groups-1)//(KB//128)
    return cnt_ref[at.start+i],full,groups-full*(KB//128)

def by_piece(first,full,rest,g,fn):
    def body(j,g):
        fn(al(first+j*KB,128),KB,g)
        return g+1
    g=lax.fori_loop(0,full,body,g)
    for r in range(1,KB//128+1):
        @pl.when(rest==r)
        def _(): fn(al(first+full*KB,128),r*128,g)
    return g+1

def attend_kernel(L,H,cnt_ref,qkvt_ref,codet_ref,meta_ref,p_hbm,att_hbm,ot_hbm,inv_ref,kaug_hbm,vaug_hbm,
                  kaug_ref,vaug_ref,kvt,vct,acc,pbuf,obuf,abuf,top_ref,psem,osem,asem,ksem):
    W=H*HEAD; at=Counts(L)
    total=cnt_ref[at.total]
    for h in range(H):
        kvt[h*128:h*128+HEAD,:]=qkvt_ref[W+h*HEAD:W+(h+1)*HEAD,:]
        kvt[h*128+HEAD:h*128+HEAD+CODE,:]=codet_ref[...]
        kvt[h*128+HEAD+CODE:(h+1)*128,:]=jnp.zeros((HEAD-CODE,L),bf)
    lane=iota((256,128),1)
    down=iota((256,SRC),0)
    def dest(d,c):
        def src(s,a):
            ssl=pl.ds(al(s*SRC,SRC),SRC)
            oh=(meta_ref[0:1,ssl]==(down+d*256)).astype(f32).astype(bf)
            ka=a[0]+dot(oh,kvt[:,ssl],1,1)
            va=a[1]+dot(oh,qkvt_ref[2*W:3*W,ssl],1,1)
            return ka,va
        ka,va=lax.fori_loop(cnt_ref[at.src+2*d],cnt_ref[at.src+1+2*d],src,(jnp.zeros((256,H*128),f32),jnp.zeros((256,W),f32)))
        dsl=pl.ds(al(d*256,256),256)
        vat=va.T
        for h in range(H):
            k1=ka[:,h*128:(h+1)*128]
            kaug_ref[h,dsl,:]=jnp.where(lane==HEAD+10,-2560.0,k1).astype(bf)
            pair=va[:,(h//2)*128:(h//2+1)*128]
            if h%2: pair=jnp.concatenate([pair[:,HEAD:],pair[:,:HEAD]],1)
            vaug_ref[h,dsl,:]=jnp.where(lane<HEAD,pair,jnp.where(lane<HEAD+3,-1.0,0.0)).astype(bf)
            vct[h,:HEAD,dsl]=vat[h*HEAD:(h+1)*HEAD,:].astype(bf)
            vct[h,HEAD:HEAD+16,dsl]=jnp.ones((16,256),bf)
        return c
    lax.fori_loop(0,(total+255)//256,dest,0)
    keep=[pltpu.make_async_copy(kaug_ref,kaug_hbm,ksem.at[0]),pltpu.make_async_copy(vaug_ref,vaug_hbm,ksem.at[1])]
    for x in keep: x.start()
    bound=jnp.float32(0)
    for h in range(H):
        q=qkvt_ref[h*HEAD:(h+1)*HEAD,:].astype(f32); k=qkvt_ref[W+h*HEAD:W+(h+1)*HEAD,:].astype(f32)
        bound=jnp.maximum(bound,jnp.max(jnp.sum(q*q,0,keepdims=True))*jnp.max(jnp.sum(k*k,0,keepdims=True)))
    safe=bound<SAFE*SAFE

    def pcopy(g):
        slot=lax.rem(g,SLOTS)
        return pltpu.make_async_copy(pbuf.at[slot],p_hbm.at[g],psem.at[slot])
    def ocopy(i):
        slot=lax.rem(i,2)
        return pltpu.make_async_copy(obuf.at[slot],ot_hbm.at[i],osem.at[slot])
    def acopy(i):
        slot=lax.rem(i,2)
        return pltpu.make_async_copy(abuf.at[slot],att_hbm.at[:,pl.ds(al(i*QB,QB),QB),:],asem.at[slot])
    def block(i,g):
        slot=lax.rem(i,2)
        qsl=pl.ds(al(i*QB,QB),QB)
        first,full,rest=window(cnt_ref,at,i)
        qa=[jnp.concatenate([qkvt_ref[h*HEAD:(h+1)*HEAD,qsl],codet_ref[:,qsl],jnp.zeros((HEAD-CODE,QB),bf)],0) for h in range(H)]
        own=meta_ref[1:2,qsl]>0
        sself=[]
        for h in range(H):
            x=qkvt_ref[h*HEAD:(h+1)*HEAD,qsl].astype(f32)*qkvt_ref[W+h*HEAD:W+(h+1)*HEAD,qsl].astype(f32)
            sself.append(jnp.where(own,jnp.sum(x,0,keepdims=True),-1e30))
        acc[...]=jnp.zeros_like(acc)
        top_ref[...]=jnp.zeros_like(top_ref)
        row=iota((128,QB),0)
        def strict(h,osl):
            k=kaug_ref[h,osl,:]
            x=qa[h].astype(f32)
            plain=dot(k,jnp.where(row<HEAD,x,0.0).astype(bf),1,0)
            return jnp.where(dot(k,jnp.where(row<HEAD,0.0,x).astype(bf),1,0)>-1.0,plain,-1e30)
        @pl.when(jnp.logical_not(safe))
        def _():
            for h in range(H):
                def more(j,m): return jnp.maximum(m,jnp.max(strict(h,pl.ds(al(first+j*128,128),128)),0,keepdims=True))
                top_ref[h:h+1,:]=lax.fori_loop(0,cnt_ref[at.size+i],more,sself[h])
        def piece(off,size,g):
            ps=lax.rem(g,SLOTS)
            osl=pl.ds(off,size)
            @pl.when(g>=SLOTS)
            def _(): pcopy(g-SLOTS).wait()
            @pl.when(safe)
            def _():
                keepp=[]
                for h in range(H):
                    p=jnp.exp2(dot(kaug_ref[h,osl,:],qa[h],1,0)).astype(bf)
                    pbuf[ps,h,:size,:]=p
                    keepp.append(p)
                for h in range(H): acc[h]+=dot(vct[h,:,osl],keepp[h],1,0)
            @pl.when(jnp.logical_not(safe))
            def _():
                for h in range(H):
                    def put(j,c):
                        jsl=pl.ds(al(off+j*128,128),128)
                        p=jnp.exp2(strict(h,jsl)-top_ref[h:h+1,:]).astype(bf)
                        pbuf[ps,h,pl.ds(al(j*128,128),128),:]=p
                        acc[h]+=dot(vct[h,:,jsl],p,1,0)
                        return c
                    lax.fori_loop(0,size//128,put,0)
            pcopy(g).start()
        g=by_piece(first,full,rest,g,piece)
        @pl.when(i>=2)
        def _(): ocopy(i-2).wait(); acopy(i-2).wait()
        for h in range(H):
            ps=jnp.exp2(sself[h]-top_ref[h:h+1,:])
            inv=1.0/(acc[h,HEAD:HEAD+1,:]+ps)
            obuf[slot,h*HEAD:(h+1)*HEAD,:]=(acc[h,:HEAD,:]+ps*qkvt_ref[2*W+h*HEAD:2*W+(h+1)*HEAD,qsl].astype(f32))*inv
            inv_ref[h,0:1,qsl]=inv
            inv_ref[h,1:2,qsl]=ps
        for hp in range(H//2): abuf[slot,hp]=obuf[slot,hp*128:(hp+1)*128,:].T.astype(bf)
        ocopy(i).start(); acopy(i).start()
        return g
    g=lax.fori_loop(0,at.nq,block,0)
    for s in range(SLOTS):
        last=g-1-s
        @pl.when(last>=0)
        def _(): pcopy(last).wait()
    for i in range(max(at.nq-2,0),at.nq): ocopy(i).wait(); acopy(i).wait()
    for x in keep: x.wait()

def attend(cnt,qkvt,codet,meta,H):
    L=qkvt.shape[1]; W=H*HEAD; nq=L//QB; cap=nq*(L//KB+1)
    V=pl.BlockSpec(memory_space=pltpu.VMEM); A=pl.BlockSpec(memory_space=pl.ANY)
    S=jax.ShapeDtypeStruct; M=pltpu.VMEM; D=pltpu.SemaphoreType.DMA
    return pl.pallas_call(functools.partial(attend_kernel,L,H),
        out_shape=[S((cap,H,KB,QB),bf),S((H//2,L,128),bf),S((nq,W,QB),f32),S((H,8,L),f32),S((H,L,128),bf),S((H,L,128),bf)],
        in_specs=[pl.BlockSpec(memory_space=pltpu.SMEM),V,V,V],
        out_specs=[A,A,A,V,A,A],
        scratch_shapes=[M((H,L,128),bf),M((H,L,128),bf),M((H*128,L),bf),M((H,HEAD+16,L),bf),M((H,HEAD+16,QB),f32),M((SLOTS,H,KB,QB),bf),
            M((2,W,QB),f32),M((2,H//2,QB,128),bf),M((8,QB),f32),D((SLOTS,)),D((2,)),D((2,)),D((2,))],
        compiler_params=pltpu.CompilerParams(vmem_limit_bytes=56<<20))(cnt,qkvt,codet,meta)

def flags(seg,pad,known):
    L=seg.shape[0]; at=Counts(L)
    use=(pad==0)&(known==1)
    csum=jnp.cumsum(use.astype(jnp.int32))
    rank=jnp.where(use,csum-1,-1)
    own=((pad==0)&(known!=1)).astype(jnp.int32)
    bits=jnp.arange(CODE,dtype=jnp.int32)[:,None]
    codet=jnp.where(bits<10,jnp.where(((seg[None,:]>>jnp.minimum(bits,9))&1)==1,16.0,-16.0),jnp.where(bits==10,1.0,0.0)).astype(bf)
    meta=jnp.concatenate([rank[None],own[None],jnp.zeros((6,L),jnp.int32)],0)
    def edges(n):
        ends=csum.reshape(n,-1)[:,-1]
        return jnp.concatenate([jnp.zeros(1,jnp.int32),ends[:-1]]),ends
    begins,ends=edges(L//SRC)
    d=jnp.arange(at.nd,dtype=jnp.int32)*256
    lo=jnp.sum((ends[None,:]<=d[:,None]).astype(jnp.int32),1)
    hi=jnp.sum((begins[None,:]<d[:,None]+256).astype(jnp.int32),1)
    blocks=seg.reshape(at.nq,QB)
    low=jnp.sum((use[None,:]&(seg[None,:]<blocks[:,:1])).astype(jnp.int32),1)//128*128
    high=jnp.sum((use[None,:]&(seg[None,:]<=blocks[:,-1:])).astype(jnp.int32),1)
    cnt=jnp.concatenate([csum[-1:],jnp.stack([lo,hi],1).reshape(-1),low,(high-low+127)//128,edges(at.nd)[0]])
    return cnt,codet,meta
LN2=math.log(2.0)
def back_kernel(L,H,cnt_ref,datt_ref,p_hbm,ot_ref,inv_ref,kaug_ref,vaug_ref,qkvt_ref,meta_ref,tok_hbm,w_ref,
                tg_hbm,grad_ref,kct,dkv,dkvt,dq_ref,pbuf,qacc,tok_ref,tbuf,psem,tsem,ksem):
    W=H*HEAD; at=Counts(L)
    total=cnt_ref[at.total]; groups=(total+127)//128
    pieces=lax.fori_loop(0,at.nq,lambda i,s:s+(cnt_ref[at.size+i]+KB//128-1)//(KB//128),0)
    def pcopy(g):
        slot=lax.rem(g,SLOTS)
        return pltpu.make_async_copy(p_hbm.at[g],pbuf.at[slot],psem.at[slot])
    for s in range(SLOTS-1):
        @pl.when(s<pieces)
        def _(): pcopy(s).start()
    tcopy=pltpu.make_async_copy(tok_hbm,tok_ref,ksem.at[0])
    tcopy.start()
    def prep(j,c):
        jsl=pl.ds(al(j*128,128),128)
        for h in range(H): kct[h,:,jsl]=kaug_ref[h,jsl,:].T[:HEAD]
        dkv[jsl,:]=jnp.zeros((128,2*W),f32)
        return c
    lax.fori_loop(0,groups,prep,0)
    def block(i,g):
        qsl=pl.ds(al(i*QB,QB),QB)
        first,full,rest=window(cnt_ref,at,i)
        dt=jnp.concatenate([datt_ref[hp,qsl,:].astype(f32).T for hp in range(H//2)],0)
        prod=dt*ot_ref[i]
        daug=[];dz=[];qz=[];deltas=[];d1s=[]
        zero=jnp.zeros((HEAD,QB),bf)
        row=iota((16,QB),0)
        for h in range(H):
            hsl=slice(h*HEAD,(h+1)*HEAD)
            inv=inv_ref[h,0:1,qsl]
            delta=jnp.sum(prod[hsl],0,keepdims=True)*inv
            d1=dt[hsl]*inv
            low=d1.astype(bf)
            a=delta.astype(bf).astype(f32); b=(delta-a).astype(bf).astype(f32)
            extra=jnp.where(row==0,a,jnp.where(row==1,b,jnp.where(row==2,delta-a-b,0.0))).astype(bf)
            daug.append(jnp.concatenate([low,extra,jnp.zeros((HEAD-16,QB),bf)],0))
            q=qkvt_ref[hsl,qsl]
            dz.append(jnp.concatenate([zero,low] if h%2 else [low,zero],0))
            qz.append(jnp.concatenate([zero,q] if h%2 else [q,zero],0))
            deltas.append(delta); d1s.append(d1)
        qacc[...]=jnp.zeros_like(qacc)
        def piece(off,size,g):
            slot=lax.rem(g,SLOTS)
            osl=pl.ds(off,size)
            @pl.when(g+SLOTS-1<pieces)
            def _(): pcopy(g+SLOTS-1).start()
            pcopy(g).wait()
            dss=[]
            for h in range(H):
                dss.append((pbuf[slot,h,:size,:].astype(f32)*dot(vaug_ref[h,osl,:],daug[h],1,0)).astype(bf))
            for h in range(H): qacc[h*HEAD:(h+1)*HEAD,:]+=dot(kct[h,:,osl],dss[h],1,0)
            for h in range(0,H,2):
                dkv[osl,h*HEAD:(h+2)*HEAD]+=dot(dss[h],qz[h],1,1)+dot(dss[h+1],qz[h+1],1,1)
                dkv[osl,W+h*HEAD:W+(h+2)*HEAD]+=dot(pbuf[slot,h,:size,:],dz[h],1,1)+dot(pbuf[slot,h+1,:size,:],dz[h+1],1,1)
        g=by_piece(first,full,rest,g,piece)
        for h in range(H):
            hsl=slice(h*HEAD,(h+1)*HEAD); ksl=slice(W+h*HEAD,W+(h+1)*HEAD); vsl=slice(2*W+h*HEAD,2*W+(h+1)*HEAD)
            ps=inv_ref[h,1:2,qsl]
            ds=ps*(jnp.sum(qkvt_ref[vsl,qsl].astype(f32)*d1s[h],0,keepdims=True)-deltas[h])
            dq_ref[hsl,qsl]=((qacc[hsl,:]+ds*qkvt_ref[ksl,qsl].astype(f32))*0.125).astype(bf)
            dq_ref[ksl,qsl]=(ds*qkvt_ref[hsl,qsl].astype(f32)*LN2).astype(bf)
            dq_ref[vsl,qsl]=(ps*d1s[h]).astype(bf)
        return g
    lax.fori_loop(0,at.nq,block,0)
    lanes=iota((128,2*W),1)
    def turn(j,c):
        jsl=pl.ds(al(j*128,128),128)
        x=jnp.where(j<groups,dkv[jsl,:],0.0)
        dkvt[:,jsl]=jnp.where(lanes<W,x*LN2,x).astype(bf).T
        return c
    lax.fori_loop(0,groups+3,turn,0)
    deep=iota((384,256),0)
    def tgcopy(s):
        slot=lax.rem(s,2)
        return pltpu.make_async_copy(tbuf.at[slot],tg_hbm.at[pl.ds(al(s*256,256),256),:],tsem.at[slot])
    def place(s,c):
        ssl=pl.ds(al(s*256,256),256)
        r0=cnt_ref[at.begin+s]//128*128
        oh=(meta_ref[0:1,ssl]==deep+r0).astype(f32).astype(bf)
        g=dot(dkvt[:,pl.ds(al(r0,128),384)],oh,1,0)+dq_ref[W:3*W,ssl].astype(f32)
        dq_ref[W:3*W,ssl]=g.astype(bf)
        @pl.when(s>=2)
        def _(): tgcopy(s-2).wait()
        tbuf[lax.rem(s,2)]=dot(dq_ref[:,ssl],w_ref[...],0,1).astype(bf)
        tgcopy(s).start()
        return c
    lax.fori_loop(0,at.nd,place,0)
    tcopy.wait()
    grad_ref[...]=dot(dq_ref[...],tok_ref[...],1,0)
    for s in range(at.nd-2,at.nd): tgcopy(s).wait()

def back(cnt,datt,p,ot,inv,kaug,vaug,qkvt,meta,tok,w,H):
    L=qkvt.shape[1]; W=H*HEAD; E=tok.shape[1]
    V=pl.BlockSpec(memory_space=pltpu.VMEM); A=pl.BlockSpec(memory_space=pl.ANY)
    S=jax.ShapeDtypeStruct; M=pltpu.VMEM; D=pltpu.SemaphoreType.DMA
    return pl.pallas_call(functools.partial(back_kernel,L,H),
        out_shape=[S((L,E),bf),S((3*W,E),f32)],
        in_specs=[pl.BlockSpec(memory_space=pltpu.SMEM),V,A]+[V]*6+[A,V],
        out_specs=[A,V],
        scratch_shapes=[M((H,HEAD,L),bf),M((L,2*W),f32),M((2*W,L+384),bf),M((3*W,L),bf),M((SLOTS,H,KB,QB),bf),M((W,QB),f32),
            M((L,E),bf),M((2,256,E),bf),D((SLOTS,)),D((2,)),D((1,))],
        compiler_params=pltpu.CompilerParams(vmem_limit_bytes=56<<20))(cnt,datt,p,ot,inv,kaug,vaug,qkvt,meta,tok,w)
EPSILON=1e-05
def erf(x):
    x=jnp.clip(x,-3.832506856900711,3.832506856900711)
    x2=x*x
    top=0.00022905065861350646
    for c in (0.0034082910107109506,0.050955695062380861,0.18520832239976145,1.128379143519084): top=top*x2+c
    low=-1.1791602954361697e-7
    for c in (0.000023547966471313185,0.0010179625278914885,0.014070470171167667,0.11098505178285362,0.49746925110067538,1.0): low=low*x2+c
    return x*top/low
def norm(x):
    center=x-jnp.mean(x,-1,keepdims=True)
    inverse=lax.rsqrt(jnp.mean(center*center,-1,keepdims=True)+EPSILON)
    return center*inverse,inverse
def norm_back(e,n,inverse):
    return inverse*(e-jnp.mean(e,-1,keepdims=True)-n*jnp.mean(e*n,-1,keepdims=True))
def middle_kernel(a0_ref,a1_ref,tok_ref,cot_ref,wo_ref,wu_ref,wd_ref,gs_ref,out_ref,r1_ref,da_ref,go_ref,gu_ref,gd_ref,gg_ref):
    @pl.when(pl.program_id(0)==0)
    def _():
        for r in (go_ref,gu_ref,gd_ref,gg_ref): r[...]=jnp.zeros_like(r)
    P2=a0_ref.shape[0]
    att=jnp.concatenate([a0_ref[p] for p in range(P2)]+[a1_ref[p] for p in range(P2)],1)
    g0,g1,b0,b1=[gs_ref[r:r+1,:] for r in range(4)]
    n1,inv1=norm(tok_ref[...].astype(f32)+dot(att,wo_ref[...],1,0))
    first=(n1*g0+b0).astype(bf)
    hidden=dot(first,wu_ref[...],1,0)
    cdf=0.5*(1.0+erf(hidden*math.sqrt(0.5)))
    act=(hidden*cdf).astype(bf)
    slope=cdf+hidden*jnp.exp(-0.5*hidden*hidden)*(1.0/math.sqrt(2.0*math.pi))
    n2,inv2=norm(first.astype(f32)+dot(act,wd_ref[...],1,0))
    out_ref[...]=(n2*g1+b1).astype(bf)
    cot=cot_ref[...].astype(f32)
    r2=norm_back(cot*g1,n2,inv2)
    feed=r2.astype(bf)
    gd_ref[...]+=dot(act,feed,0,0)
    dh=(dot(feed,wd_ref[...],1,1)*slope).astype(bf)
    gu_ref[...]+=dot(first,dh,0,0)
    df=r2+dot(dh,wu_ref[...],1,1)
    r1=norm_back(df*g0,n1,inv1)
    r1_ref[...]=r1
    db=r1.astype(bf)
    go_ref[...]+=dot(att,db,0,0)
    da=dot(db,wo_ref[...],1,1).astype(bf)
    for p in range(2*P2): da_ref[p]=da[:,p*128:(p+1)*128]
    gg_ref[0:1,:]+=jnp.sum(df*n1,0,keepdims=True)
    gg_ref[1:2,:]+=jnp.sum(cot*n2,0,keepdims=True)
    gg_ref[2:3,:]+=jnp.sum(df,0,keepdims=True)
    gg_ref[3:4,:]+=jnp.sum(cot,0,keepdims=True)

def middle(a0,a1,tok,cot,wo,wu,wd,gs):
    P2,N,_=a0.shape; D=tok.shape[1]; F=wu.shape[1]
    T=max(t for t in (256,192,128,64,32,16) if N%t==0)
    tile=pl.BlockSpec((T,D),lambda i:(i,0))
    def pairs(k): return pl.BlockSpec((k,T,128),lambda i:(0,i,0))
    def whole(s): return pl.BlockSpec(s,lambda i:(0,)*len(s))
    return pl.pallas_call(middle_kernel,grid=(N//T,),
        in_specs=[pairs(P2),pairs(P2),tile,tile,whole((D,D)),whole((D,F)),whole((F,D)),whole((8,D))],
        out_specs=[tile,tile,pairs(2*P2),whole((D,D)),whole((D,F)),whole((F,D)),whole((8,D))],
        out_shape=[jax.ShapeDtypeStruct((N,D),bf),jax.ShapeDtypeStruct((N,D),f32),jax.ShapeDtypeStruct((2*P2,N,128),bf),
            jax.ShapeDtypeStruct((D,D),f32),jax.ShapeDtypeStruct((D,F),f32),jax.ShapeDtypeStruct((F,D),f32),jax.ShapeDtypeStruct((8,D),f32)],
        compiler_params=pltpu.CompilerParams(vmem_limit_bytes=60<<20))(a0,a1,tok,cot,wo,wu,wd,gs)
MESH=pl.DeviceIdType.MESH
class Net:
    def __init__(self,Z):
        dp=lax.axis_index("dp"); blk=lax.axis_index("blk")
        self.Z=Z; self.z=dp//2; self.y=dp%2; self.j=blk//2; self.c=blk%2
        self.sent=[]
    def at(self,z=None,y=None,j=None,c=None):
        z=self.z if z is None else z; y=self.y if y is None else y; j=self.j if j is None else j; c=self.c if c is None else c
        return (z*2+y,j*2+c)
    def greet(self):
        barrier=pltpu.get_barrier_semaphore()
        def signal(d): pl.semaphore_signal(barrier,inc=1,device_id=d,device_id_type=MESH)
        signal(self.at(j=1-self.j)); signal(self.at(y=1-self.y)); signal(self.at(c=1-self.c))
        @pl.when(self.z>0)
        def _(): signal(self.at(z=self.z-1))
        @pl.when(self.z<self.Z-1)
        def _(): signal(self.at(z=self.z+1))
        pl.semaphore_wait(barrier,3+(self.z>0).astype(jnp.int32)+(self.z<self.Z-1).astype(jnp.int32))
    def copy(self,src,dst,ssem,rsem,device):
        return pltpu.make_async_remote_copy(src_ref=src,dst_ref=dst,send_sem=ssem,recv_sem=rsem,device_id=device,device_id_type=MESH)
    def send(self,src,dst,ssem,rsem,device,when=None):
        c=self.copy(src,dst,ssem,rsem,device)
        if when is None: c.start()
        else: pl.when(when)(c.start)
        self.sent.append((c,when))
    def drain(self):
        for c,when in self.sent:
            if when is None: c.wait_send()
            else: pl.when(when)(c.wait_send)

def gather_kernel(Z,block,E,W,waves,rows,tok_hbm,info_ref,pack_ref,tok_out,info_out,wall_out,wmine_out,qkvt_out,
                  tokb,infob,wall,wt,qkvt,lsem,qsem,xs,xr,zs,zr,ys,yr,cs,cr,ts,tr,iss,isr):
    net=Net(Z); z,y,j,c=net.z,net.y,net.j,net.c
    NCH=block//rows; D=E
    sib=net.at(c=1-c); xd=net.at(j=1-j); yd=net.at(y=1-y)
    mine=pltpu.make_async_copy(tok_hbm.at[j],tokb.at[j,c],lsem.at[0]); mine.start()
    wall[z,y,j,c]=pack_ref[...]
    infob[j,c]=info_ref[j]
    net.greet()
    NW=len(waves)
    cut=[pl.ds(a,b-a) for a,b in waves]
    for w in range(NW): net.send(pack_ref.at[:,cut[w]],wall.at[z,y,j,c,:,cut[w]],xs.at[w],xr.at[w],xd)
    net.send(info_ref.at[1-j],infob.at[j,c],iss.at[0],isr.at[0],xd)
    net.send(info_ref.at[j],infob.at[j,c],iss.at[1],isr.at[1],sib)
    def chunk(k): return pl.ds(k*rows,rows)
    for k in range(NCH):
        net.send(tok_hbm.at[1-j,chunk(k)],tokb.at[j,c,chunk(k)],ts.at[0,k],tr.at[0,k],xd)
        net.send(tok_hbm.at[j,chunk(k)],tokb.at[j,c,chunk(k)],ts.at[1,k],tr.at[1,k],sib)
    def piece(w,o,y_): return wall.at[o,y_,:,c,:,cut[w]]
    def arrived(w,o,y_,sem): pltpu.make_async_copy(piece(w,o,y_),piece(w,o,y_),sem).wait()
    def spread(w,o,when=None):
        net.send(piece(w,o,y),piece(w,o,y),ys.at[w,o],yr.at[w,o],yd,when)
        net.send(piece(w,o,y),piece(w,o,y),cs.at[w,0,o],cr.at[w,0,o],sib,when)
    def across(w,o,when=None):
        def go(): arrived(w,o,1-y,yr.at[w,o])
        go() if when is None else pl.when(when)(go)
        net.send(piece(w,o,1-y),piece(w,o,1-y),cs.at[w,1,o],cr.at[w,1,o],sib,when)
    def step(w,k):
        if k==0:
            pltpu.make_async_copy(wall.at[z,y,1-j,c,:,cut[w]],wall.at[z,y,1-j,c,:,cut[w]],xr.at[w]).wait()
            net.send(piece(w,z,y),piece(w,z,y),zs.at[w,0,0],zr.at[w,z],net.at(z=z+1),z<Z-1)
            net.send(piece(w,z,y),piece(w,z,y),zs.at[w,1,0],zr.at[w,z],net.at(z=z-1),z>0)
            spread(w,z)
            return
        for d,(o,here,more) in enumerate(((z-k,z-k>=0,(z-k>=0)&(z<Z-1)),(z+k,z+k<Z,(z+k<Z)&(z>0)))):
            at=jnp.clip(o,0,Z-1)
            @pl.when(here)
            def _(): arrived(w,at,y,zr.at[w,at])
            net.send(piece(w,at,y),piece(w,at,y),zs.at[w,d,k],zr.at[w,at],net.at(z=z+1 if d==0 else z-1),more)
            spread(w,at,here)
        if k==1: across(w,z)
        else:
            for o,here in ((z-k+1,z-k+1>=0),(z+k-1,z+k-1<Z)): across(w,jnp.clip(o,0,Z-1),here)
    def finish(w):
        for o,here in ((z-Z+1,z-Z+1>=0),(z+Z-1,z+Z-1<Z)): across(w,jnp.clip(o,0,Z-1),here)
    def from_sibling(w):
        for o in range(Z):
            for q in range(2):
                ref=wall.at[o,y if q==0 else 1-y,:,1-c,:,cut[w]]
                pltpu.make_async_copy(ref,ref,cr.at[w,q,o]).wait()
    def project(jj,cc,k):
        g=(jj*2+cc)*NCH+k
        r=dot(wt[...],tokb[jj,cc,chunk(k),:],1,1)
        col=pl.ds(al(g*rows,rows),rows)
        qkvt[:,col]=jnp.concatenate([r[:W]*(math.log2(math.e)/8),r[W:]],0).astype(bf)
        out=pltpu.make_async_copy(qkvt.at[:,col],qkvt_out.at[:,col],qsem.at[g])
        out.start()
        return out
    for k in range(Z):
        step(0,k)
        if k>=1: step(1,k-1)
    finish(0)
    from_sibling(0)
    keep=[]
    parts=[]
    for t in range(3):
        cols=pl.ds(al(t*2*W+c*W,W),W)
        part=wall[:,:,:,:,:,cols].reshape(D,W)
        wt[t*W:(t+1)*W,:]=part.T
        parts.append(part)
    wmine_out[...]=jnp.concatenate(parts,1)
    mine.wait()
    for k in range(NCH): keep.append(project(j,c,k))
    step(1,Z-1)
    for k in range(NCH):
        ref=tokb.at[j,1-c,chunk(k)]
        pltpu.make_async_copy(ref,ref,tr.at[1,k]).wait()
        keep.append(project(j,1-c,k))
    finish(1)
    for k in range(NCH):
        ref=tokb.at[1-j,c,chunk(k)]
        pltpu.make_async_copy(ref,ref,tr.at[0,k]).wait()
        net.send(ref,ref,ts.at[2,k],tr.at[2,k],sib)
        keep.append(project(1-j,c,k))
        if k==0:
            pltpu.make_async_copy(infob.at[1-j,c],infob.at[1-j,c],isr.at[0]).wait()
            net.send(infob.at[1-j,c],infob.at[1-j,c],iss.at[2],isr.at[2],sib)
    from_sibling(1)
    outw=pltpu.make_async_copy(wall,wall_out,lsem.at[1]); outw.start()
    for k in range(NCH):
        ref=tokb.at[1-j,1-c,chunk(k)]
        pltpu.make_async_copy(ref,ref,tr.at[2,k]).wait()
        keep.append(project(1-j,1-c,k))
    outt=pltpu.make_async_copy(tokb,tok_out,lsem.at[2]); outt.start()
    pltpu.make_async_copy(infob.at[j,1-c],infob.at[j,1-c],isr.at[1]).wait()
    pltpu.make_async_copy(infob.at[1-j,1-c],infob.at[1-j,1-c],isr.at[2]).wait()
    info_out[...]=infob[...]
    net.drain()
    for x in keep: x.wait()
    outw.wait(); outt.wait()

def gather(tok,info,pack,Z,W):
    _,block,E=tok.shape; R,C=pack.shape
    rows=256; NCH=block//rows; L=4*block
    V=pl.BlockSpec(memory_space=pltpu.VMEM); A=pl.BlockSpec(memory_space=pl.ANY)
    S=jax.ShapeDtypeStruct; M=pltpu.VMEM; D=pltpu.SemaphoreType.DMA
    waves=((0,6*W),(6*W,C))
    return pl.pallas_call(functools.partial(gather_kernel,Z,block,E,W,waves,rows),
        out_shape=[S((2,2,block,E),bf),S((2,2,1,block),jnp.int32),S((Z,2,2,2,R,C),bf),S((E,3*W),bf),S((3*W,L),bf)],
        in_specs=[A,V,V],out_specs=[A,V,A,V,A],
        scratch_shapes=[M((2,2,block,E),bf),M((2,2,1,block),jnp.int32),M((Z,2,2,2,R,C),bf),M((3*W,E),bf),M((3*W,L),bf),
            D((3,)),D((4*NCH,)),D((2,)),D((2,)),D((2,2,Z)),D((2,Z)),D((2,Z)),D((2,Z)),D((2,2,Z)),D((2,2,Z)),D((3,NCH)),D((3,NCH)),D((3,)),D((3,))],
        compiler_params=pltpu.CompilerParams(collective_id=0,has_side_effects=True,vmem_limit_bytes=48<<20))(tok,info,pack)
def reduce_kernel(Z,block,E,W,F,rows,cuts,tg_hbm,r1_hbm,gq_ref,go_ref,gu_ref,gd_ref,gg_ref,tok_out,grad_out,
                  own,r1,tgr,tgs,ob,s0,r0,g0,s1,r1b,su,ru,sd,rd,sx,rx,
                  lsem,ts,tr,xs,xr,cs,cr,ys,yr,us,ur,ds,dr,fs,fr):
    net=Net(Z); z,y,j,c=net.z,net.y,net.j,net.c
    NCH=block//rows; C=g0.shape[-1]; Q=3*W; NW=len(cuts)
    sib=net.at(c=1-c); xd=net.at(j=1-j); yd=net.at(y=1-y)
    loads=[pltpu.make_async_copy(tg_hbm.at[:,c],own,lsem.at[0]),pltpu.make_async_copy(r1_hbm,r1,lsem.at[1])]
    for x in loads: x.start()
    net.greet()
    def chunk(k): return pl.ds(k*rows,rows)
    def landed(ref,sem): pltpu.make_async_copy(ref,ref,sem).wait()
    for t in range(2):
        jj=1-j if t==0 else j
        for k in range(NCH): net.send(tg_hbm.at[jj,1-c,chunk(k)],tgr.at[jj,chunk(k)],ts.at[t,k],tr.at[t,k],sib)
    ggt=jnp.concatenate([gg_ref[...],jnp.zeros((120,E),f32)],0).T
    def split(x,n): return x.reshape(Z,2,2,2,16,n)
    s0[:,:,:,:,0:Q]=split(gq_ref[...],Q)[:,:,:,0]
    @pl.when(c==0)
    def _(): s0[:,:,:,:,0:Q]=split(gq_ref[...],Q)[:,:,:,1]
    at=Q
    places=[]
    for x in (go_ref[...],gu_ref[...],gd_ref[...],ggt):
        n=x.shape[1]
        v=split(x,n)
        @pl.when(c==0)
        def _(): s0[:,:,:,:,at:at+n]=v[:,:,:,1].astype(bf)
        @pl.when(c==1)
        def _(): s0[:,:,:,:,at:at+n]=v[:,:,:,0].astype(bf)
        places.append((v,at,n))
        at+=n
    net.send(s0.at[:,:,:,:,0:Q],r0.at[:,:,:,:,0:Q],cs.at[0],cr.at[0],sib)
    net.send(s0.at[:,:,:,:,Q:at],r0.at[:,:,:,:,Q:at],cs.at[1],cr.at[1],sib)
    for x in loads: x.wait()
    def total(jj,k): return (own[jj,chunk(k),:].astype(f32)+tgr[jj,chunk(k),:].astype(f32)+r1[jj,chunk(k),:].astype(f32)).astype(bf)
    for k in range(NCH):
        landed(tgr.at[1-j,chunk(k)],tr.at[0,k])
        tgs[chunk(k),:]=total(1-j,k)
        net.send(tgs.at[chunk(k)],ob.at[j,chunk(k)],xs.at[k],xr.at[k],xd)
    landed(r0.at[:,:,:,:,0:Q],cr.at[0])
    landed(r0.at[:,:,:,:,Q:at],cr.at[1])
    mine=split(gq_ref[...],Q)
    for cc in range(2):
        @pl.when(c==cc)
        def _():
            for t in range(3):
                for other in range(2):
                    src=mine[:,:,:,cc,:,t*W:(t+1)*W] if other==cc else r0[:,:,:,:,t*W:(t+1)*W]
                    g0[:,:,:,:,(2*t+other)*W:(2*t+other+1)*W]=src.astype(f32)
            for v,a,n in places:
                g0[:,:,:,:,Q+a:Q+a+n]=v[:,:,:,cc]+r0[:,:,:,:,a:a+n].astype(f32)
    cut=[pl.ds(a,b-a) for a,b in cuts]
    for w in range(NW):
        s1[:,:,:,cut[w]]=g0[:,1-y,:,:,cut[w]].astype(bf)
        net.send(s1.at[:,:,:,cut[w]],r1b.at[:,:,:,cut[w]],ys.at[w],yr.at[w],yd)
    for k in range(NCH):
        landed(tgr.at[j,chunk(k)],tr.at[1,k])
        ob[j,chunk(k),:]=total(j,k)
    def lines(w):
        landed(r1b.at[:,:,:,cut[w]],yr.at[w])
        def base(o): return g0[o,y,:,:,cut[w]]+r1b[o,:,:,cut[w]].astype(f32)
        for t in range(Z-1):
            up=Z-1-t
            @pl.when(z<up)
            def _():
                @pl.when(z>0)
                def _():
                    landed(ru.at[up,:,:,cut[w]],ur.at[w,up])
                    su[up,:,:,cut[w]]=(base(up)+ru[up,:,:,cut[w]].astype(f32)).astype(bf)
                @pl.when(z==0)
                def _(): su[up,:,:,cut[w]]=base(up).astype(bf)
            net.send(su.at[up,:,:,cut[w]],ru.at[up,:,:,cut[w]],us.at[w,up],ur.at[w,up],net.at(z=z+1),z<up)
            down=t
            @pl.when(z>down)
            def _():
                @pl.when(z<Z-1)
                def _():
                    landed(rd.at[down,:,:,cut[w]],dr.at[w,down])
                    sd[down,:,:,cut[w]]=(base(down)+rd[down,:,:,cut[w]].astype(f32)).astype(bf)
                @pl.when(z==Z-1)
                def _(): sd[down,:,:,cut[w]]=base(down).astype(bf)
            net.send(sd.at[down,:,:,cut[w]],rd.at[down,:,:,cut[w]],ds.at[w,down],dr.at[w,down],net.at(z=z-1),z>down)
        for o in range(Z):
            @pl.when(z==o)
            def _():
                sum_=base(o)
                if o>0:
                    landed(ru.at[o,:,:,cut[w]],ur.at[w,o])
                    sum_=sum_+ru[o,:,:,cut[w]].astype(f32)
                if o<Z-1:
                    landed(rd.at[o,:,:,cut[w]],dr.at[w,o])
                    sum_=sum_+rd[o,:,:,cut[w]].astype(f32)
                g0[o,y,:,:,cut[w]]=sum_
        sx[:,cut[w]]=g0[z,y,1-j,:,cut[w]].astype(bf)
        net.send(sx.at[:,cut[w]],rx.at[:,cut[w]],fs.at[w],fr.at[w],xd)
    for w in range(NW): lines(w)
    for w in range(NW):
        landed(rx.at[:,cut[w]],fr.at[w])
        grad_out[:,cut[w]]=g0[z,y,j,:,cut[w]]+rx[:,cut[w]].astype(f32)
    for k in range(NCH): landed(ob.at[1-j,chunk(k)],xr.at[k])
    last=pltpu.make_async_copy(ob,tok_out,lsem.at[2])
    last.start()
    net.drain()
    last.wait()

def reduce(tg,r1,gq,go,gu,gd,gg,Z,W):
    _,_,block,E=tg.shape; F=gu.shape[1]; C=6*W+2*F+E+128; Q=3*W
    rows=256; NCH=block//rows
    steps=C//128; n=4
    edges=[128*((steps*t+n-1)//n) for t in range(n+1)]
    cuts=tuple(zip(edges[:-1],edges[1:])); NW=len(cuts)
    V=pl.BlockSpec(memory_space=pltpu.VMEM); A=pl.BlockSpec(memory_space=pl.ANY)
    S=jax.ShapeDtypeStruct; M=pltpu.VMEM; D=pltpu.SemaphoreType.DMA
    return pl.pallas_call(functools.partial(reduce_kernel,Z,block,E,W,F,rows,cuts),
        out_shape=[S((2,block,E),bf),S((16,C),f32)],
        in_specs=[A,A,V,V,V,V,V],out_specs=[A,V],
        scratch_shapes=[M((2,block,E),bf),M((2,block,E),r1.dtype),M((2,block,E),bf),M((block,E),bf),M((2,block,E),bf),
            M((Z,2,2,16,C-Q),bf),M((Z,2,2,16,C-Q),bf),M((Z,2,2,16,C),f32),M((Z,2,16,C),bf),M((Z,2,16,C),bf),
            M((Z,2,16,C),bf),M((Z,2,16,C),bf),M((Z,2,16,C),bf),M((Z,2,16,C),bf),M((16,C),bf),M((16,C),bf),
            D((3,)),D((2,NCH)),D((2,NCH)),D((NCH,)),D((NCH,)),D((2,)),D((2,)),D((NW,)),D((NW,)),D((NW,Z)),D((NW,Z)),D((NW,Z)),D((NW,Z)),D((NW,)),D((NW,))],
        compiler_params=pltpu.CompilerParams(collective_id=1,has_side_effects=True,vmem_limit_bytes=56<<20))(tg,r1,gq,go,gu,gd,gg)
def shards(tokens,cotangent,segments,padding,known,w_qkv,w_out,w_up,w_down,norm_gains,norm_shifts):
    micro,rows,block,D=tokens.shape
    J=lax.axis_size("blk")//2; dps=lax.axis_size("dp")
    units=micro*rows
    assert units==J
    H=HEADS//2; W=H*HEAD; L=2*J*block; F=w_up.shape[1]
    quick=J==2 and dps%2==0 and w_qkv.shape[0]%16==0 and block%256==0
    me=lax.axis_index("blk"); chip=me//2; core=me%2
    def to_chip(s): return [(2*a+c,2*((a+s)%J)+c) for a in range(J) for c in range(2)]
    swap=[(b,b^1) for b in range(2*J)]
    def other(x): return lax.ppermute(x,"blk",swap)
    def scatter_units(x):
        got=[]
        for s in range(J):
            mine=lax.dynamic_index_in_dim(x,(chip+s)%J,0,keepdims=False)
            got.append(mine if s==0 else lax.ppermute(mine,"blk",to_chip(s)))
        return jnp.stack([lax.select_n((chip-j)%J,*got) if J==2 else lax.dynamic_index_in_dim(jnp.stack(got),(chip-j)%J,0,keepdims=False) for j in range(J)])
    def both(mine,his):
        return jnp.stack([jnp.where(core==0,mine,his),jnp.where(core==0,his,mine)],1)
    def part(x,axis,index): return lax.dynamic_index_in_dim(x,index,axis,keepdims=False)
    flat=lambda x:x.reshape((units,)+x.shape[2:])
    info=flat(segments*4+padding*2+known)
    if quick:
        gs=jnp.pad(jnp.concatenate([norm_gains,norm_shifts],0),((0,12),(0,112)))
        pack=jnp.concatenate([w_qkv,w_out,w_up,w_down,gs],1)
        all_tok,all_info,wall,w_mine,qkvt=gather(flat(tokens),info[:,None,:],pack,dps//2,W)
        own_tok=part(all_tok,1,core); all_tok=all_tok.reshape(L,D); all_info=all_info.reshape(L)
        N=lax.axis_size("blk")*dps
        wall=wall.reshape(N,16,-1)
        gs=wall[:,:4,6*W+2*D+F:6*W+2*D+F+16].transpose(1,0,2).reshape(4,D).astype(f32)
        wall=wall.reshape(D,-1)
        full_out,full_up,full_down=wall[:,6*W:6*W+D],wall[:,6*W+D:6*W+D+F],wall[:,6*W+D+F:6*W+2*D+F]
    else:
        own_info=scatter_units(info); all_info=both(own_info,other(own_info)).reshape(L)
        own_tok=scatter_units(flat(tokens)); all_tok=both(own_tok,other(own_tok)).reshape(L,D)
        full_qkv,full_out,full_up,full_down=[lax.all_gather(w,("dp","blk"),axis=0,tiled=True) for w in (w_qkv,w_out,w_up,w_down)]
        gs=lax.all_gather(jnp.concatenate([norm_gains,norm_shifts],0),("dp","blk"),axis=1,tiled=True).astype(f32)
        w_mine=part(full_qkv.reshape(D,3,2,W),2,core).reshape(D,3*W)
        scale=jnp.where(jnp.arange(3*W)<W,math.log2(math.e)/8,1.0).astype(f32)
        qkvt=(jnp.einsum("ld,de->el",all_tok,w_mine,preferred_element_type=f32)*scale[:,None]).astype(bf)
    gs=jnp.concatenate([gs,jnp.zeros_like(gs)],0)
    qkvt,cotangent=lax.optimization_barrier((qkvt,cotangent))
    own_cot=scatter_units(flat(cotangent)).reshape(L//2,D)
    cnt,codet,meta=flags(all_info//4,(all_info//2)%2,all_info%2)
    p,att,ot,inv,kaug,vaug=attend(cnt,qkvt,codet,meta,H)
    att=att.reshape(H//2,J,2,block,128)
    mine=part(att,2,core).reshape(H//2,J*block,128); his=other(part(att,2,1-core)).reshape(H//2,J*block,128)
    a0=jnp.where(core==0,mine,his); a1=jnp.where(core==0,his,mine)
    out,r1,da,go,gu,gd,gg=middle(a0,a1,own_tok.reshape(L//2,D),own_cot,full_out,full_up,full_down,gs)
    da=da.reshape(2,H//2,J,block,128)
    dmine=part(da,0,core); dhis=other(part(da,0,1-core))
    datt=jnp.stack([jnp.where(core==0,dmine,dhis),jnp.where(core==0,dhis,dmine)],2).reshape(H//2,L,128)
    tg,gq=back(cnt,datt,p,ot,inv,kaug,vaug,qkvt,meta,all_tok,w_mine,H)
    tg=tg.reshape(J,2,block,D)
    layer_out=scatter_units(out.reshape(J,block,D)).reshape(tokens.shape)
    a,b,e=6*W,6*W+D,6*W+D+F
    if quick:
        token_grad,grads=reduce(tg,r1.reshape(J,block,D),gq.T.astype(bf),go,gu,gd,gg,dps//2,W)
        token_grad=token_grad.reshape(tokens.shape)
        gg=grads[:,e+D:e+D+4].T
        return (layer_out,token_grad,grads[:,:a],grads[:,a:b],grads[:,b:e],grads[:,e:e+D],gg[:2],gg[2:])
    own_tg=(part(tg,1,core).astype(f32)+other(part(tg,1,1-core)).astype(f32)+r1.reshape(J,block,D)).astype(bf)
    token_grad=scatter_units(own_tg).reshape(tokens.shape)
    gq=gq.T.reshape(D,3,1,W)
    gq=jnp.where(core==0,jnp.concatenate([gq,jnp.zeros_like(gq)],2),jnp.concatenate([jnp.zeros_like(gq),gq],2)).reshape(D,6*W)
    grads=lax.psum_scatter(jnp.concatenate([gq,go,gu,gd],1),("dp","blk"),scatter_dimension=0,tiled=True)
    gg=lax.psum_scatter(gg[:4],("dp","blk"),scatter_dimension=1,tiled=True)
    return (layer_out,token_grad,grads[:,:a],grads[:,a:b],grads[:,b:e],grads[:,e:],gg[:2],gg[2:])

def solution(mesh):
    in_specs = (
        P(None, "dp", "blk", None),
        P(None, "dp", "blk", None),
        P(None, "dp", "blk"),
        P(None, "dp", "blk"),
        P(None, "dp", "blk"),
        P(("dp", "blk"), None),
        P(("dp", "blk"), None),
        P(("dp", "blk"), None),
        P(("dp", "blk"), None),
        P(None, ("dp", "blk")),
        P(None, ("dp", "blk")),
    )
    out_specs = (
        P(None, "dp", "blk", None),
        P(None, "dp", "blk", None),
        P(("dp", "blk"), None),
        P(("dp", "blk"), None),
        P(("dp", "blk"), None),
        P(("dp", "blk"), None),
        P(None, ("dp", "blk")),
        P(None, ("dp", "blk")),
    )
    return jax.shard_map(shards, mesh=mesh, in_specs=in_specs, out_specs=out_specs, check_vma=False)
```

```python
import functools, math
import jax, jax.numpy as jnp
from jax import lax
from jax.experimental import pallas as pl
from jax.experimental.pallas import tpu as pltpu
from jax.sharding import PartitionSpec as P

HEADS = 8
bf=jnp.bfloat16; f32=jnp.float32
HEAD=64
QB=512
KB=512
SRC=512
SAFE=60.0
CODE=16
VMEM=(64<<20)-(128<<10)
SLOTS=3
def dot(a,b,ca,cb): return lax.dot_general(a,b,(((ca,),(cb,)),((),())),preferred_element_type=f32)
def al(x,n): return pl.multiple_of(x,n)
def iota(shape,axis): return lax.broadcasted_iota(jnp.int32,shape,axis)

def begin(base_ref,b):
    return base_ref[b,0]

def window(win_ref,i):
    start=win_ref[i,0]//128*128
    groups=(win_ref[8+i,0]-start+127)//128
    full=(groups-1)//(KB//128)
    return start,full,groups-full*(KB//128),groups

def by_piece(first,full,rest,g,fn):
    def body(j,g):
        fn(al(first+j*KB,128),KB,g)
        return g+1
    g=lax.fori_loop(0,full,body,g)
    for r in range(1,KB//128+1):
        @pl.when(rest==r)
        def _(): fn(al(first+full*KB,128),r*128,g)
    return g+1

def attend_kernel(L,H,base_ref,win_ref,qkvt_ref,codet_ref,meta_ref,p_hbm,att_hbm,ot_hbm,inv_ref,kaug_hbm,vaug_hbm,
                  kaug_ref,vaug_ref,kvt,vct,acc,pbuf,obuf,abuf,top_ref,psem,osem,asem,ksem):
    W=H*HEAD; nq=L//QB
    total=begin(base_ref,L//256)
    for h in range(H):
        kvt[h*128:h*128+HEAD,:]=qkvt_ref[W+h*HEAD:W+(h+1)*HEAD,:]
        kvt[h*128+HEAD:h*128+HEAD+CODE,:]=codet_ref[...]
        kvt[h*128+HEAD+CODE:(h+1)*128,:]=jnp.zeros((HEAD-CODE,L),bf)
    lane=iota((256,128),1)
    down=iota((256,SRC),0)
    def dest(d,c):
        def src(s,a):
            ssl=pl.ds(al(s*SRC,SRC),SRC)
            oh=(meta_ref[0:1,ssl]==(down+d*256)).astype(f32).astype(bf)
            ka=a[0]+dot(oh,kvt[:,ssl],1,1)
            va=a[1]+dot(oh,qkvt_ref[2*W:3*W,ssl],1,1)
            return ka,va
        lo=hi=0
        for t in range(L//SRC):
            lo=lo+(begin(base_ref,(t+1)*(SRC//256))<=d*256).astype(jnp.int32)
            hi=hi+(begin(base_ref,t*(SRC//256))<d*256+256).astype(jnp.int32)
        ka,va=lax.fori_loop(lo,hi,src,(jnp.zeros((256,H*128),f32),jnp.zeros((256,W),f32)))
        dsl=pl.ds(al(d*256,256),256)
        vat=va.T
        for h in range(H):
            k1=ka[:,h*128:(h+1)*128]
            kaug_ref[h,dsl,:]=jnp.where(lane==HEAD+10,-2560.0,k1).astype(bf)
            pair=va[:,(h//2)*128:(h//2+1)*128]
            if h%2: pair=jnp.concatenate([pair[:,HEAD:],pair[:,:HEAD]],1)
            vaug_ref[h,dsl,:]=jnp.where(lane<HEAD,pair,jnp.where(lane<HEAD+3,-1.0,0.0)).astype(bf)
            vct[h,:HEAD,dsl]=vat[h*HEAD:(h+1)*HEAD,:].astype(bf)
            vct[h,HEAD:HEAD+16,dsl]=jnp.ones((16,256),bf)
        return c
    lax.fori_loop(0,(total+255)//256,dest,0)
    keep=[pltpu.make_async_copy(kaug_ref,kaug_hbm,ksem.at[0]),pltpu.make_async_copy(vaug_ref,vaug_hbm,ksem.at[1])]
    for x in keep: x.start()
    bound=jnp.float32(0)
    for h in range(H):
        q=qkvt_ref[h*HEAD:(h+1)*HEAD,:].astype(f32); k=qkvt_ref[W+h*HEAD:W+(h+1)*HEAD,:].astype(f32)
        bound=jnp.maximum(bound,jnp.max(jnp.sum(q*q,0,keepdims=True))*jnp.max(jnp.sum(k*k,0,keepdims=True)))
    safe=bound<SAFE*SAFE

    def pcopy(g):
        slot=lax.rem(g,SLOTS)
        return pltpu.make_async_copy(pbuf.at[slot],p_hbm.at[g],psem.at[slot])
    def ocopy(i):
        slot=lax.rem(i,2)
        return pltpu.make_async_copy(obuf.at[slot],ot_hbm.at[i],osem.at[slot])
    def acopy(i):
        slot=lax.rem(i,2)
        return pltpu.make_async_copy(abuf.at[slot],att_hbm.at[:,pl.ds(al(i*QB,QB),QB),:],asem.at[slot])
    def block(i,g):
        slot=lax.rem(i,2)
        qsl=pl.ds(al(i*QB,QB),QB)
        first,full,rest,groups=window(win_ref,i)
        qa=[jnp.concatenate([qkvt_ref[h*HEAD:(h+1)*HEAD,qsl],codet_ref[:,qsl],jnp.zeros((HEAD-CODE,QB),bf)],0) for h in range(H)]
        own=meta_ref[1:2,qsl]>0
        sself=[]
        for h in range(H):
            x=qkvt_ref[h*HEAD:(h+1)*HEAD,qsl].astype(f32)*qkvt_ref[W+h*HEAD:W+(h+1)*HEAD,qsl].astype(f32)
            sself.append(jnp.where(own,jnp.sum(x,0,keepdims=True),-1e30))
        acc[...]=jnp.zeros_like(acc)
        top_ref[...]=jnp.zeros_like(top_ref)
        row=iota((128,QB),0)
        def strict(h,osl):
            k=kaug_ref[h,osl,:]
            x=qa[h].astype(f32)
            plain=dot(k,jnp.where(row<HEAD,x,0.0).astype(bf),1,0)
            return jnp.where(dot(k,jnp.where(row<HEAD,0.0,x).astype(bf),1,0)>-1.0,plain,-1e30)
        @pl.when(jnp.logical_not(safe))
        def _():
            for h in range(H):
                def more(j,m): return jnp.maximum(m,jnp.max(strict(h,pl.ds(al(first+j*128,128),128)),0,keepdims=True))
                top_ref[h:h+1,:]=lax.fori_loop(0,groups,more,sself[h])
        def piece(off,size,g):
            ps=lax.rem(g,SLOTS)
            osl=pl.ds(off,size)
            @pl.when(g>=SLOTS)
            def _(): pcopy(g-SLOTS).wait()
            @pl.when(safe)
            def _():
                keepp=[]
                for h in range(H):
                    p=jnp.exp2(dot(kaug_ref[h,osl,:],qa[h],1,0)).astype(bf)
                    pbuf[ps,h,:size,:]=p
                    keepp.append(p)
                for h in range(H): acc[h]+=dot(vct[h,:,osl],keepp[h],1,0)
            @pl.when(jnp.logical_not(safe))
            def _():
                for h in range(H):
                    def put(j,c):
                        jsl=pl.ds(al(off+j*128,128),128)
                        p=jnp.exp2(strict(h,jsl)-top_ref[h:h+1,:]).astype(bf)
                        pbuf[ps,h,pl.ds(al(j*128,128),128),:]=p
                        acc[h]+=dot(vct[h,:,jsl],p,1,0)
                        return c
                    lax.fori_loop(0,size//128,put,0)
            pcopy(g).start()
        g=by_piece(first,full,rest,g,piece)
        @pl.when(i>=2)
        def _(): ocopy(i-2).wait(); acopy(i-2).wait()
        for h in range(H):
            ps=jnp.exp2(sself[h]-top_ref[h:h+1,:])
            inv=1.0/(acc[h,HEAD:HEAD+1,:]+ps)
            obuf[slot,h*HEAD:(h+1)*HEAD,:]=(acc[h,:HEAD,:]+ps*qkvt_ref[2*W+h*HEAD:2*W+(h+1)*HEAD,qsl].astype(f32))*inv
            inv_ref[h,0:1,qsl]=inv
            inv_ref[h,1:2,qsl]=ps
        for hp in range(H//2): abuf[slot,hp]=obuf[slot,hp*128:(hp+1)*128,:].T.astype(bf)
        ocopy(i).start(); acopy(i).start()
        return g
    g=lax.fori_loop(0,nq,block,0)
    for s in range(SLOTS):
        last=g-1-s
        @pl.when(last>=0)
        def _(): pcopy(last).wait()
    for i in range(max(nq-2,0),nq): ocopy(i).wait(); acopy(i).wait()
    for x in keep: x.wait()

def attend(base,win,qkvt,codet,meta,H):
    L=qkvt.shape[1]; W=H*HEAD; nq=L//QB; cap=nq*(L//KB+1)
    V=pl.BlockSpec(memory_space=pltpu.VMEM); A=pl.BlockSpec(memory_space=pl.ANY)
    S=jax.ShapeDtypeStruct; M=pltpu.VMEM; D=pltpu.SemaphoreType.DMA
    return pl.pallas_call(functools.partial(attend_kernel,L,H),
        out_shape=[S((cap,H,KB,QB),bf),S((H//2,L,128),bf),S((nq,W,QB),f32),S((H,8,L),f32),S((H,L,128),bf),S((H,L,128),bf)],
        in_specs=[pl.BlockSpec(memory_space=pltpu.SMEM)]*2+[V,V,V],
        out_specs=[A,A,A,V,A,A],
        scratch_shapes=[M((H,L,128),bf),M((H,L,128),bf),M((H*128,L),bf),M((H,HEAD+16,L),bf),M((H,HEAD+16,QB),f32),M((SLOTS,H,KB,QB),bf),
            M((2,W,QB),f32),M((2,H//2,QB,128),bf),M((8,QB),f32),D((SLOTS,)),D((2,)),D((2,)),D((2,))],
        compiler_params=pltpu.CompilerParams(vmem_limit_bytes=VMEM))(base,win,qkvt,codet,meta)

def flags(row):
    L=row.shape[1]; nb=L//256; nq=L//QB
    seg=row//4
    pad=row//2-2*seg
    known=row-2*(row//2)
    use=(pad==0)&(known==1)
    usef=use.astype(f32)
    x=jnp.concatenate([usef[:,b*256:(b+1)*256] for b in range(nb)]+[jnp.zeros((16-nb,256),f32)],0)
    incl=dot(x.astype(bf),(iota((256,256),0)<=iota((256,256),1)).astype(f32).astype(bf),1,0)
    tot=jnp.broadcast_to(incl[:,255:256],(16,256)).astype(bf)
    base=dot((iota((16,16),0)>iota((16,16),1)).astype(f32).astype(bf),tot,1,0)
    rank=(incl+base).astype(jnp.int32)-1
    rank=jnp.concatenate([rank[b:b+1] for b in range(nb)],1)
    rank=jnp.where(use,rank,-1)
    own=((pad==0)&(known!=1)).astype(jnp.int32)
    bits=iota((CODE,L),0)
    bit=lax.shift_right_logical(jnp.broadcast_to(seg,(CODE,L)),jnp.minimum(bits,9))&1
    codet=jnp.where(bits<10,jnp.where(bit==1,16.0,-16.0),jnp.where(bits==10,1.0,0.0)).astype(bf)
    meta=jnp.concatenate([rank,own,jnp.zeros((6,L),jnp.int32)],0)
    def edge(at): return jnp.concatenate([seg[:,i*QB+at:i*QB+at+1] for i in range(nq)]+[jnp.zeros((8-nq,1),jnp.int32)],0)
    low=jnp.sum(jnp.where(seg<edge(0),usef,0.0),1,keepdims=True)
    high=jnp.sum(jnp.where(seg<=edge(QB-1),usef,0.0),1,keepdims=True)
    win=jnp.broadcast_to(jnp.concatenate([low,high],0),(16,128)).astype(jnp.int32)
    return base[:,:128].astype(jnp.int32),win,codet,meta
LN2=math.log(2.0)
def back_kernel(L,H,base_ref,win_ref,datt_ref,p_hbm,ot_ref,inv_ref,kaug_ref,vaug_ref,qkvt_ref,meta_ref,tok_hbm,w_ref,
                tg_hbm,grad_ref,kct,dkv,dkvt,dq_ref,pbuf,qacc,tok_ref,tbuf,psem,tsem,ksem):
    W=H*HEAD; nq=L//QB; nd=L//256
    total=begin(base_ref,nd); groups=(total+127)//128
    pieces=lax.fori_loop(0,nq,lambda i,s:s+window(win_ref,i)[1]+1,0)
    def pcopy(g):
        slot=lax.rem(g,SLOTS)
        return pltpu.make_async_copy(p_hbm.at[g],pbuf.at[slot],psem.at[slot])
    for s in range(SLOTS-1):
        @pl.when(s<pieces)
        def _(): pcopy(s).start()
    tcopy=pltpu.make_async_copy(tok_hbm,tok_ref,ksem.at[0])
    tcopy.start()
    def prep(j,c):
        jsl=pl.ds(al(j*128,128),128)
        for h in range(H): kct[h,:,jsl]=kaug_ref[h,jsl,:].T[:HEAD]
        dkv[jsl,:]=jnp.zeros((128,2*W),f32)
        return c
    lax.fori_loop(0,groups,prep,0)
    def block(i,g):
        qsl=pl.ds(al(i*QB,QB),QB)
        first,full,rest,_=window(win_ref,i)
        dt=jnp.concatenate([datt_ref[hp,qsl,:].astype(f32).T for hp in range(H//2)],0)
        prod=dt*ot_ref[i]
        daug=[];dz=[];qz=[];deltas=[];d1s=[]
        zero=jnp.zeros((HEAD,QB),bf)
        row=iota((16,QB),0)
        for h in range(H):
            hsl=slice(h*HEAD,(h+1)*HEAD)
            inv=inv_ref[h,0:1,qsl]
            delta=jnp.sum(prod[hsl],0,keepdims=True)*inv
            d1=dt[hsl]*inv
            low=d1.astype(bf)
            a=delta.astype(bf).astype(f32); b=(delta-a).astype(bf).astype(f32)
            extra=jnp.where(row==0,a,jnp.where(row==1,b,jnp.where(row==2,delta-a-b,0.0))).astype(bf)
            daug.append(jnp.concatenate([low,extra,jnp.zeros((HEAD-16,QB),bf)],0))
            q=qkvt_ref[hsl,qsl]
            dz.append(jnp.concatenate([zero,low] if h%2 else [low,zero],0))
            qz.append(jnp.concatenate([zero,q] if h%2 else [q,zero],0))
            deltas.append(delta); d1s.append(d1)
        qacc[...]=jnp.zeros_like(qacc)
        def piece(off,size,g):
            slot=lax.rem(g,SLOTS)
            osl=pl.ds(off,size)
            @pl.when(g+SLOTS-1<pieces)
            def _(): pcopy(g+SLOTS-1).start()
            pcopy(g).wait()
            dss=[]
            for h in range(H):
                dss.append((pbuf[slot,h,:size,:].astype(f32)*dot(vaug_ref[h,osl,:],daug[h],1,0)).astype(bf))
            for h in range(H): qacc[h*HEAD:(h+1)*HEAD,:]+=dot(kct[h,:,osl],dss[h],1,0)
            for h in range(0,H,2):
                dkv[osl,h*HEAD:(h+2)*HEAD]+=dot(dss[h],qz[h],1,1)+dot(dss[h+1],qz[h+1],1,1)
                dkv[osl,W+h*HEAD:W+(h+2)*HEAD]+=dot(pbuf[slot,h,:size,:],dz[h],1,1)+dot(pbuf[slot,h+1,:size,:],dz[h+1],1,1)
        g=by_piece(first,full,rest,g,piece)
        for h in range(H):
            hsl=slice(h*HEAD,(h+1)*HEAD); ksl=slice(W+h*HEAD,W+(h+1)*HEAD); vsl=slice(2*W+h*HEAD,2*W+(h+1)*HEAD)
            ps=inv_ref[h,1:2,qsl]
            ds=ps*(jnp.sum(qkvt_ref[vsl,qsl].astype(f32)*d1s[h],0,keepdims=True)-deltas[h])
            dq_ref[hsl,qsl]=((qacc[hsl,:]+ds*qkvt_ref[ksl,qsl].astype(f32))*0.125).astype(bf)
            dq_ref[ksl,qsl]=(ds*qkvt_ref[hsl,qsl].astype(f32)*LN2).astype(bf)
            dq_ref[vsl,qsl]=(ps*d1s[h]).astype(bf)
        return g
    lax.fori_loop(0,nq,block,0)
    lanes=iota((128,2*W),1)
    def turn(j,c):
        jsl=pl.ds(al(j*128,128),128)
        x=jnp.where(j<groups,dkv[jsl,:],0.0)
        dkvt[:,jsl]=jnp.where(lanes<W,x*LN2,x).astype(bf).T
        return c
    lax.fori_loop(0,groups+3,turn,0)
    deep=iota((384,256),0)
    def tgcopy(s):
        slot=lax.rem(s,2)
        return pltpu.make_async_copy(tbuf.at[slot],tg_hbm.at[pl.ds(al(s*256,256),256),:],tsem.at[slot])
    def place(s,c):
        ssl=pl.ds(al(s*256,256),256)
        r0=begin(base_ref,s)//128*128
        oh=(meta_ref[0:1,ssl]==deep+r0).astype(f32).astype(bf)
        g=dot(dkvt[:,pl.ds(al(r0,128),384)],oh,1,0)+dq_ref[W:3*W,ssl].astype(f32)
        dq_ref[W:3*W,ssl]=g.astype(bf)
        @pl.when(s>=2)
        def _(): tgcopy(s-2).wait()
        tbuf[lax.rem(s,2)]=dot(dq_ref[:,ssl],w_ref[...],0,1).astype(bf)
        tgcopy(s).start()
        return c
    lax.fori_loop(0,nd,place,0)
    tcopy.wait()
    grad_ref[...]=dot(dq_ref[...],tok_ref[...],1,0).T.astype(bf)
    for s in range(nd-2,nd): tgcopy(s).wait()

def back(base,win,datt,p,ot,inv,kaug,vaug,qkvt,meta,tok,w,H):
    L=qkvt.shape[1]; W=H*HEAD; E=tok.shape[1]
    V=pl.BlockSpec(memory_space=pltpu.VMEM); A=pl.BlockSpec(memory_space=pl.ANY)
    S=jax.ShapeDtypeStruct; M=pltpu.VMEM; D=pltpu.SemaphoreType.DMA
    return pl.pallas_call(functools.partial(back_kernel,L,H),
        out_shape=[S((L,E),bf),S((E,3*W),bf)],
        in_specs=[pl.BlockSpec(memory_space=pltpu.SMEM)]*2+[V,A]+[V]*6+[A,V],
        out_specs=[A,V],
        scratch_shapes=[M((H,HEAD,L),bf),M((L,2*W),f32),M((2*W,L+384),bf),M((3*W,L),bf),M((SLOTS,H,KB,QB),bf),M((W,QB),f32),
            M((L,E),bf),M((2,256,E),bf),D((SLOTS,)),D((2,)),D((1,))],
        compiler_params=pltpu.CompilerParams(vmem_limit_bytes=VMEM))(base,win,datt,p,ot,inv,kaug,vaug,qkvt,meta,tok,w)
EPSILON=1e-05
def erf(x):
    x=jnp.clip(x,-3.832506856900711,3.832506856900711)
    x2=x*x
    top=0.00022905065861350646
    for c in (0.0034082910107109506,0.050955695062380861,0.18520832239976145,1.128379143519084): top=top*x2+c
    low=-1.1791602954361697e-7
    for c in (0.000023547966471313185,0.0010179625278914885,0.014070470171167667,0.11098505178285362,0.49746925110067538,1.0): low=low*x2+c
    return x*top/low
def norm(x):
    center=x-jnp.mean(x,-1,keepdims=True)
    inverse=lax.rsqrt(jnp.mean(center*center,-1,keepdims=True)+EPSILON)
    return center*inverse,inverse
def norm_back(e,n,inverse):
    return inverse*(e-jnp.mean(e,-1,keepdims=True)-n*jnp.mean(e*n,-1,keepdims=True))
def middle_kernel(a0_ref,a1_ref,tok_ref,cot_ref,wo_ref,wu_ref,wd_ref,gs_ref,out_ref,r1_ref,da_ref,go_ref,gu_ref,gd_ref,gg_ref):
    @pl.when(pl.program_id(0)==0)
    def _():
        for r in (go_ref,gu_ref,gd_ref,gg_ref): r[...]=jnp.zeros_like(r)
    P2=a0_ref.shape[0]
    att=jnp.concatenate([a0_ref[p] for p in range(P2)]+[a1_ref[p] for p in range(P2)],1)
    g0,g1,b0,b1=[gs_ref[r:r+1,:] for r in range(4)]
    n1,inv1=norm(tok_ref[...].astype(f32)+dot(att,wo_ref[...],1,0))
    first=(n1*g0+b0).astype(bf)
    hidden=dot(first,wu_ref[...],1,0)
    cdf=0.5*(1.0+erf(hidden*math.sqrt(0.5)))
    act=(hidden*cdf).astype(bf)
    slope=cdf+hidden*jnp.exp(-0.5*hidden*hidden)*(1.0/math.sqrt(2.0*math.pi))
    n2,inv2=norm(first.astype(f32)+dot(act,wd_ref[...],1,0))
    out_ref[...]=(n2*g1+b1).astype(bf)
    cot=cot_ref[...].astype(f32)
    r2=norm_back(cot*g1,n2,inv2)
    feed=r2.astype(bf)
    gd_ref[...]+=dot(act,feed,0,0)
    dh=(dot(feed,wd_ref[...],1,1)*slope).astype(bf)
    gu_ref[...]+=dot(first,dh,0,0)
    df=r2+dot(dh,wu_ref[...],1,1)
    r1=norm_back(df*g0,n1,inv1)
    r1_ref[...]=r1
    db=r1.astype(bf)
    go_ref[...]+=dot(att,db,0,0)
    da=dot(db,wo_ref[...],1,1).astype(bf)
    for p in range(2*P2): da_ref[p]=da[:,p*128:(p+1)*128]
    gg_ref[0:1,:]+=jnp.sum(df*n1,0,keepdims=True)
    gg_ref[1:2,:]+=jnp.sum(cot*n2,0,keepdims=True)
    gg_ref[2:3,:]+=jnp.sum(df,0,keepdims=True)
    gg_ref[3:4,:]+=jnp.sum(cot,0,keepdims=True)

def middle(a0,a1,tok,cot,wo,wu,wd,gs):
    P2,N,_=a0.shape; D=tok.shape[1]; F=wu.shape[1]
    T=max(t for t in (256,192,128,64,32,16) if N%t==0)
    tile=pl.BlockSpec((T,D),lambda i:(i,0))
    def pairs(k): return pl.BlockSpec((k,T,128),lambda i:(0,i,0))
    def whole(s): return pl.BlockSpec(s,lambda i:(0,)*len(s))
    return pl.pallas_call(middle_kernel,grid=(N//T,),
        in_specs=[pairs(P2),pairs(P2),tile,tile,whole((D,D)),whole((D,F)),whole((F,D)),whole((8,D))],
        out_specs=[tile,tile,pairs(2*P2),whole((D,D)),whole((D,F)),whole((F,D)),whole((8,D))],
        out_shape=[jax.ShapeDtypeStruct((N,D),bf),jax.ShapeDtypeStruct((N,D),f32),jax.ShapeDtypeStruct((2*P2,N,128),bf),
            jax.ShapeDtypeStruct((D,D),f32),jax.ShapeDtypeStruct((D,F),f32),jax.ShapeDtypeStruct((F,D),f32),jax.ShapeDtypeStruct((8,D),f32)],
        compiler_params=pltpu.CompilerParams(vmem_limit_bytes=60<<20))(a0,a1,tok,cot,wo,wu,wd,gs)
MESH=pl.DeviceIdType.MESH
class Net:
    def __init__(self,Z):
        dp=lax.axis_index("dp"); blk=lax.axis_index("blk")
        self.Z=Z; self.z=dp//2; self.y=dp%2; self.j=blk//2; self.c=blk%2
        self.sent=[]
    def at(self,z=None,y=None,j=None,c=None):
        z=self.z if z is None else z; y=self.y if y is None else y; j=self.j if j is None else j; c=self.c if c is None else c
        return (z*2+y,j*2+c)
    def greet(self):
        barrier=pltpu.get_barrier_semaphore()
        def signal(d): pl.semaphore_signal(barrier,inc=1,device_id=d,device_id_type=MESH)
        signal(self.at(j=1-self.j)); signal(self.at(y=1-self.y)); signal(self.at(c=1-self.c))
        for k in range(1,self.Z): signal(self.at(z=lax.rem(self.z+k,self.Z)))
        pl.semaphore_wait(barrier,2+self.Z)
    def copy(self,src,dst,ssem,rsem,device):
        return pltpu.make_async_remote_copy(src_ref=src,dst_ref=dst,send_sem=ssem,recv_sem=rsem,device_id=device,device_id_type=MESH)
    def send(self,src,dst,ssem,rsem,device,when=None):
        c=self.copy(src,dst,ssem,rsem,device)
        if when is None: c.start()
        else: pl.when(when)(c.start)
        self.sent.append((c,when))
    def drain(self):
        for c,when in self.sent:
            if when is None: c.wait_send()
            else: pl.when(when)(c.wait_send)

def gather_kernel(Z,block,E,W,rows,tok_hbm,seg_ref,pad_ref,known_ref,wq_ref,wo_ref,wu_ref,wd_ref,gain_ref,shift_ref,
                  tok_out,bund_out,wmine_out,qkvt_out,base_out,win_out,code_out,meta_out,
                  tokb,info_ref,infob,pack_ref,wall,bund,wt,qkvt,lsem,qsem,xs,xr,zs,zr,ys,yr,cs,cr,ts,tr,iss,isr):
    net=Net(Z); z,y,j,c=net.z,net.y,net.j,net.c
    NCH=block//rows; D=E
    sib=net.at(c=1-c); xd=net.at(j=1-j); yd=net.at(y=1-y)
    mine=pltpu.make_async_copy(tok_hbm.at[j],tokb.at[j,c],lsem.at[0]); mine.start()
    at=0
    for ref in (wq_ref,wo_ref,wu_ref,wd_ref):
        n=ref.shape[1]
        pack_ref[:,at:at+n]=ref[...]
        at+=n
    R=gain_ref.shape[1]
    place=(iota((R,128),1)==iota((R,128),0)+R*lax.rem(lax.axis_index("dp")*4+lax.axis_index("blk"),128//R)).astype(f32).astype(bf)
    pack_ref[:,at:]=jnp.concatenate([dot(gain_ref[...],place,1,0),dot(shift_ref[...],place,1,0),jnp.zeros((12,128),f32)],0).astype(bf)
    split=6*W
    wall[z,y,j,c]=pack_ref[:,:split]
    bund[y,j]=pack_ref[:,split:]
    info_ref[...]=seg_ref[...]*4+pad_ref[...]*2+known_ref[...]
    infob[j,c]=info_ref[j]
    net.greet()
    net.send(pack_ref.at[:,:split],wall.at[z,y,j,c],xs.at[0],xr.at[0],xd)
    net.send(pack_ref.at[:,split:],bund.at[y,j],xs.at[1],xr.at[1],xd)
    net.send(info_ref.at[1-j],infob.at[j,c],iss.at[0],isr.at[0],xd)
    net.send(info_ref.at[j],infob.at[j,c],iss.at[1],isr.at[1],sib)
    def chunk(k): return pl.ds(k*rows,rows)
    for k in range(NCH):
        net.send(tok_hbm.at[1-j,chunk(k)],tokb.at[j,c,chunk(k)],ts.at[0,k],tr.at[0,k],xd)
        net.send(tok_hbm.at[j,chunk(k)],tokb.at[j,c,chunk(k)],ts.at[1,k],tr.at[1,k],sib)
    def piece(o,y_): return wall.at[o,y_,:,c]
    def landed(ref,sem): pltpu.make_async_copy(ref,ref,sem).wait()
    def pass_on(o):
        net.send(piece(o,y),piece(o,y),ys.at[o],yr.at[o],yd)
        net.send(piece(o,y),piece(o,y),cs.at[0,o],cr.at[0,o],sib)
    landed(wall.at[z,y,1-j,c],xr.at[0])
    for k in range(1,Z):
        net.send(piece(z,y),piece(z,y),zs.at[k],zr.at[k],net.at(z=lax.rem(z+k,Z)))
    pass_on(z)
    landed(bund.at[y,1-j],xr.at[1])
    net.send(bund.at[y],bund.at[y],ys.at[Z],yr.at[Z],yd)
    for k in range(1,Z):
        o=lax.rem(z+Z-k,Z)
        landed(piece(o,y),zr.at[k])
        pass_on(o)
    for k in range(Z):
        o=lax.rem(z+Z-k,Z)
        landed(piece(o,1-y),yr.at[o])
        net.send(piece(o,1-y),piece(o,1-y),cs.at[1,o],cr.at[1,o],sib)
    for o in range(Z):
        for q in range(2): landed(wall.at[o,y if q==0 else 1-y,:,1-c],cr.at[q,o])
    landed(bund.at[1-y],yr.at[Z])
    outb=pltpu.make_async_copy(bund,bund_out,lsem.at[1]); outb.start()
    def project(jj,cc,k):
        g=(jj*2+cc)*NCH+k
        r=dot(wt[...],tokb[jj,cc,chunk(k),:],1,1)
        col=pl.ds(al(g*rows,rows),rows)
        qkvt[:,col]=jnp.concatenate([r[:W]*(math.log2(math.e)/8),r[W:]],0).astype(bf)
        out=pltpu.make_async_copy(qkvt.at[:,col],qkvt_out.at[:,col],qsem.at[g])
        out.start()
        return out
    keep=[]
    parts=[]
    for t in range(3):
        cols=pl.ds(al(t*2*W+c*W,W),W)
        part=wall[:,:,:,:,:,cols].reshape(D,W)
        wt[t*W:(t+1)*W,:]=part.T
        parts.append(part)
    wmine_out[...]=jnp.concatenate(parts,1)
    mine.wait()
    for k in range(NCH): keep.append(project(j,c,k))
    for k in range(NCH):
        ref=tokb.at[j,1-c,chunk(k)]
        pltpu.make_async_copy(ref,ref,tr.at[1,k]).wait()
        keep.append(project(j,1-c,k))
    for k in range(NCH):
        ref=tokb.at[1-j,c,chunk(k)]
        pltpu.make_async_copy(ref,ref,tr.at[0,k]).wait()
        net.send(ref,ref,ts.at[2,k],tr.at[2,k],sib)
        keep.append(project(1-j,c,k))
        if k==0:
            pltpu.make_async_copy(infob.at[1-j,c],infob.at[1-j,c],isr.at[0]).wait()
            net.send(infob.at[1-j,c],infob.at[1-j,c],iss.at[2],isr.at[2],sib)
    pltpu.make_async_copy(infob.at[j,1-c],infob.at[j,1-c],isr.at[1]).wait()
    pltpu.make_async_copy(infob.at[1-j,1-c],infob.at[1-j,1-c],isr.at[2]).wait()
    base_out[...],win_out[...],code_out[...],meta_out[...]=flags(jnp.concatenate([infob[0,0],infob[0,1],infob[1,0],infob[1,1]],1))
    for k in range(NCH):
        ref=tokb.at[1-j,1-c,chunk(k)]
        pltpu.make_async_copy(ref,ref,tr.at[2,k]).wait()
        keep.append(project(1-j,1-c,k))
    outt=pltpu.make_async_copy(tokb,tok_out,lsem.at[2]); outt.start()
    net.drain()
    for x in keep: x.wait()
    outb.wait(); outt.wait()

def gather(tok,seg,pad,known,wq,wo,wu,wd,gain,shift,Z,W):
    _,block,E=tok.shape; R=wq.shape[0]; C=6*W+wo.shape[1]+wu.shape[1]+wd.shape[1]+128
    rows=256; NCH=block//rows; L=4*block
    V=pl.BlockSpec(memory_space=pltpu.VMEM); A=pl.BlockSpec(memory_space=pl.ANY)
    S=jax.ShapeDtypeStruct; M=pltpu.VMEM; D=pltpu.SemaphoreType.DMA; I=jnp.int32
    return pl.pallas_call(functools.partial(gather_kernel,Z,block,E,W,rows),
        out_shape=[S((2,2,block,E),bf),S((2,2,R,C-6*W),bf),S((E,3*W),bf),S((3*W,L),bf),S((16,128),I),S((16,128),I),S((CODE,L),bf),S((8,L),I)],
        in_specs=[A]+[V]*9,out_specs=[A,A,V,A,V,V,V,V],
        scratch_shapes=[M((2,2,block,E),bf),M((2,1,block),I),M((2,2,1,block),I),M((R,C),bf),M((Z,2,2,2,R,6*W),bf),M((2,2,R,C-6*W),bf),M((3*W,E),bf),M((3*W,L),bf),
            D((3,)),D((4*NCH,)),D((2,)),D((2,)),D((Z,)),D((Z,)),D((Z+1,)),D((Z+1,)),D((2,Z)),D((2,Z)),D((3,NCH)),D((3,NCH)),D((3,)),D((3,))],
        compiler_params=pltpu.CompilerParams(collective_id=0,has_side_effects=True,vmem_limit_bytes=VMEM))(tok,seg,pad,known,wq,wo,wu,wd,gain,shift)
def middle_net_kernel(Z,block,E,F,W,T,att_hbm,tok_hbm,cot_hbm,cotx_hbm,*rest):
    bunds=rest[:Z]; lay_out,r1_out,datt_out=rest[Z:Z+3]; parts=rest[Z+3]
    (go_ref,gu_ref,gd_ref,gg_ref,gt_ref,aown,aget,tok,cot,wall,lay,r1,da,lsem,wsem,osem,asend,aget_sem,dsend,dget,xsend,xget,bsend,bget)=rest[Z+4:]
    net=Net(Z); z,y,j,c=net.z,net.y,net.j,net.c
    NCH=block//T; n=2*NCH; P2=att_hbm.shape[0]; D=E
    sib=net.at(c=1-c); xd=net.at(j=1-j)
    def place(t):
        jj=jnp.where(t<NCH,1-j,j)
        return jj,pl.ds(al(lax.rem(t,NCH)*T,T),T)
    def load(t):
        jj,rows=place(t)
        return [pltpu.make_async_copy(att_hbm.at[:,jj,c,rows],aown.at[t],lsem.at[0,t]),pltpu.make_async_copy(tok_hbm.at[jj,c,rows],tok.at[t],lsem.at[1,t])]
    def load_cot(t,near):
        rows=place(t)[1]
        return pltpu.make_async_copy((cot_hbm.at[j,rows] if near else cotx_hbm.at[rows]),cot.at[t],lsem.at[2,t])
    cols=[(0,E),(E,F),(E+F,E),(2*E+F,128)]
    loadw=[pltpu.make_async_copy(bunds[k],wall.at[lax.rem(z+Z-k,Z),:,:,c],wsem.at[k]) for k in range(Z)]
    for x in loadw: x.start()
    def start(t,near):
        for x in load(t): x.start()
        load_cot(t,near).start()
    for t in range(n): start(t,t>=NCH)
    barrier=pltpu.get_barrier_semaphore()
    for d in (sib,xd): pl.semaphore_signal(barrier,inc=1,device_id=d,device_id_type=MESH)
    pl.semaphore_wait(barrier,2)
    def ship(t):
        jj,rows=place(t)
        return net.copy(att_hbm.at[:,jj,1-c,rows],aget.at[t],asend.at[t],aget_sem.at[t],sib)
    ship(0).start()
    weights=[net.copy(bunds[k],wall.at[lax.rem(z+Z-k,Z),:,:,c],bsend.at[k],bget.at[k],sib) for k in range(Z)]
    for x in weights: x.start()
    for t in range(1,n): ship(t).start()
    for x in loadw: x.wait()
    for k in range(Z):
        ref=wall.at[lax.rem(z+Z-k,Z),:,:,1-c]
        pltpu.make_async_copy(ref,ref,bget.at[k]).wait()
    def whole(a,b): return wall[:,:,:,:,:,a:a+b].reshape(E,b)
    gs=wall[:,:,:,:,:,cols[3][0]:].reshape(E//16,16,128).astype(f32)
    gsr=jnp.concatenate([jnp.sum(gs[q*8:(q+1)*8],0) for q in range(E//128)],1)
    g0,g1,b0,b1=[gsr[r:r+1,:] for r in range(4)]
    for r in (go_ref,gu_ref,gd_ref,gg_ref): r[...]=jnp.zeros_like(r)
    def out_near(t):
        jj,rows=place(t)
        return pltpu.make_async_copy(lay.at[t],lay_out.at[j,rows],osem.at[0,t])
    def out_far(t):
        jj,rows=place(t)
        return net.copy(lay.at[t],lay_out.at[j,rows],xsend.at[t],xget.at[t],xd)
    def out_r1(t):
        jj,rows=place(t)
        return pltpu.make_async_copy(r1.at[t],r1_out.at[jj,rows],osem.at[1,t])
    def out_da(t):
        jj,rows=place(t)
        return pltpu.make_async_copy(da.at[0,t],datt_out.at[:,jj,c,rows],osem.at[2,t])
    def ship_da(t):
        jj,rows=place(t)
        return net.copy(da.at[1,t],datt_out.at[:,jj,c,rows],dsend.at[t],dget.at[t],sib)
    def tile(t,carry):
        for x in load(t): x.wait()
        pltpu.make_async_copy(cotx_hbm.at[place(t)[1]],cot.at[t],lsem.at[2,t]).wait()
        ship(t).wait_recv()
        mine=[aown[t,p] for p in range(P2)]; his=[aget[t,p] for p in range(P2)]
        att=jnp.where(c==0,jnp.concatenate(mine+his,1),jnp.concatenate(his+mine,1))
        wo=whole(*cols[0]); wu=whole(*cols[1]); wd=whole(*cols[2])
        n1,inv1=norm(tok[t].astype(f32)+dot(att,wo,1,0))
        first=(n1*g0+b0).astype(bf)
        hidden=dot(first,wu,1,0)
        cdf=0.5*(1.0+erf(hidden*math.sqrt(0.5)))
        act=(hidden*cdf).astype(bf)
        slope=cdf+hidden*jnp.exp(-0.5*hidden*hidden)*(1.0/math.sqrt(2.0*math.pi))
        n2,inv2=norm(first.astype(f32)+dot(act,wd,1,0))
        lay[t]=(n2*g1+b1).astype(bf)
        @pl.when(t<NCH)
        def _(): out_far(t).start()
        @pl.when(t>=NCH)
        def _(): out_near(t).start()
        ct=cot[t].astype(f32)
        r2=norm_back(ct*g1,n2,inv2)
        feed=r2.astype(bf)
        gd_ref[...]+=dot(act,feed,0,0)
        dh=(dot(feed,wd,1,1)*slope).astype(bf)
        gu_ref[...]+=dot(first,dh,0,0)
        df=r2+dot(dh,wu,1,1)
        dr=norm_back(df*g0,n1,inv1)
        r1[t]=dr.astype(r1.dtype)
        out_r1(t).start()
        db=dr.astype(bf)
        go_ref[...]+=dot(att,db,0,0)
        d=dot(db,wo,1,1).astype(bf)
        for p in range(P2):
            lo=d[:,p*128:(p+1)*128]; hi=d[:,W+p*128:W+(p+1)*128]
            da[0,t,p]=jnp.where(c==0,lo,hi)
            da[1,t,p]=jnp.where(c==0,hi,lo)
        out_da(t).start(); ship_da(t).start()
        gg_ref[0:1,:]+=jnp.sum(df*n1,0,keepdims=True)
        gg_ref[1:2,:]+=jnp.sum(ct*n2,0,keepdims=True)
        gg_ref[2:3,:]+=jnp.sum(df,0,keepdims=True)
        gg_ref[3:4,:]+=jnp.sum(ct,0,keepdims=True)
        return carry
    lax.fori_loop(0,n,tile,0)
    ggt=jnp.concatenate([gg_ref[...],jnp.zeros((120,E),f32)],0).T
    gt_ref[...]=ggt
    R=E//(2*Z)
    at=0
    for ref in (go_ref,gu_ref,gd_ref,gt_ref):
        parts[:,:,at:at+ref.shape[1]]=ref[...].astype(bf).reshape(2*Z,R,ref.shape[1])
        at+=ref.shape[1]
    for x in weights: x.wait_send()
    for t in range(n):
        ship(t).wait_send(); out_r1(t).wait(); out_da(t).wait(); ship_da(t).wait()
        if t<NCH: out_far(t).wait()
        else: out_near(t).wait()

def middle_net(att,tok,cot,cotx,bunds,Z,W,F):
    P2,_,_,block,_=att.shape; E=tok.shape[-1]; C=bunds[0].shape[-1]
    T=256; NCH=block//T; n=2*NCH
    V=pl.BlockSpec(memory_space=pltpu.VMEM); A=pl.BlockSpec(memory_space=pl.ANY)
    S=jax.ShapeDtypeStruct; M=pltpu.VMEM; D=pltpu.SemaphoreType.DMA
    return pl.pallas_call(functools.partial(middle_net_kernel,Z,block,E,F,W,T),
        out_shape=[S((2,block,E),bf),S((2,block,E),f32),S((P2,2,2,block,128),bf)]+[S((2*Z,E//(2*Z),C),bf)],
        in_specs=[A]*(4+Z),out_specs=[A,A,A,V],
        scratch_shapes=[M((E,E),f32),M((E,F),f32),M((F,E),f32),M((8,E),f32),M((E,128),f32),
            M((n,P2,T,128),bf),M((n,P2,T,128),bf),M((n,T,E),bf),M((n,T,E),bf),M((Z,2,2,2,16,C),bf),M((n,T,E),bf),M((n,T,E),f32),M((2,n,P2,T,128),bf),
            D((3,n)),D((Z,)),D((3,n)),D((n,)),D((n,)),D((n,)),D((n,)),D((n,)),D((n,)),D((Z,)),D((Z,))],
        compiler_params=pltpu.CompilerParams(collective_id=2,has_side_effects=True,vmem_limit_bytes=VMEM))(att,tok,cot,cotx,*bunds)
def reduce_kernel(Z,block,E,W,C1,rows,cuts,tg_hbm,r1_hbm,gq_ref,parts,tok_out,grad_out,*rest):
    (own,r1,tgr,tgs,ob,s0,r0,g0,s1,r1b,su,ru,fin,sx,rx,se,re,sxe,rxe,
     lsem,ts,tr,xs,xr,cs,cr,ys,yr,us,ur,fs,fr)=rest
    net=Net(Z); z,y,j,c=net.z,net.y,net.j,net.c
    NCH=block//rows; Q=3*W; NW=len(cuts)
    sib=net.at(c=1-c); xd=net.at(j=1-j); yd=net.at(y=1-y)
    loads=[pltpu.make_async_copy(tg_hbm.at[:,c],own,lsem.at[0]),pltpu.make_async_copy(r1_hbm,r1,lsem.at[1])]
    for x in loads: x.start()
    net.greet()
    def chunk(k): return pl.ds(k*rows,rows)
    def landed(ref,sem): pltpu.make_async_copy(ref,ref,sem).wait()
    def to_sibling(t):
        jj=1-j if t==0 else j
        for k in range(NCH): net.send(tg_hbm.at[jj,1-c,chunk(k)],tgr.at[jj,chunk(k)],ts.at[t,k],tr.at[t,k],sib)
    to_sibling(0)
    def split(x,n): return x.reshape(Z,2,2,2,16,n)
    s0[...]=split(gq_ref[...],Q)[:,:,:,0]
    @pl.when(c==0)
    def _(): s0[...]=split(gq_ref[...],Q)[:,:,:,1]
    net.send(s0,r0,cs.at[0],cr.at[0],sib)
    early=parts[0].astype(f32)
    for k in range(1,2*Z): early=early+parts[k].astype(f32)
    early=early.reshape(2,2,16,C1)
    early0=jnp.where(c==0,early[:,0],early[:,1])
    se[...]=jnp.where(c==0,early[:,1],early[:,0]).astype(bf)
    net.send(se,re,cs.at[1],cr.at[1],sib)
    to_sibling(1)
    for x in loads: x.wait()
    def total(jj,k): return (own[jj,chunk(k),:].astype(f32)+tgr[jj,chunk(k),:].astype(f32)+r1[jj,chunk(k),:].astype(f32)).astype(bf)
    for k in range(NCH):
        landed(tgr.at[1-j,chunk(k)],tr.at[0,k])
        tgs[chunk(k),:]=total(1-j,k)
        net.send(tgs.at[chunk(k)],ob.at[j,chunk(k)],xs.at[k],xr.at[k],xd)
    landed(r0,cr.at[0])
    mine=split(gq_ref[...],Q)
    for cc in range(2):
        @pl.when(c==cc)
        def _():
            for t in range(3):
                for other in range(2):
                    src=mine[:,:,:,cc,:,t*W:(t+1)*W] if other==cc else r0[:,:,:,:,t*W:(t+1)*W]
                    g0[:,:,:,:,(2*t+other)*W:(2*t+other+1)*W]=src
    cut=[pl.ds(a,b-a) for a,b in cuts]
    for w in range(NW):
        s1[:,:,:,cut[w]]=g0[:,1-y,:,:,cut[w]]
        net.send(s1.at[:,:,:,cut[w]],r1b.at[:,:,:,cut[w]],ys.at[w],yr.at[w],yd)
    landed(re,cr.at[1])
    early0=early0+re[...].astype(f32)
    early1=jnp.where(j==0,early0[0],early0[1])
    sxe[...]=jnp.where(j==0,early0[1],early0[0]).astype(bf)
    net.send(sxe,rxe,fs.at[NW],fr.at[NW],xd)
    for k in range(NCH):
        landed(tgr.at[j,chunk(k)],tr.at[1,k])
        ob[j,chunk(k),:]=total(j,k)
    def to_z(w):
        landed(r1b.at[:,:,:,cut[w]],yr.at[w])
        for k in range(1,Z):
            o=lax.rem(z+k,Z)
            su[k,:,:,cut[w]]=(g0[o,y,:,:,cut[w]].astype(f32)+r1b[o,:,:,cut[w]].astype(f32)).astype(bf)
            net.send(su.at[k,:,:,cut[w]],ru.at[k,:,:,cut[w]],us.at[w,k],ur.at[w,k],net.at(z=o))
    def to_x(w):
        sum_=g0[z,y,:,:,cut[w]].astype(f32)+r1b[z,:,:,cut[w]].astype(f32)
        for k in range(1,Z):
            landed(ru.at[k,:,:,cut[w]],ur.at[w,k])
            sum_=sum_+ru[k,:,:,cut[w]].astype(f32)
        fin[:,:,cut[w]]=sum_
        sx[:,cut[w]]=fin[1-j,:,cut[w]].astype(bf)
        net.send(sx.at[:,cut[w]],rx.at[:,cut[w]],fs.at[w],fr.at[w],xd)
    for w in range(NW):
        to_z(w)
        if w>0: to_x(w-1)
    to_x(NW-1)
    landed(rxe,fr.at[NW])
    grad_out[:,2*Q:]=early1+rxe[...].astype(f32)
    for w in range(NW):
        landed(rx.at[:,cut[w]],fr.at[w])
        grad_out[:,cut[w]]=fin[j,:,cut[w]]+rx[:,cut[w]].astype(f32)
    for k in range(NCH): landed(ob.at[1-j,chunk(k)],xr.at[k])
    last=pltpu.make_async_copy(ob,tok_out,lsem.at[2])
    last.start()
    net.drain()
    last.wait()

def reduce(tg,r1,gq,parts,Z,W):
    _,_,block,E=tg.shape; Q=3*W; C1=parts.shape[2]; C=2*Q
    rows=256; NCH=block//rows
    cuts=((0,Q),(Q,C)); NW=len(cuts)
    V=pl.BlockSpec(memory_space=pltpu.VMEM); A=pl.BlockSpec(memory_space=pl.ANY)
    S=jax.ShapeDtypeStruct; M=pltpu.VMEM; D=pltpu.SemaphoreType.DMA
    return pl.pallas_call(functools.partial(reduce_kernel,Z,block,E,W,C1,rows,cuts),
        out_shape=[S((2,block,E),bf),S((16,C+C1),f32)],
        in_specs=[A,A,V,V],out_specs=[A,V],
        scratch_shapes=[M((2,block,E),bf),M((2,block,E),r1.dtype),M((2,block,E),bf),M((block,E),bf),M((2,block,E),bf),
            M((Z,2,2,16,Q),bf),M((Z,2,2,16,Q),bf),M((Z,2,2,16,C),bf),M((Z,2,16,C),bf),M((Z,2,16,C),bf),
            M((Z,2,16,C),bf),M((Z,2,16,C),bf),M((2,16,C),f32),M((16,C),bf),M((16,C),bf),M((2,16,C1),bf),M((2,16,C1),bf),M((16,C1),bf),M((16,C1),bf),
            D((3,)),D((2,NCH)),D((2,NCH)),D((NCH,)),D((NCH,)),D((2,)),D((2,)),D((NW,)),D((NW,)),D((NW,Z)),D((NW,Z)),D((NW+1,)),D((NW+1,))],
        compiler_params=pltpu.CompilerParams(collective_id=1,has_side_effects=True,vmem_limit_bytes=VMEM))(tg,r1,gq,parts)
def shards(tokens,cotangent,segments,padding,known,w_qkv,w_out,w_up,w_down,norm_gains,norm_shifts):
    micro,rows,block,D=tokens.shape
    J=lax.axis_size("blk")//2; dps=lax.axis_size("dp")
    units=micro*rows
    assert units==J
    H=HEADS//2; W=H*HEAD; L=2*J*block; F=w_up.shape[1]
    quick=J==2 and dps%2==0 and w_qkv.shape[0]==16 and block%256==0
    me=lax.axis_index("blk"); chip=me//2; core=me%2
    flat=lambda x:x.reshape((units,)+x.shape[2:])
    if quick:
        Z=dps//2
        tok,bund,w_mine,qkvt,base,win,codet,meta=gather(flat(tokens),*[flat(x)[:,None,:] for x in (segments,padding,known)],w_qkv,w_out,w_up,w_down,norm_gains,norm_shifts,Z,W)
        cot=flat(cotangent)
        def move(x,k,b): return lax.ppermute(x,"dp",[(d,(d//2+k)%Z*2+(d%2^b)) for d in range(dps)])
        far,base=lax.optimization_barrier((jnp.where(chip==0,cot[1],cot[0]),base))
        bunds=[bund]+[move(bund,k,0) for k in range(1,Z)]
        cotx=lax.ppermute(far,"blk",[(b,b^2) for b in range(4)])
        p,att,ot,inv,kaug,vaug=attend(base,win,qkvt,codet,meta,H)
        layer_out,r1,datt,parts=middle_net(att.reshape(H//2,2,2,block,128),tok,cot,cotx,bunds,Z,W,F)
        parts=lax.all_to_all(parts,"dp",0,0,tiled=True)
        tg,gq=back(base,win,datt.reshape(H//2,L,128),p,ot,inv,kaug,vaug,qkvt,meta,tok.reshape(L,D),w_mine,H)
        token_grad,grads=reduce(tg.reshape(2,2,block,D),r1,gq,parts,Z,W)
        a,b,e=6*W,6*W+D,6*W+D+F
        gg=grads[:,e+D:e+D+4].T
        return (layer_out.reshape(tokens.shape),token_grad.reshape(tokens.shape),grads[:,:a],grads[:,a:b],grads[:,b:e],grads[:,e:e+D],gg[:2],gg[2:])
    def to_chip(s): return [(2*a+c,2*((a+s)%J)+c) for a in range(J) for c in range(2)]
    swap=[(b,b^1) for b in range(2*J)]
    def other(x): return lax.ppermute(x,"blk",swap)
    def scatter_units(x):
        got=[]
        for s in range(J):
            mine=lax.dynamic_index_in_dim(x,(chip+s)%J,0,keepdims=False)
            got.append(mine if s==0 else lax.ppermute(mine,"blk",to_chip(s)))
        return jnp.stack([lax.dynamic_index_in_dim(jnp.stack(got),(chip-j)%J,0,keepdims=False) for j in range(J)])
    def both(mine,his):
        return jnp.stack([jnp.where(core==0,mine,his),jnp.where(core==0,his,mine)],1)
    def part(x,axis,index): return lax.dynamic_index_in_dim(x,index,axis,keepdims=False)
    own_info=scatter_units(flat(segments*4+padding*2+known)); info=both(own_info,other(own_info)).reshape(1,L)
    own_tok=scatter_units(flat(tokens)); all_tok=both(own_tok,other(own_tok)).reshape(L,D)
    own_cot=scatter_units(flat(cotangent)).reshape(L//2,D)
    full_qkv,full_out,full_up,full_down=[lax.all_gather(w,("dp","blk"),axis=0,tiled=True) for w in (w_qkv,w_out,w_up,w_down)]
    gs=lax.all_gather(jnp.concatenate([norm_gains,norm_shifts],0),("dp","blk"),axis=1,tiled=True).astype(f32)
    gs=jnp.concatenate([gs,jnp.zeros_like(gs)],0)
    w_mine=part(full_qkv.reshape(D,3,2,W),2,core).reshape(D,3*W)
    scale=jnp.where(jnp.arange(3*W)<W,math.log2(math.e)/8,1.0).astype(f32)
    qkvt=(jnp.einsum("ld,de->el",all_tok,w_mine,preferred_element_type=f32)*scale[:,None]).astype(bf)
    base,win,codet,meta=flags(info)
    p,att,ot,inv,kaug,vaug=attend(base,win,qkvt,codet,meta,H)
    att=att.reshape(H//2,J,2,block,128)
    mine=part(att,2,core).reshape(H//2,J*block,128); his=other(part(att,2,1-core)).reshape(H//2,J*block,128)
    a0=jnp.where(core==0,mine,his); a1=jnp.where(core==0,his,mine)
    out,r1,da,go,gu,gd,gg=middle(a0,a1,own_tok.reshape(L//2,D),own_cot,full_out,full_up,full_down,gs)
    da=da.reshape(2,H//2,J,block,128)
    dmine=part(da,0,core); dhis=other(part(da,0,1-core))
    datt=jnp.stack([jnp.where(core==0,dmine,dhis),jnp.where(core==0,dhis,dmine)],2).reshape(H//2,L,128)
    tg,gq=back(base,win,datt,p,ot,inv,kaug,vaug,qkvt,meta,all_tok,w_mine,H)
    tg=tg.reshape(J,2,block,D)
    layer_out=scatter_units(out.reshape(J,block,D)).reshape(tokens.shape)
    own_tg=(part(tg,1,core).astype(f32)+other(part(tg,1,1-core)).astype(f32)+r1.reshape(J,block,D)).astype(bf)
    token_grad=scatter_units(own_tg).reshape(tokens.shape)
    gq=gq.astype(f32).reshape(D,3,1,W)
    gq=jnp.where(core==0,jnp.concatenate([gq,jnp.zeros_like(gq)],2),jnp.concatenate([jnp.zeros_like(gq),gq],2)).reshape(D,6*W)
    grads=lax.psum_scatter(jnp.concatenate([gq,go,gu,gd],1),("dp","blk"),scatter_dimension=0,tiled=True)
    gg=lax.psum_scatter(gg[:4],("dp","blk"),scatter_dimension=1,tiled=True)
    a,b,e=6*W,6*W+D,6*W+D+F
    return (layer_out,token_grad,grads[:,:a],grads[:,a:b],grads[:,b:e],grads[:,e:],gg[:2],gg[2:])

def solution(mesh):
    in_specs = (
        P(None, "dp", "blk", None),
        P(None, "dp", "blk", None),
        P(None, "dp", "blk"),
        P(None, "dp", "blk"),
        P(None, "dp", "blk"),
        P(("dp", "blk"), None),
        P(("dp", "blk"), None),
        P(("dp", "blk"), None),
        P(("dp", "blk"), None),
        P(None, ("dp", "blk")),
        P(None, ("dp", "blk")),
    )
    out_specs = (
        P(None, "dp", "blk", None),
        P(None, "dp", "blk", None),
        P(("dp", "blk"), None),
        P(("dp", "blk"), None),
        P(("dp", "blk"), None),
        P(("dp", "blk"), None),
        P(None, ("dp", "blk")),
        P(None, ("dp", "blk")),
    )
    return jax.shard_map(shards, mesh=mesh, in_specs=in_specs, out_specs=out_specs, check_vma=False)
```

```python
import functools, math
import jax, jax.numpy as jnp
from jax import lax
from jax.experimental import pallas as pl
from jax.experimental.pallas import tpu as pltpu
from jax.sharding import PartitionSpec as P

HEADS = 8
bf=jnp.bfloat16; f32=jnp.float32
HEAD=64
QB=512
KB=512
SRC=1024
SAFE=60.0
CODE=16
VMEM=(64<<20)-(128<<10)
SLOTS=3
def dot(a,b,ca,cb): return lax.dot_general(a,b,(((ca,),(cb,)),((),())),preferred_element_type=f32)
def al(x,n): return pl.multiple_of(x,n)
def iota(shape,axis): return lax.broadcasted_iota(jnp.int32,shape,axis)

def begin(base_ref,b):
    return base_ref[b,0]

def window(win_ref,i):
    start=win_ref[i,0]//128*128
    groups=(win_ref[8+i,0]-start+127)//128
    full=(groups-1)//(KB//128)
    return start,full,groups-full*(KB//128),groups

def by_piece(first,full,rest,g,fn):
    def body(j,g):
        fn(al(first+j*KB,128),KB,g)
        return g+1
    g=lax.fori_loop(0,full,body,g)
    for r in range(1,KB//128+1):
        @pl.when(rest==r)
        def _(): fn(al(first+full*KB,128),r*128,g)
    return g+1

def attend_kernel(L,H,base_ref,win_ref,qkvt_hbm,codet_ref,meta_ref,p_hbm,att_hbm,ot_hbm,inv_ref,kct_hbm,vaug_hbm,
                  kaug_ref,kct_ref,vaug_ref,kvt,q_ref,v_ref,vct,acc,pbuf,obuf,abuf,top_ref,psem,osem,asem,ksem,lsem):
    W=H*HEAD; nq=L//QB
    total=begin(base_ref,L//256)
    come=[pltpu.make_async_copy(qkvt_hbm.at[W+h*HEAD:W+(h+1)*HEAD],kvt.at[h*128:h*128+HEAD],lsem.at[h]) for h in range(H)]
    come+=[pltpu.make_async_copy(qkvt_hbm.at[2*W:],v_ref,lsem.at[H]),pltpu.make_async_copy(qkvt_hbm.at[:W],q_ref,lsem.at[H+1])]
    for x in come: x.start()
    for h in range(H):
        kvt[h*128+HEAD:h*128+HEAD+CODE,:]=codet_ref[...]
        kvt[h*128+HEAD+CODE:(h+1)*128,:]=jnp.zeros((HEAD-CODE,L),bf)
    vct[:,HEAD:,:]=jnp.ones((H,16,L),bf)
    for x in come[:H+1]: x.wait()
    row=iota((256,256),0)
    down=iota((256,SRC),0)
    def dest(d,c):
        first=jnp.minimum(win_ref[16+d,0]//128*128,L-SRC)
        last=win_ref[17+d,0]
        def src(t,a):
            ssl=pl.ds(al(jnp.minimum(first+t*SRC,L-SRC),128),SRC)
            oh=((meta_ref[0:1,ssl]==down+d*256)&(lane>=first+t*SRC-jnp.minimum(first+t*SRC,L-SRC))).astype(f32).astype(bf)
            return a[0]+dot(kvt[:,ssl],oh,1,1),a[1]+dot(v_ref[:,ssl],oh,1,1)
        lane=iota((256,SRC),1)
        ka,va=src(0,(jnp.zeros((H*128,256),f32),jnp.zeros((W,256),f32)))
        ka,va=lax.fori_loop(1,(last-first+SRC-1)//SRC,src,(ka,va))
        dsl=pl.ds(al(d*256,256),256)
        for h in range(H):
            k1=jnp.where(row[:128]==HEAD+10,-2560.0,ka[h*128:(h+1)*128])
            kaug_ref[h,dsl,:]=k1.astype(bf).T
            kct_ref[h,:,dsl]=k1[:HEAD].astype(bf)
            v1=va[h*HEAD:(h+1)*HEAD]
            vct[h,:HEAD,dsl]=v1.astype(bf)
            vaug_ref[h,dsl,:]=jnp.concatenate([v1,jnp.where(row[:HEAD]<3,-1.0,0.0)],0).astype(bf).T
        return c
    lax.fori_loop(0,(total+255)//256,dest,0)
    keep=[pltpu.make_async_copy(kct_ref,kct_hbm,ksem.at[0]),pltpu.make_async_copy(vaug_ref,vaug_hbm,ksem.at[1])]
    for x in keep: x.start()
    come[H+1].wait()
    bound=jnp.float32(0)
    for h in range(H):
        q=q_ref[h*HEAD:(h+1)*HEAD,:].astype(f32); k=kvt[h*128:h*128+HEAD,:].astype(f32)
        bound=jnp.maximum(bound,jnp.max(jnp.sum(q*q,0,keepdims=True))*jnp.max(jnp.sum(k*k,0,keepdims=True)))
    safe=bound<SAFE*SAFE

    def pcopy(g):
        slot=lax.rem(g,SLOTS)
        return pltpu.make_async_copy(pbuf.at[slot],p_hbm.at[g],psem.at[slot])
    def ocopy(i):
        slot=lax.rem(i,2)
        return pltpu.make_async_copy(obuf.at[slot],ot_hbm.at[i],osem.at[slot])
    def acopy(i):
        slot=lax.rem(i,2)
        return pltpu.make_async_copy(abuf.at[slot],att_hbm.at[:,pl.ds(al(i*QB,QB),QB),:],asem.at[slot])
    def block(i,g):
        slot=lax.rem(i,2)
        qsl=pl.ds(al(i*QB,QB),QB)
        first,full,rest,groups=window(win_ref,i)
        qa=[jnp.concatenate([q_ref[h*HEAD:(h+1)*HEAD,qsl],codet_ref[:,qsl],jnp.zeros((HEAD-CODE,QB),bf)],0) for h in range(H)]
        own=meta_ref[1:2,qsl]>0
        sself=[]
        for h in range(H):
            x=q_ref[h*HEAD:(h+1)*HEAD,qsl].astype(f32)*kvt[h*128:h*128+HEAD,qsl].astype(f32)
            sself.append(jnp.where(own,jnp.sum(x,0,keepdims=True),-1e30))
        acc[...]=jnp.zeros_like(acc)
        top_ref[...]=jnp.zeros_like(top_ref)
        row=iota((128,QB),0)
        def strict(h,osl):
            k=kaug_ref[h,osl,:]
            x=qa[h].astype(f32)
            plain=dot(k,jnp.where(row<HEAD,x,0.0).astype(bf),1,0)
            return jnp.where(dot(k,jnp.where(row<HEAD,0.0,x).astype(bf),1,0)>-1.0,plain,-1e30)
        @pl.when(jnp.logical_not(safe))
        def _():
            for h in range(H):
                def more(j,m): return jnp.maximum(m,jnp.max(strict(h,pl.ds(al(first+j*128,128),128)),0,keepdims=True))
                top_ref[h:h+1,:]=lax.fori_loop(0,groups,more,sself[h])
        def piece(off,size,g):
            ps=lax.rem(g,SLOTS)
            osl=pl.ds(off,size)
            @pl.when(g>=SLOTS)
            def _(): pcopy(g-SLOTS).wait()
            @pl.when(safe)
            def _():
                keepp=[]
                for h in range(H):
                    p=jnp.exp2(dot(kaug_ref[h,osl,:],qa[h],1,0)).astype(bf)
                    pbuf[ps,h,:size,:]=p
                    keepp.append(p)
                for h in range(H): acc[h]+=dot(vct[h,:,osl],keepp[h],1,0)
            @pl.when(jnp.logical_not(safe))
            def _():
                for h in range(H):
                    def put(j,c):
                        jsl=pl.ds(al(off+j*128,128),128)
                        p=jnp.exp2(strict(h,jsl)-top_ref[h:h+1,:]).astype(bf)
                        pbuf[ps,h,pl.ds(al(j*128,128),128),:]=p
                        acc[h]+=dot(vct[h,:,jsl],p,1,0)
                        return c
                    lax.fori_loop(0,size//128,put,0)
            pcopy(g).start()
        g=by_piece(first,full,rest,g,piece)
        @pl.when(i>=2)
        def _(): ocopy(i-2).wait(); acopy(i-2).wait()
        for h in range(H):
            ps=jnp.exp2(sself[h]-top_ref[h:h+1,:])
            inv=1.0/(acc[h,HEAD:HEAD+1,:]+ps)
            obuf[slot,h*HEAD:(h+1)*HEAD,:]=(acc[h,:HEAD,:]+ps*v_ref[h*HEAD:(h+1)*HEAD,qsl].astype(f32))*inv
            inv_ref[h,0:1,qsl]=inv
            inv_ref[h,1:2,qsl]=ps
        for hp in range(H//2): abuf[slot,hp]=obuf[slot,hp*128:(hp+1)*128,:].T.astype(bf)
        ocopy(i).start(); acopy(i).start()
        return g
    g=lax.fori_loop(0,nq,block,0)
    for s in range(SLOTS):
        last=g-1-s
        @pl.when(last>=0)
        def _(): pcopy(last).wait()
    for i in range(max(nq-2,0),nq): ocopy(i).wait(); acopy(i).wait()
    for x in keep: x.wait()

def attend(base,win,qkvt,codet,meta,H):
    L=qkvt.shape[1]; W=H*HEAD; nq=L//QB; cap=nq*(L//KB+1)
    V=pl.BlockSpec(memory_space=pltpu.VMEM); A=pl.BlockSpec(memory_space=pl.ANY)
    S=jax.ShapeDtypeStruct; M=pltpu.VMEM; D=pltpu.SemaphoreType.DMA
    return pl.pallas_call(functools.partial(attend_kernel,L,H),
        out_shape=[S((cap,H,KB,QB),bf),S((H//2,L,128),bf),S((nq,W,QB),f32),S((H,8,L),f32),S((H,HEAD,L),bf),S((H,L,128),bf)],
        in_specs=[pl.BlockSpec(memory_space=pltpu.SMEM)]*2+[A,V,V],
        out_specs=[A,A,A,V,A,A],
        scratch_shapes=[M((H,L,128),bf),M((H,HEAD,L),bf),M((H,L,128),bf),M((H*128,L),bf),M((W,L),bf),M((W,L),bf),M((H,HEAD+16,L),bf),M((H,HEAD+16,QB),f32),M((SLOTS,H,KB,QB),bf),
            M((2,W,QB),f32),M((2,H//2,QB,128),bf),M((8,QB),f32),D((SLOTS,)),D((2,)),D((2,)),D((2,)),D((H+2,))],
        compiler_params=pltpu.CompilerParams(vmem_limit_bytes=VMEM))(base,win,qkvt,codet,meta)

def flags(row):
    L=row.shape[1]; nb=L//256; nq=L//QB
    seg=row//4
    pad=row//2-2*seg
    known=row-2*(row//2)
    use=(pad==0)&(known==1)
    usef=use.astype(f32)
    x=jnp.concatenate([usef[:,b*256:(b+1)*256] for b in range(nb)]+[jnp.zeros((16-nb,256),f32)],0)
    incl=dot(x.astype(bf),(iota((256,256),0)<=iota((256,256),1)).astype(f32).astype(bf),1,0)
    tot=jnp.broadcast_to(incl[:,255:256],(16,256)).astype(bf)
    base=dot((iota((16,16),0)>iota((16,16),1)).astype(f32).astype(bf),tot,1,0)
    rank=(incl+base).astype(jnp.int32)-1
    rank=jnp.concatenate([rank[b:b+1] for b in range(nb)],1)
    rank=jnp.where(use,rank,-1)
    own=((pad==0)&(known!=1)).astype(jnp.int32)
    bits=iota((CODE,L),0)
    bit=lax.shift_right_logical(jnp.broadcast_to(seg,(CODE,L)),jnp.minimum(bits,9))&1
    codet=jnp.where(bits<10,jnp.where(bit==1,16.0,-16.0),jnp.where(bits==10,1.0,0.0)).astype(bf)
    meta=jnp.concatenate([rank,own,jnp.zeros((6,L),jnp.int32)],0)
    def edge(at): return jnp.concatenate([seg[:,i*QB+at:i*QB+at+1] for i in range(nq)]+[jnp.zeros((8-nq,1),jnp.int32)],0)
    low=jnp.sum(jnp.where(seg<edge(0),usef,0.0),1,keepdims=True)
    high=jnp.sum(jnp.where(seg<=edge(QB-1),usef,0.0),1,keepdims=True)
    csum=jnp.concatenate([(incl+base)[b:b+1] for b in range(nb)],1)
    starts=jnp.sum((csum<=(256*iota((16,1),0)).astype(f32)).astype(f32),1,keepdims=True)
    win=jnp.broadcast_to(jnp.concatenate([low,high,starts],0),(32,128)).astype(jnp.int32)
    return base[:,:128].astype(jnp.int32),win,codet,meta
LN2=math.log(2.0)
SPAN=384
def back_kernel(L,H,base_ref,win_ref,datt_hbm,p_hbm,ot_hbm,inv_ref,kct_hbm,vaug_hbm,qkvt_hbm,dq_hbm,dkvw_hbm,
                vaug_ref,kct,dkv,dkvt,pbuf,qacc,qkv,datt,ot,dq,psem,lsem,qsem,osem,tsem):
    W=H*HEAD; nq=L//QB
    groups=(begin(base_ref,L//256)+127)//128
    pieces=lax.fori_loop(0,nq,lambda i,s:s+window(win_ref,i)[1]+1,0)
    def pcopy(g):
        slot=lax.rem(g,SLOTS)
        return pltpu.make_async_copy(p_hbm.at[g],pbuf.at[slot],psem.at[slot])
    def keys(t):
        rows=pl.ds(al(t*KB,KB),KB)
        return [pltpu.make_async_copy(kct_hbm.at[:,:,rows],kct.at[:,:,rows],lsem.at[0,t]),pltpu.make_async_copy(vaug_hbm.at[:,rows],vaug_ref.at[:,rows],lsem.at[1,t])]
    def queries(i):
        slot=lax.rem(i,2); qsl=pl.ds(al(i*QB,QB),QB)
        return [pltpu.make_async_copy(a,b.at[slot],qsem.at[k,slot]) for k,(a,b) in enumerate(((qkvt_hbm.at[:,qsl],qkv),(datt_hbm.at[:,qsl],datt),(ot_hbm.at[i],ot)))]
    def each_key(fn):
        def body(t,c):
            for x in keys(t): fn(x)
            return c
        lax.fori_loop(0,(groups+KB//128-1)//(KB//128),body,0)
    each_key(lambda x:x.start())
    for x in queries(0): x.start()
    for s in range(SLOTS-1):
        @pl.when(s<pieces)
        def _(): pcopy(s).start()
    def clear(j,c):
        dkv[pl.ds(al(j*128,128),128),:]=jnp.zeros((128,2*W),f32)
        return c
    lax.fori_loop(0,groups,clear,0)
    each_key(lambda x:x.wait())
    def ocopy(i):
        slot=lax.rem(i,2)
        return pltpu.make_async_copy(dq.at[slot],dq_hbm.at[:,pl.ds(al(i*QB,QB),QB)],osem.at[slot])
    def block(i,g):
        slot=lax.rem(i,2)
        qsl=pl.ds(al(i*QB,QB),QB)
        first,full,rest,_=window(win_ref,i)
        for x in queries(i): x.wait()
        @pl.when(i+1<nq)
        def _():
            for x in queries(i+1): x.start()
        dt=jnp.concatenate([datt[slot,hp].astype(f32).T for hp in range(H//2)],0)
        prod=dt*ot[slot]
        daug=[];dz=[];qz=[];deltas=[];d1s=[]
        zero=jnp.zeros((HEAD,QB),bf)
        row=iota((16,QB),0)
        for h in range(H):
            hsl=slice(h*HEAD,(h+1)*HEAD)
            inv=inv_ref[h,0:1,qsl]
            delta=jnp.sum(prod[hsl],0,keepdims=True)*inv
            d1=dt[hsl]*inv
            low=d1.astype(bf)
            a=delta.astype(bf).astype(f32); b=(delta-a).astype(bf).astype(f32)
            extra=jnp.where(row==0,a,jnp.where(row==1,b,jnp.where(row==2,delta-a-b,0.0))).astype(bf)
            daug.append(jnp.concatenate([low,extra,jnp.zeros((HEAD-16,QB),bf)],0))
            q=qkv[slot,hsl,:]
            dz.append(jnp.concatenate([zero,low] if h%2 else [low,zero],0))
            qz.append(jnp.concatenate([zero,q] if h%2 else [q,zero],0))
            deltas.append(delta); d1s.append(d1)
        qacc[...]=jnp.zeros_like(qacc)
        def piece(off,size,g):
            ps=lax.rem(g,SLOTS)
            osl=pl.ds(off,size)
            @pl.when(g+SLOTS-1<pieces)
            def _(): pcopy(g+SLOTS-1).start()
            pcopy(g).wait()
            dss=[]
            for h in range(H):
                dss.append((pbuf[ps,h,:size,:].astype(f32)*dot(vaug_ref[h,osl,:],daug[h],1,0)).astype(bf))
            for h in range(H): qacc[h*HEAD:(h+1)*HEAD,:]+=dot(kct[h,:,osl],dss[h],1,0)
            for h in range(0,H,2):
                dkv[osl,h*HEAD:(h+2)*HEAD]+=dot(dss[h],qz[h],1,1)+dot(dss[h+1],qz[h+1],1,1)
                dkv[osl,W+h*HEAD:W+(h+2)*HEAD]+=dot(pbuf[ps,h,:size,:],dz[h],1,1)+dot(pbuf[ps,h+1,:size,:],dz[h+1],1,1)
        g=by_piece(first,full,rest,g,piece)
        @pl.when(i>=2)
        def _(): ocopy(i-2).wait()
        for h in range(H):
            hsl=slice(h*HEAD,(h+1)*HEAD); ksl=slice(W+h*HEAD,W+(h+1)*HEAD); vsl=slice(2*W+h*HEAD,2*W+(h+1)*HEAD)
            ps=inv_ref[h,1:2,qsl]
            ds=ps*(jnp.sum(qkv[slot,vsl,:].astype(f32)*d1s[h],0,keepdims=True)-deltas[h])
            dq[slot,hsl,:]=((qacc[hsl,:]+ds*qkv[slot,ksl,:].astype(f32))*0.125).astype(bf)
            dq[slot,ksl,:]=(ds*qkv[slot,hsl,:].astype(f32)*LN2).astype(bf)
            dq[slot,vsl,:]=(ps*d1s[h]).astype(bf)
        ocopy(i).start()
        return g
    lax.fori_loop(0,nq,block,0)
    lanes=iota((128,2*W),1)
    def turn(j,c):
        jsl=pl.ds(al(j*128,128),128)
        x=jnp.where(j<groups,dkv[jsl,:],0.0)
        dkvt[:,jsl]=jnp.where(lanes<W,x*LN2,x).astype(bf).T
        return c
    lax.fori_loop(0,groups+3,turn,0)
    def tcopy(s): return pltpu.make_async_copy(dkvt.at[:,pl.ds(al(begin(base_ref,s)//128*128,128),SPAN)],dkvw_hbm.at[s],tsem.at[s])
    for s in range(L//256): tcopy(s).start()
    for i in range(max(nq-2,0),nq): ocopy(i).wait()
    for s in range(L//256): tcopy(s).wait()

def back(base,win,datt,p,ot,inv,kct,vaug,qkvt,H):
    L=qkvt.shape[1]; W=H*HEAD
    V=pl.BlockSpec(memory_space=pltpu.VMEM); A=pl.BlockSpec(memory_space=pl.ANY); N=pl.BlockSpec(memory_space=pltpu.SMEM)
    S=jax.ShapeDtypeStruct; M=pltpu.VMEM; D=pltpu.SemaphoreType.DMA
    return pl.pallas_call(functools.partial(back_kernel,L,H),
        out_shape=[S((3*W,L),bf),S((L//256,2*W,SPAN),bf)],
        in_specs=[N,N,A,A,A,V,A,A,A],
        out_specs=[A,A],
        scratch_shapes=[M((H,L,128),bf),M((H,HEAD,L),bf),M((L+384,2*W),f32),M((2*W,L+384),bf),M((SLOTS,H,KB,QB),bf),M((W,QB),f32),
            M((2,3*W,QB),bf),M((2,H//2,QB,128),bf),M((2,W,QB),f32),M((2,3*W,QB),bf),
            D((SLOTS,)),D((2,L//KB)),D((3,2)),D((2,)),D((L//256,))],
        compiler_params=pltpu.CompilerParams(vmem_limit_bytes=VMEM))(base,win,datt,p,ot,inv,kct,vaug,qkvt)

def placed(base_ref,rank_row,span,own,s):
    r0=begin(base_ref,s)//128*128
    oh=(rank_row==iota((SPAN,256),0)+r0).astype(f32).astype(bf)
    return dot(span,oh,1,0)+own.astype(f32)

def place_kernel(L,W,base_ref,meta_ref,dq_in,dkvw_ref,tok_ref,w_ref,tg_ref,grad_ref,dq_ref):
    dq_ref[...]=dq_in[...]
    def place(s,c):
        ssl=pl.ds(al(s*256,256),256)
        dq_ref[W:3*W,ssl]=placed(base_ref,meta_ref[0:1,ssl],dkvw_ref[s],dq_ref[W:3*W,ssl],s).astype(bf)
        tg_ref[ssl,:]=dot(dq_ref[:,ssl],w_ref[...],0,1).astype(bf)
        return c
    lax.fori_loop(0,L//256,place,0)
    grad_ref[...]=dot(dq_ref[...],tok_ref[...],1,0).T.astype(bf)

def place_all(base,meta,dq,dkvw,tok,w,H):
    L,E=tok.shape; W=H*HEAD
    V=pl.BlockSpec(memory_space=pltpu.VMEM); S=jax.ShapeDtypeStruct
    return pl.pallas_call(functools.partial(place_kernel,L,W),out_shape=[S((L,E),bf),S((E,3*W),bf)],
        in_specs=[pl.BlockSpec(memory_space=pltpu.SMEM)]+[V]*5,out_specs=[V,V],scratch_shapes=[pltpu.VMEM((3*W,L),bf)],
        compiler_params=pltpu.CompilerParams(vmem_limit_bytes=VMEM))(base,meta,dq,dkvw,tok,w)
EPSILON=1e-05
def erf(x):
    x=jnp.clip(x,-3.832506856900711,3.832506856900711)
    x2=x*x
    top=0.00022905065861350646
    for c in (0.0034082910107109506,0.050955695062380861,0.18520832239976145,1.128379143519084): top=top*x2+c
    low=-1.1791602954361697e-7
    for c in (0.000023547966471313185,0.0010179625278914885,0.014070470171167667,0.11098505178285362,0.49746925110067538,1.0): low=low*x2+c
    return x*top/low
def norm(x):
    center=x-jnp.mean(x,-1,keepdims=True)
    inverse=lax.rsqrt(jnp.mean(center*center,-1,keepdims=True)+EPSILON)
    return center*inverse,inverse
def norm_back(e,n,inverse):
    return inverse*(e-jnp.mean(e,-1,keepdims=True)-n*jnp.mean(e*n,-1,keepdims=True))
def middle_kernel(a0_ref,a1_ref,tok_ref,cot_ref,wo_ref,wu_ref,wd_ref,gs_ref,out_ref,r1_ref,da_ref,go_ref,gu_ref,gd_ref,gg_ref):
    @pl.when(pl.program_id(0)==0)
    def _():
        for r in (go_ref,gu_ref,gd_ref,gg_ref): r[...]=jnp.zeros_like(r)
    P2=a0_ref.shape[0]
    att=jnp.concatenate([a0_ref[p] for p in range(P2)]+[a1_ref[p] for p in range(P2)],1)
    g0,g1,b0,b1=[gs_ref[r:r+1,:] for r in range(4)]
    n1,inv1=norm(tok_ref[...].astype(f32)+dot(att,wo_ref[...],1,0))
    first=(n1*g0+b0).astype(bf)
    hidden=dot(first,wu_ref[...],1,0)
    cdf=0.5*(1.0+erf(hidden*math.sqrt(0.5)))
    act=(hidden*cdf).astype(bf)
    slope=cdf+hidden*jnp.exp(-0.5*hidden*hidden)*(1.0/math.sqrt(2.0*math.pi))
    n2,inv2=norm(first.astype(f32)+dot(act,wd_ref[...],1,0))
    out_ref[...]=(n2*g1+b1).astype(bf)
    cot=cot_ref[...].astype(f32)
    r2=norm_back(cot*g1,n2,inv2)
    feed=r2.astype(bf)
    gd_ref[...]+=dot(act,feed,0,0)
    dh=(dot(feed,wd_ref[...],1,1)*slope).astype(bf)
    gu_ref[...]+=dot(first,dh,0,0)
    df=r2+dot(dh,wu_ref[...],1,1)
    r1=norm_back(df*g0,n1,inv1)
    r1_ref[...]=r1
    db=r1.astype(bf)
    go_ref[...]+=dot(att,db,0,0)
    da=dot(db,wo_ref[...],1,1).astype(bf)
    for p in range(2*P2): da_ref[p]=da[:,p*128:(p+1)*128]
    gg_ref[0:1,:]+=jnp.sum(df*n1,0,keepdims=True)
    gg_ref[1:2,:]+=jnp.sum(cot*n2,0,keepdims=True)
    gg_ref[2:3,:]+=jnp.sum(df,0,keepdims=True)
    gg_ref[3:4,:]+=jnp.sum(cot,0,keepdims=True)

def middle(a0,a1,tok,cot,wo,wu,wd,gs):
    P2,N,_=a0.shape; D=tok.shape[1]; F=wu.shape[1]
    T=max(t for t in (256,192,128,64,32,16) if N%t==0)
    tile=pl.BlockSpec((T,D),lambda i:(i,0))
    def pairs(k): return pl.BlockSpec((k,T,128),lambda i:(0,i,0))
    def whole(s): return pl.BlockSpec(s,lambda i:(0,)*len(s))
    return pl.pallas_call(middle_kernel,grid=(N//T,),
        in_specs=[pairs(P2),pairs(P2),tile,tile,whole((D,D)),whole((D,F)),whole((F,D)),whole((8,D))],
        out_specs=[tile,tile,pairs(2*P2),whole((D,D)),whole((D,F)),whole((F,D)),whole((8,D))],
        out_shape=[jax.ShapeDtypeStruct((N,D),bf),jax.ShapeDtypeStruct((N,D),f32),jax.ShapeDtypeStruct((2*P2,N,128),bf),
            jax.ShapeDtypeStruct((D,D),f32),jax.ShapeDtypeStruct((D,F),f32),jax.ShapeDtypeStruct((F,D),f32),jax.ShapeDtypeStruct((8,D),f32)],
        compiler_params=pltpu.CompilerParams(vmem_limit_bytes=60<<20))(a0,a1,tok,cot,wo,wu,wd,gs)
MESH=pl.DeviceIdType.MESH
class Net:
    def __init__(self,Z):
        dp=lax.axis_index("dp"); blk=lax.axis_index("blk")
        self.Z=Z; self.z=dp//2; self.y=dp%2; self.j=blk//2; self.c=blk%2
        self.sent=[]
    def at(self,z=None,y=None,j=None,c=None):
        z=self.z if z is None else z; y=self.y if y is None else y; j=self.j if j is None else j; c=self.c if c is None else c
        return (z*2+y,j*2+c)
    def signal(self):
        barrier=pltpu.get_barrier_semaphore()
        for d in [self.at(j=1-self.j),self.at(y=1-self.y),self.at(c=1-self.c)]+[self.at(z=lax.rem(self.z+k,self.Z)) for k in range(1,self.Z)]:
            pl.semaphore_signal(barrier,inc=1,device_id=d,device_id_type=MESH)
    def wait(self): pl.semaphore_wait(pltpu.get_barrier_semaphore(),2+self.Z)
    def greet(self):
        self.signal()
        self.wait()
    def copy(self,src,dst,ssem,rsem,device):
        return pltpu.make_async_remote_copy(src_ref=src,dst_ref=dst,send_sem=ssem,recv_sem=rsem,device_id=device,device_id_type=MESH)
    def send(self,src,dst,ssem,rsem,device,when=None):
        c=self.copy(src,dst,ssem,rsem,device)
        if when is None: c.start()
        else: pl.when(when)(c.start)
        self.sent.append((c,when))
    def drain(self):
        for c,when in self.sent:
            if when is None: c.wait_send()
            else: pl.when(when)(c.wait_send)

def gather_kernel(Z,block,E,W,rows,tok_hbm,cot_hbm,seg_ref,pad_ref,known_ref,wq_ref,wo_ref,wu_ref,wd_ref,gain_ref,shift_ref,
                  tok_out,bund_out,wmine_out,qkvt_out,base_out,win_out,code_out,meta_out,far_out,
                  tokb,farb,info_ref,infob,pack_ref,wall,bund,wt,qkvt,lsem,qsem,xs,xr,zs,zr,ys,yr,cs,cr,ts,tr,iss,isr):
    net=Net(Z); z,y,j,c=net.z,net.y,net.j,net.c
    NCH=block//rows; D=E
    sib=net.at(c=1-c); xd=net.at(j=1-j); yd=net.at(y=1-y)
    net.signal()
    mine=pltpu.make_async_copy(tok_hbm.at[j],tokb.at[j,c],lsem.at[0]); mine.start()
    far=pltpu.make_async_copy(cot_hbm.at[1-j],farb,lsem.at[3]); far.start()
    at=0
    for ref in (wq_ref,wo_ref,wu_ref,wd_ref):
        n=ref.shape[1]
        pack_ref[:,at:at+n]=ref[...]
        at+=n
    R=gain_ref.shape[1]
    place=(iota((R,128),1)==iota((R,128),0)+R*lax.rem(lax.axis_index("dp")*4+lax.axis_index("blk"),128//R)).astype(f32).astype(bf)
    pack_ref[:,at:]=jnp.concatenate([dot(gain_ref[...],place,1,0),dot(shift_ref[...],place,1,0),jnp.zeros((12,128),f32)],0).astype(bf)
    split=6*W
    wall[z,y,j,c]=pack_ref[:,:split]
    bund[y,j]=pack_ref[:,split:]
    info_ref[...]=seg_ref[...]*4+pad_ref[...]*2+known_ref[...]
    infob[j,c]=info_ref[j]
    net.wait()
    net.send(pack_ref.at[:,:split],wall.at[z,y,j,c],xs.at[0],xr.at[0],xd)
    net.send(pack_ref.at[:,split:],bund.at[y,j],xs.at[1],xr.at[1],xd)
    net.send(info_ref.at[1-j],infob.at[j,c],iss.at[0],isr.at[0],xd)
    net.send(info_ref.at[j],infob.at[j,c],iss.at[1],isr.at[1],sib)
    def chunk(k): return pl.ds(k*rows if type(k) is int else al(k*rows,rows),rows)
    for k in range(NCH):
        net.send(tok_hbm.at[1-j,chunk(k)],tokb.at[j,c,chunk(k)],ts.at[0,k],tr.at[0,k],xd)
        net.send(tok_hbm.at[j,chunk(k)],tokb.at[j,c,chunk(k)],ts.at[1,k],tr.at[1,k],sib)
    def piece(o,y_): return wall.at[o,y_,:,c]
    def landed(ref,sem): pltpu.make_async_copy(ref,ref,sem).wait()
    def pass_on(o):
        net.send(piece(o,y),piece(o,y),ys.at[o],yr.at[o],yd)
        net.send(piece(o,y),piece(o,y),cs.at[0,o],cr.at[0,o],sib)
    far.wait()
    far=pltpu.make_async_copy(farb,far_out,lsem.at[3]); far.start()
    landed(wall.at[z,y,1-j,c],xr.at[0])
    for k in range(1,Z):
        net.send(piece(z,y),piece(z,y),zs.at[k],zr.at[k],net.at(z=lax.rem(z+k,Z)))
    pass_on(z)
    landed(bund.at[y,1-j],xr.at[1])
    net.send(bund.at[y],bund.at[y],ys.at[Z],yr.at[Z],yd)
    for k in range(1,Z):
        o=lax.rem(z+Z-k,Z)
        landed(piece(o,y),zr.at[k])
        pass_on(o)
    for k in range(Z):
        o=lax.rem(z+Z-k,Z)
        landed(piece(o,1-y),yr.at[o])
        net.send(piece(o,1-y),piece(o,1-y),cs.at[1,o],cr.at[1,o],sib)
    for o in range(Z):
        for q in range(2): landed(wall.at[o,y if q==0 else 1-y,:,1-c],cr.at[q,o])
    landed(bund.at[1-y],yr.at[Z])
    outb=pltpu.make_async_copy(bund,bund_out,lsem.at[1]); outb.start()
    def qcopy(g):
        col=pl.ds(al(g*rows,rows),rows)
        return pltpu.make_async_copy(qkvt.at[:,col],qkvt_out.at[:,col],qsem.at[g])
    def project(jj,cc,come=None,onward=False):
        def body(k,carry):
            ref=tokb.at[jj,cc,chunk(k)]
            if come is not None: landed(ref,tr.at[come,k])
            if onward: net.copy(ref,ref,ts.at[2,k],tr.at[2,k],sib).start()
            g=(jj*2+cc)*NCH+k
            r=dot(wt[...],ref[...],1,1)
            qkvt[:,pl.ds(al(g*rows,rows),rows)]=jnp.concatenate([r[:W]*(math.log2(math.e)/8),r[W:]],0).astype(bf)
            qcopy(g).start()
            return carry
        lax.fori_loop(0,NCH,body,0)
    parts=[]
    for t in range(3):
        cols=pl.ds(al(t*2*W+c*W,W),W)
        part=wall[:,:,:,:,:,cols].reshape(D,W)
        wt[t*W:(t+1)*W,:]=part.T
        parts.append(part)
    wmine_out[...]=jnp.concatenate(parts,1)
    mine.wait()
    project(j,c)
    project(j,1-c,1)
    landed(infob.at[1-j,c],isr.at[0])
    net.send(infob.at[1-j,c],infob.at[1-j,c],iss.at[2],isr.at[2],sib)
    project(1-j,c,0,True)
    landed(infob.at[j,1-c],isr.at[1])
    landed(infob.at[1-j,1-c],isr.at[2])
    base_out[...],win_out[...],code_out[...],meta_out[...]=flags(jnp.concatenate([infob[0,0],infob[0,1],infob[1,0],infob[1,1]],1))
    project(1-j,1-c,2)
    outt=pltpu.make_async_copy(tokb,tok_out,lsem.at[2]); outt.start()
    net.drain()
    for k in range(NCH):
        ref=tokb.at[1-j,c,chunk(k)]
        net.copy(ref,ref,ts.at[2,k],tr.at[2,k],sib).wait_send()
    lax.fori_loop(0,4*NCH,lambda g,c:(qcopy(g).wait(),c)[1],0)
    outb.wait(); outt.wait(); far.wait()

def gather(tok,cot,seg,pad,known,wq,wo,wu,wd,gain,shift,Z,W):
    _,block,E=tok.shape; R=wq.shape[0]; C=6*W+wo.shape[1]+wu.shape[1]+wd.shape[1]+128
    rows=256; NCH=block//rows; L=4*block
    V=pl.BlockSpec(memory_space=pltpu.VMEM); A=pl.BlockSpec(memory_space=pl.ANY)
    S=jax.ShapeDtypeStruct; M=pltpu.VMEM; D=pltpu.SemaphoreType.DMA; I=jnp.int32
    return pl.pallas_call(functools.partial(gather_kernel,Z,block,E,W,rows),
        out_shape=[S((2,2,block,E),bf),S((2,2,R,C-6*W),bf),S((E,3*W),bf),S((3*W,L),bf),S((16,128),I),S((32,128),I),S((CODE,L),bf),S((8,L),I),S((block,E),bf)],
        in_specs=[A,A]+[V]*9,out_specs=[A,A,V,A,V,V,V,V,A],
        scratch_shapes=[M((2,2,block,E),bf),M((block,E),bf),M((2,1,block),I),M((2,2,1,block),I),M((R,C),bf),M((Z,2,2,2,R,6*W),bf),M((2,2,R,C-6*W),bf),M((3*W,E),bf),M((3*W,L),bf),
            D((4,)),D((4*NCH,)),D((2,)),D((2,)),D((Z,)),D((Z,)),D((Z+1,)),D((Z+1,)),D((2,Z)),D((2,Z)),D((3,NCH)),D((3,NCH)),D((3,)),D((3,))],
        compiler_params=pltpu.CompilerParams(collective_id=0,has_side_effects=True,vmem_limit_bytes=VMEM))(tok,cot,seg,pad,known,wq,wo,wu,wd,gain,shift)
def middle_net_kernel(Z,block,E,F,W,T,att_hbm,tok_hbm,cot_hbm,cotx_hbm,*rest):
    bunds=rest[:Z]; near_out,far_out,r1_out,datt_out=rest[Z:Z+4]; parts=rest[Z+4]
    (go_ref,gu_ref,gd_ref,gg_ref,gt_ref,aown,aget,tok,cot,wall,lay,r1,da,lsem,wsem,osem,asend,aget_sem,dsend,dget,bsend,bget)=rest[Z+5:]
    net=Net(Z); z,y,j,c=net.z,net.y,net.j,net.c
    NCH=block//T; n=2*NCH; P2=att_hbm.shape[0]; G=2
    sib=net.at(c=1-c)
    def place(t):
        jj=jnp.where(t<NCH,1-j,j)
        return jj,pl.ds(al(lax.rem(t,NCH)*T,T),T)
    def load(t):
        jj,rows=place(t)
        return [pltpu.make_async_copy(att_hbm.at[:,jj,c,rows],aown.at[t],lsem.at[0,t]),pltpu.make_async_copy(tok_hbm.at[jj,c,rows],tok.at[t],lsem.at[1,t])]
    def load_cot(t,near):
        rows=place(t)[1]
        return pltpu.make_async_copy((cot_hbm.at[j,rows] if near else cotx_hbm.at[rows]),cot.at[t],lsem.at[2,t])
    cols=[(0,E),(E,F),(E+F,E),(2*E+F,128)]
    loadw=[pltpu.make_async_copy(bunds[k],wall.at[lax.rem(z+Z-k,Z),:,:,c],wsem.at[k]) for k in range(Z)]
    for x in loadw: x.start()
    def start(t,near):
        for x in load(t): x.start()
        load_cot(t,near).start()
    for t in range(n): start(t,t>=NCH)
    barrier=pltpu.get_barrier_semaphore()
    pl.semaphore_signal(barrier,inc=1,device_id=sib,device_id_type=MESH)
    pl.semaphore_wait(barrier,1)
    def ship(t):
        jj,rows=place(t)
        return net.copy(att_hbm.at[:,jj,1-c,rows],aget.at[t],asend.at[t],aget_sem.at[t],sib)
    ship(0).start()
    weights=[net.copy(bunds[k],wall.at[lax.rem(z+Z-k,Z),:,:,c],bsend.at[k],bget.at[k],sib) for k in range(Z)]
    for x in weights: x.start()
    for t in range(1,n): ship(t).start()
    for x in loadw: x.wait()
    for k in range(Z):
        ref=wall.at[lax.rem(z+Z-k,Z),:,:,1-c]
        pltpu.make_async_copy(ref,ref,bget.at[k]).wait()
    def whole(a,b): return wall[:,:,:,:,:,a:a+b].reshape(E,b)
    gs=wall[:,:,:,:,:,cols[3][0]:].reshape(E//16,16,128).astype(f32)
    gsr=jnp.concatenate([jnp.sum(gs[q*8:(q+1)*8],0) for q in range(E//128)],1)
    g0,g1,b0,b1=[gsr[r:r+1,:] for r in range(4)]
    for r in (go_ref,gu_ref,gd_ref,gg_ref): r[...]=jnp.zeros_like(r)
    def out_near(t): return pltpu.make_async_copy(lay.at[t],near_out.at[place(t)[1]],osem.at[0,t])
    def out_far(t): return pltpu.make_async_copy(lay.at[t],far_out.at[place(t)[1]],osem.at[0,t])
    def out_r1(t):
        jj,rows=place(t)
        return pltpu.make_async_copy(r1.at[t],r1_out.at[jj,rows],osem.at[1,t])
    def out_da(t):
        jj,rows=place(t)
        return pltpu.make_async_copy(da.at[0,t],datt_out.at[:,jj,c,rows],osem.at[2,t])
    def ship_da(t):
        jj,rows=place(t)
        return net.copy(da.at[1,t],datt_out.at[:,jj,c,rows],dsend.at[t],dget.at[t],sib)
    def tiles(u,carry):
        ts=[G*u+g for g in range(G)]
        def each(f,*lists): return [f(*v) for v in zip(*lists)]
        for t in ts:
            for x in load(t): x.wait()
            pltpu.make_async_copy(cotx_hbm.at[place(t)[1]],cot.at[t],lsem.at[2,t]).wait()
            ship(t).wait_recv()
        def whole_att(t):
            mine=[aown[t,p] for p in range(P2)]; his=[aget[t,p] for p in range(P2)]
            return jnp.where(c==0,jnp.concatenate(mine+his,1),jnp.concatenate(his+mine,1))
        wo=whole(*cols[0]); wu=whole(*cols[1]); wd=whole(*cols[2])
        att=each(whole_att,ts)
        branch=each(lambda a:dot(a,wo,1,0),att)
        n1,inv1=zip(*each(lambda t,b:norm(tok[t].astype(f32)+b),ts,branch))
        first=each(lambda n:(n*g0+b0).astype(bf),n1)
        hidden=each(lambda a:dot(a,wu,1,0),first)
        cdf=each(lambda h:0.5*(1.0+erf(h*math.sqrt(0.5))),hidden)
        act=each(lambda h,p:(h*p).astype(bf),hidden,cdf)
        fed=each(lambda a:dot(a,wd,1,0),act)
        slope=each(lambda h,p:p+h*jnp.exp(-0.5*h*h)*(1.0/math.sqrt(2.0*math.pi)),hidden,cdf)
        n2,inv2=zip(*each(lambda a,b:norm(a.astype(f32)+b),first,fed))
        ct=each(lambda t:cot[t].astype(f32),ts)
        r2=each(lambda x,n,i:norm_back(x*g1,n,i),ct,n2,inv2)
        feed=each(lambda x:x.astype(bf),r2)
        dact=each(lambda x:dot(x,wd,1,1),feed)
        for t,n in zip(ts,n2): lay[t]=(n*g1+b1).astype(bf)
        both=lambda v:jnp.concatenate(v,0)
        gd_ref[...]+=dot(both(act),both(feed),0,0)
        dh=each(lambda x,s:(x*s).astype(bf),dact,slope)
        df=each(lambda x,h:x+dot(h,wu,1,1),r2,dh)
        gu_ref[...]+=dot(both(first),both(dh),0,0)
        dr=each(lambda x,n,i:norm_back(x*g0,n,i),df,n1,inv1)
        db=each(lambda x:x.astype(bf),dr)
        d=each(lambda x:dot(x,wo,1,1).astype(bf),db)
        go_ref[...]+=dot(both(att),both(db),0,0)
        for t,x,e in zip(ts,dr,d):
            r1[t]=x.astype(r1.dtype)
            for p in range(P2):
                lo=e[:,p*128:(p+1)*128]; hi=e[:,W+p*128:W+(p+1)*128]
                da[0,t,p]=jnp.where(c==0,lo,hi)
                da[1,t,p]=jnp.where(c==0,hi,lo)
        down=lambda v:sum(jnp.sum(x,0,keepdims=True) for x in v)
        gg_ref[0:1,:]+=down(each(lambda x,n:x*n,df,n1))
        gg_ref[1:2,:]+=down(each(lambda x,n:x*n,ct,n2))
        gg_ref[2:3,:]+=down(df)
        gg_ref[3:4,:]+=down(ct)
        for t in ts:
            @pl.when(t<NCH)
            def _(): out_far(t).start()
            @pl.when(t>=NCH)
            def _(): out_near(t).start()
            out_r1(t).start(); out_da(t).start(); ship_da(t).start()
        return carry
    lax.fori_loop(0,n//G,tiles,0)
    ggt=jnp.concatenate([gg_ref[...],jnp.zeros((120,E),f32)],0).T
    gt_ref[...]=ggt
    R=E//(2*Z)
    at=0
    for ref in (go_ref,gu_ref,gd_ref,gt_ref):
        parts[:,:,at:at+ref.shape[1]]=ref[...].astype(bf).reshape(2*Z,R,ref.shape[1])
        at+=ref.shape[1]
    for x in weights: x.wait_send()
    for t in range(n):
        ship(t).wait_send(); out_r1(t).wait(); out_da(t).wait(); ship_da(t).wait()
        (out_far if t<NCH else out_near)(t).wait()

def middle_net(att,tok,cot,cotx,bunds,Z,W,F):
    P2,_,_,block,_=att.shape; E=tok.shape[-1]; C=bunds[0].shape[-1]
    T=256; NCH=block//T; n=2*NCH
    V=pl.BlockSpec(memory_space=pltpu.VMEM); A=pl.BlockSpec(memory_space=pl.ANY)
    S=jax.ShapeDtypeStruct; M=pltpu.VMEM; D=pltpu.SemaphoreType.DMA
    return pl.pallas_call(functools.partial(middle_net_kernel,Z,block,E,F,W,T),
        out_shape=[S((block,E),bf),S((block,E),bf),S((2,block,E),f32),S((P2,2,2,block,128),bf)]+[S((2*Z,E//(2*Z),C),bf)],
        in_specs=[A]*(4+Z),out_specs=[A,A,A,A,V],
        scratch_shapes=[M((E,E),f32),M((E,F),f32),M((F,E),f32),M((8,E),f32),M((E,128),f32),
            M((n,P2,T,128),bf),M((n,P2,T,128),bf),M((n,T,E),bf),M((n,T,E),bf),M((Z,2,2,2,16,C),bf),M((n,T,E),bf),M((n,T,E),f32),M((2,n,P2,T,128),bf),
            D((3,n)),D((Z,)),D((3,n)),D((n,)),D((n,)),D((n,)),D((n,)),D((Z,)),D((Z,))],
        compiler_params=pltpu.CompilerParams(collective_id=2,has_side_effects=True,vmem_limit_bytes=VMEM))(att,tok,cot,cotx,*bunds)
def reduce_kernel(Z,block,E,W,C1,rows,base_ref,meta_ref,dq_hbm,dkvw_hbm,tok_hbm,w_hbm,r1_hbm,parts,tok_out,grad_out,
     dq,dkvw,tok,w,r1,own,tgf,tgr,tgs,ob,s0,r0,g0,s1,r1b,su,ru,fin,sx,rx,se,re,sxe,rxe,
     lsem,osem,ts,tr,xs,xr,cs,cr,ys,yr,us,ur,fs,fr):
    net=Net(Z); z,y,j,c=net.z,net.y,net.j,net.c
    NCH=block//rows; half=2*block
    sib=net.at(c=1-c); xd=net.at(j=1-j); yd=net.at(y=1-y)
    def side(jj): return pl.ds(al(jj*half,128),half)
    def spans(jj): return pl.ds(jj*2*NCH,2*NCH)
    loads=[pltpu.make_async_copy(a,b,lsem.at[k]) for k,(a,b) in enumerate(((dkvw_hbm.at[spans(1-j)],dkvw.at[spans(1-j)]),(dq_hbm.at[:,side(1-j)],dq.at[:,side(1-j)]),(w_hbm,w),(r1_hbm,r1),
        (dq_hbm.at[:,side(j)],dq.at[:,side(j)]),(tok_hbm,tok),(dkvw_hbm.at[spans(j)],dkvw.at[spans(j)])))]
    net.signal()
    for x in loads: x.start()
    def chunk(k): return pl.ds(k*rows,rows)
    def landed(ref,sem): pltpu.make_async_copy(ref,ref,sem).wait()
    def position(jj,cc,k): return pl.ds(al(((jj*2+cc)*NCH+k)*rows,rows),rows)
    def place(jj,cc,k):
        ssl=position(jj,cc,k)
        dq[W:3*W,ssl]=placed(base_ref,meta_ref[0:1,ssl],dkvw[(jj*2+cc)*NCH+k],dq[W:3*W,ssl],(jj*2+cc)*NCH+k).astype(bf)
    def to_tokens(jj,cc,k): return dot(dq[:,position(jj,cc,k)],w[...],0,1)
    def for_sibling(t):
        jj=1-j if t==0 else j
        for k in range(NCH):
            tgf[jj,chunk(k),:]=to_tokens(jj,1-c,k).astype(bf)
            net.send(tgf.at[jj,chunk(k)],tgr.at[jj,chunk(k)],ts.at[t,k],tr.at[t,k],sib)
    def split(x,n): return x.reshape(Z,2,2,2,16,n)
    def core_sum(v,lo,n):
        x=dot(dq[lo:lo+n,:],tok[...],1,0).T.astype(bf)
        x=split(x,n)
        s0[:,:,:,:,lo:lo+n]=jnp.where(c==0,x[:,:,:,1],x[:,:,:,0])
        net.send(s0.at[:,:,:,:,lo:lo+n],r0.at[:,:,:,:,lo:lo+n],cs.at[v],cr.at[v],sib)
        mine=jnp.where(c==0,x[:,:,:,0],x[:,:,:,1])
        for t in range(lo//W,(lo+n)//W):
            part=mine[:,:,:,:,t*W-lo:(t+1)*W-lo]
            @pl.when(c==0)
            def _(): g0[:,:,:,:,2*t*W:(2*t+1)*W]=part
            @pl.when(c==1)
            def _(): g0[:,:,:,:,(2*t+1)*W:(2*t+2)*W]=part
    def core_get(v,lo,n):
        landed(r0.at[:,:,:,:,lo:lo+n],cr.at[v])
        for t in range(lo//W,(lo+n)//W):
            part=r0[:,:,:,:,t*W:(t+1)*W]
            @pl.when(c==0)
            def _(): g0[:,:,:,:,(2*t+1)*W:(2*t+2)*W]=part
            @pl.when(c==1)
            def _(): g0[:,:,:,:,2*t*W:(2*t+1)*W]=part
    cut=[pl.ds(2*t*W,2*W) for t in range(3)]
    def to_y(v):
        s1[:,:,:,cut[v]]=jnp.where(y==0,g0[:,1,:,:,cut[v]],g0[:,0,:,:,cut[v]])
        net.send(s1.at[:,:,:,cut[v]],r1b.at[:,:,:,cut[v]],ys.at[v],yr.at[v],yd)
    def to_z(v):
        landed(r1b.at[:,:,:,cut[v]],yr.at[v])
        for k in range(1,Z):
            o=lax.rem(z+k,Z)
            su[k,:,:,cut[v]]=(g0[o,y,:,:,cut[v]].astype(f32)+r1b[o,:,:,cut[v]].astype(f32)).astype(bf)
            net.send(su.at[k,:,:,cut[v]],ru.at[k,:,:,cut[v]],us.at[v,k],ur.at[v,k],net.at(z=o))
    def to_x(v):
        sum_=g0[z,y,:,:,cut[v]].astype(f32)+r1b[z,:,:,cut[v]].astype(f32)
        for k in range(1,Z):
            landed(ru.at[k,:,:,cut[v]],ur.at[v,k])
            sum_=sum_+ru[k,:,:,cut[v]].astype(f32)
        fin[:,:,cut[v]]=sum_
        sx[:,cut[v]]=jnp.where(j==0,sum_[1],sum_[0]).astype(bf)
        net.send(sx.at[:,cut[v]],rx.at[:,cut[v]],fs.at[v],fr.at[v],xd)
    for x in loads[:3]: x.wait()
    for k in range(NCH): place(1-j,1-c,k)
    net.wait()
    for_sibling(0)
    for k in range(NCH): place(1-j,c,k)
    for k in range(NCH): own[1-j,chunk(k),:]=to_tokens(1-j,c,k)
    loads[3].wait()
    def total(jj,k): return (own[jj,chunk(k),:]+tgr[jj,chunk(k),:].astype(f32)+r1[jj,chunk(k),:]).astype(bf)
    for k in range(NCH):
        landed(tgr.at[1-j,chunk(k)],tr.at[0,k])
        tgs[chunk(k),:]=total(1-j,k)
        net.send(tgs.at[chunk(k)],ob.at[j,chunk(k)],xs.at[k],xr.at[k],xd)
    for x in loads[4:]: x.wait()
    core_sum(0,0,W)
    for cc in (1-c,c):
        for k in range(NCH): place(j,cc,k)
    core_get(0,0,W)
    to_y(0)
    core_sum(1,W,W)
    core_sum(2,2*W,W)
    core_get(1,W,W)
    to_y(1)
    early=parts[0].astype(f32)
    for k in range(1,2*Z): early=early+parts[k].astype(f32)
    early=early.reshape(2,2,16,C1)
    early0=jnp.where(c==0,early[:,0],early[:,1])
    se[...]=jnp.where(c==0,early[:,1],early[:,0]).astype(bf)
    net.send(se,re,cs.at[3],cr.at[3],sib)
    core_get(2,2*W,W)
    to_y(2)
    to_z(0)
    for_sibling(1)
    to_z(1)
    landed(re,cr.at[3])
    early0=early0+re[...].astype(f32)
    early1=jnp.where(j==0,early0[0],early0[1])
    sxe[...]=jnp.where(j==0,early0[1],early0[0]).astype(bf)
    net.send(sxe,rxe,fs.at[3],fr.at[3],xd)
    to_x(0)
    for k in range(NCH): own[j,chunk(k),:]=to_tokens(j,c,k)
    to_z(2)
    to_x(1)
    for k in range(NCH):
        landed(tgr.at[j,chunk(k)],tr.at[1,k])
        ob[j,chunk(k),:]=total(j,k)
    near=pltpu.make_async_copy(ob.at[j],tok_out.at[j],osem.at[0]); near.start()
    to_x(2)
    landed(rxe,fr.at[3])
    grad_out[:,6*W:]=early1+rxe[...].astype(f32)
    for v in range(3):
        landed(rx.at[:,cut[v]],fr.at[v])
        grad_out[:,cut[v]]=jnp.where(j==0,fin[0,:,cut[v]],fin[1,:,cut[v]])+rx[:,cut[v]].astype(f32)
    for k in range(NCH): landed(ob.at[1-j,chunk(k)],xr.at[k])
    last=pltpu.make_async_copy(ob.at[1-j],tok_out.at[1-j],osem.at[1]); last.start()
    net.drain()
    near.wait(); last.wait()

def reduce(base,meta,dq,dkvw,tok,w,r1,parts,Z,W):
    _,block,E=r1.shape; L=4*block; C1=parts.shape[2]; C=6*W
    rows=256; NCH=block//rows
    V=pl.BlockSpec(memory_space=pltpu.VMEM); A=pl.BlockSpec(memory_space=pl.ANY)
    S=jax.ShapeDtypeStruct; M=pltpu.VMEM; D=pltpu.SemaphoreType.DMA
    return pl.pallas_call(functools.partial(reduce_kernel,Z,block,E,W,C1,rows),
        out_shape=[S((2,block,E),bf),S((16,C+C1),f32)],
        in_specs=[pl.BlockSpec(memory_space=pltpu.SMEM),V,A,A,A,A,A,V],out_specs=[A,V],
        scratch_shapes=[M(dq.shape,bf),M(dkvw.shape,bf),M(tok.shape,bf),M(w.shape,bf),M(r1.shape,f32),M((2,block,E),f32),M((2,block,E),bf),M((2,block,E),bf),M((block,E),bf),M((2,block,E),bf),
            M((Z,2,2,16,3*W),bf),M((Z,2,2,16,3*W),bf),M((Z,2,2,16,C),bf),M((Z,2,16,C),bf),M((Z,2,16,C),bf),
            M((Z,2,16,C),bf),M((Z,2,16,C),bf),M((2,16,C),f32),M((16,C),bf),M((16,C),bf),M((2,16,C1),bf),M((2,16,C1),bf),M((16,C1),bf),M((16,C1),bf),
            D((7,)),D((2,)),D((2,NCH)),D((2,NCH)),D((NCH,)),D((NCH,)),D((4,)),D((4,)),D((3,)),D((3,)),D((3,Z)),D((3,Z)),D((4,)),D((4,))],
        compiler_params=pltpu.CompilerParams(collective_id=1,has_side_effects=True,vmem_limit_bytes=VMEM))(base,meta,dq,dkvw,tok,w,r1,parts)

def finish_kernel(W,near,far,tg_hbm,grads,lay_out,tg_out,gq,go,gu,gd,gg,gs,lay,tg,sem):
    j=lax.axis_index("blk")//2
    come=[pltpu.make_async_copy(a,b,sem.at[k]) for k,(a,b) in enumerate(((near,lay.at[j]),(far,lay.at[1-j]),(tg_hbm.at[0],tg.at[0]),(tg_hbm.at[1],tg.at[1])))]
    go_out=[pltpu.make_async_copy(a,b,sem.at[4+k]) for k,(a,b) in enumerate(((lay.at[j],lay_out.at[j]),(lay.at[1-j],lay_out.at[1-j]),(tg.at[0],tg_out.at[0]),(tg.at[1],tg_out.at[1])))]
    for x in come: x.start()
    at=0
    for ref in (gq,go,gu,gd):
        n=ref.shape[1]
        ref[...]=grads[:,at:at+n]
        at+=n
    t=grads[:,at:].T
    gg[...]=t[0:2,:]
    gs[...]=t[2:4,:]
    for x,o in zip(come,go_out):
        x.wait(); o.start()
    for o in go_out: o.wait()

def finish(near,far,tg,grads,W,F):
    _,block,E=tg.shape
    V=pl.BlockSpec(memory_space=pltpu.VMEM); A=pl.BlockSpec(memory_space=pl.ANY); S=jax.ShapeDtypeStruct
    return pl.pallas_call(functools.partial(finish_kernel,W),
        out_shape=[S(tg.shape,bf),S(tg.shape,bf),S((16,6*W),f32),S((16,E),f32),S((16,F),f32),S((16,E),f32),S((2,16),f32),S((2,16),f32)],
        in_specs=[A,A,A,V],out_specs=[A,A]+[V]*6,scratch_shapes=[pltpu.VMEM(tg.shape,bf),pltpu.VMEM(tg.shape,bf),pltpu.SemaphoreType.DMA((8,))],
        compiler_params=pltpu.CompilerParams(vmem_limit_bytes=VMEM))(near,far,tg,grads)
def shards(tokens,cotangent,segments,padding,known,w_qkv,w_out,w_up,w_down,norm_gains,norm_shifts):
    micro,rows,block,D=tokens.shape
    J=lax.axis_size("blk")//2; dps=lax.axis_size("dp")
    units=micro*rows
    assert units==J
    H=HEADS//2; W=H*HEAD; L=2*J*block; F=w_up.shape[1]
    quick=J==2 and dps%2==0 and w_qkv.shape[0]==16 and block%256==0
    me=lax.axis_index("blk"); chip=me//2; core=me%2
    flat=lambda x:x.reshape((units,)+x.shape[2:])
    if quick:
        Z=dps//2
        cot=flat(cotangent)
        tok,bund,w_mine,qkvt,base,win,codet,meta,far=gather(flat(tokens),cot,*[flat(x)[:,None,:] for x in (segments,padding,known)],w_qkv,w_out,w_up,w_down,norm_gains,norm_shifts,Z,W)
        bunds=[bund]+[lax.ppermute(bund,"dp",[(d,(d//2+k)%Z*2+d%2) for d in range(dps)]) for k in range(1,Z)]
        across=[(b,b^2) for b in range(4)]
        cotx=lax.ppermute(far,"blk",across)
        p,att,ot,inv,kct,vaug=attend(base,win,qkvt,codet,meta,H)
        near,far,r1,datt,parts=middle_net(att.reshape(H//2,2,2,block,128),tok,cot,cotx,bunds,Z,W,F)
        parts=lax.all_to_all(parts,"dp",0,0,tiled=True)
        layx=lax.ppermute(far,"blk",across)
        dq,dkvw=back(base,win,datt.reshape(H//2,L,128),p,ot,inv,kct,vaug,qkvt,H)
        tg,grads=reduce(base,meta,dq,dkvw,tok.reshape(L,D),w_mine,r1,parts,Z,W)
        out=finish(near,layx,tg,grads,W,F)
        return (out[0].reshape(tokens.shape),out[1].reshape(tokens.shape))+tuple(out[2:])
    def to_chip(s): return [(2*a+c,2*((a+s)%J)+c) for a in range(J) for c in range(2)]
    swap=[(b,b^1) for b in range(2*J)]
    def other(x): return lax.ppermute(x,"blk",swap)
    def scatter_units(x):
        got=[]
        for s in range(J):
            mine=lax.dynamic_index_in_dim(x,(chip+s)%J,0,keepdims=False)
            got.append(mine if s==0 else lax.ppermute(mine,"blk",to_chip(s)))
        return jnp.stack([lax.dynamic_index_in_dim(jnp.stack(got),(chip-j)%J,0,keepdims=False) for j in range(J)])
    def both(mine,his):
        return jnp.stack([jnp.where(core==0,mine,his),jnp.where(core==0,his,mine)],1)
    def part(x,axis,index): return lax.dynamic_index_in_dim(x,index,axis,keepdims=False)
    own_info=scatter_units(flat(segments*4+padding*2+known)); info=both(own_info,other(own_info)).reshape(1,L)
    own_tok=scatter_units(flat(tokens)); all_tok=both(own_tok,other(own_tok)).reshape(L,D)
    own_cot=scatter_units(flat(cotangent)).reshape(L//2,D)
    full_qkv,full_out,full_up,full_down=[lax.all_gather(w,("dp","blk"),axis=0,tiled=True) for w in (w_qkv,w_out,w_up,w_down)]
    gs=lax.all_gather(jnp.concatenate([norm_gains,norm_shifts],0),("dp","blk"),axis=1,tiled=True).astype(f32)
    gs=jnp.concatenate([gs,jnp.zeros_like(gs)],0)
    w_mine=part(full_qkv.reshape(D,3,2,W),2,core).reshape(D,3*W)
    scale=jnp.where(jnp.arange(3*W)<W,math.log2(math.e)/8,1.0).astype(f32)
    qkvt=(jnp.einsum("ld,de->el",all_tok,w_mine,preferred_element_type=f32)*scale[:,None]).astype(bf)
    base,win,codet,meta=flags(info)
    p,att,ot,inv,kct,vaug=attend(base,win,qkvt,codet,meta,H)
    att=att.reshape(H//2,J,2,block,128)
    mine=part(att,2,core).reshape(H//2,J*block,128); his=other(part(att,2,1-core)).reshape(H//2,J*block,128)
    a0=jnp.where(core==0,mine,his); a1=jnp.where(core==0,his,mine)
    out,r1,da,go,gu,gd,gg=middle(a0,a1,own_tok.reshape(L//2,D),own_cot,full_out,full_up,full_down,gs)
    da=da.reshape(2,H//2,J,block,128)
    dmine=part(da,0,core); dhis=other(part(da,0,1-core))
    datt=jnp.stack([jnp.where(core==0,dmine,dhis),jnp.where(core==0,dhis,dmine)],2).reshape(H//2,L,128)
    dq,dkvw=back(base,win,datt,p,ot,inv,kct,vaug,qkvt,H)
    tg,gq=place_all(base,meta,dq,dkvw,all_tok,w_mine,H)
    tg=tg.reshape(J,2,block,D)
    layer_out=scatter_units(out.reshape(J,block,D)).reshape(tokens.shape)
    own_tg=(part(tg,1,core).astype(f32)+other(part(tg,1,1-core)).astype(f32)+r1.reshape(J,block,D)).astype(bf)
    token_grad=scatter_units(own_tg).reshape(tokens.shape)
    gq=gq.astype(f32).reshape(D,3,1,W)
    gq=jnp.where(core==0,jnp.concatenate([gq,jnp.zeros_like(gq)],2),jnp.concatenate([jnp.zeros_like(gq),gq],2)).reshape(D,6*W)
    grads=lax.psum_scatter(jnp.concatenate([gq,go,gu,gd],1),("dp","blk"),scatter_dimension=0,tiled=True)
    gg=lax.psum_scatter(gg[:4],("dp","blk"),scatter_dimension=1,tiled=True)
    a,b,e=6*W,6*W+D,6*W+D+F
    return (layer_out,token_grad,grads[:,:a],grads[:,a:b],grads[:,b:e],grads[:,e:],gg[:2],gg[2:])

def solution(mesh):
    in_specs = (
        P(None, "dp", "blk", None),
        P(None, "dp", "blk", None),
        P(None, "dp", "blk"),
        P(None, "dp", "blk"),
        P(None, "dp", "blk"),
        P(("dp", "blk"), None),
        P(("dp", "blk"), None),
        P(("dp", "blk"), None),
        P(("dp", "blk"), None),
        P(None, ("dp", "blk")),
        P(None, ("dp", "blk")),
    )
    out_specs = (
        P(None, "dp", "blk", None),
        P(None, "dp", "blk", None),
        P(("dp", "blk"), None),
        P(("dp", "blk"), None),
        P(("dp", "blk"), None),
        P(("dp", "blk"), None),
        P(None, ("dp", "blk")),
        P(None, ("dp", "blk")),
    )
    return jax.shard_map(shards, mesh=mesh, in_specs=in_specs, out_specs=out_specs, check_vma=False)
```

```python
import functools, math
import jax, jax.numpy as jnp
from jax import lax
from jax.experimental import pallas as pl
from jax.experimental.pallas import tpu as pltpu
from jax.sharding import PartitionSpec as P

HEADS = 8
bf=jnp.bfloat16; f32=jnp.float32
HEAD=64
QB=512
KB=512
SRC=1024
SAFE=60.0
CODE=16
VMEM=(64<<20)-(128<<10)
SLOTS=3
def dot(a,b,ca,cb): return lax.dot_general(a,b,(((ca,),(cb,)),((),())),preferred_element_type=f32)
def al(x,n): return pl.multiple_of(x,n)
def iota(shape,axis): return lax.broadcasted_iota(jnp.int32,shape,axis)

def begin(base_ref,b):
    return base_ref[b,0]

def window(win_ref,i):
    start=win_ref[i,0]//128*128
    groups=(win_ref[8+i,0]-start+127)//128
    full=(groups-1)//(KB//128)
    return start,full,groups-full*(KB//128),groups

def by_piece(first,full,rest,g,fn):
    def body(j,g):
        fn(al(first+j*KB,128),KB,g)
        return g+1
    g=lax.fori_loop(0,full,body,g)
    for r in range(1,KB//128+1):
        @pl.when(rest==r)
        def _(): fn(al(first+full*KB,128),r*128,g)
    return g+1

def attend_kernel(L,H,base_ref,win_ref,qkvt_hbm,codet_ref,meta_ref,p_hbm,att_hbm,ot_hbm,inv_ref,kct_hbm,vaug_hbm,
                  kaug_ref,kct_ref,vaug_ref,kvt,q_ref,v_ref,vct,acc,pbuf,obuf,abuf,top_ref,psem,osem,asem,ksem,lsem):
    W=H*HEAD; nq=L//QB
    total=begin(base_ref,L//256)
    come=[pltpu.make_async_copy(qkvt_hbm.at[W+h*HEAD:W+(h+1)*HEAD],kvt.at[h*128:h*128+HEAD],lsem.at[h]) for h in range(H)]
    come+=[pltpu.make_async_copy(qkvt_hbm.at[2*W:],v_ref,lsem.at[H]),pltpu.make_async_copy(qkvt_hbm.at[:W],q_ref,lsem.at[H+1])]
    for x in come: x.start()
    for h in range(H):
        kvt[h*128+HEAD:h*128+HEAD+CODE,:]=codet_ref[...]
        kvt[h*128+HEAD+CODE:(h+1)*128,:]=jnp.zeros((HEAD-CODE,L),bf)
    vct[:,HEAD:,:]=jnp.ones((H,16,L),bf)
    for x in come[:H+1]: x.wait()
    row=iota((256,256),0)
    down=iota((256,SRC),0)
    def dest(d,c):
        first=jnp.minimum(win_ref[16+d,0]//128*128,L-SRC)
        last=win_ref[17+d,0]
        def src(t,a):
            ssl=pl.ds(al(jnp.minimum(first+t*SRC,L-SRC),128),SRC)
            oh=((meta_ref[0:1,ssl]==down+d*256)&(lane>=first+t*SRC-jnp.minimum(first+t*SRC,L-SRC))).astype(f32).astype(bf)
            return a[0]+dot(kvt[:,ssl],oh,1,1),a[1]+dot(v_ref[:,ssl],oh,1,1)
        lane=iota((256,SRC),1)
        ka,va=src(0,(jnp.zeros((H*128,256),f32),jnp.zeros((W,256),f32)))
        ka,va=lax.fori_loop(1,(last-first+SRC-1)//SRC,src,(ka,va))
        dsl=pl.ds(al(d*256,256),256)
        for h in range(H):
            k1=jnp.where(row[:128]==HEAD+10,-2560.0,ka[h*128:(h+1)*128])
            kaug_ref[h,dsl,:]=k1.astype(bf).T
            kct_ref[h,:,dsl]=k1[:HEAD].astype(bf)
            v1=va[h*HEAD:(h+1)*HEAD]
            vct[h,:HEAD,dsl]=v1.astype(bf)
            vaug_ref[h,dsl,:]=jnp.concatenate([v1,jnp.where(row[:HEAD]<3,-1.0,0.0)],0).astype(bf).T
        return c
    lax.fori_loop(0,(total+255)//256,dest,0)
    keep=[pltpu.make_async_copy(kct_ref,kct_hbm,ksem.at[0]),pltpu.make_async_copy(vaug_ref,vaug_hbm,ksem.at[1])]
    for x in keep: x.start()
    come[H+1].wait()
    bound=jnp.float32(0)
    for h in range(H):
        q=q_ref[h*HEAD:(h+1)*HEAD,:].astype(f32); k=kvt[h*128:h*128+HEAD,:].astype(f32)
        bound=jnp.maximum(bound,jnp.max(jnp.sum(q*q,0,keepdims=True))*jnp.max(jnp.sum(k*k,0,keepdims=True)))
    safe=bound<SAFE*SAFE

    def pcopy(g):
        slot=lax.rem(g,SLOTS)
        return pltpu.make_async_copy(pbuf.at[slot],p_hbm.at[g],psem.at[slot])
    def ocopy(i):
        slot=lax.rem(i,2)
        return pltpu.make_async_copy(obuf.at[slot],ot_hbm.at[i],osem.at[slot])
    def acopy(i):
        slot=lax.rem(i,2)
        return pltpu.make_async_copy(abuf.at[slot],att_hbm.at[:,pl.ds(al(i*QB,QB),QB),:],asem.at[slot])
    def block(i,g):
        slot=lax.rem(i,2)
        qsl=pl.ds(al(i*QB,QB),QB)
        first,full,rest,groups=window(win_ref,i)
        qa=[jnp.concatenate([q_ref[h*HEAD:(h+1)*HEAD,qsl],codet_ref[:,qsl],jnp.zeros((HEAD-CODE,QB),bf)],0) for h in range(H)]
        own=meta_ref[1:2,qsl]>0
        sself=[]
        for h in range(H):
            x=q_ref[h*HEAD:(h+1)*HEAD,qsl].astype(f32)*kvt[h*128:h*128+HEAD,qsl].astype(f32)
            sself.append(jnp.where(own,jnp.sum(x,0,keepdims=True),-1e30))
        acc[...]=jnp.zeros_like(acc)
        top_ref[...]=jnp.zeros_like(top_ref)
        row=iota((128,QB),0)
        def strict(h,osl):
            k=kaug_ref[h,osl,:]
            x=qa[h].astype(f32)
            plain=dot(k,jnp.where(row<HEAD,x,0.0).astype(bf),1,0)
            return jnp.where(dot(k,jnp.where(row<HEAD,0.0,x).astype(bf),1,0)>-1.0,plain,-1e30)
        @pl.when(jnp.logical_not(safe))
        def _():
            for h in range(H):
                def more(j,m): return jnp.maximum(m,jnp.max(strict(h,pl.ds(al(first+j*128,128),128)),0,keepdims=True))
                top_ref[h:h+1,:]=lax.fori_loop(0,groups,more,sself[h])
        def piece(off,size,g):
            ps=lax.rem(g,SLOTS)
            osl=pl.ds(off,size)
            @pl.when(g>=SLOTS)
            def _(): pcopy(g-SLOTS).wait()
            @pl.when(safe)
            def _():
                keepp=[]
                for h in range(H):
                    p=jnp.exp2(dot(kaug_ref[h,osl,:],qa[h],1,0)).astype(bf)
                    pbuf[ps,h,:size,:]=p
                    keepp.append(p)
                for h in range(H): acc[h]+=dot(vct[h,:,osl],keepp[h],1,0)
            @pl.when(jnp.logical_not(safe))
            def _():
                for h in range(H):
                    def put(j,c):
                        jsl=pl.ds(al(off+j*128,128),128)
                        p=jnp.exp2(strict(h,jsl)-top_ref[h:h+1,:]).astype(bf)
                        pbuf[ps,h,pl.ds(al(j*128,128),128),:]=p
                        acc[h]+=dot(vct[h,:,jsl],p,1,0)
                        return c
                    lax.fori_loop(0,size//128,put,0)
            pcopy(g).start()
        g=by_piece(first,full,rest,g,piece)
        @pl.when(i>=2)
        def _(): ocopy(i-2).wait(); acopy(i-2).wait()
        for h in range(H):
            ps=jnp.exp2(sself[h]-top_ref[h:h+1,:])
            inv=1.0/(acc[h,HEAD:HEAD+1,:]+ps)
            obuf[slot,h*HEAD:(h+1)*HEAD,:]=(acc[h,:HEAD,:]+ps*v_ref[h*HEAD:(h+1)*HEAD,qsl].astype(f32))*inv
            inv_ref[h,0:1,qsl]=inv
            inv_ref[h,1:2,qsl]=ps
        for hp in range(H//2): abuf[slot,hp]=obuf[slot,hp*128:(hp+1)*128,:].astype(bf).T
        ocopy(i).start(); acopy(i).start()
        return g
    g=lax.fori_loop(0,nq,block,0)
    for s in range(SLOTS):
        last=g-1-s
        @pl.when(last>=0)
        def _(): pcopy(last).wait()
    for i in range(max(nq-2,0),nq): ocopy(i).wait(); acopy(i).wait()
    for x in keep: x.wait()

def attend(base,win,qkvt,codet,meta,H):
    L=qkvt.shape[1]; W=H*HEAD; nq=L//QB; cap=nq*(L//KB+1)
    V=pl.BlockSpec(memory_space=pltpu.VMEM); A=pl.BlockSpec(memory_space=pl.ANY)
    S=jax.ShapeDtypeStruct; M=pltpu.VMEM; D=pltpu.SemaphoreType.DMA
    return pl.pallas_call(functools.partial(attend_kernel,L,H),
        out_shape=[S((cap,H,KB,QB),bf),S((H//2,L,128),bf),S((nq,W,QB),f32),S((H,8,L),f32),S((H,HEAD,L),bf),S((H,L,128),bf)],
        in_specs=[pl.BlockSpec(memory_space=pltpu.SMEM)]*2+[A,V,V],
        out_specs=[A,A,A,V,A,A],
        scratch_shapes=[M((H,L,128),bf),M((H,HEAD,L),bf),M((H,L,128),bf),M((H*128,L),bf),M((W,L),bf),M((W,L),bf),M((H,HEAD+16,L),bf),M((H,HEAD+16,QB),f32),M((SLOTS,H,KB,QB),bf),
            M((2,W,QB),f32),M((2,H//2,QB,128),bf),M((8,QB),f32),D((SLOTS,)),D((2,)),D((2,)),D((2,)),D((H+2,))],
        compiler_params=pltpu.CompilerParams(vmem_limit_bytes=VMEM))(base,win,qkvt,codet,meta)

def flags(row):
    L=row.shape[1]; nb=L//256; nq=L//QB
    seg=row//4
    pad=row//2-2*seg
    known=row-2*(row//2)
    use=(pad==0)&(known==1)
    usef=use.astype(f32)
    x=jnp.concatenate([usef[:,b*256:(b+1)*256] for b in range(nb)]+[jnp.zeros((16-nb,256),f32)],0)
    incl=dot(x.astype(bf),(iota((256,256),0)<=iota((256,256),1)).astype(f32).astype(bf),1,0)
    tot=jnp.broadcast_to(incl[:,255:256],(16,256)).astype(bf)
    base=dot((iota((16,16),0)>iota((16,16),1)).astype(f32).astype(bf),tot,1,0)
    rank=(incl+base).astype(jnp.int32)-1
    rank=jnp.concatenate([rank[b:b+1] for b in range(nb)],1)
    rank=jnp.where(use,rank,-1)
    own=((pad==0)&(known!=1)).astype(jnp.int32)
    bits=iota((CODE,L),0)
    bit=lax.shift_right_logical(jnp.broadcast_to(seg,(CODE,L)),jnp.minimum(bits,9))&1
    codet=jnp.where(bits<10,jnp.where(bit==1,16.0,-16.0),jnp.where(bits==10,1.0,0.0)).astype(bf)
    meta=jnp.concatenate([rank,own,jnp.zeros((6,L),jnp.int32)],0)
    def edge(at): return jnp.concatenate([seg[:,i*QB+at:i*QB+at+1] for i in range(nq)]+[jnp.zeros((8-nq,1),jnp.int32)],0)
    low=jnp.sum(jnp.where(seg<edge(0),usef,0.0),1,keepdims=True)
    high=jnp.sum(jnp.where(seg<=edge(QB-1),usef,0.0),1,keepdims=True)
    csum=jnp.concatenate([(incl+base)[b:b+1] for b in range(nb)],1)
    starts=jnp.sum((csum<=(256*iota((16,1),0)).astype(f32)).astype(f32),1,keepdims=True)
    win=jnp.broadcast_to(jnp.concatenate([low,high,starts],0),(32,128)).astype(jnp.int32)
    return base[:,:128].astype(jnp.int32),win,codet,meta
LN2=math.log(2.0)
SPAN=384
def back_kernel(L,H,base_ref,win_ref,datt_hbm,p_hbm,ot_hbm,inv_ref,kct_hbm,vaug_hbm,qkvt_hbm,dq_hbm,dkvw_hbm,
                vaug_ref,kct,dkv,dkvt,pbuf,qacc,qkv,datt,ot,dq,psem,lsem,qsem,osem,tsem):
    W=H*HEAD; nq=L//QB
    groups=(begin(base_ref,L//256)+127)//128
    pieces=lax.fori_loop(0,nq,lambda i,s:s+window(win_ref,i)[1]+1,0)
    def pcopy(g):
        slot=lax.rem(g,SLOTS)
        return pltpu.make_async_copy(p_hbm.at[g],pbuf.at[slot],psem.at[slot])
    def keys(t):
        rows=pl.ds(al(t*KB,KB),KB)
        return [pltpu.make_async_copy(kct_hbm.at[:,:,rows],kct.at[:,:,rows],lsem.at[0,t]),pltpu.make_async_copy(vaug_hbm.at[:,rows],vaug_ref.at[:,rows],lsem.at[1,t])]
    def queries(i):
        slot=lax.rem(i,2); qsl=pl.ds(al(i*QB,QB),QB)
        return [pltpu.make_async_copy(a,b.at[slot],qsem.at[k,slot]) for k,(a,b) in enumerate(((qkvt_hbm.at[:,qsl],qkv),(datt_hbm.at[:,qsl],datt),(ot_hbm.at[i],ot)))]
    def each_key(fn,least=0):
        def body(t,c):
            for x in keys(t): fn(x)
            return c
        lax.fori_loop(least,(groups+KB//128-1)//(KB//128),body,0)
    for x in queries(0): x.start()
    each_key(lambda x:x.start())
    for s in range(SLOTS-1):
        @pl.when(s<pieces)
        def _(): pcopy(s).start()
    def clear(j,c):
        dkv[pl.ds(al(j*128,128),128),:]=jnp.zeros((128,2*W),f32)
        return c
    lax.fori_loop(0,groups,clear,0)
    def ocopy(i):
        slot=lax.rem(i,2)
        return pltpu.make_async_copy(dq.at[slot],dq_hbm.at[:,pl.ds(al(i*QB,QB),QB)],osem.at[slot])
    def block(i,g):
        slot=lax.rem(i,2)
        qsl=pl.ds(al(i*QB,QB),QB)
        first,full,rest,_=window(win_ref,i)
        for x in queries(i): x.wait()
        @pl.when(i+1<nq)
        def _():
            for x in queries(i+1): x.start()
        dt=datt[slot].astype(f32)
        prod=dt*ot[slot]
        daug=[];dz=[];qz=[];deltas=[];d1s=[]
        zero=jnp.zeros((HEAD,QB),bf)
        row=iota((16,QB),0)
        for h in range(H):
            hsl=slice(h*HEAD,(h+1)*HEAD)
            inv=inv_ref[h,0:1,qsl]
            delta=jnp.sum(prod[hsl],0,keepdims=True)*inv
            d1=dt[hsl]*inv
            low=d1.astype(bf)
            a=delta.astype(bf).astype(f32); b=(delta-a).astype(bf).astype(f32)
            extra=jnp.where(row==0,a,jnp.where(row==1,b,jnp.where(row==2,delta-a-b,0.0))).astype(bf)
            daug.append(jnp.concatenate([low,extra,jnp.zeros((HEAD-16,QB),bf)],0))
            q=qkv[slot,hsl,:]
            dz.append(jnp.concatenate([zero,low] if h%2 else [low,zero],0))
            qz.append(jnp.concatenate([zero,q] if h%2 else [q,zero],0))
            deltas.append(delta); d1s.append(d1)
        qacc[...]=jnp.zeros_like(qacc)
        def wide(v): return jnp.concatenate(v,1)
        def piece(off,size,g):
            ps=lax.rem(g,SLOTS)
            osl=pl.ds(off,size)
            @pl.when(g+SLOTS-1<pieces)
            def _(): pcopy(g+SLOTS-1).start()
            @pl.when(i==0)
            def _():
                for x in keys(g): x.wait()
            pcopy(g).wait()
            dss=[]
            for h in range(H):
                dss.append((pbuf[ps,h,:size,:].astype(f32)*dot(vaug_ref[h,osl,:],daug[h],1,0)).astype(bf))
            for h in range(H): qacc[h*HEAD:(h+1)*HEAD,:]+=dot(kct[h,:,osl],dss[h],1,0)
            for h in range(0,H,2):
                dkv[osl,h*HEAD:(h+2)*HEAD]+=dot(wide(dss[h:h+2]),wide(qz[h:h+2]),1,1)
                dkv[osl,W+h*HEAD:W+(h+2)*HEAD]+=dot(wide([pbuf[ps,h,:size,:],pbuf[ps,h+1,:size,:]]),wide(dz[h:h+2]),1,1)
        g=by_piece(first,full,rest,g,piece)
        @pl.when(i==0)
        def _(): each_key(lambda x:x.wait(),g)
        @pl.when(i>=2)
        def _(): ocopy(i-2).wait()
        for h in range(H):
            hsl=slice(h*HEAD,(h+1)*HEAD); ksl=slice(W+h*HEAD,W+(h+1)*HEAD); vsl=slice(2*W+h*HEAD,2*W+(h+1)*HEAD)
            ps=inv_ref[h,1:2,qsl]
            ds=ps*(jnp.sum(qkv[slot,vsl,:].astype(f32)*d1s[h],0,keepdims=True)-deltas[h])
            dq[slot,hsl,:]=((qacc[hsl,:]+ds*qkv[slot,ksl,:].astype(f32))*0.125).astype(bf)
            dq[slot,ksl,:]=(ds*qkv[slot,hsl,:].astype(f32)*LN2).astype(bf)
            dq[slot,vsl,:]=(ps*d1s[h]).astype(bf)
        ocopy(i).start()
        return g
    lax.fori_loop(0,nq,block,0)
    lanes=iota((128,2*W),1)
    def tcopy(s): return pltpu.make_async_copy(dkvt.at[:,pl.ds(al(begin(base_ref,s)//128*128,128),SPAN)],dkvw_hbm.at[s],tsem.at[s])
    def turn(j,c):
        jsl=pl.ds(al(j*128,128),128)
        x=jnp.where(j<groups,dkv[jsl,:],0.0)
        dkvt[:,jsl]=jnp.where(lanes<W,x*LN2,x).astype(bf).T
        for s in range(L//256):
            @pl.when(begin(base_ref,s)//128+SPAN//128-1==j)
            def _(): tcopy(s).start()
        return c
    lax.fori_loop(0,groups+SPAN//128,turn,0)
    for i in range(max(nq-2,0),nq): ocopy(i).wait()
    for s in range(L//256): tcopy(s).wait()

def back(base,win,datt,p,ot,inv,kct,vaug,qkvt,H):
    L=qkvt.shape[1]; W=H*HEAD
    V=pl.BlockSpec(memory_space=pltpu.VMEM); A=pl.BlockSpec(memory_space=pl.ANY); N=pl.BlockSpec(memory_space=pltpu.SMEM)
    S=jax.ShapeDtypeStruct; M=pltpu.VMEM; D=pltpu.SemaphoreType.DMA
    return pl.pallas_call(functools.partial(back_kernel,L,H),
        out_shape=[S((3*W,L),bf),S((L//256,2*W,SPAN),bf)],
        in_specs=[N,N,A,A,A,V,A,A,A],
        out_specs=[A,A],
        scratch_shapes=[M((H,L,128),bf),M((H,HEAD,L),bf),M((L+384,2*W),f32),M((2*W,L+384),bf),M((SLOTS,H,KB,QB),bf),M((W,QB),f32),
            M((2,3*W,QB),bf),M((2,W,QB),bf),M((2,W,QB),f32),M((2,3*W,QB),bf),
            D((SLOTS,)),D((2,L//KB)),D((3,2)),D((2,)),D((L//256,))],
        compiler_params=pltpu.CompilerParams(vmem_limit_bytes=VMEM))(base,win,datt,p,ot,inv,kct,vaug,qkvt)

def placed(base_ref,rank_row,span,own,s):
    r0=begin(base_ref,s)//128*128
    oh=(rank_row==iota((SPAN,256),0)+r0).astype(f32).astype(bf)
    return dot(span,oh,1,0)+own.astype(f32)

def place_kernel(L,W,base_ref,meta_ref,dq_in,dkvw_ref,tok_ref,w_ref,tg_ref,grad_ref,dq_ref):
    dq_ref[...]=dq_in[...]
    def place(s,c):
        ssl=pl.ds(al(s*256,256),256)
        dq_ref[W:3*W,ssl]=placed(base_ref,meta_ref[0:1,ssl],dkvw_ref[s],dq_ref[W:3*W,ssl],s).astype(bf)
        tg_ref[ssl,:]=dot(dq_ref[:,ssl],w_ref[...],0,1).astype(bf)
        return c
    lax.fori_loop(0,L//256,place,0)
    grad_ref[...]=dot(dq_ref[...],tok_ref[...],1,0).T.astype(bf)

def place_all(base,meta,dq,dkvw,tok,w,H):
    L,E=tok.shape; W=H*HEAD
    V=pl.BlockSpec(memory_space=pltpu.VMEM); S=jax.ShapeDtypeStruct
    return pl.pallas_call(functools.partial(place_kernel,L,W),out_shape=[S((L,E),bf),S((E,3*W),bf)],
        in_specs=[pl.BlockSpec(memory_space=pltpu.SMEM)]+[V]*5,out_specs=[V,V],scratch_shapes=[pltpu.VMEM((3*W,L),bf)],
        compiler_params=pltpu.CompilerParams(vmem_limit_bytes=VMEM))(base,meta,dq,dkvw,tok,w)
EPSILON=1e-05
def gelu_parts(h):
    bell=jnp.exp(-0.5*h*h)
    t=1.0/(1.0+(0.3275911*math.sqrt(0.5))*jnp.abs(h))
    tail=0.5*1.061405429
    for c in (-1.453152027,1.421413741,-0.284496736,0.254829592): tail=tail*t+0.5*c
    tail=tail*t*bell
    cdf=jnp.where(h<0.0,tail,1.0-tail)
    return cdf,cdf+h*bell*(1.0/math.sqrt(2.0*math.pi))
def norm(x):
    center=x-jnp.mean(x,-1,keepdims=True)
    inverse=lax.rsqrt(jnp.mean(center*center,-1,keepdims=True)+EPSILON)
    return center*inverse,inverse
def norm_back(e,n,inverse):
    return inverse*(e-jnp.mean(e,-1,keepdims=True)-n*jnp.mean(e*n,-1,keepdims=True))
def middle_kernel(a0_ref,a1_ref,tok_ref,cot_ref,wo_ref,wu_ref,wd_ref,gs_ref,out_ref,r1_ref,da_ref,go_ref,gu_ref,gd_ref,gg_ref):
    @pl.when(pl.program_id(0)==0)
    def _():
        for r in (go_ref,gu_ref,gd_ref,gg_ref): r[...]=jnp.zeros_like(r)
    P2=a0_ref.shape[0]
    att=jnp.concatenate([a0_ref[p] for p in range(P2)]+[a1_ref[p] for p in range(P2)],1)
    g0,g1,b0,b1=[gs_ref[r:r+1,:] for r in range(4)]
    n1,inv1=norm(tok_ref[...].astype(f32)+dot(att,wo_ref[...],1,0))
    first=(n1*g0+b0).astype(bf)
    hidden=dot(first,wu_ref[...],1,0)
    cdf,slope=gelu_parts(hidden)
    act=(hidden*cdf).astype(bf)
    n2,inv2=norm(first.astype(f32)+dot(act,wd_ref[...],1,0))
    out_ref[...]=(n2*g1+b1).astype(bf)
    cot=cot_ref[...].astype(f32)
    r2=norm_back(cot*g1,n2,inv2)
    feed=r2.astype(bf)
    gd_ref[...]+=dot(act,feed,0,0)
    dh=(dot(feed,wd_ref[...],1,1)*slope).astype(bf)
    gu_ref[...]+=dot(first,dh,0,0)
    df=r2+dot(dh,wu_ref[...],1,1)
    r1=norm_back(df*g0,n1,inv1)
    r1_ref[...]=r1
    db=r1.astype(bf)
    go_ref[...]+=dot(att,db,0,0)
    da=dot(db,wo_ref[...],1,1).astype(bf)
    for p in range(2*P2): da_ref[p]=da[:,p*128:(p+1)*128]
    gg_ref[0:1,:]+=jnp.sum(df*n1,0,keepdims=True)
    gg_ref[1:2,:]+=jnp.sum(cot*n2,0,keepdims=True)
    gg_ref[2:3,:]+=jnp.sum(df,0,keepdims=True)
    gg_ref[3:4,:]+=jnp.sum(cot,0,keepdims=True)

def middle(a0,a1,tok,cot,wo,wu,wd,gs):
    P2,N,_=a0.shape; D=tok.shape[1]; F=wu.shape[1]
    T=max(t for t in (256,192,128,64,32,16) if N%t==0)
    tile=pl.BlockSpec((T,D),lambda i:(i,0))
    def pairs(k): return pl.BlockSpec((k,T,128),lambda i:(0,i,0))
    def whole(s): return pl.BlockSpec(s,lambda i:(0,)*len(s))
    return pl.pallas_call(middle_kernel,grid=(N//T,),
        in_specs=[pairs(P2),pairs(P2),tile,tile,whole((D,D)),whole((D,F)),whole((F,D)),whole((8,D))],
        out_specs=[tile,tile,pairs(2*P2),whole((D,D)),whole((D,F)),whole((F,D)),whole((8,D))],
        out_shape=[jax.ShapeDtypeStruct((N,D),bf),jax.ShapeDtypeStruct((N,D),f32),jax.ShapeDtypeStruct((2*P2,N,128),bf),
            jax.ShapeDtypeStruct((D,D),f32),jax.ShapeDtypeStruct((D,F),f32),jax.ShapeDtypeStruct((F,D),f32),jax.ShapeDtypeStruct((8,D),f32)],
        compiler_params=pltpu.CompilerParams(vmem_limit_bytes=60<<20))(a0,a1,tok,cot,wo,wu,wd,gs)
MESH=pl.DeviceIdType.MESH
class Net:
    def __init__(self,Z):
        dp=lax.axis_index("dp"); blk=lax.axis_index("blk")
        self.Z=Z; self.z=dp//2; self.y=dp%2; self.j=blk//2; self.c=blk%2
        self.sent=[]
    def at(self,z=None,y=None,j=None,c=None):
        z=self.z if z is None else z; y=self.y if y is None else y; j=self.j if j is None else j; c=self.c if c is None else c
        return (z*2+y,j*2+c)
    def signal(self):
        barrier=pltpu.get_barrier_semaphore()
        for d in [self.at(j=1-self.j),self.at(y=1-self.y),self.at(c=1-self.c)]+[self.at(z=lax.rem(self.z+k,self.Z)) for k in range(1,self.Z)]:
            pl.semaphore_signal(barrier,inc=1,device_id=d,device_id_type=MESH)
    def wait(self): pl.semaphore_wait(pltpu.get_barrier_semaphore(),2+self.Z)
    def greet(self):
        self.signal()
        self.wait()
    def copy(self,src,dst,ssem,rsem,device):
        return pltpu.make_async_remote_copy(src_ref=src,dst_ref=dst,send_sem=ssem,recv_sem=rsem,device_id=device,device_id_type=MESH)
    def send(self,src,dst,ssem,rsem,device,when=None):
        c=self.copy(src,dst,ssem,rsem,device)
        if when is None: c.start()
        else: pl.when(when)(c.start)
        self.sent.append((c,when))
    def drain(self):
        for c,when in self.sent:
            if when is None: c.wait_send()
            else: pl.when(when)(c.wait_send)

def gather_kernel(Z,block,E,W,rows,tok_hbm,cot_hbm,seg_ref,pad_ref,known_ref,wq_ref,wo_ref,wu_ref,wd_ref,gain_ref,shift_ref,
                  tok_out,bund_out,wmine_out,qkvt_out,base_out,win_out,code_out,meta_out,far_out,
                  tokb,farb,info_ref,infob,pack_ref,wall,bund,wt,qkvt,lsem,qsem,xs,xr,zs,zr,ys,yr,cs,cr,ts,tr,iss,isr):
    net=Net(Z); z,y,j,c=net.z,net.y,net.j,net.c
    NCH=block//rows; D=E
    sib=net.at(c=1-c); xd=net.at(j=1-j); yd=net.at(y=1-y)
    net.signal()
    mine=pltpu.make_async_copy(tok_hbm.at[j],tokb.at[j,c],lsem.at[0]); mine.start()
    far=pltpu.make_async_copy(cot_hbm.at[1-j],farb,lsem.at[3]); far.start()
    at=0
    for ref in (wq_ref,wo_ref,wu_ref,wd_ref):
        n=ref.shape[1]
        pack_ref[:,at:at+n]=ref[...]
        at+=n
    R=gain_ref.shape[1]
    place=(iota((R,128),1)==iota((R,128),0)+R*lax.rem(lax.axis_index("dp")*4+lax.axis_index("blk"),128//R)).astype(f32).astype(bf)
    pack_ref[:,at:]=jnp.concatenate([dot(gain_ref[...],place,1,0),dot(shift_ref[...],place,1,0),jnp.zeros((12,128),f32)],0).astype(bf)
    split=6*W
    wall[z,y,j,c]=pack_ref[:,:split]
    bund[y,j]=pack_ref[:,split:]
    info_ref[...]=seg_ref[...]*4+pad_ref[...]*2+known_ref[...]
    infob[j,c]=info_ref[j]
    net.wait()
    net.send(pack_ref.at[:,:split],wall.at[z,y,j,c],xs.at[0],xr.at[0],xd)
    net.send(pack_ref.at[:,split:],bund.at[y,j],xs.at[1],xr.at[1],xd)
    net.send(info_ref.at[1-j],infob.at[j,c],iss.at[0],isr.at[0],xd)
    net.send(info_ref.at[j],infob.at[j,c],iss.at[1],isr.at[1],sib)
    def chunk(k): return pl.ds(k*rows if type(k) is int else al(k*rows,rows),rows)
    for k in range(NCH):
        net.send(tok_hbm.at[1-j,chunk(k)],tokb.at[j,c,chunk(k)],ts.at[0,k],tr.at[0,k],xd)
        net.send(tok_hbm.at[j,chunk(k)],tokb.at[j,c,chunk(k)],ts.at[1,k],tr.at[1,k],sib)
    def piece(o,y_): return wall.at[o,y_,:,c]
    def landed(ref,sem): pltpu.make_async_copy(ref,ref,sem).wait()
    def pass_on(o):
        net.send(piece(o,y),piece(o,y),ys.at[o],yr.at[o],yd)
        net.send(piece(o,y),piece(o,y),cs.at[0,o],cr.at[0,o],sib)
    far.wait()
    far=pltpu.make_async_copy(farb,far_out,lsem.at[3]); far.start()
    landed(wall.at[z,y,1-j,c],xr.at[0])
    for k in range(1,Z):
        net.send(piece(z,y),piece(z,y),zs.at[k],zr.at[k],net.at(z=lax.rem(z+k,Z)))
    pass_on(z)
    landed(bund.at[y,1-j],xr.at[1])
    net.send(bund.at[y],bund.at[y],ys.at[Z],yr.at[Z],yd)
    for k in range(1,Z):
        o=lax.rem(z+Z-k,Z)
        landed(piece(o,y),zr.at[k])
        pass_on(o)
    for k in range(Z):
        o=lax.rem(z+Z-k,Z)
        landed(piece(o,1-y),yr.at[o])
        net.send(piece(o,1-y),piece(o,1-y),cs.at[1,o],cr.at[1,o],sib)
    for o in range(Z):
        for q in range(2): landed(wall.at[o,y if q==0 else 1-y,:,1-c],cr.at[q,o])
    landed(bund.at[1-y],yr.at[Z])
    outb=pltpu.make_async_copy(bund,bund_out,lsem.at[1]); outb.start()
    def qcopy(g):
        col=pl.ds(al(g*rows,rows),rows)
        return pltpu.make_async_copy(qkvt.at[:,col],qkvt_out.at[:,col],qsem.at[g])
    def project(jj,cc,come=None,onward=False):
        def body(k,carry):
            ref=tokb.at[jj,cc,chunk(k)]
            if come is not None: landed(ref,tr.at[come,k])
            if onward: net.copy(ref,ref,ts.at[2,k],tr.at[2,k],sib).start()
            g=(jj*2+cc)*NCH+k
            r=dot(wt[...],ref[...],1,1)
            qkvt[:,pl.ds(al(g*rows,rows),rows)]=jnp.concatenate([r[:W]*(math.log2(math.e)/8),r[W:]],0).astype(bf)
            qcopy(g).start()
            return carry
        lax.fori_loop(0,NCH,body,0)
    parts=[]
    for t in range(3):
        cols=pl.ds(al(t*2*W+c*W,W),W)
        part=wall[:,:,:,:,:,cols].reshape(D,W)
        wt[t*W:(t+1)*W,:]=part.T
        parts.append(part)
    wmine_out[...]=jnp.concatenate(parts,1)
    mine.wait()
    project(j,c)
    project(j,1-c,1)
    landed(infob.at[1-j,c],isr.at[0])
    net.send(infob.at[1-j,c],infob.at[1-j,c],iss.at[2],isr.at[2],sib)
    project(1-j,c,0,True)
    landed(infob.at[j,1-c],isr.at[1])
    landed(infob.at[1-j,1-c],isr.at[2])
    base_out[...],win_out[...],code_out[...],meta_out[...]=flags(jnp.concatenate([infob[0,0],infob[0,1],infob[1,0],infob[1,1]],1))
    project(1-j,1-c,2)
    outt=pltpu.make_async_copy(tokb,tok_out,lsem.at[2]); outt.start()
    net.drain()
    for k in range(NCH):
        ref=tokb.at[1-j,c,chunk(k)]
        net.copy(ref,ref,ts.at[2,k],tr.at[2,k],sib).wait_send()
    lax.fori_loop(0,4*NCH,lambda g,c:(qcopy(g).wait(),c)[1],0)
    outb.wait(); outt.wait(); far.wait()

def gather(tok,cot,seg,pad,known,wq,wo,wu,wd,gain,shift,Z,W):
    _,block,E=tok.shape; R=wq.shape[0]; C=6*W+wo.shape[1]+wu.shape[1]+wd.shape[1]+128
    rows=256; NCH=block//rows; L=4*block
    V=pl.BlockSpec(memory_space=pltpu.VMEM); A=pl.BlockSpec(memory_space=pl.ANY)
    S=jax.ShapeDtypeStruct; M=pltpu.VMEM; D=pltpu.SemaphoreType.DMA; I=jnp.int32
    return pl.pallas_call(functools.partial(gather_kernel,Z,block,E,W,rows),
        out_shape=[S((2,2,block,E),bf),S((2,2,R,C-6*W),bf),S((E,3*W),bf),S((3*W,L),bf),S((16,128),I),S((32,128),I),S((CODE,L),bf),S((8,L),I),S((block,E),bf)],
        in_specs=[A,A]+[V]*9,out_specs=[A,A,V,A,V,V,V,V,A],
        scratch_shapes=[M((2,2,block,E),bf),M((block,E),bf),M((2,1,block),I),M((2,2,1,block),I),M((R,C),bf),M((Z,2,2,2,R,6*W),bf),M((2,2,R,C-6*W),bf),M((3*W,E),bf),M((3*W,L),bf),
            D((4,)),D((4*NCH,)),D((2,)),D((2,)),D((Z,)),D((Z,)),D((Z+1,)),D((Z+1,)),D((2,Z)),D((2,Z)),D((3,NCH)),D((3,NCH)),D((3,)),D((3,))],
        compiler_params=pltpu.CompilerParams(collective_id=0,has_side_effects=True,vmem_limit_bytes=VMEM))(tok,cot,seg,pad,known,wq,wo,wu,wd,gain,shift)
def middle_net_kernel(Z,block,E,F,W,T,att_hbm,tok_hbm,cot_hbm,cotx_hbm,*rest):
    bunds=rest[:Z]; near_out,far_out,r1_out,datt_out=rest[Z:Z+4]; parts=rest[Z+4]
    (go_ref,gu_ref,gd_ref,gg_ref,gt_ref,aown,aget,tok,cot,wall,lay,r1,da,lsem,wsem,osem,asend,aget_sem,dsend,dget,bsend,bget)=rest[Z+5:]
    net=Net(Z); z,y,j,c=net.z,net.y,net.j,net.c
    NCH=block//T; n=2*NCH; P2=att_hbm.shape[0]; G=2
    sib=net.at(c=1-c)
    def place(t):
        jj=jnp.where(t<NCH,1-j,j)
        return jj,pl.ds(al(lax.rem(t,NCH)*T,T),T)
    def where(t): return pl.ds(al((jnp.where(t<NCH,1-j,j)*2+c)*block+lax.rem(t,NCH)*T,T),T)
    def load(t):
        jj,rows=place(t)
        return [pltpu.make_async_copy(att_hbm.at[:,jj,c,rows],aown.at[t],lsem.at[0,t]),pltpu.make_async_copy(tok_hbm.at[jj,c,rows],tok.at[t],lsem.at[1,t])]
    def load_cot(t,near):
        rows=place(t)[1]
        return pltpu.make_async_copy((cot_hbm.at[j,rows] if near else cotx_hbm.at[rows]),cot.at[t],lsem.at[2,t])
    cols=[(0,E),(E,F),(E+F,E),(2*E+F,128)]
    loadw=[pltpu.make_async_copy(bunds[k],wall.at[lax.rem(z+Z-k,Z),:,:,c],wsem.at[k]) for k in range(Z)]
    for x in loadw: x.start()
    def start(t,near):
        for x in load(t): x.start()
        load_cot(t,near).start()
    for t in range(n): start(t,t>=NCH)
    barrier=pltpu.get_barrier_semaphore()
    pl.semaphore_signal(barrier,inc=1,device_id=sib,device_id_type=MESH)
    pl.semaphore_wait(barrier,1)
    def ship(t):
        jj,rows=place(t)
        return net.copy(att_hbm.at[:,jj,1-c,rows],aget.at[t],asend.at[t],aget_sem.at[t],sib)
    ship(0).start()
    weights=[net.copy(bunds[k],wall.at[lax.rem(z+Z-k,Z),:,:,c],bsend.at[k],bget.at[k],sib) for k in range(Z)]
    for x in weights: x.start()
    for t in range(1,n): ship(t).start()
    for x in loadw: x.wait()
    for k in range(Z):
        ref=wall.at[lax.rem(z+Z-k,Z),:,:,1-c]
        pltpu.make_async_copy(ref,ref,bget.at[k]).wait()
    def whole(a,b): return wall[:,:,:,:,:,a:a+b].reshape(E,b)
    gs=wall[:,:,:,:,:,cols[3][0]:].reshape(E//16,16,128).astype(f32)
    gsr=jnp.concatenate([jnp.sum(gs[q*8:(q+1)*8],0) for q in range(E//128)],1)
    g0,g1,b0,b1=[gsr[r:r+1,:] for r in range(4)]
    for r in (go_ref,gu_ref,gd_ref,gg_ref): r[...]=jnp.zeros_like(r)
    def out_near(t): return pltpu.make_async_copy(lay.at[t],near_out.at[place(t)[1]],osem.at[0,t])
    def out_far(t): return pltpu.make_async_copy(lay.at[t],far_out.at[place(t)[1]],osem.at[0,t])
    def out_r1(t):
        jj,rows=place(t)
        return pltpu.make_async_copy(r1.at[t],r1_out.at[jj,rows],osem.at[1,t])
    def out_da(t):
        return pltpu.make_async_copy(da.at[0,t],datt_out.at[:,where(t)],osem.at[2,t])
    def ship_da(t):
        return net.copy(da.at[1,t],datt_out.at[:,where(t)],dsend.at[t],dget.at[t],sib)
    def tiles(u,carry):
        ts=[G*u+g for g in range(G)]
        def each(f,*lists): return [f(*v) for v in zip(*lists)]
        for t in ts:
            for x in load(t): x.wait()
            pltpu.make_async_copy(cotx_hbm.at[place(t)[1]],cot.at[t],lsem.at[2,t]).wait()
            ship(t).wait_recv()
        def whole_att(t):
            mine=[aown[t,p] for p in range(P2)]; his=[aget[t,p] for p in range(P2)]
            return jnp.where(c==0,jnp.concatenate(mine+his,1),jnp.concatenate(his+mine,1))
        wo=whole(*cols[0]); wu=whole(*cols[1]); wd=whole(*cols[2])
        att=each(whole_att,ts)
        branch=each(lambda a:dot(a,wo,1,0),att)
        n1,inv1=zip(*each(lambda t,b:norm(tok[t].astype(f32)+b),ts,branch))
        first=each(lambda n:(n*g0+b0).astype(bf),n1)
        hidden=each(lambda a:dot(a,wu,1,0),first)
        cdf,slope=zip(*each(gelu_parts,hidden))
        act=each(lambda h,p:(h*p).astype(bf),hidden,cdf)
        fed=each(lambda a:dot(a,wd,1,0),act)
        n2,inv2=zip(*each(lambda a,b:norm(a.astype(f32)+b),first,fed))
        ct=each(lambda t:cot[t].astype(f32),ts)
        r2=each(lambda x,n,i:norm_back(x*g1,n,i),ct,n2,inv2)
        feed=each(lambda x:x.astype(bf),r2)
        dact=each(lambda x:dot(x,wd,1,1),feed)
        for t,n in zip(ts,n2): lay[t]=(n*g1+b1).astype(bf)
        both=lambda v:jnp.concatenate(v,0)
        gd_ref[...]+=dot(both(act),both(feed),0,0)
        dh=each(lambda x,s:(x*s).astype(bf),dact,slope)
        df=each(lambda x,h:x+dot(h,wu,1,1),r2,dh)
        gu_ref[...]+=dot(both(first),both(dh),0,0)
        dr=each(lambda x,n,i:norm_back(x*g0,n,i),df,n1,inv1)
        db=each(lambda x:x.astype(bf),dr)
        d=each(lambda x:dot(wo,x,1,1).astype(bf),db)
        go_ref[...]+=dot(both(att),both(db),0,0)
        for t,x,e in zip(ts,dr,d):
            r1[t]=x.astype(r1.dtype)
            da[0,t]=jnp.where(c==0,e[:W],e[W:])
            da[1,t]=jnp.where(c==0,e[W:],e[:W])
        down=lambda v:sum(jnp.sum(x,0,keepdims=True) for x in v)
        gg_ref[0:1,:]+=down(each(lambda x,n:x*n,df,n1))
        gg_ref[1:2,:]+=down(each(lambda x,n:x*n,ct,n2))
        gg_ref[2:3,:]+=down(df)
        gg_ref[3:4,:]+=down(ct)
        for t in ts:
            @pl.when(t<NCH)
            def _(): out_far(t).start()
            @pl.when(t>=NCH)
            def _(): out_near(t).start()
            out_r1(t).start(); out_da(t).start(); ship_da(t).start()
        return carry
    lax.fori_loop(0,n//G,tiles,0)
    ggt=jnp.concatenate([gg_ref[...],jnp.zeros((120,E),f32)],0).T
    gt_ref[...]=ggt
    R=E//(2*Z)
    at=0
    for ref in (go_ref,gu_ref,gd_ref,gt_ref):
        parts[:,:,at:at+ref.shape[1]]=ref[...].astype(bf).reshape(2*Z,R,ref.shape[1])
        at+=ref.shape[1]
    for x in weights: x.wait_send()
    for t in range(n):
        ship(t).wait_send(); out_r1(t).wait(); out_da(t).wait(); ship_da(t).wait()
        (out_far if t<NCH else out_near)(t).wait()

def middle_net(att,tok,cot,cotx,bunds,Z,W,F):
    P2,_,_,block,_=att.shape; E=tok.shape[-1]; C=bunds[0].shape[-1]
    T=256; NCH=block//T; n=2*NCH
    V=pl.BlockSpec(memory_space=pltpu.VMEM); A=pl.BlockSpec(memory_space=pl.ANY)
    S=jax.ShapeDtypeStruct; M=pltpu.VMEM; D=pltpu.SemaphoreType.DMA
    return pl.pallas_call(functools.partial(middle_net_kernel,Z,block,E,F,W,T),
        out_shape=[S((block,E),bf),S((block,E),bf),S((2,block,E),bf),S((W,4*block),bf)]+[S((2*Z,E//(2*Z),C),bf)],
        in_specs=[A]*(4+Z),out_specs=[A,A,A,A,V],
        scratch_shapes=[M((E,E),f32),M((E,F),f32),M((F,E),f32),M((8,E),f32),M((E,128),f32),
            M((n,P2,T,128),bf),M((n,P2,T,128),bf),M((n,T,E),bf),M((n,T,E),bf),M((Z,2,2,2,16,C),bf),M((n,T,E),bf),M((n,T,E),bf),M((2,n,W,T),bf),
            D((3,n)),D((Z,)),D((3,n)),D((n,)),D((n,)),D((n,)),D((n,)),D((Z,)),D((Z,))],
        compiler_params=pltpu.CompilerParams(collective_id=2,has_side_effects=True,vmem_limit_bytes=VMEM))(att,tok,cot,cotx,*bunds)
def reduce_kernel(Z,block,E,W,C1,rows,base_ref,meta_ref,dq_hbm,dkvw_hbm,tok_hbm,w_hbm,r1_hbm,parts_hbm,tok_out,grad_out,
     dq,dkvw,tok,w,r1,parts,own,tgf,tgr,tgs,ob,s0,r0,g0,s1,r1b,su,ru,fin,sx,rx,se,re,sxe,rxe,
     lsem,nsem,osem,ts,tr,xs,xr,cs,cr,ys,yr,us,ur,fs,fr):
    net=Net(Z); z,y,j,c=net.z,net.y,net.j,net.c
    NCH=block//rows; half=2*block
    sib=net.at(c=1-c); xd=net.at(j=1-j); yd=net.at(y=1-y)
    def side(jj): return pl.ds(al(jj*half,128),half)
    def spans(jj): return pl.ds(jj*2*NCH,2*NCH)
    def need(cc,k):
        at=((1-j)*2+cc)*NCH+k; cols=pl.ds(al(at*rows,rows),rows)
        return [pltpu.make_async_copy(dkvw_hbm.at[at],dkvw.at[at],nsem.at[0,cc,k]),pltpu.make_async_copy(dq_hbm.at[:,cols],dq.at[:,cols],nsem.at[1,cc,k])]
    loads=[pltpu.make_async_copy(a,b,lsem.at[k]) for k,(a,b) in enumerate(((w_hbm,w),(r1_hbm,r1),(parts_hbm,parts),
        (dq_hbm.at[:,side(j)],dq.at[:,side(j)]),(tok_hbm,tok),(dkvw_hbm.at[spans(j)],dkvw.at[spans(j)])))]
    net.signal()
    for x in need(1-c,0)+loads[:1]+need(c,0): x.start()
    for k in range(1,NCH):
        for x in need(1-c,k)+need(c,k): x.start()
    for x in loads[1:]: x.start()
    def chunk(k): return pl.ds(k*rows,rows)
    def landed(ref,sem): pltpu.make_async_copy(ref,ref,sem).wait()
    def position(jj,cc,k): return pl.ds(al(((jj*2+cc)*NCH+k)*rows,rows),rows)
    def place(jj,cc,k):
        ssl=position(jj,cc,k)
        dq[W:3*W,ssl]=placed(base_ref,meta_ref[0:1,ssl],dkvw[(jj*2+cc)*NCH+k],dq[W:3*W,ssl],(jj*2+cc)*NCH+k).astype(bf)
    def to_tokens(jj,cc,k): return dot(dq[:,position(jj,cc,k)],w[...],0,1)
    def for_sibling(t,k):
        jj=1-j if t==0 else j
        tgf[jj,chunk(k),:]=to_tokens(jj,1-c,k).astype(bf)
        net.send(tgf.at[jj,chunk(k)],tgr.at[jj,chunk(k)],ts.at[t,k],tr.at[t,k],sib)
    def split(x,n): return x.reshape(Z,2,2,2,16,n)
    def core_sum(v,lo,n):
        x=dot(dq[lo:lo+n,:],tok[...],1,0).T.astype(bf)
        x=split(x,n)
        s0[:,:,:,:,lo:lo+n]=jnp.where(c==0,x[:,:,:,1],x[:,:,:,0])
        net.send(s0.at[:,:,:,:,lo:lo+n],r0.at[:,:,:,:,lo:lo+n],cs.at[v],cr.at[v],sib)
        mine=jnp.where(c==0,x[:,:,:,0],x[:,:,:,1])
        for t in range(lo//W,(lo+n)//W):
            part=mine[:,:,:,:,t*W-lo:(t+1)*W-lo]
            @pl.when(c==0)
            def _(): g0[:,:,:,:,2*t*W:(2*t+1)*W]=part
            @pl.when(c==1)
            def _(): g0[:,:,:,:,(2*t+1)*W:(2*t+2)*W]=part
    def core_get(v,lo,n):
        landed(r0.at[:,:,:,:,lo:lo+n],cr.at[v])
        for t in range(lo//W,(lo+n)//W):
            part=r0[:,:,:,:,t*W:(t+1)*W]
            @pl.when(c==0)
            def _(): g0[:,:,:,:,(2*t+1)*W:(2*t+2)*W]=part
            @pl.when(c==1)
            def _(): g0[:,:,:,:,2*t*W:(2*t+1)*W]=part
    cut=[pl.ds(2*t*W,2*W) for t in range(3)]
    def to_y(v):
        s1[:,:,:,cut[v]]=jnp.where(y==0,g0[:,1,:,:,cut[v]],g0[:,0,:,:,cut[v]])
        net.send(s1.at[:,:,:,cut[v]],r1b.at[:,:,:,cut[v]],ys.at[v],yr.at[v],yd)
    def to_z(v):
        landed(r1b.at[:,:,:,cut[v]],yr.at[v])
        for k in range(1,Z):
            o=lax.rem(z+k,Z)
            su[k,:,:,cut[v]]=(g0[o,y,:,:,cut[v]].astype(f32)+r1b[o,:,:,cut[v]].astype(f32)).astype(bf)
            net.send(su.at[k,:,:,cut[v]],ru.at[k,:,:,cut[v]],us.at[v,k],ur.at[v,k],net.at(z=o))
    def to_x(v):
        sum_=g0[z,y,:,:,cut[v]].astype(f32)+r1b[z,:,:,cut[v]].astype(f32)
        for k in range(1,Z):
            landed(ru.at[k,:,:,cut[v]],ur.at[v,k])
            sum_=sum_+ru[k,:,:,cut[v]].astype(f32)
        fin[:,:,cut[v]]=sum_
        sx[:,cut[v]]=jnp.where(j==0,sum_[1],sum_[0]).astype(bf)
        net.send(sx.at[:,cut[v]],rx.at[:,cut[v]],fs.at[v],fr.at[v],xd)
    def total(jj,k): return (own[jj,chunk(k),:]+tgr[jj,chunk(k),:].astype(f32)+r1[jj,chunk(k),:].astype(f32)).astype(bf)
    def far(k):
        landed(tgr.at[1-j,chunk(k)],tr.at[0,k])
        tgs[chunk(k),:]=total(1-j,k)
        net.send(tgs.at[chunk(k)],ob.at[j,chunk(k)],xs.at[k],xr.at[k],xd)
    for k in range(NCH):
        for x in need(1-c,k): x.wait()
        place(1-j,1-c,k)
        if k==0:
            loads[0].wait()
            net.wait()
        for_sibling(0,k)
        for x in need(c,k): x.wait()
        place(1-j,c,k)
        own[1-j,chunk(k),:]=to_tokens(1-j,c,k)
        if k==0: loads[1].wait()
        else: far(k-1)
    for x in loads[2:]: x.wait()
    core_sum(0,0,W)
    far(NCH-1)
    for cc in (1-c,c):
        for k in range(NCH): place(j,cc,k)
    core_get(0,0,W)
    to_y(0)
    core_sum(1,W,W)
    core_sum(2,2*W,W)
    core_get(1,W,W)
    to_y(1)
    early=parts[0].astype(f32)
    for k in range(1,2*Z): early=early+parts[k].astype(f32)
    early=early.reshape(2,2,16,C1)
    early0=jnp.where(c==0,early[:,0],early[:,1])
    se[...]=jnp.where(c==0,early[:,1],early[:,0]).astype(bf)
    net.send(se,re,cs.at[3],cr.at[3],sib)
    core_get(2,2*W,W)
    to_y(2)
    to_z(0)
    for k in range(NCH): for_sibling(1,k)
    to_z(1)
    landed(re,cr.at[3])
    early0=early0+re[...].astype(f32)
    early1=jnp.where(j==0,early0[0],early0[1])
    sxe[...]=jnp.where(j==0,early0[1],early0[0]).astype(bf)
    net.send(sxe,rxe,fs.at[3],fr.at[3],xd)
    to_x(0)
    for k in range(NCH): own[j,chunk(k),:]=to_tokens(j,c,k)
    to_z(2)
    to_x(1)
    for k in range(NCH):
        landed(tgr.at[j,chunk(k)],tr.at[1,k])
        ob[j,chunk(k),:]=total(j,k)
    near=pltpu.make_async_copy(ob.at[j],tok_out.at[j],osem.at[0]); near.start()
    to_x(2)
    landed(rxe,fr.at[3])
    grad_out[:,6*W:]=early1+rxe[...].astype(f32)
    for v in range(3):
        landed(rx.at[:,cut[v]],fr.at[v])
        grad_out[:,cut[v]]=jnp.where(j==0,fin[0,:,cut[v]],fin[1,:,cut[v]])+rx[:,cut[v]].astype(f32)
    last=[pltpu.make_async_copy(ob.at[1-j,chunk(k)],tok_out.at[1-j,chunk(k)],osem.at[1+k]) for k in range(NCH)]
    for k in range(NCH):
        landed(ob.at[1-j,chunk(k)],xr.at[k])
        last[k].start()
    net.drain()
    near.wait()
    for x in last: x.wait()

def reduce(base,meta,dq,dkvw,tok,w,r1,parts,Z,W):
    _,block,E=r1.shape; L=4*block; C1=parts.shape[2]; C=6*W
    rows=256; NCH=block//rows
    V=pl.BlockSpec(memory_space=pltpu.VMEM); A=pl.BlockSpec(memory_space=pl.ANY)
    S=jax.ShapeDtypeStruct; M=pltpu.VMEM; D=pltpu.SemaphoreType.DMA
    return pl.pallas_call(functools.partial(reduce_kernel,Z,block,E,W,C1,rows),
        out_shape=[S((2,block,E),bf),S((16,C+C1),f32)],
        in_specs=[pl.BlockSpec(memory_space=pltpu.SMEM),V,A,A,A,A,A,A],out_specs=[A,V],
        scratch_shapes=[M(dq.shape,bf),M(dkvw.shape,bf),M(tok.shape,bf),M(w.shape,bf),M(r1.shape,bf),M(parts.shape,bf),M((2,block,E),f32),M((2,block,E),bf),M((2,block,E),bf),M((block,E),bf),M((2,block,E),bf),
            M((Z,2,2,16,3*W),bf),M((Z,2,2,16,3*W),bf),M((Z,2,2,16,C),bf),M((Z,2,16,C),bf),M((Z,2,16,C),bf),
            M((Z,2,16,C),bf),M((Z,2,16,C),bf),M((2,16,C),f32),M((16,C),bf),M((16,C),bf),M((2,16,C1),bf),M((2,16,C1),bf),M((16,C1),bf),M((16,C1),bf),
            D((6,)),D((2,2,NCH)),D((1+NCH,)),D((2,NCH)),D((2,NCH)),D((NCH,)),D((NCH,)),D((4,)),D((4,)),D((3,)),D((3,)),D((3,Z)),D((3,Z)),D((4,)),D((4,))],
        compiler_params=pltpu.CompilerParams(collective_id=1,has_side_effects=True,vmem_limit_bytes=VMEM))(base,meta,dq,dkvw,tok,w,r1,parts)

def finish_kernel(W,E,F,near,far,tg_hbm,grads_hbm,lay_out,tg_out,gq,go,gu,gd,gg,gs,lay,tg,grads,small,isem,osem):
    j=lax.axis_index("blk")//2; block=near.shape[0]; n=4; rows=block//n
    gcopy=pltpu.make_async_copy(grads_hbm,grads,isem.at[4*n]); gcopy.start()
    come=[];leave=[]
    for k in range(n):
        r=pl.ds(k*rows,rows)
        for a,b,o in ((near.at[r],lay.at[j,r],lay_out.at[j,r]),(far.at[r],lay.at[1-j,r],lay_out.at[1-j,r]),(tg_hbm.at[0,r],tg.at[0,r],tg_out.at[0,r]),(tg_hbm.at[1,r],tg.at[1,r],tg_out.at[1,r])):
            at=len(come)
            come.append(pltpu.make_async_copy(a,b,isem.at[at])); leave.append(pltpu.make_async_copy(b,o,osem.at[at]))
    for x in come: x.start()
    gcopy.wait()
    at=0
    for k,ref in enumerate((gq,go,gu,gd)):
        width=ref.shape[1]
        leave.append(pltpu.make_async_copy(grads.at[:,at:at+width],ref,osem.at[4*n+k]))
        at+=width
        leave[-1].start()
    t=grads[:,at:].T
    small[0]=t[0:2,:]; small[1]=t[2:4,:]
    for k,ref in enumerate((gg,gs)):
        leave.append(pltpu.make_async_copy(small.at[k],ref,osem.at[4*n+4+k]))
        leave[-1].start()
    for x,o in zip(come,leave):
        x.wait(); o.start()
    for o in leave: o.wait()

def finish(near,far,tg,grads,W,F):
    _,block,E=tg.shape
    A=pl.BlockSpec(memory_space=pl.ANY); S=jax.ShapeDtypeStruct; M=pltpu.VMEM; D=pltpu.SemaphoreType.DMA
    return pl.pallas_call(functools.partial(finish_kernel,W,E,F),
        out_shape=[S(tg.shape,bf),S(tg.shape,bf),S((16,6*W),f32),S((16,E),f32),S((16,F),f32),S((16,E),f32),S((2,16),f32),S((2,16),f32)],
        in_specs=[A]*4,out_specs=[A]*8,scratch_shapes=[M(tg.shape,bf),M(tg.shape,bf),M(grads.shape,f32),M((2,2,16),f32),D((17,)),D((22,))],
        compiler_params=pltpu.CompilerParams(vmem_limit_bytes=VMEM))(near,far,tg,grads)
def shards(tokens,cotangent,segments,padding,known,w_qkv,w_out,w_up,w_down,norm_gains,norm_shifts):
    micro,rows,block,D=tokens.shape
    J=lax.axis_size("blk")//2; dps=lax.axis_size("dp")
    units=micro*rows
    assert units==J
    H=HEADS//2; W=H*HEAD; L=2*J*block; F=w_up.shape[1]
    quick=J==2 and dps%2==0 and w_qkv.shape[0]==16 and block%256==0
    me=lax.axis_index("blk"); chip=me//2; core=me%2
    flat=lambda x:x.reshape((units,)+x.shape[2:])
    if quick:
        Z=dps//2
        cot=flat(cotangent)
        tok,bund,w_mine,qkvt,base,win,codet,meta,far=gather(flat(tokens),cot,*[flat(x)[:,None,:] for x in (segments,padding,known)],w_qkv,w_out,w_up,w_down,norm_gains,norm_shifts,Z,W)
        bunds=[bund]+[lax.ppermute(bund,"dp",[(d,(d//2+k)%Z*2+d%2) for d in range(dps)]) for k in range(1,Z)]
        across=[(b,b^2) for b in range(4)]
        cotx=lax.ppermute(far,"blk",across)
        p,att,ot,inv,kct,vaug=attend(base,win,qkvt,codet,meta,H)
        near,far,r1,datt,parts=middle_net(att.reshape(H//2,2,2,block,128),tok,cot,cotx,bunds,Z,W,F)
        parts=lax.all_to_all(parts,"dp",0,0,tiled=True)
        layx=lax.ppermute(far,"blk",across)
        dq,dkvw=back(base,win,datt,p,ot,inv,kct,vaug,qkvt,H)
        tg,grads=reduce(base,meta,dq,dkvw,tok.reshape(L,D),w_mine,r1,parts,Z,W)
        out=finish(near,layx,tg,grads,W,F)
        return (out[0].reshape(tokens.shape),out[1].reshape(tokens.shape))+tuple(out[2:])
    def to_chip(s): return [(2*a+c,2*((a+s)%J)+c) for a in range(J) for c in range(2)]
    swap=[(b,b^1) for b in range(2*J)]
    def other(x): return lax.ppermute(x,"blk",swap)
    def scatter_units(x):
        got=[]
        for s in range(J):
            mine=lax.dynamic_index_in_dim(x,(chip+s)%J,0,keepdims=False)
            got.append(mine if s==0 else lax.ppermute(mine,"blk",to_chip(s)))
        return jnp.stack([lax.dynamic_index_in_dim(jnp.stack(got),(chip-j)%J,0,keepdims=False) for j in range(J)])
    def both(mine,his):
        return jnp.stack([jnp.where(core==0,mine,his),jnp.where(core==0,his,mine)],1)
    def part(x,axis,index): return lax.dynamic_index_in_dim(x,index,axis,keepdims=False)
    own_info=scatter_units(flat(segments*4+padding*2+known)); info=both(own_info,other(own_info)).reshape(1,L)
    own_tok=scatter_units(flat(tokens)); all_tok=both(own_tok,other(own_tok)).reshape(L,D)
    own_cot=scatter_units(flat(cotangent)).reshape(L//2,D)
    full_qkv,full_out,full_up,full_down=[lax.all_gather(w,("dp","blk"),axis=0,tiled=True) for w in (w_qkv,w_out,w_up,w_down)]
    gs=lax.all_gather(jnp.concatenate([norm_gains,norm_shifts],0),("dp","blk"),axis=1,tiled=True).astype(f32)
    gs=jnp.concatenate([gs,jnp.zeros_like(gs)],0)
    w_mine=part(full_qkv.reshape(D,3,2,W),2,core).reshape(D,3*W)
    scale=jnp.where(jnp.arange(3*W)<W,math.log2(math.e)/8,1.0).astype(f32)
    qkvt=(jnp.einsum("ld,de->el",all_tok,w_mine,preferred_element_type=f32)*scale[:,None]).astype(bf)
    base,win,codet,meta=flags(info)
    p,att,ot,inv,kct,vaug=attend(base,win,qkvt,codet,meta,H)
    att=att.reshape(H//2,J,2,block,128)
    mine=part(att,2,core).reshape(H//2,J*block,128); his=other(part(att,2,1-core)).reshape(H//2,J*block,128)
    a0=jnp.where(core==0,mine,his); a1=jnp.where(core==0,his,mine)
    out,r1,da,go,gu,gd,gg=middle(a0,a1,own_tok.reshape(L//2,D),own_cot,full_out,full_up,full_down,gs)
    da=da.reshape(2,H//2,J,block,128)
    dmine=part(da,0,core); dhis=other(part(da,0,1-core))
    datt=jnp.stack([jnp.where(core==0,dmine,dhis),jnp.where(core==0,dhis,dmine)],2).reshape(H//2,L,128).transpose(0,2,1).reshape(W,L)
    dq,dkvw=back(base,win,datt,p,ot,inv,kct,vaug,qkvt,H)
    tg,gq=place_all(base,meta,dq,dkvw,all_tok,w_mine,H)
    tg=tg.reshape(J,2,block,D)
    layer_out=scatter_units(out.reshape(J,block,D)).reshape(tokens.shape)
    own_tg=(part(tg,1,core).astype(f32)+other(part(tg,1,1-core)).astype(f32)+r1.reshape(J,block,D)).astype(bf)
    token_grad=scatter_units(own_tg).reshape(tokens.shape)
    gq=gq.astype(f32).reshape(D,3,1,W)
    gq=jnp.where(core==0,jnp.concatenate([gq,jnp.zeros_like(gq)],2),jnp.concatenate([jnp.zeros_like(gq),gq],2)).reshape(D,6*W)
    grads=lax.psum_scatter(jnp.concatenate([gq,go,gu,gd],1),("dp","blk"),scatter_dimension=0,tiled=True)
    gg=lax.psum_scatter(gg[:4],("dp","blk"),scatter_dimension=1,tiled=True)
    a,b,e=6*W,6*W+D,6*W+D+F
    return (layer_out,token_grad,grads[:,:a],grads[:,a:b],grads[:,b:e],grads[:,e:],gg[:2],gg[2:])

def solution(mesh):
    in_specs = (
        P(None, "dp", "blk", None),
        P(None, "dp", "blk", None),
        P(None, "dp", "blk"),
        P(None, "dp", "blk"),
        P(None, "dp", "blk"),
        P(("dp", "blk"), None),
        P(("dp", "blk"), None),
        P(("dp", "blk"), None),
        P(("dp", "blk"), None),
        P(None, ("dp", "blk")),
        P(None, ("dp", "blk")),
    )
    out_specs = (
        P(None, "dp", "blk", None),
        P(None, "dp", "blk", None),
        P(("dp", "blk"), None),
        P(("dp", "blk"), None),
        P(("dp", "blk"), None),
        P(("dp", "blk"), None),
        P(None, ("dp", "blk")),
        P(None, ("dp", "blk")),
    )
    return jax.shard_map(shards, mesh=mesh, in_specs=in_specs, out_specs=out_specs, check_vma=False)
```

```python
import functools, math
import jax, jax.numpy as jnp
from jax import lax
from jax.experimental import pallas as pl
from jax.experimental.pallas import tpu as pltpu
from jax.sharding import PartitionSpec as P

HEADS = 8
bf=jnp.bfloat16; f32=jnp.float32
HEAD=64
QB=512
KB=512
SRC=1024
SAFE=60.0
CODE=16
VMEM=(64<<20)-(128<<10)
SLOTS=3
def dot(a,b,ca,cb): return lax.dot_general(a,b,(((ca,),(cb,)),((),())),preferred_element_type=f32)
def al(x,n): return pl.multiple_of(x,n)
def iota(shape,axis): return lax.broadcasted_iota(jnp.int32,shape,axis)

def begin(base_ref,b):
    return base_ref[b,0]

def window(win_ref,i):
    start=win_ref[i,0]//128*128
    groups=(win_ref[8+i,0]-start+127)//128
    full=(groups-1)//(KB//128)
    return start,full,groups-full*(KB//128),groups

def by_piece(first,full,rest,g,fn):
    def body(j,g):
        fn(al(first+j*KB,128),KB,g)
        return g+1
    g=lax.fori_loop(0,full,body,g)
    for r in range(1,KB//128+1):
        @pl.when(rest==r)
        def _(): fn(al(first+full*KB,128),r*128,g)
    return g+1

def attend_kernel(L,H,base_ref,win_ref,qkvt_hbm,codet_ref,meta_ref,p_hbm,att_hbm,ot_hbm,inv_ref,kct_hbm,vct_hbm,
                  kaug_ref,kct_ref,kvt,q_ref,v_ref,vct,acc,pbuf,obuf,abuf,top_ref,psem,osem,asem,ksem,lsem):
    W=H*HEAD; nq=L//QB
    total=begin(base_ref,L//256)
    come=[pltpu.make_async_copy(qkvt_hbm.at[W+h*HEAD:W+(h+1)*HEAD],kvt.at[h*128:h*128+HEAD],lsem.at[h]) for h in range(H)]
    come+=[pltpu.make_async_copy(qkvt_hbm.at[2*W:],v_ref,lsem.at[H]),pltpu.make_async_copy(qkvt_hbm.at[:W],q_ref,lsem.at[H+1])]
    for x in come: x.start()
    for h in range(H):
        kvt[h*128+HEAD:h*128+HEAD+CODE,:]=codet_ref[...]
        kvt[h*128+HEAD+CODE:(h+1)*128,:]=jnp.zeros((HEAD-CODE,L),bf)
    vct[:,HEAD:,:]=jnp.ones((H,16,L),bf)
    for x in come[:H+1]: x.wait()
    row=iota((256,256),0)
    down=iota((256,SRC),0)
    def dest(d,c):
        first=jnp.minimum(win_ref[16+d,0]//128*128,L-SRC)
        last=win_ref[17+d,0]
        def src(t,a):
            ssl=pl.ds(al(jnp.minimum(first+t*SRC,L-SRC),128),SRC)
            oh=((meta_ref[0:1,ssl]==down+d*256)&(lane>=first+t*SRC-jnp.minimum(first+t*SRC,L-SRC))).astype(f32).astype(bf)
            return a[0]+dot(kvt[:,ssl],oh,1,1),a[1]+dot(v_ref[:,ssl],oh,1,1)
        lane=iota((256,SRC),1)
        ka,va=src(0,(jnp.zeros((H*128,256),f32),jnp.zeros((W,256),f32)))
        ka,va=lax.fori_loop(1,(last-first+SRC-1)//SRC,src,(ka,va))
        dsl=pl.ds(al(d*256,256),256)
        for h in range(H):
            k1=jnp.where(row[:128]==HEAD+10,-2560.0,ka[h*128:(h+1)*128])
            kaug_ref[h,dsl,:]=k1.astype(bf).T
            kct_ref[h,:,dsl]=k1[:HEAD].astype(bf)
            vct[h,:HEAD,dsl]=va[h*HEAD:(h+1)*HEAD].astype(bf)
        return c
    lax.fori_loop(0,(total+255)//256,dest,0)
    keep=[pltpu.make_async_copy(kct_ref,kct_hbm,ksem.at[0]),pltpu.make_async_copy(vct,vct_hbm,ksem.at[1])]
    for x in keep: x.start()
    come[H+1].wait()
    bound=jnp.float32(0)
    for h in range(H):
        q=q_ref[h*HEAD:(h+1)*HEAD,:].astype(f32); k=kvt[h*128:h*128+HEAD,:].astype(f32)
        bound=jnp.maximum(bound,jnp.max(jnp.sum(q*q,0,keepdims=True))*jnp.max(jnp.sum(k*k,0,keepdims=True)))
    safe=bound<SAFE*SAFE

    def pcopy(g):
        slot=lax.rem(g,SLOTS)
        return pltpu.make_async_copy(pbuf.at[slot],p_hbm.at[g],psem.at[slot])
    def ocopy(i):
        slot=lax.rem(i,2)
        return pltpu.make_async_copy(obuf.at[slot],ot_hbm.at[i],osem.at[slot])
    def acopy(i):
        slot=lax.rem(i,2)
        return pltpu.make_async_copy(abuf.at[slot],att_hbm.at[:,pl.ds(al(i*QB,QB),QB),:],asem.at[slot])
    def block(i,g):
        slot=lax.rem(i,2)
        qsl=pl.ds(al(i*QB,QB),QB)
        first,full,rest,groups=window(win_ref,i)
        qa=[jnp.concatenate([q_ref[h*HEAD:(h+1)*HEAD,qsl],codet_ref[:,qsl],jnp.zeros((HEAD-CODE,QB),bf)],0) for h in range(H)]
        own=meta_ref[1:2,qsl]>0
        sself=[]
        for h in range(H):
            x=q_ref[h*HEAD:(h+1)*HEAD,qsl].astype(f32)*kvt[h*128:h*128+HEAD,qsl].astype(f32)
            sself.append(jnp.where(own,jnp.sum(x,0,keepdims=True),-1e30))
        acc[...]=jnp.zeros_like(acc)
        top_ref[...]=jnp.zeros_like(top_ref)
        row=iota((128,QB),0)
        def strict(h,osl):
            k=kaug_ref[h,osl,:]
            x=qa[h].astype(f32)
            plain=dot(k,jnp.where(row<HEAD,x,0.0).astype(bf),1,0)
            return jnp.where(dot(k,jnp.where(row<HEAD,0.0,x).astype(bf),1,0)>-1.0,plain,-1e30)
        @pl.when(jnp.logical_not(safe))
        def _():
            for h in range(H):
                def more(j,m): return jnp.maximum(m,jnp.max(strict(h,pl.ds(al(first+j*128,128),128)),0,keepdims=True))
                top_ref[h:h+1,:]=lax.fori_loop(0,groups,more,sself[h])
        def piece(off,size,g):
            ps=lax.rem(g,SLOTS)
            osl=pl.ds(off,size)
            @pl.when(g>=SLOTS)
            def _(): pcopy(g-SLOTS).wait()
            @pl.when(safe)
            def _():
                keepp=[]
                for h in range(H):
                    p=jnp.exp2(dot(kaug_ref[h,osl,:],qa[h],1,0)).astype(bf)
                    pbuf[ps,h,:,:size]=p.T
                    keepp.append(p)
                for h in range(H): acc[h]+=dot(vct[h,:,osl],keepp[h],1,0)
            @pl.when(jnp.logical_not(safe))
            def _():
                for h in range(H):
                    def put(j,c):
                        jsl=pl.ds(al(off+j*128,128),128)
                        p=jnp.exp2(strict(h,jsl)-top_ref[h:h+1,:]).astype(bf)
                        pbuf[ps,h,:,pl.ds(al(j*128,128),128)]=p.T
                        acc[h]+=dot(vct[h,:,jsl],p,1,0)
                        return c
                    lax.fori_loop(0,size//128,put,0)
            pcopy(g).start()
        g=by_piece(first,full,rest,g,piece)
        @pl.when(i>=2)
        def _(): ocopy(i-2).wait(); acopy(i-2).wait()
        for h in range(H):
            ps=jnp.exp2(sself[h]-top_ref[h:h+1,:])
            inv=1.0/(acc[h,HEAD:HEAD+1,:]+ps)
            obuf[slot,h*HEAD:(h+1)*HEAD,:]=(acc[h,:HEAD,:]+ps*v_ref[h*HEAD:(h+1)*HEAD,qsl].astype(f32))*inv
            inv_ref[h,0:1,qsl]=inv
            inv_ref[h,1:2,qsl]=ps
        for hp in range(H//2): abuf[slot,hp]=obuf[slot,hp*128:(hp+1)*128,:].astype(bf).T
        ocopy(i).start(); acopy(i).start()
        return g
    g=lax.fori_loop(0,nq,block,0)
    for s in range(SLOTS):
        last=g-1-s
        @pl.when(last>=0)
        def _(): pcopy(last).wait()
    for i in range(max(nq-2,0),nq): ocopy(i).wait(); acopy(i).wait()
    for x in keep: x.wait()

def attend(base,win,qkvt,codet,meta,H):
    L=qkvt.shape[1]; W=H*HEAD; nq=L//QB; cap=nq*(L//KB+1)
    V=pl.BlockSpec(memory_space=pltpu.VMEM); A=pl.BlockSpec(memory_space=pl.ANY)
    S=jax.ShapeDtypeStruct; M=pltpu.VMEM; D=pltpu.SemaphoreType.DMA
    return pl.pallas_call(functools.partial(attend_kernel,L,H),
        out_shape=[S((cap,H,QB,KB),bf),S((H//2,L,128),bf),S((nq,W,QB),f32),S((H,8,L),f32),S((H,HEAD,L),bf),S((H,HEAD+16,L),bf)],
        in_specs=[pl.BlockSpec(memory_space=pltpu.SMEM)]*2+[A,V,V],
        out_specs=[A,A,A,V,A,A],
        scratch_shapes=[M((H,L,128),bf),M((H,HEAD,L),bf),M((H*128,L),bf),M((W,L),bf),M((W,L),bf),M((H,HEAD+16,L),bf),M((H,HEAD+16,QB),f32),M((SLOTS,H,QB,KB),bf),
            M((2,W,QB),f32),M((2,H//2,QB,128),bf),M((8,QB),f32),D((SLOTS,)),D((2,)),D((2,)),D((2,)),D((H+2,))],
        compiler_params=pltpu.CompilerParams(vmem_limit_bytes=VMEM))(base,win,qkvt,codet,meta)

def flags(row):
    L=row.shape[1]; nb=L//256; nq=L//QB
    seg=row//4
    pad=row//2-2*seg
    known=row-2*(row//2)
    use=(pad==0)&(known==1)
    usef=use.astype(f32)
    x=jnp.concatenate([usef[:,b*256:(b+1)*256] for b in range(nb)]+[jnp.zeros((16-nb,256),f32)],0)
    incl=dot(x.astype(bf),(iota((256,256),0)<=iota((256,256),1)).astype(f32).astype(bf),1,0)
    tot=jnp.broadcast_to(incl[:,255:256],(16,256)).astype(bf)
    base=dot((iota((16,16),0)>iota((16,16),1)).astype(f32).astype(bf),tot,1,0)
    mid=seg[:,L//2:L//2+1]
    late=(seg>=mid).astype(f32)
    early=jnp.sum(usef*(1.0-late),1,keepdims=True)
    shift=jnp.ceil(early*(1.0/128.0))*128.0-early
    shift=jnp.where(jnp.sum(usef,1,keepdims=True)+shift<=L,shift,0.0)
    csum=jnp.concatenate([(incl+base)[b:b+1] for b in range(nb)],1)+late*shift
    rank=jnp.where(use,csum.astype(jnp.int32)-1,-1)
    base=base+shift*jnp.concatenate([late[:,b*256:b*256+1] for b in range(nb)]+[jnp.ones((16-nb,1),f32)],0)
    own=((pad==0)&(known!=1)).astype(jnp.int32)
    bits=iota((CODE,L),0)
    bit=lax.shift_right_logical(jnp.broadcast_to(seg,(CODE,L)),jnp.minimum(bits,9))&1
    codet=jnp.where(bits<10,jnp.where(bit==1,16.0,-16.0),jnp.where(bits==10,1.0,0.0)).astype(bf)
    meta=jnp.concatenate([rank,own,jnp.zeros((6,L),jnp.int32)],0)
    def edge(at): return jnp.concatenate([seg[:,i*QB+at:i*QB+at+1] for i in range(nq)]+[jnp.zeros((8-nq,1),jnp.int32)],0)
    low=jnp.sum(jnp.where(seg<edge(0),usef,0.0),1,keepdims=True)+shift*(edge(0)>=mid).astype(f32)
    high=jnp.sum(jnp.where(seg<=edge(QB-1),usef,0.0),1,keepdims=True)+shift*(edge(QB-1)>=mid).astype(f32)
    starts=jnp.sum((csum<=(256*iota((16,1),0)).astype(f32)).astype(f32),1,keepdims=True)
    win=jnp.broadcast_to(jnp.concatenate([low,high,starts],0),(32,128)).astype(jnp.int32)
    return base[:,:128].astype(jnp.int32),win,codet,meta
LN2=math.log(2.0)
SPAN=512
def back_kernel(L,H,base_ref,win_ref,datt_hbm,p_hbm,ot_hbm,inv_ref,kct_hbm,vct_hbm,qkvt_hbm,dq_hbm,dkvw_hbm,
                kct,vct,dkv,dkvt,pbuf,qacc,qkv,datt,ot,dq,psem,lsem,qsem,osem,tsem):
    W=H*HEAD; nq=L//QB
    groups=(begin(base_ref,L//256)+127)//128
    pieces=lax.fori_loop(0,nq,lambda i,s:s+window(win_ref,i)[1]+1,0)
    def pcopy(g):
        slot=lax.rem(g,SLOTS)
        return pltpu.make_async_copy(p_hbm.at[g],pbuf.at[slot],psem.at[slot])
    def keys(t):
        rows=pl.ds(al(t*KB,KB),KB)
        return [pltpu.make_async_copy(vct_hbm.at[:,:,rows],vct.at[:,:,rows],lsem.at[0,t]),pltpu.make_async_copy(kct_hbm.at[:,:,rows],kct.at[:,:,rows],lsem.at[1,t])]
    def queries(i):
        slot=lax.rem(i,2); qsl=pl.ds(al(i*QB,QB),QB)
        return [pltpu.make_async_copy(a,b.at[slot],qsem.at[k,slot]) for k,(a,b) in enumerate(((qkvt_hbm.at[:,qsl],qkv),(datt_hbm.at[:,qsl],datt),(ot_hbm.at[i],ot)))]
    def each_key(fn,least=0):
        def body(t,c):
            for x in keys(t): fn(x)
            return c
        lax.fori_loop(least,(groups+KB//128-1)//(KB//128),body,0)
    for x in queries(0): x.start()
    each_key(lambda x:x.start())
    for s in range(SLOTS-1):
        @pl.when(s<pieces)
        def _(): pcopy(s).start()
    def clear(j,c):
        dkv[:,pl.ds(al(j*128,128),128)]=jnp.zeros((2*W,128),f32)
        return c
    lax.fori_loop(0,groups,clear,0)
    def ocopy(i):
        slot=lax.rem(i,2)
        return pltpu.make_async_copy(dq.at[slot],dq_hbm.at[:,pl.ds(al(i*QB,QB),QB)],osem.at[slot])
    def block(i,g):
        slot=lax.rem(i,2)
        qsl=pl.ds(al(i*QB,QB),QB)
        first,full,rest,_=window(win_ref,i)
        for x in queries(i): x.wait()
        @pl.when(i+1<nq)
        def _():
            for x in queries(i+1): x.start()
        dt=datt[slot].astype(f32)
        prod=dt*ot[slot]
        daug=[];lows=[];deltas=[];d1s=[]
        row=iota((16,QB),0)
        for h in range(H):
            hsl=slice(h*HEAD,(h+1)*HEAD)
            inv=inv_ref[h,0:1,qsl]
            delta=jnp.sum(prod[hsl],0,keepdims=True)*inv
            d1=dt[hsl]*inv
            low=d1.astype(bf)
            a=delta.astype(bf).astype(f32); b=(delta-a).astype(bf).astype(f32)
            extra=jnp.where(row==0,-a,jnp.where(row==1,-b,jnp.where(row==2,a+b-delta,0.0))).astype(bf)
            daug.append(jnp.concatenate([low,extra,jnp.zeros((HEAD-16,QB),bf)],0).T[:,:HEAD+16])
            lows.append(low); deltas.append(delta); d1s.append(d1)
        qacc[...]=jnp.zeros_like(qacc)
        def piece(off,size,g):
            ps=lax.rem(g,SLOTS)
            osl=pl.ds(off,size)
            @pl.when(g+SLOTS-1<pieces)
            def _(): pcopy(g+SLOTS-1).start()
            @pl.when(i==0)
            def _():
                for x in keys(g): x.wait()
            pcopy(g).wait()
            dss=[]
            for h in range(H):
                dss.append((pbuf[ps,h,:,:size].astype(f32)*dot(daug[h],vct[h,:,osl],1,0)).astype(bf))
                dkv[W+h*HEAD:W+(h+1)*HEAD,osl]+=dot(lows[h],pbuf[ps,h,:,:size],1,0)
            for h in range(H): qacc[h]+=dot(kct[h,:,osl],dss[h].T,1,0)
            for h in range(H):
                dkv[h*HEAD:(h+1)*HEAD,osl]+=dot(qkv[slot,h*HEAD:(h+1)*HEAD,:],dss[h],1,0)
        g=by_piece(first,full,rest,g,piece)
        @pl.when(i==0)
        def _(): each_key(lambda x:x.wait(),g)
        @pl.when(i>=2)
        def _(): ocopy(i-2).wait()
        for h in range(H):
            hsl=slice(h*HEAD,(h+1)*HEAD); ksl=slice(W+h*HEAD,W+(h+1)*HEAD); vsl=slice(2*W+h*HEAD,2*W+(h+1)*HEAD)
            ps=inv_ref[h,1:2,qsl]
            ds=ps*(jnp.sum(qkv[slot,vsl,:].astype(f32)*d1s[h],0,keepdims=True)-deltas[h])
            dq[slot,hsl,:]=((qacc[h]+ds*qkv[slot,ksl,:].astype(f32))*0.125).astype(bf)
            dq[slot,ksl,:]=(ds*qkv[slot,hsl,:].astype(f32)*LN2).astype(bf)
            dq[slot,vsl,:]=(ps*d1s[h]).astype(bf)
        ocopy(i).start()
        return g
    lax.fori_loop(0,nq,block,0)
    rows=iota((2*W,128),0)
    def tcopy(s): return pltpu.make_async_copy(dkvt.at[:,pl.ds(al(begin(base_ref,s)//128*128,128),SPAN)],dkvw_hbm.at[s],tsem.at[s])
    def turn(j,c):
        jsl=pl.ds(al(j*128,128),128)
        x=jnp.where(j<groups,dkv[:,jsl],0.0)
        dkvt[:,jsl]=jnp.where(rows<W,x*LN2,x).astype(bf)
        for s in range(L//256):
            @pl.when(begin(base_ref,s)//128+SPAN//128-1==j)
            def _(): tcopy(s).start()
        return c
    lax.fori_loop(0,groups+SPAN//128,turn,0)
    for i in range(max(nq-2,0),nq): ocopy(i).wait()
    for s in range(L//256): tcopy(s).wait()

def back(base,win,datt,p,ot,inv,kct,vct,qkvt,H):
    L=qkvt.shape[1]; W=H*HEAD
    V=pl.BlockSpec(memory_space=pltpu.VMEM); A=pl.BlockSpec(memory_space=pl.ANY); N=pl.BlockSpec(memory_space=pltpu.SMEM)
    S=jax.ShapeDtypeStruct; M=pltpu.VMEM; D=pltpu.SemaphoreType.DMA
    return pl.pallas_call(functools.partial(back_kernel,L,H),
        out_shape=[S((3*W,L),bf),S((L//256,2*W,SPAN),bf)],
        in_specs=[N,N,A,A,A,V,A,A,A],
        out_specs=[A,A],
        scratch_shapes=[M((H,HEAD,L),bf),M((H,HEAD+16,L),bf),M((2*W,L+SPAN),f32),M((2*W,L+SPAN),bf),M((SLOTS,H,QB,KB),bf),M((H,HEAD,QB),f32),
            M((2,3*W,QB),bf),M((2,W,QB),bf),M((2,W,QB),f32),M((2,3*W,QB),bf),
            D((SLOTS,)),D((2,L//KB)),D((3,2)),D((2,)),D((L//256,))],
        compiler_params=pltpu.CompilerParams(vmem_limit_bytes=VMEM))(base,win,datt,p,ot,inv,kct,vct,qkvt)

def placed(base_ref,rank_row,span,own,s):
    r0=begin(base_ref,s)//128*128
    oh=(rank_row==iota((SPAN,256),0)+r0).astype(f32).astype(bf)
    return dot(span,oh,1,0)+own.astype(f32)

def place_kernel(L,W,base_ref,meta_ref,dq_in,dkvw_ref,tok_ref,w_ref,tg_ref,grad_ref,dq_ref):
    dq_ref[...]=dq_in[...]
    def place(s,c):
        ssl=pl.ds(al(s*256,256),256)
        dq_ref[W:3*W,ssl]=placed(base_ref,meta_ref[0:1,ssl],dkvw_ref[s],dq_ref[W:3*W,ssl],s).astype(bf)
        tg_ref[ssl,:]=dot(dq_ref[:,ssl],w_ref[...],0,1).astype(bf)
        return c
    lax.fori_loop(0,L//256,place,0)
    grad_ref[...]=dot(dq_ref[...],tok_ref[...],1,0).T.astype(bf)

def place_all(base,meta,dq,dkvw,tok,w,H):
    L,E=tok.shape; W=H*HEAD
    V=pl.BlockSpec(memory_space=pltpu.VMEM); S=jax.ShapeDtypeStruct
    return pl.pallas_call(functools.partial(place_kernel,L,W),out_shape=[S((L,E),bf),S((E,3*W),bf)],
        in_specs=[pl.BlockSpec(memory_space=pltpu.SMEM)]+[V]*5,out_specs=[V,V],scratch_shapes=[pltpu.VMEM((3*W,L),bf)],
        compiler_params=pltpu.CompilerParams(vmem_limit_bytes=VMEM))(base,meta,dq,dkvw,tok,w)
EPSILON=1e-05
def gelu_parts(h):
    bell=jnp.exp(-0.5*h*h)
    t=1.0/(1.0+(0.3275911*math.sqrt(0.5))*jnp.abs(h))
    tail=0.5*1.061405429
    for c in (-1.453152027,1.421413741,-0.284496736,0.254829592): tail=tail*t+0.5*c
    tail=tail*t*bell
    cdf=jnp.where(h<0.0,tail,1.0-tail)
    return cdf,cdf+h*bell*(1.0/math.sqrt(2.0*math.pi))
def norm(x):
    center=x-jnp.mean(x,-1,keepdims=True)
    inverse=lax.rsqrt(jnp.mean(center*center,-1,keepdims=True)+EPSILON)
    return center*inverse,inverse
def norm_back(e,n,inverse):
    return inverse*(e-jnp.mean(e,-1,keepdims=True)-n*jnp.mean(e*n,-1,keepdims=True))
def middle_kernel(a0_ref,a1_ref,tok_ref,cot_ref,wo_ref,wu_ref,wd_ref,gs_ref,out_ref,r1_ref,da_ref,go_ref,gu_ref,gd_ref,gg_ref):
    @pl.when(pl.program_id(0)==0)
    def _():
        for r in (go_ref,gu_ref,gd_ref,gg_ref): r[...]=jnp.zeros_like(r)
    P2=a0_ref.shape[0]
    att=jnp.concatenate([a0_ref[p] for p in range(P2)]+[a1_ref[p] for p in range(P2)],1)
    g0,g1,b0,b1=[gs_ref[r:r+1,:] for r in range(4)]
    n1,inv1=norm(tok_ref[...].astype(f32)+dot(att,wo_ref[...],1,0))
    first=(n1*g0+b0).astype(bf)
    hidden=dot(first,wu_ref[...],1,0)
    cdf,slope=gelu_parts(hidden)
    act=(hidden*cdf).astype(bf)
    n2,inv2=norm(first.astype(f32)+dot(act,wd_ref[...],1,0))
    out_ref[...]=(n2*g1+b1).astype(bf)
    cot=cot_ref[...].astype(f32)
    r2=norm_back(cot*g1,n2,inv2)
    feed=r2.astype(bf)
    gd_ref[...]+=dot(act,feed,0,0)
    dh=(dot(feed,wd_ref[...],1,1)*slope).astype(bf)
    gu_ref[...]+=dot(first,dh,0,0)
    df=r2+dot(dh,wu_ref[...],1,1)
    r1=norm_back(df*g0,n1,inv1)
    r1_ref[...]=r1
    db=r1.astype(bf)
    go_ref[...]+=dot(att,db,0,0)
    da=dot(db,wo_ref[...],1,1).astype(bf)
    for p in range(2*P2): da_ref[p]=da[:,p*128:(p+1)*128]
    gg_ref[0:1,:]+=jnp.sum(df*n1,0,keepdims=True)
    gg_ref[1:2,:]+=jnp.sum(cot*n2,0,keepdims=True)
    gg_ref[2:3,:]+=jnp.sum(df,0,keepdims=True)
    gg_ref[3:4,:]+=jnp.sum(cot,0,keepdims=True)

def middle(a0,a1,tok,cot,wo,wu,wd,gs):
    P2,N,_=a0.shape; D=tok.shape[1]; F=wu.shape[1]
    T=max(t for t in (256,192,128,64,32,16) if N%t==0)
    tile=pl.BlockSpec((T,D),lambda i:(i,0))
    def pairs(k): return pl.BlockSpec((k,T,128),lambda i:(0,i,0))
    def whole(s): return pl.BlockSpec(s,lambda i:(0,)*len(s))
    return pl.pallas_call(middle_kernel,grid=(N//T,),
        in_specs=[pairs(P2),pairs(P2),tile,tile,whole((D,D)),whole((D,F)),whole((F,D)),whole((8,D))],
        out_specs=[tile,tile,pairs(2*P2),whole((D,D)),whole((D,F)),whole((F,D)),whole((8,D))],
        out_shape=[jax.ShapeDtypeStruct((N,D),bf),jax.ShapeDtypeStruct((N,D),f32),jax.ShapeDtypeStruct((2*P2,N,128),bf),
            jax.ShapeDtypeStruct((D,D),f32),jax.ShapeDtypeStruct((D,F),f32),jax.ShapeDtypeStruct((F,D),f32),jax.ShapeDtypeStruct((8,D),f32)],
        compiler_params=pltpu.CompilerParams(vmem_limit_bytes=60<<20))(a0,a1,tok,cot,wo,wu,wd,gs)
MESH=pl.DeviceIdType.MESH
class Net:
    def __init__(self,Z):
        dp=lax.axis_index("dp"); blk=lax.axis_index("blk")
        self.Z=Z; self.z=dp//2; self.y=dp%2; self.j=blk//2; self.c=blk%2
        self.sent=[]
    def at(self,z=None,y=None,j=None,c=None):
        z=self.z if z is None else z; y=self.y if y is None else y; j=self.j if j is None else j; c=self.c if c is None else c
        return (z*2+y,j*2+c)
    def signal(self):
        barrier=pltpu.get_barrier_semaphore()
        for d in [self.at(j=1-self.j),self.at(y=1-self.y),self.at(c=1-self.c)]+[self.at(z=lax.rem(self.z+k,self.Z)) for k in range(1,self.Z)]:
            pl.semaphore_signal(barrier,inc=1,device_id=d,device_id_type=MESH)
    def wait(self): pl.semaphore_wait(pltpu.get_barrier_semaphore(),2+self.Z)
    def greet(self):
        self.signal()
        self.wait()
    def copy(self,src,dst,ssem,rsem,device):
        return pltpu.make_async_remote_copy(src_ref=src,dst_ref=dst,send_sem=ssem,recv_sem=rsem,device_id=device,device_id_type=MESH)
    def send(self,src,dst,ssem,rsem,device,when=None):
        c=self.copy(src,dst,ssem,rsem,device)
        if when is None: c.start()
        else: pl.when(when)(c.start)
        self.sent.append((c,when))
    def drain(self):
        for c,when in self.sent:
            if when is None: c.wait_send()
            else: pl.when(when)(c.wait_send)

def gather_kernel(Z,block,E,W,rows,tok_hbm,cot_hbm,seg_ref,pad_ref,known_ref,wq_ref,wo_ref,wu_ref,wd_ref,gain_ref,shift_ref,
                  tok_out,bund_out,wmine_out,qkvt_out,base_out,win_out,code_out,meta_out,far_out,
                  tokb,farb,info_ref,infob,pack_ref,wall,bund,wt,qkvt,lsem,qsem,xs,xr,zs,zr,ys,yr,cs,cr,ts,tr,iss,isr):
    net=Net(Z); z,y,j,c=net.z,net.y,net.j,net.c
    NCH=block//rows; D=E
    sib=net.at(c=1-c); xd=net.at(j=1-j); yd=net.at(y=1-y)
    net.signal()
    mine=pltpu.make_async_copy(tok_hbm.at[j],tokb.at[j,c],lsem.at[0]); mine.start()
    far=pltpu.make_async_copy(cot_hbm.at[1-j],farb,lsem.at[3]); far.start()
    at=0
    for ref in (wq_ref,wo_ref,wu_ref,wd_ref):
        n=ref.shape[1]
        pack_ref[:,at:at+n]=ref[...]
        at+=n
    R=gain_ref.shape[1]
    place=(iota((R,128),1)==iota((R,128),0)+R*lax.rem(lax.axis_index("dp")*4+lax.axis_index("blk"),128//R)).astype(f32).astype(bf)
    pack_ref[:,at:]=jnp.concatenate([dot(gain_ref[...],place,1,0),dot(shift_ref[...],place,1,0),jnp.zeros((12,128),f32)],0).astype(bf)
    split=6*W
    wall[z,y,j,c]=pack_ref[:,:split]
    bund[y,j]=pack_ref[:,split:]
    info_ref[...]=seg_ref[...]*4+pad_ref[...]*2+known_ref[...]
    infob[j,c]=info_ref[j]
    net.wait()
    net.send(pack_ref.at[:,:split],wall.at[z,y,j,c],xs.at[0],xr.at[0],xd)
    net.send(pack_ref.at[:,split:],bund.at[y,j],xs.at[1],xr.at[1],xd)
    net.send(info_ref.at[1-j],infob.at[j,c],iss.at[0],isr.at[0],xd)
    net.send(info_ref.at[j],infob.at[j,c],iss.at[1],isr.at[1],sib)
    def chunk(k): return pl.ds(k*rows if type(k) is int else al(k*rows,rows),rows)
    for k in range(NCH):
        net.send(tok_hbm.at[1-j,chunk(k)],tokb.at[j,c,chunk(k)],ts.at[0,k],tr.at[0,k],xd)
        net.send(tok_hbm.at[j,chunk(k)],tokb.at[j,c,chunk(k)],ts.at[1,k],tr.at[1,k],sib)
    def piece(o,y_): return wall.at[o,y_,:,c]
    def landed(ref,sem): pltpu.make_async_copy(ref,ref,sem).wait()
    def pass_on(o):
        net.send(piece(o,y),piece(o,y),ys.at[o],yr.at[o],yd)
        net.send(piece(o,y),piece(o,y),cs.at[0,o],cr.at[0,o],sib)
    far.wait()
    far=pltpu.make_async_copy(farb,far_out,lsem.at[3]); far.start()
    landed(wall.at[z,y,1-j,c],xr.at[0])
    for k in range(1,Z):
        net.send(piece(z,y),piece(z,y),zs.at[k],zr.at[k],net.at(z=lax.rem(z+k,Z)))
    pass_on(z)
    landed(bund.at[y,1-j],xr.at[1])
    net.send(bund.at[y],bund.at[y],ys.at[Z],yr.at[Z],yd)
    for k in range(1,Z):
        o=lax.rem(z+Z-k,Z)
        landed(piece(o,y),zr.at[k])
        pass_on(o)
    for k in range(Z):
        o=lax.rem(z+Z-k,Z)
        landed(piece(o,1-y),yr.at[o])
        net.send(piece(o,1-y),piece(o,1-y),cs.at[1,o],cr.at[1,o],sib)
    for o in range(Z):
        for q in range(2): landed(wall.at[o,y if q==0 else 1-y,:,1-c],cr.at[q,o])
    landed(bund.at[1-y],yr.at[Z])
    outb=pltpu.make_async_copy(bund,bund_out,lsem.at[1]); outb.start()
    def qcopy(g):
        col=pl.ds(al(g*rows,rows),rows)
        return pltpu.make_async_copy(qkvt.at[:,col],qkvt_out.at[:,col],qsem.at[g])
    def project(jj,cc,come=None,onward=False):
        def body(k,carry):
            ref=tokb.at[jj,cc,chunk(k)]
            if come is not None: landed(ref,tr.at[come,k])
            if onward: net.copy(ref,ref,ts.at[2,k],tr.at[2,k],sib).start()
            g=(jj*2+cc)*NCH+k
            r=dot(wt[...],ref[...],1,1)
            qkvt[:,pl.ds(al(g*rows,rows),rows)]=jnp.concatenate([r[:W]*(math.log2(math.e)/8),r[W:]],0).astype(bf)
            qcopy(g).start()
            return carry
        lax.fori_loop(0,NCH,body,0)
    parts=[]
    for t in range(3):
        cols=pl.ds(al(t*2*W+c*W,W),W)
        part=wall[:,:,:,:,:,cols].reshape(D,W)
        wt[t*W:(t+1)*W,:]=part.T
        parts.append(part)
    wmine_out[...]=jnp.concatenate(parts,1)
    mine.wait()
    project(j,c)
    project(j,1-c,1)
    landed(infob.at[1-j,c],isr.at[0])
    net.send(infob.at[1-j,c],infob.at[1-j,c],iss.at[2],isr.at[2],sib)
    project(1-j,c,0,True)
    landed(infob.at[j,1-c],isr.at[1])
    landed(infob.at[1-j,1-c],isr.at[2])
    base_out[...],win_out[...],code_out[...],meta_out[...]=flags(jnp.concatenate([infob[0,0],infob[0,1],infob[1,0],infob[1,1]],1))
    project(1-j,1-c,2)
    outt=pltpu.make_async_copy(tokb,tok_out,lsem.at[2]); outt.start()
    net.drain()
    for k in range(NCH):
        ref=tokb.at[1-j,c,chunk(k)]
        net.copy(ref,ref,ts.at[2,k],tr.at[2,k],sib).wait_send()
    lax.fori_loop(0,4*NCH,lambda g,c:(qcopy(g).wait(),c)[1],0)
    outb.wait(); outt.wait(); far.wait()

def gather(tok,cot,seg,pad,known,wq,wo,wu,wd,gain,shift,Z,W):
    _,block,E=tok.shape; R=wq.shape[0]; C=6*W+wo.shape[1]+wu.shape[1]+wd.shape[1]+128
    rows=256; NCH=block//rows; L=4*block
    V=pl.BlockSpec(memory_space=pltpu.VMEM); A=pl.BlockSpec(memory_space=pl.ANY)
    S=jax.ShapeDtypeStruct; M=pltpu.VMEM; D=pltpu.SemaphoreType.DMA; I=jnp.int32
    return pl.pallas_call(functools.partial(gather_kernel,Z,block,E,W,rows),
        out_shape=[S((2,2,block,E),bf),S((2,2,R,C-6*W),bf),S((E,3*W),bf),S((3*W,L),bf),S((16,128),I),S((32,128),I),S((CODE,L),bf),S((8,L),I),S((block,E),bf)],
        in_specs=[A,A]+[V]*9,out_specs=[A,A,V,A,V,V,V,V,A],
        scratch_shapes=[M((2,2,block,E),bf),M((block,E),bf),M((2,1,block),I),M((2,2,1,block),I),M((R,C),bf),M((Z,2,2,2,R,6*W),bf),M((2,2,R,C-6*W),bf),M((3*W,E),bf),M((3*W,L),bf),
            D((4,)),D((4*NCH,)),D((2,)),D((2,)),D((Z,)),D((Z,)),D((Z+1,)),D((Z+1,)),D((2,Z)),D((2,Z)),D((3,NCH)),D((3,NCH)),D((3,)),D((3,))],
        compiler_params=pltpu.CompilerParams(collective_id=0,has_side_effects=True,vmem_limit_bytes=VMEM))(tok,cot,seg,pad,known,wq,wo,wu,wd,gain,shift)
def middle_net_kernel(Z,block,E,F,W,T,att_hbm,tok_hbm,cot_hbm,cotx_hbm,*rest):
    bunds=rest[:Z]; near_out,far_out,r1_out,datt_out=rest[Z:Z+4]; parts=rest[Z+4]
    (go_ref,gu_ref,gd_ref,gg_ref,gt_ref,aown,aget,tok,cot,wall,lay,r1,da,lsem,wsem,osem,asend,aget_sem,dsend,dget,bsend,bget)=rest[Z+5:]
    net=Net(Z); z,y,j,c=net.z,net.y,net.j,net.c
    NCH=block//T; n=2*NCH; P2=att_hbm.shape[0]; G=2
    sib=net.at(c=1-c)
    def place(t):
        jj=jnp.where(t<NCH,1-j,j)
        return jj,pl.ds(al(lax.rem(t,NCH)*T,T),T)
    def where(t): return pl.ds(al((jnp.where(t<NCH,1-j,j)*2+c)*block+lax.rem(t,NCH)*T,T),T)
    def load(t):
        jj,rows=place(t)
        return [pltpu.make_async_copy(att_hbm.at[:,jj,c,rows],aown.at[t],lsem.at[0,t]),pltpu.make_async_copy(tok_hbm.at[jj,c,rows],tok.at[t],lsem.at[1,t])]
    def load_cot(t,near):
        rows=place(t)[1]
        return pltpu.make_async_copy((cot_hbm.at[j,rows] if near else cotx_hbm.at[rows]),cot.at[t],lsem.at[2,t])
    cols=[(0,E),(E,F),(E+F,E),(2*E+F,128)]
    loadw=[pltpu.make_async_copy(bunds[k],wall.at[lax.rem(z+Z-k,Z),:,:,c],wsem.at[k]) for k in range(Z)]
    for x in loadw: x.start()
    def start(t,near):
        for x in load(t): x.start()
        load_cot(t,near).start()
    for t in range(n): start(t,t>=NCH)
    barrier=pltpu.get_barrier_semaphore()
    pl.semaphore_signal(barrier,inc=1,device_id=sib,device_id_type=MESH)
    pl.semaphore_wait(barrier,1)
    def ship(t):
        jj,rows=place(t)
        return net.copy(att_hbm.at[:,jj,1-c,rows],aget.at[t],asend.at[t],aget_sem.at[t],sib)
    ship(0).start()
    weights=[net.copy(bunds[k],wall.at[lax.rem(z+Z-k,Z),:,:,c],bsend.at[k],bget.at[k],sib) for k in range(Z)]
    for x in weights: x.start()
    for t in range(1,n): ship(t).start()
    for x in loadw: x.wait()
    for k in range(Z):
        ref=wall.at[lax.rem(z+Z-k,Z),:,:,1-c]
        pltpu.make_async_copy(ref,ref,bget.at[k]).wait()
    def whole(a,b): return wall[:,:,:,:,:,a:a+b].reshape(E,b)
    gs=wall[:,:,:,:,:,cols[3][0]:].reshape(E//16,16,128).astype(f32)
    gsr=jnp.concatenate([jnp.sum(gs[q*8:(q+1)*8],0) for q in range(E//128)],1)
    g0,g1,b0,b1=[gsr[r:r+1,:] for r in range(4)]
    for r in (go_ref,gu_ref,gd_ref,gg_ref): r[...]=jnp.zeros_like(r)
    def out_near(t): return pltpu.make_async_copy(lay.at[t],near_out.at[place(t)[1]],osem.at[0,t])
    def out_far(t): return pltpu.make_async_copy(lay.at[t],far_out.at[place(t)[1]],osem.at[0,t])
    def out_r1(t):
        jj,rows=place(t)
        return pltpu.make_async_copy(r1.at[t],r1_out.at[jj,rows],osem.at[1,t])
    def out_da(t):
        return pltpu.make_async_copy(da.at[0,t],datt_out.at[:,where(t)],osem.at[2,t])
    def ship_da(t):
        return net.copy(da.at[1,t],datt_out.at[:,where(t)],dsend.at[t],dget.at[t],sib)
    def tiles(u,carry):
        ts=[G*u+g for g in range(G)]
        def each(f,*lists): return [f(*v) for v in zip(*lists)]
        for t in ts:
            for x in load(t): x.wait()
            pltpu.make_async_copy(cotx_hbm.at[place(t)[1]],cot.at[t],lsem.at[2,t]).wait()
            ship(t).wait_recv()
        def whole_att(t):
            mine=[aown[t,p] for p in range(P2)]; his=[aget[t,p] for p in range(P2)]
            return jnp.where(c==0,jnp.concatenate(mine+his,1),jnp.concatenate(his+mine,1))
        wo=whole(*cols[0]); wu=whole(*cols[1]); wd=whole(*cols[2])
        att=each(whole_att,ts)
        branch=each(lambda a:dot(a,wo,1,0),att)
        n1,inv1=zip(*each(lambda t,b:norm(tok[t].astype(f32)+b),ts,branch))
        first=each(lambda n:(n*g0+b0).astype(bf),n1)
        hidden=each(lambda a:dot(a,wu,1,0),first)
        cdf,slope=zip(*each(gelu_parts,hidden))
        act=each(lambda h,p:(h*p).astype(bf),hidden,cdf)
        fed=each(lambda a:dot(a,wd,1,0),act)
        n2,inv2=zip(*each(lambda a,b:norm(a.astype(f32)+b),first,fed))
        ct=each(lambda t:cot[t].astype(f32),ts)
        r2=each(lambda x,n,i:norm_back(x*g1,n,i),ct,n2,inv2)
        feed=each(lambda x:x.astype(bf),r2)
        dact=each(lambda x:dot(x,wd,1,1),feed)
        for t,n in zip(ts,n2): lay[t]=(n*g1+b1).astype(bf)
        both=lambda v:jnp.concatenate(v,0)
        gd_ref[...]+=dot(both(act),both(feed),0,0)
        dh=each(lambda x,s:(x*s).astype(bf),dact,slope)
        df=each(lambda x,h:x+dot(h,wu,1,1),r2,dh)
        gu_ref[...]+=dot(both(first),both(dh),0,0)
        dr=each(lambda x,n,i:norm_back(x*g0,n,i),df,n1,inv1)
        db=each(lambda x:x.astype(bf),dr)
        d=each(lambda x:dot(wo,x,1,1).astype(bf),db)
        go_ref[...]+=dot(both(att),both(db),0,0)
        for t,x,e in zip(ts,dr,d):
            r1[t]=x.astype(r1.dtype)
            da[0,t]=jnp.where(c==0,e[:W],e[W:])
            da[1,t]=jnp.where(c==0,e[W:],e[:W])
        down=lambda v:sum(jnp.sum(x,0,keepdims=True) for x in v)
        gg_ref[0:1,:]+=down(each(lambda x,n:x*n,df,n1))
        gg_ref[1:2,:]+=down(each(lambda x,n:x*n,ct,n2))
        gg_ref[2:3,:]+=down(df)
        gg_ref[3:4,:]+=down(ct)
        for t in ts:
            @pl.when(t<NCH)
            def _(): out_far(t).start()
            @pl.when(t>=NCH)
            def _(): out_near(t).start()
            out_r1(t).start(); out_da(t).start(); ship_da(t).start()
        return carry
    lax.fori_loop(0,n//G,tiles,0)
    ggt=jnp.concatenate([gg_ref[...],jnp.zeros((120,E),f32)],0).T
    gt_ref[...]=ggt
    R=E//(2*Z)
    at=0
    for ref in (go_ref,gu_ref,gd_ref,gt_ref):
        parts[:,:,at:at+ref.shape[1]]=ref[...].astype(bf).reshape(2*Z,R,ref.shape[1])
        at+=ref.shape[1]
    for x in weights: x.wait_send()
    for t in range(n):
        ship(t).wait_send(); out_r1(t).wait(); out_da(t).wait(); ship_da(t).wait()
        (out_far if t<NCH else out_near)(t).wait()

def middle_net(att,tok,cot,cotx,bunds,Z,W,F):
    P2,_,_,block,_=att.shape; E=tok.shape[-1]; C=bunds[0].shape[-1]
    T=256; NCH=block//T; n=2*NCH
    V=pl.BlockSpec(memory_space=pltpu.VMEM); A=pl.BlockSpec(memory_space=pl.ANY)
    S=jax.ShapeDtypeStruct; M=pltpu.VMEM; D=pltpu.SemaphoreType.DMA
    return pl.pallas_call(functools.partial(middle_net_kernel,Z,block,E,F,W,T),
        out_shape=[S((block,E),bf),S((block,E),bf),S((2,block,E),bf),S((W,4*block),bf)]+[S((2*Z,E//(2*Z),C),bf)],
        in_specs=[A]*(4+Z),out_specs=[A,A,A,A,V],
        scratch_shapes=[M((E,E),f32),M((E,F),f32),M((F,E),f32),M((8,E),f32),M((E,128),f32),
            M((n,P2,T,128),bf),M((n,P2,T,128),bf),M((n,T,E),bf),M((n,T,E),bf),M((Z,2,2,2,16,C),bf),M((n,T,E),bf),M((n,T,E),bf),M((2,n,W,T),bf),
            D((3,n)),D((Z,)),D((3,n)),D((n,)),D((n,)),D((n,)),D((n,)),D((Z,)),D((Z,))],
        compiler_params=pltpu.CompilerParams(collective_id=2,has_side_effects=True,vmem_limit_bytes=VMEM))(att,tok,cot,cotx,*bunds)
def reduce_kernel(Z,block,E,W,C1,rows,base_ref,meta_ref,dq_hbm,dkvw_hbm,tok_hbm,w_hbm,r1_hbm,parts_hbm,tok_out,grad_out,
     dq,dkvw,tok,w,r1,parts,own,tgf,tgr,tgs,ob,s0,r0,g0,s1,r1b,su,ru,fin,sx,rx,se,re,sxe,rxe,
     lsem,nsem,osem,ts,tr,xs,xr,cs,cr,ys,yr,us,ur,fs,fr):
    net=Net(Z); z,y,j,c=net.z,net.y,net.j,net.c
    NCH=block//rows; half=2*block
    sib=net.at(c=1-c); xd=net.at(j=1-j); yd=net.at(y=1-y)
    def side(jj): return pl.ds(al(jj*half,128),half)
    def spans(jj): return pl.ds(jj*2*NCH,2*NCH)
    def need(cc,k):
        at=((1-j)*2+cc)*NCH+k; cols=pl.ds(al(at*rows,rows),rows)
        return [pltpu.make_async_copy(dkvw_hbm.at[at],dkvw.at[at],nsem.at[0,cc,k]),pltpu.make_async_copy(dq_hbm.at[:,cols],dq.at[:,cols],nsem.at[1,cc,k])]
    loads=[pltpu.make_async_copy(a,b,lsem.at[k]) for k,(a,b) in enumerate(((w_hbm,w),(r1_hbm,r1),(parts_hbm,parts),
        (dq_hbm.at[:,side(j)],dq.at[:,side(j)]),(tok_hbm,tok),(dkvw_hbm.at[spans(j)],dkvw.at[spans(j)])))]
    net.signal()
    for x in need(1-c,0)+loads[:1]+need(c,0): x.start()
    for k in range(1,NCH):
        for x in need(1-c,k)+need(c,k): x.start()
    for x in loads[1:]: x.start()
    def chunk(k): return pl.ds(k*rows,rows)
    def landed(ref,sem): pltpu.make_async_copy(ref,ref,sem).wait()
    def position(jj,cc,k): return pl.ds(al(((jj*2+cc)*NCH+k)*rows,rows),rows)
    def place(jj,cc,k):
        ssl=position(jj,cc,k)
        dq[W:3*W,ssl]=placed(base_ref,meta_ref[0:1,ssl],dkvw[(jj*2+cc)*NCH+k],dq[W:3*W,ssl],(jj*2+cc)*NCH+k).astype(bf)
    def to_tokens(jj,cc,k): return dot(dq[:,position(jj,cc,k)],w[...],0,1)
    def for_sibling(t,k):
        jj=1-j if t==0 else j
        tgf[jj,chunk(k),:]=to_tokens(jj,1-c,k).astype(bf)
        net.send(tgf.at[jj,chunk(k)],tgr.at[jj,chunk(k)],ts.at[t,k],tr.at[t,k],sib)
    def split(x,n): return x.reshape(Z,2,2,2,16,n)
    def core_sum(v,lo,n):
        x=dot(dq[lo:lo+n,:],tok[...],1,0).T.astype(bf)
        x=split(x,n)
        s0[:,:,:,:,lo:lo+n]=jnp.where(c==0,x[:,:,:,1],x[:,:,:,0])
        net.send(s0.at[:,:,:,:,lo:lo+n],r0.at[:,:,:,:,lo:lo+n],cs.at[v],cr.at[v],sib)
        mine=jnp.where(c==0,x[:,:,:,0],x[:,:,:,1])
        for t in range(lo//W,(lo+n)//W):
            part=mine[:,:,:,:,t*W-lo:(t+1)*W-lo]
            @pl.when(c==0)
            def _(): g0[:,:,:,:,2*t*W:(2*t+1)*W]=part
            @pl.when(c==1)
            def _(): g0[:,:,:,:,(2*t+1)*W:(2*t+2)*W]=part
    def core_get(v,lo,n):
        landed(r0.at[:,:,:,:,lo:lo+n],cr.at[v])
        for t in range(lo//W,(lo+n)//W):
            part=r0[:,:,:,:,t*W:(t+1)*W]
            @pl.when(c==0)
            def _(): g0[:,:,:,:,(2*t+1)*W:(2*t+2)*W]=part
            @pl.when(c==1)
            def _(): g0[:,:,:,:,2*t*W:(2*t+1)*W]=part
    cut=[pl.ds(2*t*W,2*W) for t in range(3)]
    def to_y(v):
        s1[:,:,:,cut[v]]=jnp.where(y==0,g0[:,1,:,:,cut[v]],g0[:,0,:,:,cut[v]])
        net.send(s1.at[:,:,:,cut[v]],r1b.at[:,:,:,cut[v]],ys.at[v],yr.at[v],yd)
    def to_z(v):
        landed(r1b.at[:,:,:,cut[v]],yr.at[v])
        for k in range(1,Z):
            o=lax.rem(z+k,Z)
            su[k,:,:,cut[v]]=(g0[o,y,:,:,cut[v]].astype(f32)+r1b[o,:,:,cut[v]].astype(f32)).astype(bf)
            net.send(su.at[k,:,:,cut[v]],ru.at[k,:,:,cut[v]],us.at[v,k],ur.at[v,k],net.at(z=o))
    def to_x(v):
        sum_=g0[z,y,:,:,cut[v]].astype(f32)+r1b[z,:,:,cut[v]].astype(f32)
        for k in range(1,Z):
            landed(ru.at[k,:,:,cut[v]],ur.at[v,k])
            sum_=sum_+ru[k,:,:,cut[v]].astype(f32)
        fin[:,:,cut[v]]=sum_
        sx[:,cut[v]]=jnp.where(j==0,sum_[1],sum_[0]).astype(bf)
        net.send(sx.at[:,cut[v]],rx.at[:,cut[v]],fs.at[v],fr.at[v],xd)
    def total(jj,k): return (own[jj,chunk(k),:]+tgr[jj,chunk(k),:].astype(f32)+r1[jj,chunk(k),:].astype(f32)).astype(bf)
    def far(k):
        landed(tgr.at[1-j,chunk(k)],tr.at[0,k])
        tgs[chunk(k),:]=total(1-j,k)
        net.send(tgs.at[chunk(k)],ob.at[j,chunk(k)],xs.at[k],xr.at[k],xd)
    for k in range(NCH):
        for x in need(1-c,k): x.wait()
        place(1-j,1-c,k)
        if k==0:
            loads[0].wait()
            net.wait()
        for_sibling(0,k)
        for x in need(c,k): x.wait()
        place(1-j,c,k)
        own[1-j,chunk(k),:]=to_tokens(1-j,c,k)
        if k==0: loads[1].wait()
        else: far(k-1)
    for x in loads[2:]: x.wait()
    core_sum(0,0,W)
    far(NCH-1)
    for cc in (1-c,c):
        for k in range(NCH): place(j,cc,k)
    core_get(0,0,W)
    to_y(0)
    core_sum(1,W,W)
    core_sum(2,2*W,W)
    core_get(1,W,W)
    to_y(1)
    early=parts[0].astype(f32)
    for k in range(1,2*Z): early=early+parts[k].astype(f32)
    early=early.reshape(2,2,16,C1)
    early0=jnp.where(c==0,early[:,0],early[:,1])
    se[...]=jnp.where(c==0,early[:,1],early[:,0]).astype(bf)
    net.send(se,re,cs.at[3],cr.at[3],sib)
    core_get(2,2*W,W)
    to_y(2)
    to_z(0)
    for k in range(NCH): for_sibling(1,k)
    to_z(1)
    landed(re,cr.at[3])
    early0=early0+re[...].astype(f32)
    early1=jnp.where(j==0,early0[0],early0[1])
    sxe[...]=jnp.where(j==0,early0[1],early0[0]).astype(bf)
    net.send(sxe,rxe,fs.at[3],fr.at[3],xd)
    to_x(0)
    for k in range(NCH): own[j,chunk(k),:]=to_tokens(j,c,k)
    to_z(2)
    to_x(1)
    for k in range(NCH):
        landed(tgr.at[j,chunk(k)],tr.at[1,k])
        ob[j,chunk(k),:]=total(j,k)
    near=pltpu.make_async_copy(ob.at[j],tok_out.at[j],osem.at[0]); near.start()
    to_x(2)
    landed(rxe,fr.at[3])
    grad_out[:,6*W:]=early1+rxe[...].astype(f32)
    for v in range(3):
        landed(rx.at[:,cut[v]],fr.at[v])
        grad_out[:,cut[v]]=jnp.where(j==0,fin[0,:,cut[v]],fin[1,:,cut[v]])+rx[:,cut[v]].astype(f32)
    last=[pltpu.make_async_copy(ob.at[1-j,chunk(k)],tok_out.at[1-j,chunk(k)],osem.at[1+k]) for k in range(NCH)]
    for k in range(NCH):
        landed(ob.at[1-j,chunk(k)],xr.at[k])
        last[k].start()
    net.drain()
    near.wait()
    for x in last: x.wait()

def reduce(base,meta,dq,dkvw,tok,w,r1,parts,Z,W):
    _,block,E=r1.shape; L=4*block; C1=parts.shape[2]; C=6*W
    rows=256; NCH=block//rows
    V=pl.BlockSpec(memory_space=pltpu.VMEM); A=pl.BlockSpec(memory_space=pl.ANY)
    S=jax.ShapeDtypeStruct; M=pltpu.VMEM; D=pltpu.SemaphoreType.DMA
    return pl.pallas_call(functools.partial(reduce_kernel,Z,block,E,W,C1,rows),
        out_shape=[S((2,block,E),bf),S((16,C+C1),f32)],
        in_specs=[pl.BlockSpec(memory_space=pltpu.SMEM),V,A,A,A,A,A,A],out_specs=[A,V],
        scratch_shapes=[M(dq.shape,bf),M(dkvw.shape,bf),M(tok.shape,bf),M(w.shape,bf),M(r1.shape,bf),M(parts.shape,bf),M((2,block,E),f32),M((2,block,E),bf),M((2,block,E),bf),M((block,E),bf),M((2,block,E),bf),
            M((Z,2,2,16,3*W),bf),M((Z,2,2,16,3*W),bf),M((Z,2,2,16,C),bf),M((Z,2,16,C),bf),M((Z,2,16,C),bf),
            M((Z,2,16,C),bf),M((Z,2,16,C),bf),M((2,16,C),f32),M((16,C),bf),M((16,C),bf),M((2,16,C1),bf),M((2,16,C1),bf),M((16,C1),bf),M((16,C1),bf),
            D((6,)),D((2,2,NCH)),D((1+NCH,)),D((2,NCH)),D((2,NCH)),D((NCH,)),D((NCH,)),D((4,)),D((4,)),D((3,)),D((3,)),D((3,Z)),D((3,Z)),D((4,)),D((4,))],
        compiler_params=pltpu.CompilerParams(collective_id=1,has_side_effects=True,vmem_limit_bytes=VMEM))(base,meta,dq,dkvw,tok,w,r1,parts)

def finish_kernel(W,E,F,near,far,tg_hbm,grads_hbm,lay_out,tg_out,gq,go,gu,gd,gg,gs,lay,tg,grads,small,isem,osem):
    j=lax.axis_index("blk")//2; block=near.shape[0]; n=4; rows=block//n
    gcopy=pltpu.make_async_copy(grads_hbm,grads,isem.at[4*n]); gcopy.start()
    come=[];leave=[]
    for k in range(n):
        r=pl.ds(k*rows,rows)
        for a,b,o in ((near.at[r],lay.at[j,r],lay_out.at[j,r]),(far.at[r],lay.at[1-j,r],lay_out.at[1-j,r]),(tg_hbm.at[0,r],tg.at[0,r],tg_out.at[0,r]),(tg_hbm.at[1,r],tg.at[1,r],tg_out.at[1,r])):
            at=len(come)
            come.append(pltpu.make_async_copy(a,b,isem.at[at])); leave.append(pltpu.make_async_copy(b,o,osem.at[at]))
    for x in come: x.start()
    gcopy.wait()
    at=0
    for k,ref in enumerate((gq,go,gu,gd)):
        width=ref.shape[1]
        leave.append(pltpu.make_async_copy(grads.at[:,at:at+width],ref,osem.at[4*n+k]))
        at+=width
        leave[-1].start()
    t=grads[:,at:].T
    small[0]=t[0:2,:]; small[1]=t[2:4,:]
    for k,ref in enumerate((gg,gs)):
        leave.append(pltpu.make_async_copy(small.at[k],ref,osem.at[4*n+4+k]))
        leave[-1].start()
    for x,o in zip(come,leave):
        x.wait(); o.start()
    for o in leave: o.wait()

def finish(near,far,tg,grads,W,F):
    _,block,E=tg.shape
    A=pl.BlockSpec(memory_space=pl.ANY); S=jax.ShapeDtypeStruct; M=pltpu.VMEM; D=pltpu.SemaphoreType.DMA
    return pl.pallas_call(functools.partial(finish_kernel,W,E,F),
        out_shape=[S(tg.shape,bf),S(tg.shape,bf),S((16,6*W),f32),S((16,E),f32),S((16,F),f32),S((16,E),f32),S((2,16),f32),S((2,16),f32)],
        in_specs=[A]*4,out_specs=[A]*8,scratch_shapes=[M(tg.shape,bf),M(tg.shape,bf),M(grads.shape,f32),M((2,2,16),f32),D((17,)),D((22,))],
        compiler_params=pltpu.CompilerParams(vmem_limit_bytes=VMEM))(near,far,tg,grads)
def shards(tokens,cotangent,segments,padding,known,w_qkv,w_out,w_up,w_down,norm_gains,norm_shifts):
    micro,rows,block,D=tokens.shape
    J=lax.axis_size("blk")//2; dps=lax.axis_size("dp")
    units=micro*rows
    assert units==J
    H=HEADS//2; W=H*HEAD; L=2*J*block; F=w_up.shape[1]
    quick=J==2 and dps%2==0 and w_qkv.shape[0]==16 and block%256==0
    me=lax.axis_index("blk"); chip=me//2; core=me%2
    flat=lambda x:x.reshape((units,)+x.shape[2:])
    if quick:
        Z=dps//2
        cot=flat(cotangent)
        tok,bund,w_mine,qkvt,base,win,codet,meta,far=gather(flat(tokens),cot,*[flat(x)[:,None,:] for x in (segments,padding,known)],w_qkv,w_out,w_up,w_down,norm_gains,norm_shifts,Z,W)
        bunds=[bund]+[lax.ppermute(bund,"dp",[(d,(d//2+k)%Z*2+d%2) for d in range(dps)]) for k in range(1,Z)]
        across=[(b,b^2) for b in range(4)]
        cotx=lax.ppermute(far,"blk",across)
        p,att,ot,inv,kct,vct=attend(base,win,qkvt,codet,meta,H)
        near,far,r1,datt,parts=middle_net(att.reshape(H//2,2,2,block,128),tok,cot,cotx,bunds,Z,W,F)
        parts=lax.all_to_all(parts,"dp",0,0,tiled=True)
        layx=lax.ppermute(far,"blk",across)
        dq,dkvw=back(base,win,datt,p,ot,inv,kct,vct,qkvt,H)
        tg,grads=reduce(base,meta,dq,dkvw,tok.reshape(L,D),w_mine,r1,parts,Z,W)
        out=finish(near,layx,tg,grads,W,F)
        return (out[0].reshape(tokens.shape),out[1].reshape(tokens.shape))+tuple(out[2:])
    def to_chip(s): return [(2*a+c,2*((a+s)%J)+c) for a in range(J) for c in range(2)]
    swap=[(b,b^1) for b in range(2*J)]
    def other(x): return lax.ppermute(x,"blk",swap)
    def scatter_units(x):
        got=[]
        for s in range(J):
            mine=lax.dynamic_index_in_dim(x,(chip+s)%J,0,keepdims=False)
            got.append(mine if s==0 else lax.ppermute(mine,"blk",to_chip(s)))
        return jnp.stack([lax.dynamic_index_in_dim(jnp.stack(got),(chip-j)%J,0,keepdims=False) for j in range(J)])
    def both(mine,his):
        return jnp.stack([jnp.where(core==0,mine,his),jnp.where(core==0,his,mine)],1)
    def part(x,axis,index): return lax.dynamic_index_in_dim(x,index,axis,keepdims=False)
    own_info=scatter_units(flat(segments*4+padding*2+known)); info=both(own_info,other(own_info)).reshape(1,L)
    own_tok=scatter_units(flat(tokens)); all_tok=both(own_tok,other(own_tok)).reshape(L,D)
    own_cot=scatter_units(flat(cotangent)).reshape(L//2,D)
    full_qkv,full_out,full_up,full_down=[lax.all_gather(w,("dp","blk"),axis=0,tiled=True) for w in (w_qkv,w_out,w_up,w_down)]
    gs=lax.all_gather(jnp.concatenate([norm_gains,norm_shifts],0),("dp","blk"),axis=1,tiled=True).astype(f32)
    gs=jnp.concatenate([gs,jnp.zeros_like(gs)],0)
    w_mine=part(full_qkv.reshape(D,3,2,W),2,core).reshape(D,3*W)
    scale=jnp.where(jnp.arange(3*W)<W,math.log2(math.e)/8,1.0).astype(f32)
    qkvt=(jnp.einsum("ld,de->el",all_tok,w_mine,preferred_element_type=f32)*scale[:,None]).astype(bf)
    base,win,codet,meta=flags(info)
    p,att,ot,inv,kct,vct=attend(base,win,qkvt,codet,meta,H)
    att=att.reshape(H//2,J,2,block,128)
    mine=part(att,2,core).reshape(H//2,J*block,128); his=other(part(att,2,1-core)).reshape(H//2,J*block,128)
    a0=jnp.where(core==0,mine,his); a1=jnp.where(core==0,his,mine)
    out,r1,da,go,gu,gd,gg=middle(a0,a1,own_tok.reshape(L//2,D),own_cot,full_out,full_up,full_down,gs)
    da=da.reshape(2,H//2,J,block,128)
    dmine=part(da,0,core); dhis=other(part(da,0,1-core))
    datt=jnp.stack([jnp.where(core==0,dmine,dhis),jnp.where(core==0,dhis,dmine)],2).reshape(H//2,L,128).transpose(0,2,1).reshape(W,L)
    dq,dkvw=back(base,win,datt,p,ot,inv,kct,vct,qkvt,H)
    tg,gq=place_all(base,meta,dq,dkvw,all_tok,w_mine,H)
    tg=tg.reshape(J,2,block,D)
    layer_out=scatter_units(out.reshape(J,block,D)).reshape(tokens.shape)
    own_tg=(part(tg,1,core).astype(f32)+other(part(tg,1,1-core)).astype(f32)+r1.reshape(J,block,D)).astype(bf)
    token_grad=scatter_units(own_tg).reshape(tokens.shape)
    gq=gq.astype(f32).reshape(D,3,1,W)
    gq=jnp.where(core==0,jnp.concatenate([gq,jnp.zeros_like(gq)],2),jnp.concatenate([jnp.zeros_like(gq),gq],2)).reshape(D,6*W)
    grads=lax.psum_scatter(jnp.concatenate([gq,go,gu,gd],1),("dp","blk"),scatter_dimension=0,tiled=True)
    gg=lax.psum_scatter(gg[:4],("dp","blk"),scatter_dimension=1,tiled=True)
    a,b,e=6*W,6*W+D,6*W+D+F
    return (layer_out,token_grad,grads[:,:a],grads[:,a:b],grads[:,b:e],grads[:,e:],gg[:2],gg[2:])

def solution(mesh):
    in_specs = (
        P(None, "dp", "blk", None),
        P(None, "dp", "blk", None),
        P(None, "dp", "blk"),
        P(None, "dp", "blk"),
        P(None, "dp", "blk"),
        P(("dp", "blk"), None),
        P(("dp", "blk"), None),
        P(("dp", "blk"), None),
        P(("dp", "blk"), None),
        P(None, ("dp", "blk")),
        P(None, ("dp", "blk")),
    )
    out_specs = (
        P(None, "dp", "blk", None),
        P(None, "dp", "blk", None),
        P(("dp", "blk"), None),
        P(("dp", "blk"), None),
        P(("dp", "blk"), None),
        P(("dp", "blk"), None),
        P(None, ("dp", "blk")),
        P(None, ("dp", "blk")),
    )
    return jax.shard_map(shards, mesh=mesh, in_specs=in_specs, out_specs=out_specs, check_vma=False)
```

```python
import functools, math
import jax, jax.numpy as jnp
from jax import lax
from jax.experimental import pallas as pl
from jax.experimental.pallas import tpu as pltpu
from jax.sharding import PartitionSpec as P

HEADS = 8
bf=jnp.bfloat16; f32=jnp.float32
HEAD=64
QB=512
KB=512
SRC=768
SAFE=60.0
RATE=math.log2(math.e)*HEAD**-0.5
CODE=16
VMEM=(64<<20)-(128<<10)
SLOTS=3
def dot(a,b,ca,cb): return lax.dot_general(a,b,(((ca,),(cb,)),((),())),preferred_element_type=f32)
def al(x,n): return pl.multiple_of(x,n)
def iota(shape,axis): return lax.broadcasted_iota(jnp.int32,shape,axis)

def begin(base_ref,b):
    return base_ref[b,0]

def window(win_ref,i):
    start=win_ref[i,0]//128*128
    groups=(win_ref[8+i,0]-start+127)//128
    full=(groups-1)//(KB//128)
    return start,full,groups-full*(KB//128),groups

def by_piece(first,full,rest,g,fn):
    def body(j,g):
        fn(al(first+j*KB,128),KB,g)
        return g+1
    g=lax.fori_loop(0,full,body,g)
    for r in range(1,KB//128+1):
        @pl.when(rest==r)
        def _(): fn(al(first+full*KB,128),r*128,g)
    return g+1

def attend_kernel(L,H,base_ref,win_ref,qkvt_hbm,codet_ref,meta_ref,p_hbm,att_hbm,ot_hbm,inv_ref,kct_hbm,vct_hbm,
                  kaug_ref,kct_ref,kvt,q_ref,v_ref,vct,acc,pbuf,obuf,abuf,top_ref,psem,osem,asem,ksem,lsem):
    W=H*HEAD; nq=L//QB
    total=begin(base_ref,L//256)
    come=[pltpu.make_async_copy(qkvt_hbm.at[W+h*HEAD:W+(h+1)*HEAD],kvt.at[h*128:h*128+HEAD],lsem.at[h]) for h in range(H)]
    come+=[pltpu.make_async_copy(qkvt_hbm.at[2*W:],v_ref,lsem.at[H]),pltpu.make_async_copy(qkvt_hbm.at[:W],q_ref,lsem.at[H+1])]
    for x in come: x.start()
    for h in range(H):
        kvt[h*128+HEAD:h*128+HEAD+CODE,:]=codet_ref[...]
        kvt[h*128+HEAD+CODE:(h+1)*128,:]=jnp.zeros((HEAD-CODE,L),bf)
    vct[:,HEAD:,:]=jnp.ones((H,16,L),bf)
    for x in come[:H+1]: x.wait()
    row=iota((256,256),0)
    down=iota((256,SRC),0)
    def dest(d,c):
        first=jnp.minimum(win_ref[16+d,0]//128*128,L-SRC)
        last=win_ref[17+d,0]
        def src(t,a):
            ssl=pl.ds(al(jnp.minimum(first+t*SRC,L-SRC),128),SRC)
            oh=((meta_ref[0:1,ssl]==down+d*256)&(lane>=first+t*SRC-jnp.minimum(first+t*SRC,L-SRC))).astype(f32).astype(bf)
            return a[0]+dot(kvt[:,ssl],oh,1,1),a[1]+dot(v_ref[:,ssl],oh,1,1)
        lane=iota((256,SRC),1)
        ka,va=src(0,(jnp.zeros((H*128,256),f32),jnp.zeros((W,256),f32)))
        ka,va=lax.fori_loop(1,(last-first+SRC-1)//SRC,src,(ka,va))
        dsl=pl.ds(al(d*256,256),256)
        for h in range(H):
            k1=jnp.where(row[:128]==HEAD+10,-10240.0,ka[h*128:(h+1)*128])
            kaug_ref[h,dsl,:]=k1.astype(bf).T
            kct_ref[h,:,dsl]=k1[:HEAD].astype(bf)
            vct[h,:HEAD,dsl]=va[h*HEAD:(h+1)*HEAD].astype(bf)
        return c
    lax.fori_loop(0,(total+255)//256,dest,0)
    keep=[pltpu.make_async_copy(kct_ref,kct_hbm,ksem.at[0]),pltpu.make_async_copy(vct,vct_hbm,ksem.at[1])]
    for x in keep: x.start()
    come[H+1].wait()
    bound=jnp.float32(0)
    for h in range(H):
        q=q_ref[h*HEAD:(h+1)*HEAD,:].astype(f32); k=kvt[h*128:h*128+HEAD,:].astype(f32)
        bound=jnp.maximum(bound,jnp.max(jnp.sum(q*q,0,keepdims=True))*jnp.max(jnp.sum(k*k,0,keepdims=True)))
    safe=bound*(RATE*RATE)<SAFE*SAFE

    def pcopy(g):
        slot=lax.rem(g,SLOTS)
        return pltpu.make_async_copy(pbuf.at[slot],p_hbm.at[g],psem.at[slot])
    def ocopy(i):
        slot=lax.rem(i,2)
        return pltpu.make_async_copy(obuf.at[slot],ot_hbm.at[i],osem.at[slot])
    def acopy(i):
        slot=lax.rem(i,2)
        return pltpu.make_async_copy(abuf.at[slot],att_hbm.at[:,pl.ds(al(i*QB,QB),QB),:],asem.at[slot])
    def block(i,g):
        slot=lax.rem(i,2)
        qsl=pl.ds(al(i*QB,QB),QB)
        first,full,rest,groups=window(win_ref,i)
        qa=[jnp.concatenate([q_ref[h*HEAD:(h+1)*HEAD,qsl],codet_ref[:,qsl],jnp.zeros((HEAD-CODE,QB),bf)],0) for h in range(H)]
        own=meta_ref[1:2,qsl]>0
        sself=[]
        for h in range(H):
            x=q_ref[h*HEAD:(h+1)*HEAD,qsl].astype(f32)*kvt[h*128:h*128+HEAD,qsl].astype(f32)
            sself.append(jnp.where(own,jnp.sum(x,0,keepdims=True),-1e30))
        acc[...]=jnp.zeros_like(acc)
        top_ref[...]=jnp.zeros_like(top_ref)
        row=iota((128,QB),0)
        def strict(h,osl):
            k=kaug_ref[h,osl,:]
            x=qa[h].astype(f32)
            plain=dot(k,jnp.where(row<HEAD,x,0.0).astype(bf),1,0)
            return jnp.where(dot(k,jnp.where(row<HEAD,0.0,x).astype(bf),1,0)>-1.0,plain,-1e30)
        @pl.when(jnp.logical_not(safe))
        def _():
            for h in range(H):
                def more(j,m): return jnp.maximum(m,jnp.max(strict(h,pl.ds(al(first+j*128,128),128)),0,keepdims=True))
                top_ref[h:h+1,:]=lax.fori_loop(0,groups,more,sself[h])
        def piece(off,size,g):
            ps=lax.rem(g,SLOTS)
            osl=pl.ds(off,size)
            @pl.when(g>=SLOTS)
            def _(): pcopy(g-SLOTS).wait()
            @pl.when(safe)
            def _():
                keepp=[]
                for h in range(H):
                    p=jnp.exp2(RATE*dot(kaug_ref[h,osl,:],qa[h],1,0)).astype(bf)
                    pbuf[ps,h,:,:size]=p.T
                    keepp.append(p)
                for h in range(H): acc[h]+=dot(vct[h,:,osl],keepp[h],1,0)
            @pl.when(jnp.logical_not(safe))
            def _():
                for h in range(H):
                    def put(j,c):
                        jsl=pl.ds(al(off+j*128,128),128)
                        p=jnp.exp2(RATE*(strict(h,jsl)-top_ref[h:h+1,:])).astype(bf)
                        pbuf[ps,h,:,pl.ds(al(j*128,128),128)]=p.T
                        acc[h]+=dot(vct[h,:,jsl],p,1,0)
                        return c
                    lax.fori_loop(0,size//128,put,0)
            pcopy(g).start()
        g=by_piece(first,full,rest,g,piece)
        @pl.when(i>=2)
        def _(): ocopy(i-2).wait(); acopy(i-2).wait()
        for h in range(H):
            ps=jnp.exp2(RATE*(sself[h]-top_ref[h:h+1,:]))
            inv=1.0/(acc[h,HEAD:HEAD+1,:]+ps)
            obuf[slot,h*HEAD:(h+1)*HEAD,:]=(acc[h,:HEAD,:]+ps*v_ref[h*HEAD:(h+1)*HEAD,qsl].astype(f32))*inv
            inv_ref[h,0:1,qsl]=inv
            inv_ref[h,1:2,qsl]=ps
        for hp in range(H//2): abuf[slot,hp]=obuf[slot,hp*128:(hp+1)*128,:].astype(bf).T
        ocopy(i).start(); acopy(i).start()
        return g
    g=lax.fori_loop(0,nq,block,0)
    for s in range(SLOTS):
        last=g-1-s
        @pl.when(last>=0)
        def _(): pcopy(last).wait()
    for i in range(max(nq-2,0),nq): ocopy(i).wait(); acopy(i).wait()
    for x in keep: x.wait()

def attend(base,win,qkvt,codet,meta,H):
    L=qkvt.shape[1]; W=H*HEAD; nq=L//QB; cap=nq*(L//KB+1)
    V=pl.BlockSpec(memory_space=pltpu.VMEM); A=pl.BlockSpec(memory_space=pl.ANY)
    S=jax.ShapeDtypeStruct; M=pltpu.VMEM; D=pltpu.SemaphoreType.DMA
    return pl.pallas_call(functools.partial(attend_kernel,L,H),
        out_shape=[S((cap,H,QB,KB),bf),S((H//2,L,128),bf),S((nq,W,QB),f32),S((H,8,L),f32),S((H,HEAD,L),bf),S((H,HEAD+16,L),bf)],
        in_specs=[pl.BlockSpec(memory_space=pltpu.SMEM)]*2+[A,V,V],
        out_specs=[A,A,A,V,A,A],
        scratch_shapes=[M((H,L,128),bf),M((H,HEAD,L),bf),M((H*128,L),bf),M((W,L),bf),M((W,L),bf),M((H,HEAD+16,L),bf),M((H,HEAD+16,QB),f32),M((SLOTS,H,QB,KB),bf),
            M((2,W,QB),f32),M((2,H//2,QB,128),bf),M((8,QB),f32),D((SLOTS,)),D((2,)),D((2,)),D((2,)),D((H+2,))],
        compiler_params=pltpu.CompilerParams(vmem_limit_bytes=VMEM))(base,win,qkvt,codet,meta)

def flags(row):
    L=row.shape[1]; nb=L//256; nq=L//QB
    seg=row//4
    pad=row//2-2*seg
    known=row-2*(row//2)
    use=(pad==0)&(known==1)
    usef=use.astype(f32)
    x=jnp.concatenate([usef[:,b*256:(b+1)*256] for b in range(nb)]+[jnp.zeros((16-nb,256),f32)],0)
    incl=dot(x.astype(bf),(iota((256,256),0)<=iota((256,256),1)).astype(f32).astype(bf),1,0)
    tot=jnp.broadcast_to(incl[:,255:256],(16,256)).astype(bf)
    base=dot((iota((16,16),0)>iota((16,16),1)).astype(f32).astype(bf),tot,1,0)
    mid=seg[:,L//2:L//2+1]
    late=(seg>=mid).astype(f32)
    early=jnp.sum(usef*(1.0-late),1,keepdims=True)
    shift=jnp.ceil(early*(1.0/128.0))*128.0-early
    shift=jnp.where(jnp.sum(usef,1,keepdims=True)+shift<=L,shift,0.0)
    csum=jnp.concatenate([(incl+base)[b:b+1] for b in range(nb)],1)+late*shift
    rank=jnp.where(use,csum.astype(jnp.int32)-1,-1)
    base=base+shift*jnp.concatenate([late[:,b*256:b*256+1] for b in range(nb)]+[jnp.ones((16-nb,1),f32)],0)
    own=((pad==0)&(known!=1)).astype(jnp.int32)
    bits=iota((CODE,L),0)
    bit=lax.shift_right_logical(jnp.broadcast_to(seg,(CODE,L)),jnp.minimum(bits,9))&1
    codet=jnp.where(bits<10,jnp.where(bit==1,32.0,-32.0),jnp.where(bits==10,1.0,0.0)).astype(bf)
    meta=jnp.concatenate([rank,own,jnp.zeros((6,L),jnp.int32)],0)
    def edge(at): return jnp.concatenate([seg[:,i*QB+at:i*QB+at+1] for i in range(nq)]+[jnp.zeros((8-nq,1),jnp.int32)],0)
    low=jnp.sum(jnp.where(seg<edge(0),usef,0.0),1,keepdims=True)+shift*(edge(0)>=mid).astype(f32)
    high=jnp.sum(jnp.where(seg<=edge(QB-1),usef,0.0),1,keepdims=True)+shift*(edge(QB-1)>=mid).astype(f32)
    starts=jnp.sum((csum<=(256*iota((16,1),0)).astype(f32)).astype(f32),1,keepdims=True)
    win=jnp.broadcast_to(jnp.concatenate([low,high,starts],0),(32,128)).astype(jnp.int32)
    return base[:,:128].astype(jnp.int32),win,codet,meta
SPAN=512
def back_kernel(L,H,base_ref,win_ref,datt_hbm,p_hbm,ot_hbm,inv_ref,kct_hbm,vct_hbm,qkvt_hbm,dq_hbm,dkvw_hbm,
                kct,vct,dkv,dkvt,pbuf,qacc,qkv,datt,ot,dq,psem,lsem,qsem,osem,tsem):
    W=H*HEAD; nq=L//QB
    groups=(begin(base_ref,L//256)+127)//128
    pieces=lax.fori_loop(0,nq,lambda i,s:s+window(win_ref,i)[1]+1,0)
    def pcopy(g):
        slot=lax.rem(g,SLOTS)
        return pltpu.make_async_copy(p_hbm.at[g],pbuf.at[slot],psem.at[slot])
    def keys(t):
        rows=pl.ds(al(t*KB,KB),KB)
        return [pltpu.make_async_copy(vct_hbm.at[:,:,rows],vct.at[:,:,rows],lsem.at[0,t]),pltpu.make_async_copy(kct_hbm.at[:,:,rows],kct.at[:,:,rows],lsem.at[1,t])]
    def queries(i):
        slot=lax.rem(i,2); qsl=pl.ds(al(i*QB,QB),QB)
        return [pltpu.make_async_copy(a,b.at[slot],qsem.at[k,slot]) for k,(a,b) in enumerate(((qkvt_hbm.at[:,qsl],qkv),(datt_hbm.at[:,qsl],datt),(ot_hbm.at[i],ot)))]
    def each_key(fn,least=0):
        def body(t,c):
            for x in keys(t): fn(x)
            return c
        lax.fori_loop(least,(groups+KB//128-1)//(KB//128),body,0)
    for x in queries(0): x.start()
    each_key(lambda x:x.start())
    for s in range(SLOTS-1):
        @pl.when(s<pieces)
        def _(): pcopy(s).start()
    def clear(j,c):
        dkv[:,pl.ds(al(j*128,128),128)]=jnp.zeros((2*W,128),f32)
        return c
    lax.fori_loop(0,groups,clear,0)
    def ocopy(i):
        slot=lax.rem(i,2)
        return pltpu.make_async_copy(dq.at[slot],dq_hbm.at[:,pl.ds(al(i*QB,QB),QB)],osem.at[slot])
    def block(i,g):
        slot=lax.rem(i,2)
        qsl=pl.ds(al(i*QB,QB),QB)
        first,full,rest,_=window(win_ref,i)
        for x in queries(i): x.wait()
        @pl.when(i+1<nq)
        def _():
            for x in queries(i+1): x.start()
        dt=datt[slot].astype(f32)
        prod=dt*ot[slot]
        daug=[];lows=[];deltas=[];d1s=[]
        row=iota((16,QB),0)
        for h in range(H):
            hsl=slice(h*HEAD,(h+1)*HEAD)
            inv=inv_ref[h,0:1,qsl]
            delta=jnp.sum(prod[hsl],0,keepdims=True)*inv
            d1=dt[hsl]*inv
            low=d1.astype(bf)
            a=delta.astype(bf).astype(f32); b=(delta-a).astype(bf).astype(f32)
            extra=jnp.where(row==0,-a,jnp.where(row==1,-b,jnp.where(row==2,a+b-delta,0.0))).astype(bf)
            daug.append(jnp.concatenate([low,extra,jnp.zeros((HEAD-16,QB),bf)],0).T[:,:HEAD+16])
            lows.append(low); deltas.append(delta); d1s.append(d1)
        qacc[...]=jnp.zeros_like(qacc)
        def piece(off,size,g):
            ps=lax.rem(g,SLOTS)
            osl=pl.ds(off,size)
            @pl.when(g+SLOTS-1<pieces)
            def _(): pcopy(g+SLOTS-1).start()
            @pl.when(i==0)
            def _():
                for x in keys(g): x.wait()
            pcopy(g).wait()
            dss=[]
            for h in range(H):
                dss.append((pbuf[ps,h,:,:size].astype(f32)*dot(daug[h],vct[h,:,osl],1,0)).astype(bf))
                dkv[W+h*HEAD:W+(h+1)*HEAD,osl]+=dot(lows[h],pbuf[ps,h,:,:size],1,0)
            for h in range(H): qacc[h]+=dot(kct[h,:,osl],dss[h].T,1,0)
            for h in range(H):
                dkv[h*HEAD:(h+1)*HEAD,osl]+=dot(qkv[slot,h*HEAD:(h+1)*HEAD,:],dss[h],1,0)
        g=by_piece(first,full,rest,g,piece)
        @pl.when(i==0)
        def _(): each_key(lambda x:x.wait(),g)
        @pl.when(i>=2)
        def _(): ocopy(i-2).wait()
        for h in range(H):
            hsl=slice(h*HEAD,(h+1)*HEAD); ksl=slice(W+h*HEAD,W+(h+1)*HEAD); vsl=slice(2*W+h*HEAD,2*W+(h+1)*HEAD)
            ps=inv_ref[h,1:2,qsl]
            ds=ps*(jnp.sum(qkv[slot,vsl,:].astype(f32)*d1s[h],0,keepdims=True)-deltas[h])
            dq[slot,hsl,:]=((qacc[h]+ds*qkv[slot,ksl,:].astype(f32))*HEAD**-0.5).astype(bf)
            dq[slot,ksl,:]=(ds*qkv[slot,hsl,:].astype(f32)*HEAD**-0.5).astype(bf)
            dq[slot,vsl,:]=(ps*d1s[h]).astype(bf)
        ocopy(i).start()
        return g
    lax.fori_loop(0,nq,block,0)
    rows=iota((2*W,128),0)
    def tcopy(s): return pltpu.make_async_copy(dkvt.at[:,pl.ds(al(begin(base_ref,s)//128*128,128),SPAN)],dkvw_hbm.at[s],tsem.at[s])
    def turn(j,c):
        jsl=pl.ds(al(j*128,128),128)
        x=jnp.where(j<groups,dkv[:,jsl],0.0)
        dkvt[:,jsl]=jnp.where(rows<W,x*HEAD**-0.5,x).astype(bf)
        for s in range(L//256):
            @pl.when(begin(base_ref,s)//128+SPAN//128-1==j)
            def _(): tcopy(s).start()
        return c
    lax.fori_loop(0,groups+SPAN//128,turn,0)
    for i in range(max(nq-2,0),nq): ocopy(i).wait()
    for s in range(L//256): tcopy(s).wait()

def back(base,win,datt,p,ot,inv,kct,vct,qkvt,H):
    L=qkvt.shape[1]; W=H*HEAD
    V=pl.BlockSpec(memory_space=pltpu.VMEM); A=pl.BlockSpec(memory_space=pl.ANY); N=pl.BlockSpec(memory_space=pltpu.SMEM)
    S=jax.ShapeDtypeStruct; M=pltpu.VMEM; D=pltpu.SemaphoreType.DMA
    return pl.pallas_call(functools.partial(back_kernel,L,H),
        out_shape=[S((3*W,L),bf),S((L//256,2*W,SPAN),bf)],
        in_specs=[N,N,A,A,A,V,A,A,A],
        out_specs=[A,A],
        scratch_shapes=[M((H,HEAD,L),bf),M((H,HEAD+16,L),bf),M((2*W,L+SPAN),f32),M((2*W,L+SPAN),bf),M((SLOTS,H,QB,KB),bf),M((H,HEAD,QB),f32),
            M((2,3*W,QB),bf),M((2,W,QB),bf),M((2,W,QB),f32),M((2,3*W,QB),bf),
            D((SLOTS,)),D((2,L//KB)),D((3,2)),D((2,)),D((L//256,))],
        compiler_params=pltpu.CompilerParams(vmem_limit_bytes=VMEM))(base,win,datt,p,ot,inv,kct,vct,qkvt)

def placed(base_ref,rank_row,span,own,s):
    r0=begin(base_ref,s)//128*128
    oh=(rank_row==iota((SPAN,256),0)+r0).astype(f32).astype(bf)
    return dot(span,oh,1,0)+own.astype(f32)

def place_kernel(L,W,base_ref,meta_ref,dq_in,dkvw_ref,tok_ref,w_ref,tg_ref,grad_ref,dq_ref):
    dq_ref[...]=dq_in[...]
    def place(s,c):
        ssl=pl.ds(al(s*256,256),256)
        dq_ref[W:3*W,ssl]=placed(base_ref,meta_ref[0:1,ssl],dkvw_ref[s],dq_ref[W:3*W,ssl],s).astype(bf)
        tg_ref[ssl,:]=dot(dq_ref[:,ssl],w_ref[...],0,1).astype(bf)
        return c
    lax.fori_loop(0,L//256,place,0)
    grad_ref[...]=dot(dq_ref[...],tok_ref[...],1,0).T.astype(bf)

def place_all(base,meta,dq,dkvw,tok,w,H):
    L,E=tok.shape; W=H*HEAD
    V=pl.BlockSpec(memory_space=pltpu.VMEM); S=jax.ShapeDtypeStruct
    return pl.pallas_call(functools.partial(place_kernel,L,W),out_shape=[S((L,E),bf),S((E,3*W),bf)],
        in_specs=[pl.BlockSpec(memory_space=pltpu.SMEM)]+[V]*5,out_specs=[V,V],scratch_shapes=[pltpu.VMEM((3*W,L),bf)],
        compiler_params=pltpu.CompilerParams(vmem_limit_bytes=VMEM))(base,meta,dq,dkvw,tok,w)
EPSILON=1e-05
def gelu_parts(h):
    bell=jnp.exp(-0.5*h*h)
    t=1.0/(1.0+(0.3275911*math.sqrt(0.5))*jnp.abs(h))
    tail=0.5*1.061405429
    for c in (-1.453152027,1.421413741,-0.284496736,0.254829592): tail=tail*t+0.5*c
    tail=tail*t*bell
    cdf=jnp.where(h<0.0,tail,1.0-tail)
    return cdf,cdf+h*bell*(1.0/math.sqrt(2.0*math.pi))
def norm(x):
    center=x-jnp.mean(x,-1,keepdims=True)
    inverse=lax.rsqrt(jnp.mean(center*center,-1,keepdims=True)+EPSILON)
    return center*inverse,inverse
def norm_back(e,n,inverse):
    return inverse*(e-jnp.mean(e,-1,keepdims=True)-n*jnp.mean(e*n,-1,keepdims=True))
def middle_kernel(a0_ref,a1_ref,tok_ref,cot_ref,wo_ref,wu_ref,wd_ref,gs_ref,out_ref,r1_ref,da_ref,go_ref,gu_ref,gd_ref,gg_ref):
    @pl.when(pl.program_id(0)==0)
    def _():
        for r in (go_ref,gu_ref,gd_ref,gg_ref): r[...]=jnp.zeros_like(r)
    P2=a0_ref.shape[0]
    att=jnp.concatenate([a0_ref[p] for p in range(P2)]+[a1_ref[p] for p in range(P2)],1)
    g0,g1,b0,b1=[gs_ref[r:r+1,:] for r in range(4)]
    n1,inv1=norm(tok_ref[...].astype(f32)+dot(att,wo_ref[...],1,0))
    first=(n1*g0+b0).astype(bf)
    hidden=dot(first,wu_ref[...],1,0)
    cdf,slope=gelu_parts(hidden)
    act=(hidden*cdf).astype(bf)
    n2,inv2=norm(first.astype(f32)+dot(act,wd_ref[...],1,0))
    out_ref[...]=(n2*g1+b1).astype(bf)
    cot=cot_ref[...].astype(f32)
    r2=norm_back(cot*g1,n2,inv2)
    feed=r2.astype(bf)
    gd_ref[...]+=dot(act,feed,0,0)
    dh=(dot(feed,wd_ref[...],1,1)*slope).astype(bf)
    gu_ref[...]+=dot(first,dh,0,0)
    df=r2+dot(dh,wu_ref[...],1,1)
    r1=norm_back(df*g0,n1,inv1)
    r1_ref[...]=r1
    db=r1.astype(bf)
    go_ref[...]+=dot(att,db,0,0)
    da=dot(db,wo_ref[...],1,1).astype(bf)
    for p in range(2*P2): da_ref[p]=da[:,p*128:(p+1)*128]
    gg_ref[0:1,:]+=jnp.sum(df*n1,0,keepdims=True)
    gg_ref[1:2,:]+=jnp.sum(cot*n2,0,keepdims=True)
    gg_ref[2:3,:]+=jnp.sum(df,0,keepdims=True)
    gg_ref[3:4,:]+=jnp.sum(cot,0,keepdims=True)

def middle(a0,a1,tok,cot,wo,wu,wd,gs):
    P2,N,_=a0.shape; D=tok.shape[1]; F=wu.shape[1]
    T=max(t for t in (256,192,128,64,32,16) if N%t==0)
    tile=pl.BlockSpec((T,D),lambda i:(i,0))
    def pairs(k): return pl.BlockSpec((k,T,128),lambda i:(0,i,0))
    def whole(s): return pl.BlockSpec(s,lambda i:(0,)*len(s))
    return pl.pallas_call(middle_kernel,grid=(N//T,),
        in_specs=[pairs(P2),pairs(P2),tile,tile,whole((D,D)),whole((D,F)),whole((F,D)),whole((8,D))],
        out_specs=[tile,tile,pairs(2*P2),whole((D,D)),whole((D,F)),whole((F,D)),whole((8,D))],
        out_shape=[jax.ShapeDtypeStruct((N,D),bf),jax.ShapeDtypeStruct((N,D),f32),jax.ShapeDtypeStruct((2*P2,N,128),bf),
            jax.ShapeDtypeStruct((D,D),f32),jax.ShapeDtypeStruct((D,F),f32),jax.ShapeDtypeStruct((F,D),f32),jax.ShapeDtypeStruct((8,D),f32)],
        compiler_params=pltpu.CompilerParams(vmem_limit_bytes=60<<20))(a0,a1,tok,cot,wo,wu,wd,gs)
MESH=pl.DeviceIdType.MESH
class Net:
    def __init__(self,Z):
        dp=lax.axis_index("dp"); blk=lax.axis_index("blk")
        self.Z=Z; self.z=dp//2; self.y=dp%2; self.j=blk//2; self.c=blk%2
        self.sent=[]
    def at(self,z=None,y=None,j=None,c=None):
        z=self.z if z is None else z; y=self.y if y is None else y; j=self.j if j is None else j; c=self.c if c is None else c
        return (z*2+y,j*2+c)
    def signal(self):
        barrier=pltpu.get_barrier_semaphore()
        for d in [self.at(j=1-self.j),self.at(y=1-self.y),self.at(c=1-self.c)]+[self.at(z=lax.rem(self.z+k,self.Z)) for k in range(1,self.Z)]:
            pl.semaphore_signal(barrier,inc=1,device_id=d,device_id_type=MESH)
    def wait(self): pl.semaphore_wait(pltpu.get_barrier_semaphore(),2+self.Z)
    def greet(self):
        self.signal()
        self.wait()
    def copy(self,src,dst,ssem,rsem,device):
        return pltpu.make_async_remote_copy(src_ref=src,dst_ref=dst,send_sem=ssem,recv_sem=rsem,device_id=device,device_id_type=MESH)
    def send(self,src,dst,ssem,rsem,device,when=None):
        c=self.copy(src,dst,ssem,rsem,device)
        if when is None: c.start()
        else: pl.when(when)(c.start)
        self.sent.append((c,when))
    def drain(self):
        for c,when in self.sent:
            if when is None: c.wait_send()
            else: pl.when(when)(c.wait_send)

def gather_kernel(Z,block,E,W,rows,tok_hbm,cot_hbm,seg_ref,pad_ref,known_ref,wq_ref,wo_ref,wu_ref,wd_ref,gain_ref,shift_ref,
                  tok_out,bund_out,wmine_out,qkvt_out,base_out,win_out,code_out,meta_out,far_out,
                  tokb,farb,info_ref,infob,pack_ref,wall,bund,wt,qkvt,lsem,qsem,xs,xr,zs,zr,ys,yr,cs,cr,ts,tr,iss,isr):
    net=Net(Z); z,y,j,c=net.z,net.y,net.j,net.c
    NCH=block//rows; D=E
    sib=net.at(c=1-c); xd=net.at(j=1-j); yd=net.at(y=1-y)
    net.signal()
    mine=pltpu.make_async_copy(tok_hbm.at[j],tokb.at[j,c],lsem.at[0]); mine.start()
    far=pltpu.make_async_copy(cot_hbm.at[1-j],farb,lsem.at[3]); far.start()
    at=0
    for ref in (wq_ref,wo_ref,wu_ref,wd_ref):
        n=ref.shape[1]
        pack_ref[:,at:at+n]=ref[...]
        at+=n
    R=gain_ref.shape[1]
    place=(iota((R,128),1)==iota((R,128),0)+R*lax.rem(lax.axis_index("dp")*4+lax.axis_index("blk"),128//R)).astype(f32).astype(bf)
    pack_ref[:,at:]=jnp.concatenate([dot(gain_ref[...],place,1,0),dot(shift_ref[...],place,1,0),jnp.zeros((12,128),f32)],0).astype(bf)
    split=6*W
    wall[z,y,j,c]=pack_ref[:,:split]
    bund[y,j]=pack_ref[:,split:]
    info_ref[...]=seg_ref[...]*4+pad_ref[...]*2+known_ref[...]
    infob[j,c]=info_ref[j]
    net.wait()
    net.send(pack_ref.at[:,:split],wall.at[z,y,j,c],xs.at[0],xr.at[0],xd)
    net.send(pack_ref.at[:,split:],bund.at[y,j],xs.at[1],xr.at[1],xd)
    net.send(info_ref.at[1-j],infob.at[j,c],iss.at[0],isr.at[0],xd)
    net.send(info_ref.at[j],infob.at[j,c],iss.at[1],isr.at[1],sib)
    def chunk(k): return pl.ds(k*rows if type(k) is int else al(k*rows,rows),rows)
    for k in range(NCH):
        net.send(tok_hbm.at[1-j,chunk(k)],tokb.at[j,c,chunk(k)],ts.at[0,k],tr.at[0,k],xd)
        net.send(tok_hbm.at[j,chunk(k)],tokb.at[j,c,chunk(k)],ts.at[1,k],tr.at[1,k],sib)
    def piece(o,y_): return wall.at[o,y_,:,c]
    def landed(ref,sem): pltpu.make_async_copy(ref,ref,sem).wait()
    def pass_on(o):
        net.send(piece(o,y),piece(o,y),ys.at[o],yr.at[o],yd)
        net.send(piece(o,y),piece(o,y),cs.at[0,o],cr.at[0,o],sib)
    far.wait()
    far=pltpu.make_async_copy(farb,far_out,lsem.at[3]); far.start()
    landed(wall.at[z,y,1-j,c],xr.at[0])
    for k in range(1,Z):
        net.send(piece(z,y),piece(z,y),zs.at[k],zr.at[k],net.at(z=lax.rem(z+k,Z)))
    pass_on(z)
    landed(bund.at[y,1-j],xr.at[1])
    net.send(bund.at[y],bund.at[y],ys.at[Z],yr.at[Z],yd)
    for k in range(1,Z):
        o=lax.rem(z+Z-k,Z)
        landed(piece(o,y),zr.at[k])
        pass_on(o)
    for k in range(Z):
        o=lax.rem(z+Z-k,Z)
        landed(piece(o,1-y),yr.at[o])
        net.send(piece(o,1-y),piece(o,1-y),cs.at[1,o],cr.at[1,o],sib)
    for o in range(Z):
        for q in range(2): landed(wall.at[o,y if q==0 else 1-y,:,1-c],cr.at[q,o])
    landed(bund.at[1-y],yr.at[Z])
    outb=pltpu.make_async_copy(bund,bund_out,lsem.at[1]); outb.start()
    def qcopy(g):
        col=pl.ds(al(g*rows,rows),rows)
        return pltpu.make_async_copy(qkvt.at[:,col],qkvt_out.at[:,col],qsem.at[g])
    def project(jj,cc,come=None,onward=False):
        def body(k,carry):
            ref=tokb.at[jj,cc,chunk(k)]
            if come is not None: landed(ref,tr.at[come,k])
            if onward: net.copy(ref,ref,ts.at[2,k],tr.at[2,k],sib).start()
            g=(jj*2+cc)*NCH+k
            r=dot(wt[...],ref[...],1,1)
            qkvt[:,pl.ds(al(g*rows,rows),rows)]=r.astype(bf)
            qcopy(g).start()
            return carry
        lax.fori_loop(0,NCH,body,0)
    parts=[]
    for t in range(3):
        cols=pl.ds(al(t*2*W+c*W,W),W)
        part=wall[:,:,:,:,:,cols].reshape(D,W)
        wt[t*W:(t+1)*W,:]=part.T
        parts.append(part)
    wmine_out[...]=jnp.concatenate(parts,1)
    mine.wait()
    project(j,c)
    project(j,1-c,1)
    landed(infob.at[1-j,c],isr.at[0])
    net.send(infob.at[1-j,c],infob.at[1-j,c],iss.at[2],isr.at[2],sib)
    project(1-j,c,0,True)
    landed(infob.at[j,1-c],isr.at[1])
    landed(infob.at[1-j,1-c],isr.at[2])
    base_out[...],win_out[...],code_out[...],meta_out[...]=flags(jnp.concatenate([infob[0,0],infob[0,1],infob[1,0],infob[1,1]],1))
    project(1-j,1-c,2)
    outt=pltpu.make_async_copy(tokb,tok_out,lsem.at[2]); outt.start()
    net.drain()
    for k in range(NCH):
        ref=tokb.at[1-j,c,chunk(k)]
        net.copy(ref,ref,ts.at[2,k],tr.at[2,k],sib).wait_send()
    lax.fori_loop(0,4*NCH,lambda g,c:(qcopy(g).wait(),c)[1],0)
    outb.wait(); outt.wait(); far.wait()

def gather(tok,cot,seg,pad,known,wq,wo,wu,wd,gain,shift,Z,W):
    _,block,E=tok.shape; R=wq.shape[0]; C=6*W+wo.shape[1]+wu.shape[1]+wd.shape[1]+128
    rows=256; NCH=block//rows; L=4*block
    V=pl.BlockSpec(memory_space=pltpu.VMEM); A=pl.BlockSpec(memory_space=pl.ANY)
    S=jax.ShapeDtypeStruct; M=pltpu.VMEM; D=pltpu.SemaphoreType.DMA; I=jnp.int32
    return pl.pallas_call(functools.partial(gather_kernel,Z,block,E,W,rows),
        out_shape=[S((2,2,block,E),bf),S((2,2,R,C-6*W),bf),S((E,3*W),bf),S((3*W,L),bf),S((16,128),I),S((32,128),I),S((CODE,L),bf),S((8,L),I),S((block,E),bf)],
        in_specs=[A,A]+[V]*9,out_specs=[A,A,V,A,V,V,V,V,A],
        scratch_shapes=[M((2,2,block,E),bf),M((block,E),bf),M((2,1,block),I),M((2,2,1,block),I),M((R,C),bf),M((Z,2,2,2,R,6*W),bf),M((2,2,R,C-6*W),bf),M((3*W,E),bf),M((3*W,L),bf),
            D((4,)),D((4*NCH,)),D((2,)),D((2,)),D((Z,)),D((Z,)),D((Z+1,)),D((Z+1,)),D((2,Z)),D((2,Z)),D((3,NCH)),D((3,NCH)),D((3,)),D((3,))],
        compiler_params=pltpu.CompilerParams(collective_id=0,has_side_effects=True,vmem_limit_bytes=VMEM))(tok,cot,seg,pad,known,wq,wo,wu,wd,gain,shift)
def middle_net_kernel(Z,block,E,F,W,T,att_hbm,tok_hbm,cot_hbm,cotx_hbm,*rest):
    bunds=rest[:Z]; near_out,far_out,r1_out,datt_out=rest[Z:Z+4]; parts=rest[Z+4]
    (go_ref,gu_ref,gd_ref,gg_ref,gt_ref,aown,aget,tok,cot,wall,lay,r1,da,lsem,wsem,osem,asend,aget_sem,dsend,dget,bsend,bget)=rest[Z+5:]
    net=Net(Z); z,y,j,c=net.z,net.y,net.j,net.c
    NCH=block//T; n=2*NCH; P2=att_hbm.shape[0]; G=2
    sib=net.at(c=1-c)
    def place(t):
        jj=jnp.where(t<NCH,1-j,j)
        return jj,pl.ds(al(lax.rem(t,NCH)*T,T),T)
    def where(t): return pl.ds(al((jnp.where(t<NCH,1-j,j)*2+c)*block+lax.rem(t,NCH)*T,T),T)
    def load(t):
        jj,rows=place(t)
        return [pltpu.make_async_copy(att_hbm.at[:,jj,c,rows],aown.at[t],lsem.at[0,t]),pltpu.make_async_copy(tok_hbm.at[jj,c,rows],tok.at[t],lsem.at[1,t])]
    def load_cot(t,near):
        rows=place(t)[1]
        return pltpu.make_async_copy((cot_hbm.at[j,rows] if near else cotx_hbm.at[rows]),cot.at[t],lsem.at[2,t])
    cols=[(0,E),(E,F),(E+F,E),(2*E+F,128)]
    loadw=[pltpu.make_async_copy(bunds[k],wall.at[lax.rem(z+Z-k,Z),:,:,c],wsem.at[k]) for k in range(Z)]
    for x in loadw: x.start()
    def start(t,near):
        for x in load(t): x.start()
        load_cot(t,near).start()
    for t in range(n): start(t,t>=NCH)
    barrier=pltpu.get_barrier_semaphore()
    pl.semaphore_signal(barrier,inc=1,device_id=sib,device_id_type=MESH)
    pl.semaphore_wait(barrier,1)
    def ship(t):
        jj,rows=place(t)
        return net.copy(att_hbm.at[:,jj,1-c,rows],aget.at[t],asend.at[t],aget_sem.at[t],sib)
    ship(0).start()
    weights=[net.copy(bunds[k],wall.at[lax.rem(z+Z-k,Z),:,:,c],bsend.at[k],bget.at[k],sib) for k in range(Z)]
    for x in weights: x.start()
    for t in range(1,n): ship(t).start()
    for x in loadw: x.wait()
    for k in range(Z):
        ref=wall.at[lax.rem(z+Z-k,Z),:,:,1-c]
        pltpu.make_async_copy(ref,ref,bget.at[k]).wait()
    def whole(a,b): return wall[:,:,:,:,:,a:a+b].reshape(E,b)
    gs=wall[:,:,:,:,:,cols[3][0]:].reshape(E//16,16,128).astype(f32)
    gsr=jnp.concatenate([jnp.sum(gs[q*8:(q+1)*8],0) for q in range(E//128)],1)
    g0,g1,b0,b1=[gsr[r:r+1,:] for r in range(4)]
    for r in (go_ref,gu_ref,gd_ref,gg_ref): r[...]=jnp.zeros_like(r)
    def out_near(t): return pltpu.make_async_copy(lay.at[t],near_out.at[place(t)[1]],osem.at[0,t])
    def out_far(t): return pltpu.make_async_copy(lay.at[t],far_out.at[place(t)[1]],osem.at[0,t])
    def out_r1(t):
        jj,rows=place(t)
        return pltpu.make_async_copy(r1.at[t],r1_out.at[jj,rows],osem.at[1,t])
    def out_da(t):
        return pltpu.make_async_copy(da.at[0,t],datt_out.at[:,where(t)],osem.at[2,t])
    def ship_da(t):
        return net.copy(da.at[1,t],datt_out.at[:,where(t)],dsend.at[t],dget.at[t],sib)
    def tiles(u,carry):
        ts=[G*u+g for g in range(G)]
        def each(f,*lists): return [f(*v) for v in zip(*lists)]
        for t in ts:
            for x in load(t): x.wait()
            pltpu.make_async_copy(cotx_hbm.at[place(t)[1]],cot.at[t],lsem.at[2,t]).wait()
            ship(t).wait_recv()
        def whole_att(t):
            mine=[aown[t,p] for p in range(P2)]; his=[aget[t,p] for p in range(P2)]
            return jnp.where(c==0,jnp.concatenate(mine+his,1),jnp.concatenate(his+mine,1))
        wo=whole(*cols[0]); wu=whole(*cols[1]); wd=whole(*cols[2])
        att=each(whole_att,ts)
        branch=each(lambda a:dot(a,wo,1,0),att)
        n1,inv1=zip(*each(lambda t,b:norm(tok[t].astype(f32)+b),ts,branch))
        first=each(lambda n:(n*g0+b0).astype(bf),n1)
        hidden=each(lambda a:dot(a,wu,1,0),first)
        cdf,slope=zip(*each(gelu_parts,hidden))
        act=each(lambda h,p:(h*p).astype(bf),hidden,cdf)
        fed=each(lambda a:dot(a,wd,1,0),act)
        n2,inv2=zip(*each(lambda a,b:norm(a.astype(f32)+b),first,fed))
        ct=each(lambda t:cot[t].astype(f32),ts)
        r2=each(lambda x,n,i:norm_back(x*g1,n,i),ct,n2,inv2)
        feed=each(lambda x:x.astype(bf),r2)
        dact=each(lambda x:dot(x,wd,1,1),feed)
        for t,n in zip(ts,n2): lay[t]=(n*g1+b1).astype(bf)
        both=lambda v:jnp.concatenate(v,0)
        gd_ref[...]+=dot(both(act),both(feed),0,0)
        dh=each(lambda x,s:(x*s).astype(bf),dact,slope)
        df=each(lambda x,h:x+dot(h,wu,1,1),r2,dh)
        gu_ref[...]+=dot(both(first),both(dh),0,0)
        dr=each(lambda x,n,i:norm_back(x*g0,n,i),df,n1,inv1)
        db=each(lambda x:x.astype(bf),dr)
        d=each(lambda x:dot(wo,x,1,1).astype(bf),db)
        go_ref[...]+=dot(both(att),both(db),0,0)
        for t,x,e in zip(ts,dr,d):
            r1[t]=x.astype(r1.dtype)
            da[0,t]=jnp.where(c==0,e[:W],e[W:])
            da[1,t]=jnp.where(c==0,e[W:],e[:W])
        down=lambda v:sum(jnp.sum(x,0,keepdims=True) for x in v)
        gg_ref[0:1,:]+=down(each(lambda x,n:x*n,df,n1))
        gg_ref[1:2,:]+=down(each(lambda x,n:x*n,ct,n2))
        gg_ref[2:3,:]+=down(df)
        gg_ref[3:4,:]+=down(ct)
        for t in ts:
            @pl.when(t<NCH)
            def _(): out_far(t).start()
            @pl.when(t>=NCH)
            def _(): out_near(t).start()
            out_r1(t).start(); out_da(t).start(); ship_da(t).start()
        return carry
    lax.fori_loop(0,n//G,tiles,0)
    ggt=jnp.concatenate([gg_ref[...],jnp.zeros((120,E),f32)],0).T
    gt_ref[...]=ggt
    R=E//(2*Z)
    at=0
    for ref in (go_ref,gu_ref,gd_ref,gt_ref):
        parts[:,:,at:at+ref.shape[1]]=ref[...].astype(bf).reshape(2*Z,R,ref.shape[1])
        at+=ref.shape[1]
    for x in weights: x.wait_send()
    for t in range(n):
        ship(t).wait_send(); out_r1(t).wait(); out_da(t).wait(); ship_da(t).wait()
        (out_far if t<NCH else out_near)(t).wait()

def middle_net(att,tok,cot,cotx,bunds,Z,W,F):
    P2,_,_,block,_=att.shape; E=tok.shape[-1]; C=bunds[0].shape[-1]
    T=256; NCH=block//T; n=2*NCH
    V=pl.BlockSpec(memory_space=pltpu.VMEM); A=pl.BlockSpec(memory_space=pl.ANY)
    S=jax.ShapeDtypeStruct; M=pltpu.VMEM; D=pltpu.SemaphoreType.DMA
    return pl.pallas_call(functools.partial(middle_net_kernel,Z,block,E,F,W,T),
        out_shape=[S((block,E),bf),S((block,E),bf),S((2,block,E),bf),S((W,4*block),bf)]+[S((2*Z,E//(2*Z),C),bf)],
        in_specs=[A]*(4+Z),out_specs=[A,A,A,A,V],
        scratch_shapes=[M((E,E),f32),M((E,F),f32),M((F,E),f32),M((8,E),f32),M((E,128),f32),
            M((n,P2,T,128),bf),M((n,P2,T,128),bf),M((n,T,E),bf),M((n,T,E),bf),M((Z,2,2,2,16,C),bf),M((n,T,E),bf),M((n,T,E),bf),M((2,n,W,T),bf),
            D((3,n)),D((Z,)),D((3,n)),D((n,)),D((n,)),D((n,)),D((n,)),D((Z,)),D((Z,))],
        compiler_params=pltpu.CompilerParams(collective_id=2,has_side_effects=True,vmem_limit_bytes=VMEM))(att,tok,cot,cotx,*bunds)
def reduce_kernel(Z,block,E,W,C1,rows,base_ref,meta_ref,dq_hbm,dkvw_hbm,tok_hbm,w_hbm,r1_hbm,parts_hbm,tok_out,grad_out,
     dq,dkvw,tok,w,r1,parts,own,tgf,tgr,tgs,ob,s0,r0,g0,s1,r1b,su,ru,fin,sx,rx,se,re,sxe,rxe,
     lsem,nsem,osem,ts,tr,xs,xr,cs,cr,ys,yr,us,ur,fs,fr):
    net=Net(Z); z,y,j,c=net.z,net.y,net.j,net.c
    NCH=block//rows; half=2*block
    sib=net.at(c=1-c); xd=net.at(j=1-j); yd=net.at(y=1-y)
    def side(jj): return pl.ds(al(jj*half,128),half)
    def spans(jj): return pl.ds(jj*2*NCH,2*NCH)
    def need(cc,k):
        at=((1-j)*2+cc)*NCH+k; cols=pl.ds(al(at*rows,rows),rows)
        return [pltpu.make_async_copy(dkvw_hbm.at[at],dkvw.at[at],nsem.at[0,cc,k]),pltpu.make_async_copy(dq_hbm.at[:,cols],dq.at[:,cols],nsem.at[1,cc,k])]
    loads=[pltpu.make_async_copy(a,b,lsem.at[k]) for k,(a,b) in enumerate(((w_hbm,w),(r1_hbm,r1),(parts_hbm,parts),
        (dq_hbm.at[:,side(j)],dq.at[:,side(j)]),(tok_hbm,tok),(dkvw_hbm.at[spans(j)],dkvw.at[spans(j)])))]
    net.signal()
    for x in need(1-c,0)+loads[:1]+need(c,0): x.start()
    for k in range(1,NCH):
        for x in need(1-c,k)+need(c,k): x.start()
    for x in loads[1:]: x.start()
    def chunk(k): return pl.ds(k*rows,rows)
    def landed(ref,sem): pltpu.make_async_copy(ref,ref,sem).wait()
    def position(jj,cc,k): return pl.ds(al(((jj*2+cc)*NCH+k)*rows,rows),rows)
    def place(jj,cc,k):
        ssl=position(jj,cc,k)
        dq[W:3*W,ssl]=placed(base_ref,meta_ref[0:1,ssl],dkvw[(jj*2+cc)*NCH+k],dq[W:3*W,ssl],(jj*2+cc)*NCH+k).astype(bf)
    def to_tokens(jj,cc,k): return dot(dq[:,position(jj,cc,k)],w[...],0,1)
    def for_sibling(t,k):
        jj=1-j if t==0 else j
        tgf[jj,chunk(k),:]=to_tokens(jj,1-c,k).astype(bf)
        net.send(tgf.at[jj,chunk(k)],tgr.at[jj,chunk(k)],ts.at[t,k],tr.at[t,k],sib)
    def split(x,n): return x.reshape(Z,2,2,2,16,n)
    def core_sum(v,lo,n):
        x=dot(dq[lo:lo+n,:],tok[...],1,0).T.astype(bf)
        x=split(x,n)
        s0[:,:,:,:,lo:lo+n]=jnp.where(c==0,x[:,:,:,1],x[:,:,:,0])
        net.send(s0.at[:,:,:,:,lo:lo+n],r0.at[:,:,:,:,lo:lo+n],cs.at[v],cr.at[v],sib)
        mine=jnp.where(c==0,x[:,:,:,0],x[:,:,:,1])
        for t in range(lo//W,(lo+n)//W):
            part=mine[:,:,:,:,t*W-lo:(t+1)*W-lo]
            @pl.when(c==0)
            def _(): g0[:,:,:,:,2*t*W:(2*t+1)*W]=part
            @pl.when(c==1)
            def _(): g0[:,:,:,:,(2*t+1)*W:(2*t+2)*W]=part
    def core_get(v,lo,n):
        landed(r0.at[:,:,:,:,lo:lo+n],cr.at[v])
        for t in range(lo//W,(lo+n)//W):
            part=r0[:,:,:,:,t*W:(t+1)*W]
            @pl.when(c==0)
            def _(): g0[:,:,:,:,(2*t+1)*W:(2*t+2)*W]=part
            @pl.when(c==1)
            def _(): g0[:,:,:,:,2*t*W:(2*t+1)*W]=part
    cut=[pl.ds(2*t*W,2*W) for t in range(3)]
    def to_y(v):
        s1[:,:,:,cut[v]]=jnp.where(y==0,g0[:,1,:,:,cut[v]],g0[:,0,:,:,cut[v]])
        net.send(s1.at[:,:,:,cut[v]],r1b.at[:,:,:,cut[v]],ys.at[v],yr.at[v],yd)
    def to_z(v):
        landed(r1b.at[:,:,:,cut[v]],yr.at[v])
        for k in range(1,Z):
            o=lax.rem(z+k,Z)
            su[k,:,:,cut[v]]=(g0[o,y,:,:,cut[v]].astype(f32)+r1b[o,:,:,cut[v]].astype(f32)).astype(bf)
            net.send(su.at[k,:,:,cut[v]],ru.at[k,:,:,cut[v]],us.at[v,k],ur.at[v,k],net.at(z=o))
    def to_x(v):
        sum_=g0[z,y,:,:,cut[v]].astype(f32)+r1b[z,:,:,cut[v]].astype(f32)
        for k in range(1,Z):
            landed(ru.at[k,:,:,cut[v]],ur.at[v,k])
            sum_=sum_+ru[k,:,:,cut[v]].astype(f32)
        fin[:,:,cut[v]]=sum_
        sx[:,cut[v]]=jnp.where(j==0,sum_[1],sum_[0]).astype(bf)
        net.send(sx.at[:,cut[v]],rx.at[:,cut[v]],fs.at[v],fr.at[v],xd)
    def total(jj,k): return (own[jj,chunk(k),:]+tgr[jj,chunk(k),:].astype(f32)+r1[jj,chunk(k),:].astype(f32)).astype(bf)
    def far(k):
        landed(tgr.at[1-j,chunk(k)],tr.at[0,k])
        tgs[chunk(k),:]=total(1-j,k)
        net.send(tgs.at[chunk(k)],ob.at[j,chunk(k)],xs.at[k],xr.at[k],xd)
    for k in range(NCH):
        for x in need(1-c,k): x.wait()
        place(1-j,1-c,k)
        if k==0:
            loads[0].wait()
            net.wait()
        for_sibling(0,k)
        for x in need(c,k): x.wait()
        place(1-j,c,k)
        own[1-j,chunk(k),:]=to_tokens(1-j,c,k)
        if k==0: loads[1].wait()
        else: far(k-1)
    for x in loads[2:]: x.wait()
    core_sum(0,0,W)
    far(NCH-1)
    for cc in (1-c,c):
        for k in range(NCH): place(j,cc,k)
    core_get(0,0,W)
    to_y(0)
    core_sum(1,W,W)
    core_sum(2,2*W,W)
    core_get(1,W,W)
    to_y(1)
    early=parts[0].astype(f32)
    for k in range(1,2*Z): early=early+parts[k].astype(f32)
    early=early.reshape(2,2,16,C1)
    early0=jnp.where(c==0,early[:,0],early[:,1])
    se[...]=jnp.where(c==0,early[:,1],early[:,0]).astype(bf)
    net.send(se,re,cs.at[3],cr.at[3],sib)
    core_get(2,2*W,W)
    to_y(2)
    to_z(0)
    for k in range(NCH): for_sibling(1,k)
    to_z(1)
    landed(re,cr.at[3])
    early0=early0+re[...].astype(f32)
    early1=jnp.where(j==0,early0[0],early0[1])
    sxe[...]=jnp.where(j==0,early0[1],early0[0]).astype(bf)
    net.send(sxe,rxe,fs.at[3],fr.at[3],xd)
    to_x(0)
    for k in range(NCH): own[j,chunk(k),:]=to_tokens(j,c,k)
    to_z(2)
    to_x(1)
    for k in range(NCH):
        landed(tgr.at[j,chunk(k)],tr.at[1,k])
        ob[j,chunk(k),:]=total(j,k)
    near=pltpu.make_async_copy(ob.at[j],tok_out.at[j],osem.at[0]); near.start()
    to_x(2)
    landed(rxe,fr.at[3])
    grad_out[:,6*W:]=early1+rxe[...].astype(f32)
    for v in range(3):
        landed(rx.at[:,cut[v]],fr.at[v])
        grad_out[:,cut[v]]=jnp.where(j==0,fin[0,:,cut[v]],fin[1,:,cut[v]])+rx[:,cut[v]].astype(f32)
    last=[pltpu.make_async_copy(ob.at[1-j,chunk(k)],tok_out.at[1-j,chunk(k)],osem.at[1+k]) for k in range(NCH)]
    for k in range(NCH):
        landed(ob.at[1-j,chunk(k)],xr.at[k])
        last[k].start()
    net.drain()
    near.wait()
    for x in last: x.wait()

def reduce(base,meta,dq,dkvw,tok,w,r1,parts,Z,W):
    _,block,E=r1.shape; L=4*block; C1=parts.shape[2]; C=6*W
    rows=256; NCH=block//rows
    V=pl.BlockSpec(memory_space=pltpu.VMEM); A=pl.BlockSpec(memory_space=pl.ANY)
    S=jax.ShapeDtypeStruct; M=pltpu.VMEM; D=pltpu.SemaphoreType.DMA
    return pl.pallas_call(functools.partial(reduce_kernel,Z,block,E,W,C1,rows),
        out_shape=[S((2,block,E),bf),S((16,C+C1),f32)],
        in_specs=[pl.BlockSpec(memory_space=pltpu.SMEM),V,A,A,A,A,A,A],out_specs=[A,V],
        scratch_shapes=[M(dq.shape,bf),M(dkvw.shape,bf),M(tok.shape,bf),M(w.shape,bf),M(r1.shape,bf),M(parts.shape,bf),M((2,block,E),f32),M((2,block,E),bf),M((2,block,E),bf),M((block,E),bf),M((2,block,E),bf),
            M((Z,2,2,16,3*W),bf),M((Z,2,2,16,3*W),bf),M((Z,2,2,16,C),bf),M((Z,2,16,C),bf),M((Z,2,16,C),bf),
            M((Z,2,16,C),bf),M((Z,2,16,C),bf),M((2,16,C),f32),M((16,C),bf),M((16,C),bf),M((2,16,C1),bf),M((2,16,C1),bf),M((16,C1),bf),M((16,C1),bf),
            D((6,)),D((2,2,NCH)),D((1+NCH,)),D((2,NCH)),D((2,NCH)),D((NCH,)),D((NCH,)),D((4,)),D((4,)),D((3,)),D((3,)),D((3,Z)),D((3,Z)),D((4,)),D((4,))],
        compiler_params=pltpu.CompilerParams(collective_id=1,has_side_effects=True,vmem_limit_bytes=VMEM))(base,meta,dq,dkvw,tok,w,r1,parts)

def finish_kernel(W,E,F,near,far,tg_hbm,grads_hbm,lay_out,tg_out,gq,go,gu,gd,gg,gs,lay,tg,grads,small,isem,osem):
    j=lax.axis_index("blk")//2; block=near.shape[0]; n=4; rows=block//n
    gcopy=pltpu.make_async_copy(grads_hbm,grads,isem.at[4*n]); gcopy.start()
    come=[];leave=[]
    for k in range(n):
        r=pl.ds(k*rows,rows)
        for a,b,o in ((near.at[r],lay.at[j,r],lay_out.at[j,r]),(far.at[r],lay.at[1-j,r],lay_out.at[1-j,r]),(tg_hbm.at[0,r],tg.at[0,r],tg_out.at[0,r]),(tg_hbm.at[1,r],tg.at[1,r],tg_out.at[1,r])):
            at=len(come)
            come.append(pltpu.make_async_copy(a,b,isem.at[at])); leave.append(pltpu.make_async_copy(b,o,osem.at[at]))
    for x in come: x.start()
    gcopy.wait()
    at=0
    for k,ref in enumerate((gq,go,gu,gd)):
        width=ref.shape[1]
        leave.append(pltpu.make_async_copy(grads.at[:,at:at+width],ref,osem.at[4*n+k]))
        at+=width
        leave[-1].start()
    t=grads[:,at:].T
    small[0]=t[0:2,:]; small[1]=t[2:4,:]
    for k,ref in enumerate((gg,gs)):
        leave.append(pltpu.make_async_copy(small.at[k],ref,osem.at[4*n+4+k]))
        leave[-1].start()
    for x,o in zip(come,leave):
        x.wait(); o.start()
    for o in leave: o.wait()

def finish(near,far,tg,grads,W,F):
    _,block,E=tg.shape
    A=pl.BlockSpec(memory_space=pl.ANY); S=jax.ShapeDtypeStruct; M=pltpu.VMEM; D=pltpu.SemaphoreType.DMA
    return pl.pallas_call(functools.partial(finish_kernel,W,E,F),
        out_shape=[S(tg.shape,bf),S(tg.shape,bf),S((16,6*W),f32),S((16,E),f32),S((16,F),f32),S((16,E),f32),S((2,16),f32),S((2,16),f32)],
        in_specs=[A]*4,out_specs=[A]*8,scratch_shapes=[M(tg.shape,bf),M(tg.shape,bf),M(grads.shape,f32),M((2,2,16),f32),D((17,)),D((22,))],
        compiler_params=pltpu.CompilerParams(vmem_limit_bytes=VMEM))(near,far,tg,grads)
def shards(tokens,cotangent,segments,padding,known,w_qkv,w_out,w_up,w_down,norm_gains,norm_shifts):
    micro,rows,block,D=tokens.shape
    J=lax.axis_size("blk")//2; dps=lax.axis_size("dp")
    units=micro*rows
    assert units==J
    H=HEADS//2; W=H*HEAD; L=2*J*block; F=w_up.shape[1]
    quick=J==2 and dps%2==0 and w_qkv.shape[0]==16 and block%256==0
    me=lax.axis_index("blk"); chip=me//2; core=me%2
    flat=lambda x:x.reshape((units,)+x.shape[2:])
    if quick:
        Z=dps//2
        cot=flat(cotangent)
        tok,bund,w_mine,qkvt,base,win,codet,meta,far=gather(flat(tokens),cot,*[flat(x)[:,None,:] for x in (segments,padding,known)],w_qkv,w_out,w_up,w_down,norm_gains,norm_shifts,Z,W)
        bunds=[bund]+[lax.ppermute(bund,"dp",[(d,(d//2+k)%Z*2+d%2) for d in range(dps)]) for k in range(1,Z)]
        across=[(b,b^2) for b in range(4)]
        cotx=lax.ppermute(far,"blk",across)
        p,att,ot,inv,kct,vct=attend(base,win,qkvt,codet,meta,H)
        near,far,r1,datt,parts=middle_net(att.reshape(H//2,2,2,block,128),tok,cot,cotx,bunds,Z,W,F)
        parts=lax.all_to_all(parts,"dp",0,0,tiled=True)
        layx=lax.ppermute(far,"blk",across)
        dq,dkvw=back(base,win,datt,p,ot,inv,kct,vct,qkvt,H)
        tg,grads=reduce(base,meta,dq,dkvw,tok.reshape(L,D),w_mine,r1,parts,Z,W)
        out=finish(near,layx,tg,grads,W,F)
        return (out[0].reshape(tokens.shape),out[1].reshape(tokens.shape))+tuple(out[2:])
    def to_chip(s): return [(2*a+c,2*((a+s)%J)+c) for a in range(J) for c in range(2)]
    swap=[(b,b^1) for b in range(2*J)]
    def other(x): return lax.ppermute(x,"blk",swap)
    def scatter_units(x):
        got=[]
        for s in range(J):
            mine=lax.dynamic_index_in_dim(x,(chip+s)%J,0,keepdims=False)
            got.append(mine if s==0 else lax.ppermute(mine,"blk",to_chip(s)))
        return jnp.stack([lax.dynamic_index_in_dim(jnp.stack(got),(chip-j)%J,0,keepdims=False) for j in range(J)])
    def both(mine,his):
        return jnp.stack([jnp.where(core==0,mine,his),jnp.where(core==0,his,mine)],1)
    def part(x,axis,index): return lax.dynamic_index_in_dim(x,index,axis,keepdims=False)
    own_info=scatter_units(flat(segments*4+padding*2+known)); info=both(own_info,other(own_info)).reshape(1,L)
    own_tok=scatter_units(flat(tokens)); all_tok=both(own_tok,other(own_tok)).reshape(L,D)
    own_cot=scatter_units(flat(cotangent)).reshape(L//2,D)
    full_qkv,full_out,full_up,full_down=[lax.all_gather(w,("dp","blk"),axis=0,tiled=True) for w in (w_qkv,w_out,w_up,w_down)]
    gs=lax.all_gather(jnp.concatenate([norm_gains,norm_shifts],0),("dp","blk"),axis=1,tiled=True).astype(f32)
    gs=jnp.concatenate([gs,jnp.zeros_like(gs)],0)
    w_mine=part(full_qkv.reshape(D,3,2,W),2,core).reshape(D,3*W)
    qkvt=jnp.einsum("ld,de->el",all_tok,w_mine,preferred_element_type=f32).astype(bf)
    base,win,codet,meta=flags(info)
    p,att,ot,inv,kct,vct=attend(base,win,qkvt,codet,meta,H)
    att=att.reshape(H//2,J,2,block,128)
    mine=part(att,2,core).reshape(H//2,J*block,128); his=other(part(att,2,1-core)).reshape(H//2,J*block,128)
    a0=jnp.where(core==0,mine,his); a1=jnp.where(core==0,his,mine)
    out,r1,da,go,gu,gd,gg=middle(a0,a1,own_tok.reshape(L//2,D),own_cot,full_out,full_up,full_down,gs)
    da=da.reshape(2,H//2,J,block,128)
    dmine=part(da,0,core); dhis=other(part(da,0,1-core))
    datt=jnp.stack([jnp.where(core==0,dmine,dhis),jnp.where(core==0,dhis,dmine)],2).reshape(H//2,L,128).transpose(0,2,1).reshape(W,L)
    dq,dkvw=back(base,win,datt,p,ot,inv,kct,vct,qkvt,H)
    tg,gq=place_all(base,meta,dq,dkvw,all_tok,w_mine,H)
    tg=tg.reshape(J,2,block,D)
    layer_out=scatter_units(out.reshape(J,block,D)).reshape(tokens.shape)
    own_tg=(part(tg,1,core).astype(f32)+other(part(tg,1,1-core)).astype(f32)+r1.reshape(J,block,D)).astype(bf)
    token_grad=scatter_units(own_tg).reshape(tokens.shape)
    gq=gq.astype(f32).reshape(D,3,1,W)
    gq=jnp.where(core==0,jnp.concatenate([gq,jnp.zeros_like(gq)],2),jnp.concatenate([jnp.zeros_like(gq),gq],2)).reshape(D,6*W)
    grads=lax.psum_scatter(jnp.concatenate([gq,go,gu,gd],1),("dp","blk"),scatter_dimension=0,tiled=True)
    gg=lax.psum_scatter(gg[:4],("dp","blk"),scatter_dimension=1,tiled=True)
    a,b,e=6*W,6*W+D,6*W+D+F
    return (layer_out,token_grad,grads[:,:a],grads[:,a:b],grads[:,b:e],grads[:,e:],gg[:2],gg[2:])

def solution(mesh):
    in_specs = (
        P(None, "dp", "blk", None),
        P(None, "dp", "blk", None),
        P(None, "dp", "blk"),
        P(None, "dp", "blk"),
        P(None, "dp", "blk"),
        P(("dp", "blk"), None),
        P(("dp", "blk"), None),
        P(("dp", "blk"), None),
        P(("dp", "blk"), None),
        P(None, ("dp", "blk")),
        P(None, ("dp", "blk")),
    )
    out_specs = (
        P(None, "dp", "blk", None),
        P(None, "dp", "blk", None),
        P(("dp", "blk"), None),
        P(("dp", "blk"), None),
        P(("dp", "blk"), None),
        P(("dp", "blk"), None),
        P(None, ("dp", "blk")),
        P(None, ("dp", "blk")),
    )
    return jax.shard_map(shards, mesh=mesh, in_specs=in_specs, out_specs=out_specs, check_vma=False)
```

```python
import functools, math
import jax, jax.numpy as jnp
from jax import lax
from jax.experimental import pallas as pl
from jax.experimental.pallas import tpu as pltpu
from jax.sharding import PartitionSpec as P

HEADS = 8
bf=jnp.bfloat16; f32=jnp.float32
HEAD=64
QB=512
KB=512
SRC=768
SAFE=60.0
RATE=math.log2(math.e)*HEAD**-0.5
CODE=16
VMEM=(64<<20)-(128<<10)
SLOTS=4
def dot(a,b,ca,cb): return lax.dot_general(a,b,(((ca,),(cb,)),((),())),preferred_element_type=f32)
def al(x,n): return pl.multiple_of(x,n)
def iota(shape,axis): return lax.broadcasted_iota(jnp.int32,shape,axis)

def begin(base_ref,b):
    return base_ref[b,0]

def window(win_ref,i):
    start=win_ref[i,0]//128*128
    groups=(win_ref[8+i,0]-start+127)//128
    full=(groups-1)//(KB//128)
    return start,full,groups-full*(KB//128),groups

def by_piece(first,full,rest,g,fn):
    def body(j,g):
        fn(al(first+j*KB,128),KB,g)
        return g+1
    g=lax.fori_loop(0,full,body,g)
    for r in range(1,KB//128+1):
        @pl.when(rest==r)
        def _(): fn(al(first+full*KB,128),r*128,g)
    return g+1

def attend_kernel(L,H,base_ref,win_ref,qkvt_hbm,codet_ref,meta_ref,p_hbm,att_hbm,ot_hbm,inv_ref,kct_hbm,vct_hbm,
                  kaug_ref,kct_ref,kvt,q_ref,v_ref,vct,acc,pbuf,obuf,abuf,top_ref,psem,osem,asem,ksem,lsem):
    W=H*HEAD; nq=L//QB
    total=begin(base_ref,L//256)
    third=L//3
    def part(t):
        cols=slice(t*third,(t+1)*third)
        x=[pltpu.make_async_copy(qkvt_hbm.at[W+h*HEAD:W+(h+1)*HEAD,cols],kvt.at[h*128:h*128+HEAD,cols],lsem.at[t,h]) for h in range(H)]
        return x+[pltpu.make_async_copy(qkvt_hbm.at[2*W:,cols],v_ref.at[:,cols],lsem.at[t,H])]
    for t in range(3):
        for x in part(t): x.start()
    queries=pltpu.make_async_copy(qkvt_hbm.at[:W],q_ref,lsem.at[0,H+1]); queries.start()
    for h in range(H):
        kvt[h*128+HEAD:h*128+HEAD+CODE,:]=codet_ref[...]
        kvt[h*128+HEAD+CODE:(h+1)*128,:]=jnp.zeros((HEAD-CODE,L),bf)
    vct[:,HEAD:,:]=jnp.ones((H,16,L),bf)
    row=iota((256,256),0)
    down=iota((256,SRC),0)
    def dest(d,c):
        first=jnp.minimum(win_ref[16+d,0]//128*128,L-SRC)
        last=win_ref[17+d,0]
        def src(t,a):
            ssl=pl.ds(al(jnp.minimum(first+t*SRC,L-SRC),128),SRC)
            oh=((meta_ref[0:1,ssl]==down+d*256)&(lane>=first+t*SRC-jnp.minimum(first+t*SRC,L-SRC))).astype(f32).astype(bf)
            return a[0]+dot(kvt[:,ssl],oh,1,1),a[1]+dot(v_ref[:,ssl],oh,1,1)
        lane=iota((256,SRC),1)
        reach=jnp.minimum(first+jnp.maximum((last-first+SRC-1)//SRC,1)*SRC,L)
        for t in range(3):
            @pl.when((c<=t)&(reach>t*third))
            def _():
                for x in part(t): x.wait()
        ka,va=src(0,(jnp.zeros((H*128,256),f32),jnp.zeros((W,256),f32)))
        ka,va=lax.fori_loop(1,(last-first+SRC-1)//SRC,src,(ka,va))
        dsl=pl.ds(al(d*256,256),256)
        for h in range(H):
            k1=jnp.where(row[:128]==HEAD+10,-10240.0,ka[h*128:(h+1)*128])
            kaug_ref[h,dsl,:]=k1.astype(bf).T
            kct_ref[h,:,dsl]=k1[:HEAD].astype(bf)
            vct[h,:HEAD,dsl]=va[h*HEAD:(h+1)*HEAD].astype(bf)
        return jnp.maximum(c,(reach+third-1)//third)
    ready=lax.fori_loop(0,(total+255)//256,dest,0)
    for t in range(3):
        @pl.when(ready<=t)
        def _():
            for x in part(t): x.wait()
    keep=[pltpu.make_async_copy(kct_ref,kct_hbm,ksem.at[0]),pltpu.make_async_copy(vct,vct_hbm,ksem.at[1])]
    for x in keep: x.start()
    queries.wait()
    bound=jnp.float32(0)
    for h in range(H):
        q=q_ref[h*HEAD:(h+1)*HEAD,:].astype(f32); k=kvt[h*128:h*128+HEAD,:].astype(f32)
        bound=jnp.maximum(bound,jnp.max(jnp.sum(q*q,0,keepdims=True))*jnp.max(jnp.sum(k*k,0,keepdims=True)))
    safe=bound*(RATE*RATE)<SAFE*SAFE

    def pcopy(g):
        slot=lax.rem(g,SLOTS)
        return pltpu.make_async_copy(pbuf.at[slot],p_hbm.at[g],psem.at[slot])
    def ocopy(i):
        slot=lax.rem(i,2)
        return pltpu.make_async_copy(obuf.at[slot],ot_hbm.at[i],osem.at[slot])
    def acopy(i):
        slot=lax.rem(i,2)
        return pltpu.make_async_copy(abuf.at[slot],att_hbm.at[:,pl.ds(al(i*QB,QB),QB),:],asem.at[slot])
    def block(i,g):
        slot=lax.rem(i,2)
        qsl=pl.ds(al(i*QB,QB),QB)
        first,full,rest,groups=window(win_ref,i)
        qa=[jnp.concatenate([q_ref[h*HEAD:(h+1)*HEAD,qsl],codet_ref[:,qsl],jnp.zeros((HEAD-CODE,QB),bf)],0) for h in range(H)]
        own=meta_ref[1:2,qsl]>0
        sself=[]
        for h in range(H):
            x=q_ref[h*HEAD:(h+1)*HEAD,qsl].astype(f32)*kvt[h*128:h*128+HEAD,qsl].astype(f32)
            sself.append(jnp.where(own,jnp.sum(x,0,keepdims=True),-1e30))
        acc[...]=jnp.zeros_like(acc)
        top_ref[...]=jnp.zeros_like(top_ref)
        row=iota((128,QB),0)
        def strict(h,osl):
            k=kaug_ref[h,osl,:]
            x=qa[h].astype(f32)
            plain=dot(k,jnp.where(row<HEAD,x,0.0).astype(bf),1,0)
            return jnp.where(dot(k,jnp.where(row<HEAD,0.0,x).astype(bf),1,0)>-1.0,plain,-1e30)
        @pl.when(jnp.logical_not(safe))
        def _():
            for h in range(H):
                def more(j,m): return jnp.maximum(m,jnp.max(strict(h,pl.ds(al(first+j*128,128),128)),0,keepdims=True))
                top_ref[h:h+1,:]=lax.fori_loop(0,groups,more,sself[h])
        def piece(off,size,g):
            ps=lax.rem(g,SLOTS)
            osl=pl.ds(off,size)
            @pl.when(g>=SLOTS)
            def _(): pcopy(g-SLOTS).wait()
            @pl.when(safe)
            def _():
                keepp=[]
                for h in range(H):
                    p=jnp.exp2(RATE*dot(kaug_ref[h,osl,:],qa[h],1,0)).astype(bf)
                    pbuf[ps,h,:,:size]=p.T
                    keepp.append(p)
                for h in range(H): acc[h]+=dot(vct[h,:,osl],keepp[h],1,0)
            @pl.when(jnp.logical_not(safe))
            def _():
                for h in range(H):
                    def put(j,c):
                        jsl=pl.ds(al(off+j*128,128),128)
                        p=jnp.exp2(RATE*(strict(h,jsl)-top_ref[h:h+1,:])).astype(bf)
                        pbuf[ps,h,:,pl.ds(al(j*128,128),128)]=p.T
                        acc[h]+=dot(vct[h,:,jsl],p,1,0)
                        return c
                    lax.fori_loop(0,size//128,put,0)
            pcopy(g).start()
        g=by_piece(first,full,rest,g,piece)
        @pl.when(i>=2)
        def _(): ocopy(i-2).wait(); acopy(i-2).wait()
        for h in range(H):
            ps=jnp.exp2(RATE*(sself[h]-top_ref[h:h+1,:]))
            inv=1.0/(acc[h,HEAD:HEAD+1,:]+ps)
            obuf[slot,h*HEAD:(h+1)*HEAD,:]=(acc[h,:HEAD,:]+ps*v_ref[h*HEAD:(h+1)*HEAD,qsl].astype(f32))*inv
            inv_ref[h,0:1,qsl]=inv
            inv_ref[h,1:2,qsl]=ps
        for hp in range(H//2): abuf[slot,hp]=obuf[slot,hp*128:(hp+1)*128,:].astype(bf).T
        ocopy(i).start(); acopy(i).start()
        return g
    g=lax.fori_loop(0,nq,block,0)
    for s in range(SLOTS):
        last=g-1-s
        @pl.when(last>=0)
        def _(): pcopy(last).wait()
    for i in range(max(nq-2,0),nq): ocopy(i).wait(); acopy(i).wait()
    for x in keep: x.wait()

def attend(base,win,qkvt,codet,meta,H):
    L=qkvt.shape[1]; W=H*HEAD; nq=L//QB; cap=nq*((L+KB-1)//KB)
    V=pl.BlockSpec(memory_space=pltpu.VMEM); A=pl.BlockSpec(memory_space=pl.ANY)
    S=jax.ShapeDtypeStruct; M=pltpu.VMEM; D=pltpu.SemaphoreType.DMA
    return pl.pallas_call(functools.partial(attend_kernel,L,H),
        out_shape=[S((cap,H,QB,KB),bf),S((H//2,L,128),bf),S((nq,W,QB),f32),S((H,8,L),f32),S((H,HEAD,L),bf),S((H,HEAD+16,L),bf)],
        in_specs=[pl.BlockSpec(memory_space=pltpu.SMEM)]*2+[A,V,V],
        out_specs=[A,A,A,V,A,A],
        scratch_shapes=[M((H,L,128),bf),M((H,HEAD,L),bf),M((H*128,L),bf),M((W,L),bf),M((W,L),bf),M((H,HEAD+16,L),bf),M((H,HEAD+16,QB),f32),M((SLOTS,H,QB,KB),bf),
            M((2,W,QB),f32),M((2,H//2,QB,128),bf),M((8,QB),f32),D((SLOTS,)),D((2,)),D((2,)),D((2,)),D((3,H+2))],
        compiler_params=pltpu.CompilerParams(vmem_limit_bytes=VMEM))(base,win,qkvt,codet,meta)

def flags(row):
    L=row.shape[1]; nb=L//256; nq=L//QB
    seg=row//4
    pad=row//2-2*seg
    known=row-2*(row//2)
    use=(pad==0)&(known==1)
    usef=use.astype(f32)
    x=jnp.concatenate([usef[:,b*256:(b+1)*256] for b in range(nb)]+[jnp.zeros((16-nb,256),f32)],0)
    incl=dot(x.astype(bf),(iota((256,256),0)<=iota((256,256),1)).astype(f32).astype(bf),1,0)
    tot=jnp.broadcast_to(incl[:,255:256],(16,256)).astype(bf)
    base=dot((iota((16,16),0)>iota((16,16),1)).astype(f32).astype(bf),tot,1,0)
    mid=seg[:,L//2:L//2+1]
    late=(seg>=mid).astype(f32)
    early=jnp.sum(usef*(1.0-late),1,keepdims=True)
    shift=jnp.ceil(early*(1.0/128.0))*128.0-early
    shift=jnp.where(jnp.sum(usef,1,keepdims=True)+shift<=L,shift,0.0)
    csum=jnp.concatenate([(incl+base)[b:b+1] for b in range(nb)],1)+late*shift
    rank=jnp.where(use,csum.astype(jnp.int32)-1,-1)
    base=base+shift*jnp.concatenate([late[:,b*256:b*256+1] for b in range(nb)]+[jnp.ones((16-nb,1),f32)],0)
    own=((pad==0)&(known!=1)).astype(jnp.int32)
    bits=iota((CODE,L),0)
    bit=lax.shift_right_logical(jnp.broadcast_to(seg,(CODE,L)),jnp.minimum(bits,9))&1
    codet=jnp.where(bits<10,jnp.where(bit==1,32.0,-32.0),jnp.where(bits==10,1.0,0.0)).astype(bf)
    meta=jnp.concatenate([rank,own,jnp.zeros((6,L),jnp.int32)],0)
    def edge(at): return jnp.concatenate([seg[:,i*QB+at:i*QB+at+1] for i in range(nq)]+[jnp.zeros((8-nq,1),jnp.int32)],0)
    low=jnp.sum(jnp.where(seg<edge(0),usef,0.0),1,keepdims=True)+shift*(edge(0)>=mid).astype(f32)
    high=jnp.sum(jnp.where(seg<=edge(QB-1),usef,0.0),1,keepdims=True)+shift*(edge(QB-1)>=mid).astype(f32)
    starts=jnp.sum((csum<=(256*iota((16,1),0)).astype(f32)).astype(f32),1,keepdims=True)
    win=jnp.broadcast_to(jnp.concatenate([low,high,starts],0),(32,128)).astype(jnp.int32)
    return base[:,:128].astype(jnp.int32),win,codet,meta
SPAN=512
def back_kernel(L,H,base_ref,win_ref,datt_hbm,p_hbm,ot_hbm,inv_ref,kct_hbm,vct_hbm,qkvt_hbm,dq_hbm,dkvw_hbm,
                kct,vct,dkv,dkvt,pbuf,qacc,qkv,datt,ot,dq,psem,lsem,qsem,osem,tsem):
    W=H*HEAD; nq=L//QB
    groups=(begin(base_ref,L//256)+127)//128
    pieces=lax.fori_loop(0,nq,lambda i,s:s+window(win_ref,i)[1]+1,0)
    def pcopy(g):
        slot=lax.rem(g,SLOTS)
        return pltpu.make_async_copy(p_hbm.at[g],pbuf.at[slot],psem.at[slot])
    def keys(t):
        rows=pl.ds(al(t*KB,KB),KB)
        return [pltpu.make_async_copy(vct_hbm.at[:,:,rows],vct.at[:,:,rows],lsem.at[0,t]),pltpu.make_async_copy(kct_hbm.at[:,:,rows],kct.at[:,:,rows],lsem.at[1,t])]
    def queries(i):
        slot=lax.rem(i,2); qsl=pl.ds(al(i*QB,QB),QB)
        return [pltpu.make_async_copy(a,b.at[slot],qsem.at[k,slot]) for k,(a,b) in enumerate(((qkvt_hbm.at[:,qsl],qkv),(datt_hbm.at[:,qsl],datt),(ot_hbm.at[i],ot)))]
    def each_key(fn,least=0):
        def body(t,c):
            for x in keys(t): fn(x)
            return c
        lax.fori_loop(least,(groups+KB//128-1)//(KB//128),body,0)
    for x in queries(0): x.start()
    each_key(lambda x:x.start())
    for s in range(SLOTS-1):
        @pl.when(s<pieces)
        def _(): pcopy(s).start()
    def clear(j,c):
        dkv[:,pl.ds(al(j*128,128),128)]=jnp.zeros((2*W,128),f32)
        return c
    lax.fori_loop(0,groups,clear,0)
    def ocopy(i):
        slot=lax.rem(i,2)
        return pltpu.make_async_copy(dq.at[slot],dq_hbm.at[:,pl.ds(al(i*QB,QB),QB)],osem.at[slot])
    def block(i,g):
        slot=lax.rem(i,2)
        qsl=pl.ds(al(i*QB,QB),QB)
        first,full,rest,_=window(win_ref,i)
        for x in queries(i): x.wait()
        @pl.when(i+1<nq)
        def _():
            for x in queries(i+1): x.start()
        dt=datt[slot].astype(f32)
        prod=dt*ot[slot]
        daug=[];lows=[];deltas=[];d1s=[]
        row=iota((16,QB),0)
        for h in range(H):
            hsl=slice(h*HEAD,(h+1)*HEAD)
            inv=inv_ref[h,0:1,qsl]
            delta=jnp.sum(prod[hsl],0,keepdims=True)*inv
            d1=dt[hsl]*inv
            low=d1.astype(bf)
            a=delta.astype(bf).astype(f32); b=(delta-a).astype(bf).astype(f32)
            extra=jnp.where(row==0,-a,jnp.where(row==1,-b,jnp.where(row==2,a+b-delta,0.0))).astype(bf)
            daug.append(jnp.concatenate([low,extra,jnp.zeros((HEAD-16,QB),bf)],0).T[:,:HEAD+16])
            lows.append(low); deltas.append(delta); d1s.append(d1)
        qacc[...]=jnp.zeros_like(qacc)
        def piece(off,size,g):
            ps=lax.rem(g,SLOTS)
            osl=pl.ds(off,size)
            @pl.when(g+SLOTS-1<pieces)
            def _(): pcopy(g+SLOTS-1).start()
            @pl.when(i==0)
            def _():
                for x in keys(g): x.wait()
            pcopy(g).wait()
            dss=[]
            for h in range(H):
                dss.append((pbuf[ps,h,:,:size].astype(f32)*dot(daug[h],vct[h,:,osl],1,0)).astype(bf))
                dkv[W+h*HEAD:W+(h+1)*HEAD,osl]+=dot(lows[h],pbuf[ps,h,:,:size],1,0)
            for h in range(H): qacc[h]+=dot(kct[h,:,osl],dss[h].T,1,0)
            for h in range(H):
                dkv[h*HEAD:(h+1)*HEAD,osl]+=dot(qkv[slot,h*HEAD:(h+1)*HEAD,:],dss[h],1,0)
        g=by_piece(first,full,rest,g,piece)
        @pl.when(i==0)
        def _(): each_key(lambda x:x.wait(),g)
        @pl.when(i>=2)
        def _(): ocopy(i-2).wait()
        for h in range(H):
            hsl=slice(h*HEAD,(h+1)*HEAD); ksl=slice(W+h*HEAD,W+(h+1)*HEAD); vsl=slice(2*W+h*HEAD,2*W+(h+1)*HEAD)
            ps=inv_ref[h,1:2,qsl]
            ds=ps*(jnp.sum(qkv[slot,vsl,:].astype(f32)*d1s[h],0,keepdims=True)-deltas[h])
            dq[slot,hsl,:]=((qacc[h]+ds*qkv[slot,ksl,:].astype(f32))*HEAD**-0.5).astype(bf)
            dq[slot,ksl,:]=(ds*qkv[slot,hsl,:].astype(f32)*HEAD**-0.5).astype(bf)
            dq[slot,vsl,:]=(ps*d1s[h]).astype(bf)
        ocopy(i).start()
        return g
    lax.fori_loop(0,nq,block,0)
    rows=iota((2*W,128),0)
    def tcopy(s): return pltpu.make_async_copy(dkvt.at[:,pl.ds(al(begin(base_ref,s)//128*128,128),SPAN)],dkvw_hbm.at[s],tsem.at[s])
    def turn(j,c):
        jsl=pl.ds(al(j*128,128),128)
        x=jnp.where(j<groups,dkv[:,jsl],0.0)
        dkvt[:,jsl]=jnp.where(rows<W,x*HEAD**-0.5,x).astype(bf)
        for s in range(L//256):
            @pl.when(begin(base_ref,s)//128+SPAN//128-1==j)
            def _(): tcopy(s).start()
        return c
    lax.fori_loop(0,groups+SPAN//128,turn,0)
    for i in range(max(nq-2,0),nq): ocopy(i).wait()
    for s in range(L//256): tcopy(s).wait()

def back(base,win,datt,p,ot,inv,kct,vct,qkvt,H):
    L=qkvt.shape[1]; W=H*HEAD
    V=pl.BlockSpec(memory_space=pltpu.VMEM); A=pl.BlockSpec(memory_space=pl.ANY); N=pl.BlockSpec(memory_space=pltpu.SMEM)
    S=jax.ShapeDtypeStruct; M=pltpu.VMEM; D=pltpu.SemaphoreType.DMA
    return pl.pallas_call(functools.partial(back_kernel,L,H),
        out_shape=[S((3*W,L),bf),S((L//256,2*W,SPAN),bf)],
        in_specs=[N,N,A,A,A,V,A,A,A],
        out_specs=[A,A],
        scratch_shapes=[M((H,HEAD,L),bf),M((H,HEAD+16,L),bf),M((2*W,L+SPAN),f32),M((2*W,L+SPAN),bf),M((SLOTS,H,QB,KB),bf),M((H,HEAD,QB),f32),
            M((2,3*W,QB),bf),M((2,W,QB),bf),M((2,W,QB),f32),M((2,3*W,QB),bf),
            D((SLOTS,)),D((2,L//KB)),D((3,2)),D((2,)),D((L//256,))],
        compiler_params=pltpu.CompilerParams(vmem_limit_bytes=VMEM))(base,win,datt,p,ot,inv,kct,vct,qkvt)

def placed(base_ref,rank_row,span,own,s):
    r0=begin(base_ref,s)//128*128
    oh=(rank_row==iota((SPAN,256),0)+r0).astype(f32).astype(bf)
    return dot(span,oh,1,0)+own.astype(f32)

def place_kernel(L,W,base_ref,meta_ref,dq_in,dkvw_ref,tok_ref,w_ref,tg_ref,grad_ref,dq_ref):
    dq_ref[...]=dq_in[...]
    def place(s,c):
        ssl=pl.ds(al(s*256,256),256)
        dq_ref[W:3*W,ssl]=placed(base_ref,meta_ref[0:1,ssl],dkvw_ref[s],dq_ref[W:3*W,ssl],s).astype(bf)
        tg_ref[ssl,:]=dot(dq_ref[:,ssl],w_ref[...],0,1).astype(bf)
        return c
    lax.fori_loop(0,L//256,place,0)
    grad_ref[...]=dot(dq_ref[...],tok_ref[...],1,0).T.astype(bf)

def place_all(base,meta,dq,dkvw,tok,w,H):
    L,E=tok.shape; W=H*HEAD
    V=pl.BlockSpec(memory_space=pltpu.VMEM); S=jax.ShapeDtypeStruct
    return pl.pallas_call(functools.partial(place_kernel,L,W),out_shape=[S((L,E),bf),S((E,3*W),bf)],
        in_specs=[pl.BlockSpec(memory_space=pltpu.SMEM)]+[V]*5,out_specs=[V,V],scratch_shapes=[pltpu.VMEM((3*W,L),bf)],
        compiler_params=pltpu.CompilerParams(vmem_limit_bytes=VMEM))(base,meta,dq,dkvw,tok,w)
EPSILON=1e-05
def gelu_parts(h):
    bell=jnp.exp(-0.5*h*h)
    t=1.0/(1.0+(0.3275911*math.sqrt(0.5))*jnp.abs(h))
    tail=0.5*1.061405429
    for c in (-1.453152027,1.421413741,-0.284496736,0.254829592): tail=tail*t+0.5*c
    tail=tail*t*bell
    cdf=jnp.where(h<0.0,tail,1.0-tail)
    return cdf,cdf+h*bell*(1.0/math.sqrt(2.0*math.pi))
def norm(x):
    center=x-jnp.mean(x,-1,keepdims=True)
    inverse=lax.rsqrt(jnp.mean(center*center,-1,keepdims=True)+EPSILON)
    return center*inverse,inverse
def norm_back(e,n,inverse):
    return inverse*(e-jnp.mean(e,-1,keepdims=True)-n*jnp.mean(e*n,-1,keepdims=True))
def middle_kernel(a0_ref,a1_ref,tok_ref,cot_ref,wo_ref,wu_ref,wd_ref,gs_ref,out_ref,r1_ref,da_ref,go_ref,gu_ref,gd_ref,gg_ref):
    @pl.when(pl.program_id(0)==0)
    def _():
        for r in (go_ref,gu_ref,gd_ref,gg_ref): r[...]=jnp.zeros_like(r)
    P2=a0_ref.shape[0]
    att=jnp.concatenate([a0_ref[p] for p in range(P2)]+[a1_ref[p] for p in range(P2)],1)
    g0,g1,b0,b1=[gs_ref[r:r+1,:] for r in range(4)]
    n1,inv1=norm(tok_ref[...].astype(f32)+dot(att,wo_ref[...],1,0))
    first=(n1*g0+b0).astype(bf)
    hidden=dot(first,wu_ref[...],1,0)
    cdf,slope=gelu_parts(hidden)
    act=(hidden*cdf).astype(bf)
    n2,inv2=norm(first.astype(f32)+dot(act,wd_ref[...],1,0))
    out_ref[...]=(n2*g1+b1).astype(bf)
    cot=cot_ref[...].astype(f32)
    r2=norm_back(cot*g1,n2,inv2)
    feed=r2.astype(bf)
    gd_ref[...]+=dot(act,feed,0,0)
    dh=(dot(feed,wd_ref[...],1,1)*slope).astype(bf)
    gu_ref[...]+=dot(first,dh,0,0)
    df=r2+dot(dh,wu_ref[...],1,1)
    r1=norm_back(df*g0,n1,inv1)
    r1_ref[...]=r1
    db=r1.astype(bf)
    go_ref[...]+=dot(att,db,0,0)
    da=dot(db,wo_ref[...],1,1).astype(bf)
    for p in range(2*P2): da_ref[p]=da[:,p*128:(p+1)*128]
    gg_ref[0:1,:]+=jnp.sum(df*n1,0,keepdims=True)
    gg_ref[1:2,:]+=jnp.sum(cot*n2,0,keepdims=True)
    gg_ref[2:3,:]+=jnp.sum(df,0,keepdims=True)
    gg_ref[3:4,:]+=jnp.sum(cot,0,keepdims=True)

def middle(a0,a1,tok,cot,wo,wu,wd,gs):
    P2,N,_=a0.shape; D=tok.shape[1]; F=wu.shape[1]
    T=max(t for t in (256,192,128,64,32,16) if N%t==0)
    tile=pl.BlockSpec((T,D),lambda i:(i,0))
    def pairs(k): return pl.BlockSpec((k,T,128),lambda i:(0,i,0))
    def whole(s): return pl.BlockSpec(s,lambda i:(0,)*len(s))
    return pl.pallas_call(middle_kernel,grid=(N//T,),
        in_specs=[pairs(P2),pairs(P2),tile,tile,whole((D,D)),whole((D,F)),whole((F,D)),whole((8,D))],
        out_specs=[tile,tile,pairs(2*P2),whole((D,D)),whole((D,F)),whole((F,D)),whole((8,D))],
        out_shape=[jax.ShapeDtypeStruct((N,D),bf),jax.ShapeDtypeStruct((N,D),f32),jax.ShapeDtypeStruct((2*P2,N,128),bf),
            jax.ShapeDtypeStruct((D,D),f32),jax.ShapeDtypeStruct((D,F),f32),jax.ShapeDtypeStruct((F,D),f32),jax.ShapeDtypeStruct((8,D),f32)],
        compiler_params=pltpu.CompilerParams(vmem_limit_bytes=60<<20))(a0,a1,tok,cot,wo,wu,wd,gs)
MESH=pl.DeviceIdType.MESH
class Net:
    def __init__(self,Z):
        dp=lax.axis_index("dp"); blk=lax.axis_index("blk")
        self.Z=Z; self.z=dp//2; self.y=dp%2; self.j=blk//2; self.c=blk%2
        self.sent=[]
    def at(self,z=None,y=None,j=None,c=None):
        z=self.z if z is None else z; y=self.y if y is None else y; j=self.j if j is None else j; c=self.c if c is None else c
        return (z*2+y,j*2+c)
    def signal(self):
        barrier=pltpu.get_barrier_semaphore()
        for d in [self.at(j=1-self.j),self.at(y=1-self.y),self.at(c=1-self.c)]+[self.at(z=lax.rem(self.z+k,self.Z)) for k in range(1,self.Z)]:
            pl.semaphore_signal(barrier,inc=1,device_id=d,device_id_type=MESH)
    def wait(self): pl.semaphore_wait(pltpu.get_barrier_semaphore(),2+self.Z)
    def greet(self):
        self.signal()
        self.wait()
    def copy(self,src,dst,ssem,rsem,device):
        return pltpu.make_async_remote_copy(src_ref=src,dst_ref=dst,send_sem=ssem,recv_sem=rsem,device_id=device,device_id_type=MESH)
    def send(self,src,dst,ssem,rsem,device,when=None):
        c=self.copy(src,dst,ssem,rsem,device)
        if when is None: c.start()
        else: pl.when(when)(c.start)
        self.sent.append((c,when))
    def drain(self):
        for c,when in self.sent:
            if when is None: c.wait_send()
            else: pl.when(when)(c.wait_send)

def gather_kernel(Z,block,E,W,rows,tok_hbm,cot_hbm,seg_ref,pad_ref,known_ref,wq_ref,wo_ref,wu_ref,wd_ref,gain_ref,shift_ref,
                  tok_out,bund_out,wmine_out,qkvt_out,base_out,win_out,code_out,meta_out,far_out,
                  tokb,farb,info_ref,infob,pack_ref,wall,bund,wt,qkvt,lsem,qsem,xs,xr,zs,zr,ys,yr,cs,cr,ts,tr,iss,isr):
    net=Net(Z); z,y,j,c=net.z,net.y,net.j,net.c
    NCH=block//rows; D=E
    sib=net.at(c=1-c); xd=net.at(j=1-j); yd=net.at(y=1-y)
    net.signal()
    mine=pltpu.make_async_copy(tok_hbm.at[j],tokb.at[j,c],lsem.at[0]); mine.start()
    far=pltpu.make_async_copy(cot_hbm.at[1-j],farb,lsem.at[3]); far.start()
    at=0
    for ref in (wq_ref,wo_ref,wu_ref,wd_ref):
        n=ref.shape[1]
        pack_ref[:,at:at+n]=ref[...]
        at+=n
    R=gain_ref.shape[1]
    place=(iota((R,128),1)==iota((R,128),0)+R*lax.rem(lax.axis_index("dp")*4+lax.axis_index("blk"),128//R)).astype(f32).astype(bf)
    pack_ref[:,at:]=jnp.concatenate([dot(gain_ref[...],place,1,0),dot(shift_ref[...],place,1,0),jnp.zeros((12,128),f32)],0).astype(bf)
    split=6*W
    wall[z,y,j,c]=pack_ref[:,:split]
    bund[y,j]=pack_ref[:,split:]
    info_ref[...]=seg_ref[...]*4+pad_ref[...]*2+known_ref[...]
    infob[j,c]=info_ref[j]
    net.wait()
    net.send(pack_ref.at[:,:split],wall.at[z,y,j,c],xs.at[0],xr.at[0],xd)
    net.send(pack_ref.at[:,split:],bund.at[y,j],xs.at[1],xr.at[1],xd)
    net.send(info_ref.at[1-j],infob.at[j,c],iss.at[0],isr.at[0],xd)
    net.send(info_ref.at[j],infob.at[j,c],iss.at[1],isr.at[1],sib)
    def chunk(k): return pl.ds(k*rows if type(k) is int else al(k*rows,rows),rows)
    for k in range(NCH):
        net.send(tok_hbm.at[1-j,chunk(k)],tokb.at[j,c,chunk(k)],ts.at[0,k],tr.at[0,k],xd)
        net.send(tok_hbm.at[j,chunk(k)],tokb.at[j,c,chunk(k)],ts.at[1,k],tr.at[1,k],sib)
    def piece(o,y_): return wall.at[o,y_,:,c]
    def landed(ref,sem): pltpu.make_async_copy(ref,ref,sem).wait()
    def pass_on(o):
        net.send(piece(o,y),piece(o,y),ys.at[o],yr.at[o],yd)
        net.send(piece(o,y),piece(o,y),cs.at[0,o],cr.at[0,o],sib)
    far.wait()
    far=pltpu.make_async_copy(farb,far_out,lsem.at[3]); far.start()
    landed(wall.at[z,y,1-j,c],xr.at[0])
    for k in range(1,Z):
        net.send(piece(z,y),piece(z,y),zs.at[k],zr.at[k],net.at(z=lax.rem(z+k,Z)))
    pass_on(z)
    landed(bund.at[y,1-j],xr.at[1])
    net.send(bund.at[y],bund.at[y],ys.at[Z],yr.at[Z],yd)
    for k in range(1,Z):
        o=lax.rem(z+Z-k,Z)
        landed(piece(o,y),zr.at[k])
        pass_on(o)
    for k in range(Z):
        o=lax.rem(z+Z-k,Z)
        landed(piece(o,1-y),yr.at[o])
        net.send(piece(o,1-y),piece(o,1-y),cs.at[1,o],cr.at[1,o],sib)
    for o in range(Z):
        for q in range(2): landed(wall.at[o,y if q==0 else 1-y,:,1-c],cr.at[q,o])
    landed(bund.at[1-y],yr.at[Z])
    outb=pltpu.make_async_copy(bund,bund_out,lsem.at[1]); outb.start()
    def qcopy(g):
        col=pl.ds(al(g*rows,rows),rows)
        return pltpu.make_async_copy(qkvt.at[:,col],qkvt_out.at[:,col],qsem.at[g])
    def project(jj,cc,come=None,onward=False):
        def body(k,carry):
            ref=tokb.at[jj,cc,chunk(k)]
            if come is not None: landed(ref,tr.at[come,k])
            if onward: net.copy(ref,ref,ts.at[2,k],tr.at[2,k],sib).start()
            g=(jj*2+cc)*NCH+k
            r=dot(wt[...],ref[...],1,1)
            qkvt[:,pl.ds(al(g*rows,rows),rows)]=r.astype(bf)
            qcopy(g).start()
            return carry
        lax.fori_loop(0,NCH,body,0)
    parts=[]
    for t in range(3):
        cols=pl.ds(al(t*2*W+c*W,W),W)
        part=wall[:,:,:,:,:,cols].reshape(D,W)
        wt[t*W:(t+1)*W,:]=part.T
        parts.append(part)
    wmine_out[...]=jnp.concatenate(parts,1)
    mine.wait()
    project(j,c)
    project(j,1-c,1)
    landed(infob.at[1-j,c],isr.at[0])
    net.send(infob.at[1-j,c],infob.at[1-j,c],iss.at[2],isr.at[2],sib)
    project(1-j,c,0,True)
    landed(infob.at[j,1-c],isr.at[1])
    landed(infob.at[1-j,1-c],isr.at[2])
    base_out[...],win_out[...],code_out[...],meta_out[...]=flags(jnp.concatenate([infob[0,0],infob[0,1],infob[1,0],infob[1,1]],1))
    project(1-j,1-c,2)
    outt=pltpu.make_async_copy(tokb,tok_out,lsem.at[2]); outt.start()
    net.drain()
    for k in range(NCH):
        ref=tokb.at[1-j,c,chunk(k)]
        net.copy(ref,ref,ts.at[2,k],tr.at[2,k],sib).wait_send()
    lax.fori_loop(0,4*NCH,lambda g,c:(qcopy(g).wait(),c)[1],0)
    outb.wait(); outt.wait(); far.wait()

def gather(tok,cot,seg,pad,known,wq,wo,wu,wd,gain,shift,Z,W):
    _,block,E=tok.shape; R=wq.shape[0]; C=6*W+wo.shape[1]+wu.shape[1]+wd.shape[1]+128
    rows=256; NCH=block//rows; L=4*block
    V=pl.BlockSpec(memory_space=pltpu.VMEM); A=pl.BlockSpec(memory_space=pl.ANY)
    S=jax.ShapeDtypeStruct; M=pltpu.VMEM; D=pltpu.SemaphoreType.DMA; I=jnp.int32
    return pl.pallas_call(functools.partial(gather_kernel,Z,block,E,W,rows),
        out_shape=[S((2,2,block,E),bf),S((2,2,R,C-6*W),bf),S((E,3*W),bf),S((3*W,L),bf),S((16,128),I),S((32,128),I),S((CODE,L),bf),S((8,L),I),S((block,E),bf)],
        in_specs=[A,A]+[V]*9,out_specs=[A,A,V,A,V,V,V,V,A],
        scratch_shapes=[M((2,2,block,E),bf),M((block,E),bf),M((2,1,block),I),M((2,2,1,block),I),M((R,C),bf),M((Z,2,2,2,R,6*W),bf),M((2,2,R,C-6*W),bf),M((3*W,E),bf),M((3*W,L),bf),
            D((4,)),D((4*NCH,)),D((2,)),D((2,)),D((Z,)),D((Z,)),D((Z+1,)),D((Z+1,)),D((2,Z)),D((2,Z)),D((3,NCH)),D((3,NCH)),D((3,)),D((3,))],
        compiler_params=pltpu.CompilerParams(collective_id=0,has_side_effects=True,vmem_limit_bytes=VMEM))(tok,cot,seg,pad,known,wq,wo,wu,wd,gain,shift)
def middle_net_kernel(Z,block,E,F,W,T,att_hbm,tok_hbm,cot_hbm,cotx_hbm,*rest):
    bunds=rest[:Z]; near_out,far_out,r1_out,datt_out=rest[Z:Z+4]; parts=rest[Z+4]
    (go_ref,gu_ref,gd_ref,gg_ref,gt_ref,aown,aget,tok,cot,wall,lay,r1,da,lsem,wsem,osem,asend,aget_sem,dsend,dget,bsend,bget)=rest[Z+5:]
    net=Net(Z); z,y,j,c=net.z,net.y,net.j,net.c
    NCH=block//T; n=2*NCH; P2=att_hbm.shape[0]; G=2
    sib=net.at(c=1-c)
    def place(t):
        jj=jnp.where(t<NCH,1-j,j)
        return jj,pl.ds(al(lax.rem(t,NCH)*T,T),T)
    def where(t): return pl.ds(al((jnp.where(t<NCH,1-j,j)*2+c)*block+lax.rem(t,NCH)*T,T),T)
    def load(t):
        jj,rows=place(t)
        return [pltpu.make_async_copy(att_hbm.at[:,jj,c,rows],aown.at[t],lsem.at[0,t]),pltpu.make_async_copy(tok_hbm.at[jj,c,rows],tok.at[t],lsem.at[1,t])]
    def load_cot(t,near):
        rows=place(t)[1]
        return pltpu.make_async_copy((cot_hbm.at[j,rows] if near else cotx_hbm.at[rows]),cot.at[t],lsem.at[2,t])
    cols=[(0,E),(E,F),(E+F,E),(2*E+F,128)]
    loadw=[pltpu.make_async_copy(bunds[k],wall.at[lax.rem(z+Z-k,Z),:,:,c],wsem.at[k]) for k in range(Z)]
    for x in loadw: x.start()
    def start(t,near):
        for x in load(t): x.start()
        load_cot(t,near).start()
    for t in range(n): start(t,t>=NCH)
    barrier=pltpu.get_barrier_semaphore()
    pl.semaphore_signal(barrier,inc=1,device_id=sib,device_id_type=MESH)
    pl.semaphore_wait(barrier,1)
    def ship(t):
        jj,rows=place(t)
        return net.copy(att_hbm.at[:,jj,1-c,rows],aget.at[t],asend.at[t],aget_sem.at[t],sib)
    ship(0).start()
    weights=[net.copy(bunds[k],wall.at[lax.rem(z+Z-k,Z),:,:,c],bsend.at[k],bget.at[k],sib) for k in range(Z)]
    for x in weights: x.start()
    for t in range(1,n): ship(t).start()
    for x in loadw: x.wait()
    for k in range(Z):
        ref=wall.at[lax.rem(z+Z-k,Z),:,:,1-c]
        pltpu.make_async_copy(ref,ref,bget.at[k]).wait()
    def whole(a,b): return wall[:,:,:,:,:,a:a+b].reshape(E,b)
    gs=wall[:,:,:,:,:,cols[3][0]:].reshape(E//16,16,128).astype(f32)
    gsr=jnp.concatenate([jnp.sum(gs[q*8:(q+1)*8],0) for q in range(E//128)],1)
    g0,g1,b0,b1=[gsr[r:r+1,:] for r in range(4)]
    for r in (go_ref,gu_ref,gd_ref,gg_ref): r[...]=jnp.zeros_like(r)
    def out_near(t): return pltpu.make_async_copy(lay.at[t],near_out.at[place(t)[1]],osem.at[0,t])
    def out_far(t): return pltpu.make_async_copy(lay.at[t],far_out.at[place(t)[1]],osem.at[0,t])
    def out_r1(t):
        jj,rows=place(t)
        return pltpu.make_async_copy(r1.at[t],r1_out.at[jj,rows],osem.at[1,t])
    def out_da(t):
        return pltpu.make_async_copy(da.at[0,t],datt_out.at[:,where(t)],osem.at[2,t])
    def ship_da(t):
        return net.copy(da.at[1,t],datt_out.at[:,where(t)],dsend.at[t],dget.at[t],sib)
    def tiles(u,carry):
        ts=[G*u+g for g in range(G)]
        def each(f,*lists): return [f(*v) for v in zip(*lists)]
        for t in ts:
            for x in load(t): x.wait()
            pltpu.make_async_copy(cotx_hbm.at[place(t)[1]],cot.at[t],lsem.at[2,t]).wait()
            ship(t).wait_recv()
        def whole_att(t):
            mine=[aown[t,p] for p in range(P2)]; his=[aget[t,p] for p in range(P2)]
            return jnp.where(c==0,jnp.concatenate(mine+his,1),jnp.concatenate(his+mine,1))
        wo=whole(*cols[0]); wu=whole(*cols[1]); wd=whole(*cols[2])
        att=each(whole_att,ts)
        branch=each(lambda a:dot(a,wo,1,0),att)
        n1,inv1=zip(*each(lambda t,b:norm(tok[t].astype(f32)+b),ts,branch))
        first=each(lambda n:(n*g0+b0).astype(bf),n1)
        hidden=each(lambda a:dot(a,wu,1,0),first)
        cdf,slope=zip(*each(gelu_parts,hidden))
        act=each(lambda h,p:(h*p).astype(bf),hidden,cdf)
        fed=each(lambda a:dot(a,wd,1,0),act)
        n2,inv2=zip(*each(lambda a,b:norm(a.astype(f32)+b),first,fed))
        ct=each(lambda t:cot[t].astype(f32),ts)
        r2=each(lambda x,n,i:norm_back(x*g1,n,i),ct,n2,inv2)
        feed=each(lambda x:x.astype(bf),r2)
        dact=each(lambda x:dot(x,wd,1,1),feed)
        for t,n in zip(ts,n2): lay[t]=(n*g1+b1).astype(bf)
        both=lambda v:jnp.concatenate(v,0)
        gd_ref[...]+=dot(both(act),both(feed),0,0)
        dh=each(lambda x,s:(x*s).astype(bf),dact,slope)
        df=each(lambda x,h:x+dot(h,wu,1,1),r2,dh)
        gu_ref[...]+=dot(both(first),both(dh),0,0)
        dr=each(lambda x,n,i:norm_back(x*g0,n,i),df,n1,inv1)
        db=each(lambda x:x.astype(bf),dr)
        d=each(lambda x:dot(wo,x,1,1).astype(bf),db)
        go_ref[...]+=dot(both(att),both(db),0,0)
        for t,x,e in zip(ts,dr,d):
            r1[t]=x.astype(r1.dtype)
            da[0,t]=jnp.where(c==0,e[:W],e[W:])
            da[1,t]=jnp.where(c==0,e[W:],e[:W])
        down=lambda v:sum(jnp.sum(x,0,keepdims=True) for x in v)
        gg_ref[0:1,:]+=down(each(lambda x,n:x*n,df,n1))
        gg_ref[1:2,:]+=down(each(lambda x,n:x*n,ct,n2))
        gg_ref[2:3,:]+=down(df)
        gg_ref[3:4,:]+=down(ct)
        for t in ts:
            @pl.when(t<NCH)
            def _(): out_far(t).start()
            @pl.when(t>=NCH)
            def _(): out_near(t).start()
            out_r1(t).start(); out_da(t).start(); ship_da(t).start()
        return carry
    lax.fori_loop(0,n//G,tiles,0)
    ggt=jnp.concatenate([gg_ref[...],jnp.zeros((120,E),f32)],0).T
    gt_ref[...]=ggt
    R=E//(2*Z)
    at=0
    for ref in (go_ref,gu_ref,gd_ref,gt_ref):
        parts[:,:,at:at+ref.shape[1]]=ref[...].astype(bf).reshape(2*Z,R,ref.shape[1])
        at+=ref.shape[1]
    for x in weights: x.wait_send()
    for t in range(n):
        ship(t).wait_send(); out_r1(t).wait(); out_da(t).wait(); ship_da(t).wait()
        (out_far if t<NCH else out_near)(t).wait()

def middle_net(att,tok,cot,cotx,bunds,Z,W,F):
    P2,_,_,block,_=att.shape; E=tok.shape[-1]; C=bunds[0].shape[-1]
    T=256; NCH=block//T; n=2*NCH
    V=pl.BlockSpec(memory_space=pltpu.VMEM); A=pl.BlockSpec(memory_space=pl.ANY)
    S=jax.ShapeDtypeStruct; M=pltpu.VMEM; D=pltpu.SemaphoreType.DMA
    return pl.pallas_call(functools.partial(middle_net_kernel,Z,block,E,F,W,T),
        out_shape=[S((block,E),bf),S((block,E),bf),S((2,block,E),bf),S((W,4*block),bf)]+[S((2*Z,E//(2*Z),C),bf)],
        in_specs=[A]*(4+Z),out_specs=[A,A,A,A,V],
        scratch_shapes=[M((E,E),f32),M((E,F),f32),M((F,E),f32),M((8,E),f32),M((E,128),f32),
            M((n,P2,T,128),bf),M((n,P2,T,128),bf),M((n,T,E),bf),M((n,T,E),bf),M((Z,2,2,2,16,C),bf),M((n,T,E),bf),M((n,T,E),bf),M((2,n,W,T),bf),
            D((3,n)),D((Z,)),D((3,n)),D((n,)),D((n,)),D((n,)),D((n,)),D((Z,)),D((Z,))],
        compiler_params=pltpu.CompilerParams(collective_id=2,has_side_effects=True,vmem_limit_bytes=VMEM))(att,tok,cot,cotx,*bunds)
def reduce_kernel(Z,block,E,W,C1,rows,base_ref,meta_ref,dq_hbm,dkvw_hbm,tok_hbm,w_hbm,r1_hbm,parts_hbm,tok_out,grad_out,
     dq,dkvw,tok,w,r1,parts,own,tgf,tgr,tgs,ob,s0,r0,g0,s1,r1b,su,ru,fin,sx,rx,se,re,sxe,rxe,
     lsem,nsem,osem,ts,tr,xs,xr,cs,cr,ys,yr,us,ur,fs,fr):
    net=Net(Z); z,y,j,c=net.z,net.y,net.j,net.c
    NCH=block//rows; half=2*block
    sib=net.at(c=1-c); xd=net.at(j=1-j); yd=net.at(y=1-y)
    def side(jj): return pl.ds(al(jj*half,128),half)
    def spans(jj): return pl.ds(jj*2*NCH,2*NCH)
    def need(cc,k):
        at=((1-j)*2+cc)*NCH+k; cols=pl.ds(al(at*rows,rows),rows)
        return [pltpu.make_async_copy(dkvw_hbm.at[at],dkvw.at[at],nsem.at[0,cc,k]),pltpu.make_async_copy(dq_hbm.at[:,cols],dq.at[:,cols],nsem.at[1,cc,k])]
    loads=[pltpu.make_async_copy(a,b,lsem.at[k]) for k,(a,b) in enumerate(((w_hbm,w),(r1_hbm,r1),(parts_hbm,parts),
        (dq_hbm.at[:,side(j)],dq.at[:,side(j)]),(tok_hbm,tok),(dkvw_hbm.at[spans(j)],dkvw.at[spans(j)])))]
    net.signal()
    for x in need(1-c,0)+loads[:1]+need(c,0): x.start()
    for k in range(1,NCH):
        for x in need(1-c,k)+need(c,k): x.start()
    for x in loads[1:]: x.start()
    def chunk(k): return pl.ds(k*rows,rows)
    def landed(ref,sem): pltpu.make_async_copy(ref,ref,sem).wait()
    def position(jj,cc,k): return pl.ds(al(((jj*2+cc)*NCH+k)*rows,rows),rows)
    def place(jj,cc,k):
        ssl=position(jj,cc,k)
        dq[W:3*W,ssl]=placed(base_ref,meta_ref[0:1,ssl],dkvw[(jj*2+cc)*NCH+k],dq[W:3*W,ssl],(jj*2+cc)*NCH+k).astype(bf)
    def to_tokens(jj,cc,k): return dot(dq[:,position(jj,cc,k)],w[...],0,1)
    def for_sibling(t,k):
        jj=1-j if t==0 else j
        tgf[jj,chunk(k),:]=to_tokens(jj,1-c,k).astype(bf)
        net.send(tgf.at[jj,chunk(k)],tgr.at[jj,chunk(k)],ts.at[t,k],tr.at[t,k],sib)
    def split(x,n): return x.reshape(Z,2,2,2,16,n)
    def core_sum(v,lo,n):
        x=dot(dq[lo:lo+n,:],tok[...],1,0).T.astype(bf)
        x=split(x,n)
        s0[:,:,:,:,lo:lo+n]=jnp.where(c==0,x[:,:,:,1],x[:,:,:,0])
        net.send(s0.at[:,:,:,:,lo:lo+n],r0.at[:,:,:,:,lo:lo+n],cs.at[v],cr.at[v],sib)
        mine=jnp.where(c==0,x[:,:,:,0],x[:,:,:,1])
        for t in range(lo//W,(lo+n)//W):
            part=mine[:,:,:,:,t*W-lo:(t+1)*W-lo]
            @pl.when(c==0)
            def _(): g0[:,:,:,:,2*t*W:(2*t+1)*W]=part
            @pl.when(c==1)
            def _(): g0[:,:,:,:,(2*t+1)*W:(2*t+2)*W]=part
    def core_get(v,lo,n):
        landed(r0.at[:,:,:,:,lo:lo+n],cr.at[v])
        for t in range(lo//W,(lo+n)//W):
            part=r0[:,:,:,:,t*W:(t+1)*W]
            @pl.when(c==0)
            def _(): g0[:,:,:,:,(2*t+1)*W:(2*t+2)*W]=part
            @pl.when(c==1)
            def _(): g0[:,:,:,:,2*t*W:(2*t+1)*W]=part
    cut=[pl.ds(2*t*W,2*W) for t in range(3)]
    def to_y(v):
        s1[:,:,:,cut[v]]=jnp.where(y==0,g0[:,1,:,:,cut[v]],g0[:,0,:,:,cut[v]])
        net.send(s1.at[:,:,:,cut[v]],r1b.at[:,:,:,cut[v]],ys.at[v],yr.at[v],yd)
    def to_z(v):
        landed(r1b.at[:,:,:,cut[v]],yr.at[v])
        for k in range(1,Z):
            o=lax.rem(z+k,Z)
            su[k,:,:,cut[v]]=(g0[o,y,:,:,cut[v]].astype(f32)+r1b[o,:,:,cut[v]].astype(f32)).astype(bf)
            net.send(su.at[k,:,:,cut[v]],ru.at[k,:,:,cut[v]],us.at[v,k],ur.at[v,k],net.at(z=o))
    def to_x(v):
        sum_=g0[z,y,:,:,cut[v]].astype(f32)+r1b[z,:,:,cut[v]].astype(f32)
        for k in range(1,Z):
            landed(ru.at[k,:,:,cut[v]],ur.at[v,k])
            sum_=sum_+ru[k,:,:,cut[v]].astype(f32)
        fin[:,:,cut[v]]=sum_
        sx[:,cut[v]]=jnp.where(j==0,sum_[1],sum_[0]).astype(bf)
        net.send(sx.at[:,cut[v]],rx.at[:,cut[v]],fs.at[v],fr.at[v],xd)
    def total(jj,k): return (own[jj,chunk(k),:]+tgr[jj,chunk(k),:].astype(f32)+r1[jj,chunk(k),:].astype(f32)).astype(bf)
    def far(k):
        landed(tgr.at[1-j,chunk(k)],tr.at[0,k])
        tgs[chunk(k),:]=total(1-j,k)
        net.send(tgs.at[chunk(k)],ob.at[j,chunk(k)],xs.at[k],xr.at[k],xd)
    for k in range(NCH):
        for x in need(1-c,k): x.wait()
        place(1-j,1-c,k)
        if k==0:
            loads[0].wait()
            net.wait()
        for_sibling(0,k)
        for x in need(c,k): x.wait()
        place(1-j,c,k)
        own[1-j,chunk(k),:]=to_tokens(1-j,c,k)
        if k==0: loads[1].wait()
        else: far(k-1)
    for x in loads[2:]: x.wait()
    core_sum(0,0,W)
    far(NCH-1)
    for cc in (1-c,c):
        for k in range(NCH): place(j,cc,k)
    core_get(0,0,W)
    to_y(0)
    core_sum(1,W,W)
    core_sum(2,2*W,W)
    core_get(1,W,W)
    to_y(1)
    early=parts[0].astype(f32)
    for k in range(1,2*Z): early=early+parts[k].astype(f32)
    early=early.reshape(2,2,16,C1)
    early0=jnp.where(c==0,early[:,0],early[:,1])
    se[...]=jnp.where(c==0,early[:,1],early[:,0]).astype(bf)
    net.send(se,re,cs.at[3],cr.at[3],sib)
    core_get(2,2*W,W)
    to_y(2)
    to_z(0)
    for k in range(NCH): for_sibling(1,k)
    to_z(1)
    landed(re,cr.at[3])
    early0=early0+re[...].astype(f32)
    early1=jnp.where(j==0,early0[0],early0[1])
    sxe[...]=jnp.where(j==0,early0[1],early0[0]).astype(bf)
    net.send(sxe,rxe,fs.at[3],fr.at[3],xd)
    to_x(0)
    for k in range(NCH): own[j,chunk(k),:]=to_tokens(j,c,k)
    to_z(2)
    to_x(1)
    for k in range(NCH):
        landed(tgr.at[j,chunk(k)],tr.at[1,k])
        ob[j,chunk(k),:]=total(j,k)
    near=pltpu.make_async_copy(ob.at[j],tok_out.at[j],osem.at[0]); near.start()
    to_x(2)
    landed(rxe,fr.at[3])
    grad_out[:,6*W:]=early1+rxe[...].astype(f32)
    for v in range(3):
        landed(rx.at[:,cut[v]],fr.at[v])
        grad_out[:,cut[v]]=jnp.where(j==0,fin[0,:,cut[v]],fin[1,:,cut[v]])+rx[:,cut[v]].astype(f32)
    last=[pltpu.make_async_copy(ob.at[1-j,chunk(k)],tok_out.at[1-j,chunk(k)],osem.at[1+k]) for k in range(NCH)]
    for k in range(NCH):
        landed(ob.at[1-j,chunk(k)],xr.at[k])
        last[k].start()
    net.drain()
    near.wait()
    for x in last: x.wait()

def reduce(base,meta,dq,dkvw,tok,w,r1,parts,Z,W):
    _,block,E=r1.shape; L=4*block; C1=parts.shape[2]; C=6*W
    rows=256; NCH=block//rows
    V=pl.BlockSpec(memory_space=pltpu.VMEM); A=pl.BlockSpec(memory_space=pl.ANY)
    S=jax.ShapeDtypeStruct; M=pltpu.VMEM; D=pltpu.SemaphoreType.DMA
    return pl.pallas_call(functools.partial(reduce_kernel,Z,block,E,W,C1,rows),
        out_shape=[S((2,block,E),bf),S((16,C+C1),f32)],
        in_specs=[pl.BlockSpec(memory_space=pltpu.SMEM),V,A,A,A,A,A,A],out_specs=[A,V],
        scratch_shapes=[M(dq.shape,bf),M(dkvw.shape,bf),M(tok.shape,bf),M(w.shape,bf),M(r1.shape,bf),M(parts.shape,bf),M((2,block,E),f32),M((2,block,E),bf),M((2,block,E),bf),M((block,E),bf),M((2,block,E),bf),
            M((Z,2,2,16,3*W),bf),M((Z,2,2,16,3*W),bf),M((Z,2,2,16,C),bf),M((Z,2,16,C),bf),M((Z,2,16,C),bf),
            M((Z,2,16,C),bf),M((Z,2,16,C),bf),M((2,16,C),f32),M((16,C),bf),M((16,C),bf),M((2,16,C1),bf),M((2,16,C1),bf),M((16,C1),bf),M((16,C1),bf),
            D((6,)),D((2,2,NCH)),D((1+NCH,)),D((2,NCH)),D((2,NCH)),D((NCH,)),D((NCH,)),D((4,)),D((4,)),D((3,)),D((3,)),D((3,Z)),D((3,Z)),D((4,)),D((4,))],
        compiler_params=pltpu.CompilerParams(collective_id=1,has_side_effects=True,vmem_limit_bytes=VMEM))(base,meta,dq,dkvw,tok,w,r1,parts)

def finish_kernel(W,E,F,near,far,tg_hbm,grads_hbm,lay_out,tg_out,gq,go,gu,gd,gg,gs,lay,tg,grads,small,isem,osem):
    j=lax.axis_index("blk")//2; block=near.shape[0]; n=4; rows=block//n
    gcopy=pltpu.make_async_copy(grads_hbm,grads,isem.at[4*n]); gcopy.start()
    come=[];leave=[]
    for k in range(n):
        r=pl.ds(k*rows,rows)
        for a,b,o in ((near.at[r],lay.at[j,r],lay_out.at[j,r]),(far.at[r],lay.at[1-j,r],lay_out.at[1-j,r]),(tg_hbm.at[0,r],tg.at[0,r],tg_out.at[0,r]),(tg_hbm.at[1,r],tg.at[1,r],tg_out.at[1,r])):
            at=len(come)
            come.append(pltpu.make_async_copy(a,b,isem.at[at])); leave.append(pltpu.make_async_copy(b,o,osem.at[at]))
    for x in come: x.start()
    gcopy.wait()
    at=0
    for k,ref in enumerate((gq,go,gu,gd)):
        width=ref.shape[1]
        leave.append(pltpu.make_async_copy(grads.at[:,at:at+width],ref,osem.at[4*n+k]))
        at+=width
        leave[-1].start()
    t=grads[:,at:].T
    small[0]=t[0:2,:]; small[1]=t[2:4,:]
    for k,ref in enumerate((gg,gs)):
        leave.append(pltpu.make_async_copy(small.at[k],ref,osem.at[4*n+4+k]))
        leave[-1].start()
    for x,o in zip(come,leave):
        x.wait(); o.start()
    for o in leave: o.wait()

def finish(near,far,tg,grads,W,F):
    _,block,E=tg.shape
    A=pl.BlockSpec(memory_space=pl.ANY); S=jax.ShapeDtypeStruct; M=pltpu.VMEM; D=pltpu.SemaphoreType.DMA
    return pl.pallas_call(functools.partial(finish_kernel,W,E,F),
        out_shape=[S(tg.shape,bf),S(tg.shape,bf),S((16,6*W),f32),S((16,E),f32),S((16,F),f32),S((16,E),f32),S((2,16),f32),S((2,16),f32)],
        in_specs=[A]*4,out_specs=[A]*8,scratch_shapes=[M(tg.shape,bf),M(tg.shape,bf),M(grads.shape,f32),M((2,2,16),f32),D((17,)),D((22,))],
        compiler_params=pltpu.CompilerParams(vmem_limit_bytes=VMEM))(near,far,tg,grads)
def shards(tokens,cotangent,segments,padding,known,w_qkv,w_out,w_up,w_down,norm_gains,norm_shifts):
    micro,rows,block,D=tokens.shape
    J=lax.axis_size("blk")//2; dps=lax.axis_size("dp")
    units=micro*rows
    assert units==J
    H=HEADS//2; W=H*HEAD; L=2*J*block; F=w_up.shape[1]
    quick=J==2 and dps%2==0 and w_qkv.shape[0]==16 and block%256==0
    me=lax.axis_index("blk"); chip=me//2; core=me%2
    flat=lambda x:x.reshape((units,)+x.shape[2:])
    if quick:
        Z=dps//2
        cot=flat(cotangent)
        tok,bund,w_mine,qkvt,base,win,codet,meta,far=gather(flat(tokens),cot,*[flat(x)[:,None,:] for x in (segments,padding,known)],w_qkv,w_out,w_up,w_down,norm_gains,norm_shifts,Z,W)
        bunds=[bund]+[lax.ppermute(bund,"dp",[(d,(d//2+k)%Z*2+d%2) for d in range(dps)]) for k in range(1,Z)]
        across=[(b,b^2) for b in range(4)]
        cotx=lax.ppermute(far,"blk",across)
        p,att,ot,inv,kct,vct=attend(base,win,qkvt,codet,meta,H)
        near,far,r1,datt,parts=middle_net(att.reshape(H//2,2,2,block,128),tok,cot,cotx,bunds,Z,W,F)
        parts=lax.all_to_all(parts,"dp",0,0,tiled=True)
        layx=lax.ppermute(far,"blk",across)
        dq,dkvw=back(base,win,datt,p,ot,inv,kct,vct,qkvt,H)
        tg,grads=reduce(base,meta,dq,dkvw,tok.reshape(L,D),w_mine,r1,parts,Z,W)
        out=finish(near,layx,tg,grads,W,F)
        return (out[0].reshape(tokens.shape),out[1].reshape(tokens.shape))+tuple(out[2:])
    def to_chip(s): return [(2*a+c,2*((a+s)%J)+c) for a in range(J) for c in range(2)]
    swap=[(b,b^1) for b in range(2*J)]
    def other(x): return lax.ppermute(x,"blk",swap)
    def scatter_units(x):
        got=[]
        for s in range(J):
            mine=lax.dynamic_index_in_dim(x,(chip+s)%J,0,keepdims=False)
            got.append(mine if s==0 else lax.ppermute(mine,"blk",to_chip(s)))
        return jnp.stack([lax.dynamic_index_in_dim(jnp.stack(got),(chip-j)%J,0,keepdims=False) for j in range(J)])
    def both(mine,his):
        return jnp.stack([jnp.where(core==0,mine,his),jnp.where(core==0,his,mine)],1)
    def part(x,axis,index): return lax.dynamic_index_in_dim(x,index,axis,keepdims=False)
    own_info=scatter_units(flat(segments*4+padding*2+known)); info=both(own_info,other(own_info)).reshape(1,L)
    own_tok=scatter_units(flat(tokens)); all_tok=both(own_tok,other(own_tok)).reshape(L,D)
    own_cot=scatter_units(flat(cotangent)).reshape(L//2,D)
    full_qkv,full_out,full_up,full_down=[lax.all_gather(w,("dp","blk"),axis=0,tiled=True) for w in (w_qkv,w_out,w_up,w_down)]
    gs=lax.all_gather(jnp.concatenate([norm_gains,norm_shifts],0),("dp","blk"),axis=1,tiled=True).astype(f32)
    gs=jnp.concatenate([gs,jnp.zeros_like(gs)],0)
    w_mine=part(full_qkv.reshape(D,3,2,W),2,core).reshape(D,3*W)
    qkvt=jnp.einsum("ld,de->el",all_tok,w_mine,preferred_element_type=f32).astype(bf)
    base,win,codet,meta=flags(info)
    p,att,ot,inv,kct,vct=attend(base,win,qkvt,codet,meta,H)
    att=att.reshape(H//2,J,2,block,128)
    mine=part(att,2,core).reshape(H//2,J*block,128); his=other(part(att,2,1-core)).reshape(H//2,J*block,128)
    a0=jnp.where(core==0,mine,his); a1=jnp.where(core==0,his,mine)
    out,r1,da,go,gu,gd,gg=middle(a0,a1,own_tok.reshape(L//2,D),own_cot,full_out,full_up,full_down,gs)
    da=da.reshape(2,H//2,J,block,128)
    dmine=part(da,0,core); dhis=other(part(da,0,1-core))
    datt=jnp.stack([jnp.where(core==0,dmine,dhis),jnp.where(core==0,dhis,dmine)],2).reshape(H//2,L,128).transpose(0,2,1).reshape(W,L)
    dq,dkvw=back(base,win,datt,p,ot,inv,kct,vct,qkvt,H)
    tg,gq=place_all(base,meta,dq,dkvw,all_tok,w_mine,H)
    tg=tg.reshape(J,2,block,D)
    layer_out=scatter_units(out.reshape(J,block,D)).reshape(tokens.shape)
    own_tg=(part(tg,1,core).astype(f32)+other(part(tg,1,1-core)).astype(f32)+r1.reshape(J,block,D)).astype(bf)
    token_grad=scatter_units(own_tg).reshape(tokens.shape)
    gq=gq.astype(f32).reshape(D,3,1,W)
    gq=jnp.where(core==0,jnp.concatenate([gq,jnp.zeros_like(gq)],2),jnp.concatenate([jnp.zeros_like(gq),gq],2)).reshape(D,6*W)
    grads=lax.psum_scatter(jnp.concatenate([gq,go,gu,gd],1),("dp","blk"),scatter_dimension=0,tiled=True)
    gg=lax.psum_scatter(gg[:4],("dp","blk"),scatter_dimension=1,tiled=True)
    a,b,e=6*W,6*W+D,6*W+D+F
    return (layer_out,token_grad,grads[:,:a],grads[:,a:b],grads[:,b:e],grads[:,e:],gg[:2],gg[2:])

def solution(mesh):
    in_specs = (
        P(None, "dp", "blk", None),
        P(None, "dp", "blk", None),
        P(None, "dp", "blk"),
        P(None, "dp", "blk"),
        P(None, "dp", "blk"),
        P(("dp", "blk"), None),
        P(("dp", "blk"), None),
        P(("dp", "blk"), None),
        P(("dp", "blk"), None),
        P(None, ("dp", "blk")),
        P(None, ("dp", "blk")),
    )
    out_specs = (
        P(None, "dp", "blk", None),
        P(None, "dp", "blk", None),
        P(("dp", "blk"), None),
        P(("dp", "blk"), None),
        P(("dp", "blk"), None),
        P(("dp", "blk"), None),
        P(None, ("dp", "blk")),
        P(None, ("dp", "blk")),
    )
    return jax.shard_map(shards, mesh=mesh, in_specs=in_specs, out_specs=out_specs, check_vma=False)
```

```python
import functools, math
import jax, jax.numpy as jnp
from jax import lax
from jax.experimental import pallas as pl
from jax.experimental.pallas import tpu as pltpu
from jax.sharding import PartitionSpec as P

HEADS = 8
bf=jnp.bfloat16; f32=jnp.float32
HEAD=64
QB=512
KB=512
SRC=768
SAFE=60.0
RATE=math.log2(math.e)*HEAD**-0.5
CODE=16
VMEM=(64<<20)-(128<<10)
SLOTS=4
def dot(a,b,ca,cb): return lax.dot_general(a,b,(((ca,),(cb,)),((),())),preferred_element_type=f32)
def al(x,n): return pl.multiple_of(x,n)
def iota(shape,axis): return lax.broadcasted_iota(jnp.int32,shape,axis)

def begin(base_ref,b):
    return base_ref[b,0]

def window(win_ref,i):
    start=win_ref[i,0]//128*128
    groups=(win_ref[8+i,0]-start+127)//128
    full=(groups-1)//(KB//128)
    return start,full,groups-full*(KB//128),groups

def by_piece(first,full,rest,g,fn):
    def body(j,g):
        fn(al(first+j*KB,128),KB,g)
        return g+1
    g=lax.fori_loop(0,full,body,g)
    for r in range(1,KB//128+1):
        @pl.when(rest==r)
        def _(): fn(al(first+full*KB,128),r*128,g)
    return g+1

def attend_kernel(L,H,base_ref,win_ref,qkvt_hbm,codet_ref,meta_ref,p_hbm,att_hbm,ot_hbm,inv_ref,kct_hbm,vct_hbm,
                  kaug_ref,kct_ref,kvt,q_ref,v_ref,vct,acc,pbuf,obuf,abuf,top_ref,psem,osem,asem,ksem,lsem):
    W=H*HEAD; nq=L//QB
    total=begin(base_ref,L//256)
    third=L//3
    def part(t):
        cols=slice(t*third,(t+1)*third)
        x=[pltpu.make_async_copy(qkvt_hbm.at[W+h*HEAD:W+(h+1)*HEAD,cols],kvt.at[h*128:h*128+HEAD,cols],lsem.at[t,h]) for h in range(H)]
        return x+[pltpu.make_async_copy(qkvt_hbm.at[2*W:,cols],v_ref.at[:,cols],lsem.at[t,H])]
    for t in range(3):
        for x in part(t): x.start()
    queries=pltpu.make_async_copy(qkvt_hbm.at[:W],q_ref,lsem.at[0,H+1]); queries.start()
    for h in range(H):
        kvt[h*128+HEAD:h*128+HEAD+CODE,:]=codet_ref[...]
        kvt[h*128+HEAD+CODE:(h+1)*128,:]=jnp.zeros((HEAD-CODE,L),bf)
    vct[:,HEAD:,:]=jnp.ones((H,16,L),bf)
    row=iota((256,256),0)
    down=iota((256,SRC),0)
    def dest(d,c):
        first=jnp.minimum(win_ref[16+d,0]//128*128,L-SRC)
        last=win_ref[17+d,0]
        def src(t,a):
            ssl=pl.ds(al(jnp.minimum(first+t*SRC,L-SRC),128),SRC)
            oh=((meta_ref[0:1,ssl]==down+d*256)&(lane>=first+t*SRC-jnp.minimum(first+t*SRC,L-SRC))).astype(f32).astype(bf)
            return a[0]+dot(kvt[:,ssl],oh,1,1),a[1]+dot(v_ref[:,ssl],oh,1,1)
        lane=iota((256,SRC),1)
        reach=jnp.minimum(first+jnp.maximum((last-first+SRC-1)//SRC,1)*SRC,L)
        for t in range(3):
            @pl.when((c<=t)&(reach>t*third))
            def _():
                for x in part(t): x.wait()
        ka,va=src(0,(jnp.zeros((H*128,256),f32),jnp.zeros((W,256),f32)))
        ka,va=lax.fori_loop(1,(last-first+SRC-1)//SRC,src,(ka,va))
        dsl=pl.ds(al(d*256,256),256)
        for h in range(H):
            k1=jnp.where(row[:128]==HEAD+10,-10240.0,ka[h*128:(h+1)*128])
            kaug_ref[h,dsl,:]=k1.astype(bf).T
            kct_ref[h,:,dsl]=k1[:HEAD].astype(bf)
            vct[h,:HEAD,dsl]=va[h*HEAD:(h+1)*HEAD].astype(bf)
        return jnp.maximum(c,(reach+third-1)//third)
    ready=lax.fori_loop(0,(total+255)//256,dest,0)
    for t in range(3):
        @pl.when(ready<=t)
        def _():
            for x in part(t): x.wait()
    keep=[pltpu.make_async_copy(kct_ref,kct_hbm,ksem.at[0]),pltpu.make_async_copy(vct,vct_hbm,ksem.at[1])]
    for x in keep: x.start()
    queries.wait()
    bound=jnp.float32(0)
    for h in range(H):
        q=q_ref[h*HEAD:(h+1)*HEAD,:].astype(f32); k=kvt[h*128:h*128+HEAD,:].astype(f32)
        bound=jnp.maximum(bound,jnp.max(jnp.sum(q*q,0,keepdims=True))*jnp.max(jnp.sum(k*k,0,keepdims=True)))
    safe=bound*(RATE*RATE)<SAFE*SAFE

    def pcopy(g):
        slot=lax.rem(g,SLOTS)
        return pltpu.make_async_copy(pbuf.at[slot],p_hbm.at[g],psem.at[slot])
    def ocopy(i):
        slot=lax.rem(i,2)
        return pltpu.make_async_copy(obuf.at[slot],ot_hbm.at[i],osem.at[slot])
    def acopy(i):
        slot=lax.rem(i,2)
        return pltpu.make_async_copy(abuf.at[slot],att_hbm.at[:,pl.ds(al(i*QB,QB),QB),:],asem.at[slot])
    def block(i,g):
        slot=lax.rem(i,2)
        qsl=pl.ds(al(i*QB,QB),QB)
        first,full,rest,groups=window(win_ref,i)
        qa=[jnp.concatenate([q_ref[h*HEAD:(h+1)*HEAD,qsl],codet_ref[:,qsl],jnp.zeros((HEAD-CODE,QB),bf)],0) for h in range(H)]
        own=meta_ref[1:2,qsl]>0
        sself=[]
        for h in range(H):
            x=q_ref[h*HEAD:(h+1)*HEAD,qsl].astype(f32)*kvt[h*128:h*128+HEAD,qsl].astype(f32)
            sself.append(jnp.where(own,jnp.sum(x,0,keepdims=True),-1e30))
        acc[...]=jnp.zeros_like(acc)
        top_ref[...]=jnp.zeros_like(top_ref)
        row=iota((128,QB),0)
        def strict(h,osl):
            k=kaug_ref[h,osl,:]
            x=qa[h].astype(f32)
            plain=dot(k,jnp.where(row<HEAD,x,0.0).astype(bf),1,0)
            return jnp.where(dot(k,jnp.where(row<HEAD,0.0,x).astype(bf),1,0)>-1.0,plain,-1e30)
        @pl.when(jnp.logical_not(safe))
        def _():
            for h in range(H):
                def more(j,m): return jnp.maximum(m,jnp.max(strict(h,pl.ds(al(first+j*128,128),128)),0,keepdims=True))
                top_ref[h:h+1,:]=lax.fori_loop(0,groups,more,sself[h])
        def piece(off,size,g):
            ps=lax.rem(g,SLOTS)
            osl=pl.ds(off,size)
            @pl.when(g>=SLOTS)
            def _(): pcopy(g-SLOTS).wait()
            @pl.when(safe)
            def _():
                keepp=[]
                for h in range(H):
                    p=jnp.exp2(RATE*dot(kaug_ref[h,osl,:],qa[h],1,0)).astype(bf)
                    pbuf[ps,h,:,:size]=p.T
                    keepp.append(p)
                for h in range(H): acc[h]+=dot(vct[h,:,osl],keepp[h],1,0)
            @pl.when(jnp.logical_not(safe))
            def _():
                for h in range(H):
                    def put(j,c):
                        jsl=pl.ds(al(off+j*128,128),128)
                        p=jnp.exp2(RATE*(strict(h,jsl)-top_ref[h:h+1,:])).astype(bf)
                        pbuf[ps,h,:,pl.ds(al(j*128,128),128)]=p.T
                        acc[h]+=dot(vct[h,:,jsl],p,1,0)
                        return c
                    lax.fori_loop(0,size//128,put,0)
            pcopy(g).start()
        g=by_piece(first,full,rest,g,piece)
        @pl.when(i>=2)
        def _(): ocopy(i-2).wait(); acopy(i-2).wait()
        for h in range(H):
            ps=jnp.exp2(RATE*(sself[h]-top_ref[h:h+1,:]))
            inv=1.0/(acc[h,HEAD:HEAD+1,:]+ps)
            obuf[slot,h*HEAD:(h+1)*HEAD,:]=(acc[h,:HEAD,:]+ps*v_ref[h*HEAD:(h+1)*HEAD,qsl].astype(f32))*inv
            inv_ref[h,0:1,qsl]=inv
            inv_ref[h,1:2,qsl]=ps
        for hp in range(H//2): abuf[slot,hp]=obuf[slot,hp*128:(hp+1)*128,:].astype(bf).T
        ocopy(i).start(); acopy(i).start()
        return g
    g=lax.fori_loop(0,nq,block,0)
    for s in range(SLOTS):
        last=g-1-s
        @pl.when(last>=0)
        def _(): pcopy(last).wait()
    for i in range(max(nq-2,0),nq): ocopy(i).wait(); acopy(i).wait()
    for x in keep: x.wait()

def attend(base,win,qkvt,codet,meta,H):
    L=qkvt.shape[1]; W=H*HEAD; nq=L//QB; cap=nq*((L+KB-1)//KB)
    V=pl.BlockSpec(memory_space=pltpu.VMEM); A=pl.BlockSpec(memory_space=pl.ANY)
    S=jax.ShapeDtypeStruct; M=pltpu.VMEM; D=pltpu.SemaphoreType.DMA
    return pl.pallas_call(functools.partial(attend_kernel,L,H),
        out_shape=[S((cap,H,QB,KB),bf),S((H//2,L,128),bf),S((nq,W,QB),f32),S((H,8,L),f32),S((H,HEAD,L),bf),S((H,HEAD+16,L),bf)],
        in_specs=[pl.BlockSpec(memory_space=pltpu.SMEM)]*2+[A,V,V],
        out_specs=[A,A,A,V,A,A],
        scratch_shapes=[M((H,L,128),bf),M((H,HEAD,L),bf),M((H*128,L),bf),M((W,L),bf),M((W,L),bf),M((H,HEAD+16,L),bf),M((H,HEAD+16,QB),f32),M((SLOTS,H,QB,KB),bf),
            M((2,W,QB),f32),M((2,H//2,QB,128),bf),M((8,QB),f32),D((SLOTS,)),D((2,)),D((2,)),D((2,)),D((3,H+2))],
        compiler_params=pltpu.CompilerParams(vmem_limit_bytes=VMEM))(base,win,qkvt,codet,meta)

def flags(row):
    L=row.shape[1]; nb=L//256; nq=L//QB
    seg=row//4
    pad=row//2-2*seg
    known=row-2*(row//2)
    use=(pad==0)&(known==1)
    usef=use.astype(f32)
    x=jnp.concatenate([usef[:,b*256:(b+1)*256] for b in range(nb)]+[jnp.zeros((16-nb,256),f32)],0)
    incl=dot(x.astype(bf),(iota((256,256),0)<=iota((256,256),1)).astype(f32).astype(bf),1,0)
    tot=jnp.broadcast_to(incl[:,255:256],(16,256)).astype(bf)
    base=dot((iota((16,16),0)>iota((16,16),1)).astype(f32).astype(bf),tot,1,0)
    mid=seg[:,L//2:L//2+1]
    late=(seg>=mid).astype(f32)
    early=jnp.sum(usef*(1.0-late),1,keepdims=True)
    shift=jnp.ceil(early*(1.0/128.0))*128.0-early
    shift=jnp.where(jnp.sum(usef,1,keepdims=True)+shift<=L,shift,0.0)
    csum=jnp.concatenate([(incl+base)[b:b+1] for b in range(nb)],1)+late*shift
    rank=jnp.where(use,csum.astype(jnp.int32)-1,-1)
    base=base+shift*jnp.concatenate([late[:,b*256:b*256+1] for b in range(nb)]+[jnp.ones((16-nb,1),f32)],0)
    own=((pad==0)&(known!=1)).astype(jnp.int32)
    bits=iota((CODE,L),0)
    bit=lax.shift_right_logical(jnp.broadcast_to(seg,(CODE,L)),jnp.minimum(bits,9))&1
    codet=jnp.where(bits<10,jnp.where(bit==1,32.0,-32.0),jnp.where(bits==10,1.0,0.0)).astype(bf)
    meta=jnp.concatenate([rank,own,jnp.zeros((6,L),jnp.int32)],0)
    def edge(at): return jnp.concatenate([seg[:,i*QB+at:i*QB+at+1] for i in range(nq)]+[jnp.zeros((8-nq,1),jnp.int32)],0)
    low=jnp.sum(jnp.where(seg<edge(0),usef,0.0),1,keepdims=True)+shift*(edge(0)>=mid).astype(f32)
    high=jnp.sum(jnp.where(seg<=edge(QB-1),usef,0.0),1,keepdims=True)+shift*(edge(QB-1)>=mid).astype(f32)
    starts=jnp.sum((csum<=(256*iota((16,1),0)).astype(f32)).astype(f32),1,keepdims=True)
    win=jnp.broadcast_to(jnp.concatenate([low,high,starts],0),(32,128)).astype(jnp.int32)
    return base[:,:128].astype(jnp.int32),win,codet,meta
SPAN=512
def back_kernel(L,H,base_ref,win_ref,datt_hbm,p_hbm,ot_hbm,inv_ref,kct_hbm,vct_hbm,qkvt_hbm,dq_hbm,dkvw_hbm,
                kct,vct,dkv,dkvt,pbuf,qacc,qkv,datt,ot,dq,psem,lsem,qsem,osem,tsem):
    W=H*HEAD; nq=L//QB
    groups=(begin(base_ref,L//256)+127)//128
    pieces=lax.fori_loop(0,nq,lambda i,s:s+window(win_ref,i)[1]+1,0)
    def pcopy(g):
        slot=lax.rem(g,SLOTS)
        return pltpu.make_async_copy(p_hbm.at[g],pbuf.at[slot],psem.at[slot])
    def keys(t):
        rows=pl.ds(al(t*KB,KB),KB)
        return [pltpu.make_async_copy(vct_hbm.at[:,:,rows],vct.at[:,:,rows],lsem.at[0,t]),pltpu.make_async_copy(kct_hbm.at[:,:,rows],kct.at[:,:,rows],lsem.at[1,t])]
    def queries(i):
        slot=lax.rem(i,2); qsl=pl.ds(al(i*QB,QB),QB)
        return [pltpu.make_async_copy(a,b.at[slot],qsem.at[k,slot]) for k,(a,b) in enumerate(((qkvt_hbm.at[:,qsl],qkv),(datt_hbm.at[:,qsl],datt),(ot_hbm.at[i],ot)))]
    def each_key(fn,least=0):
        def body(t,c):
            for x in keys(t): fn(x)
            return c
        lax.fori_loop(least,(groups+KB//128-1)//(KB//128),body,0)
    for x in queries(0): x.start()
    each_key(lambda x:x.start())
    for s in range(SLOTS-1):
        @pl.when(s<pieces)
        def _(): pcopy(s).start()
    def clear(j,c):
        dkv[:,pl.ds(al(j*128,128),128)]=jnp.zeros((2*W,128),f32)
        return c
    lax.fori_loop(0,groups,clear,0)
    def ocopy(i):
        slot=lax.rem(i,2)
        return pltpu.make_async_copy(dq.at[slot],dq_hbm.at[:,pl.ds(al(i*QB,QB),QB)],osem.at[slot])
    def block(i,g):
        slot=lax.rem(i,2)
        qsl=pl.ds(al(i*QB,QB),QB)
        first,full,rest,_=window(win_ref,i)
        for x in queries(i): x.wait()
        @pl.when(i+1<nq)
        def _():
            for x in queries(i+1): x.start()
        dt=datt[slot].astype(f32)
        prod=dt*ot[slot]
        daug=[];lows=[];deltas=[];d1s=[]
        row=iota((16,QB),0)
        for h in range(H):
            hsl=slice(h*HEAD,(h+1)*HEAD)
            inv=inv_ref[h,0:1,qsl]
            delta=jnp.sum(prod[hsl],0,keepdims=True)*inv
            d1=dt[hsl]*inv
            low=d1.astype(bf)
            a=delta.astype(bf).astype(f32); b=(delta-a).astype(bf).astype(f32)
            extra=jnp.where(row==0,-a,jnp.where(row==1,-b,jnp.where(row==2,a+b-delta,0.0))).astype(bf)
            daug.append(jnp.concatenate([low,extra,jnp.zeros((HEAD-16,QB),bf)],0).T[:,:HEAD+16])
            lows.append(low); deltas.append(delta); d1s.append(d1)
        qacc[...]=jnp.zeros_like(qacc)
        def piece(off,size,g):
            ps=lax.rem(g,SLOTS)
            osl=pl.ds(off,size)
            @pl.when(g+SLOTS-1<pieces)
            def _(): pcopy(g+SLOTS-1).start()
            @pl.when(i==0)
            def _():
                for x in keys(g): x.wait()
            pcopy(g).wait()
            dss=[]
            for h in range(H):
                dss.append((pbuf[ps,h,:,:size].astype(f32)*dot(daug[h],vct[h,:,osl],1,0)).astype(bf))
                dkv[W+h*HEAD:W+(h+1)*HEAD,osl]+=dot(lows[h],pbuf[ps,h,:,:size],1,0)
            for h in range(H): qacc[h]+=dot(kct[h,:,osl],dss[h],1,1)
            for h in range(H):
                dkv[h*HEAD:(h+1)*HEAD,osl]+=dot(qkv[slot,h*HEAD:(h+1)*HEAD,:],dss[h],1,0)
        g=by_piece(first,full,rest,g,piece)
        @pl.when(i==0)
        def _(): each_key(lambda x:x.wait(),g)
        @pl.when(i>=2)
        def _(): ocopy(i-2).wait()
        for h in range(H):
            hsl=slice(h*HEAD,(h+1)*HEAD); ksl=slice(W+h*HEAD,W+(h+1)*HEAD); vsl=slice(2*W+h*HEAD,2*W+(h+1)*HEAD)
            ps=inv_ref[h,1:2,qsl]
            ds=ps*(jnp.sum(qkv[slot,vsl,:].astype(f32)*d1s[h],0,keepdims=True)-deltas[h])
            dq[slot,hsl,:]=((qacc[h]+ds*qkv[slot,ksl,:].astype(f32))*HEAD**-0.5).astype(bf)
            dq[slot,ksl,:]=(ds*qkv[slot,hsl,:].astype(f32)*HEAD**-0.5).astype(bf)
            dq[slot,vsl,:]=(ps*d1s[h]).astype(bf)
        ocopy(i).start()
        return g
    lax.fori_loop(0,nq,block,0)
    rows=iota((2*W,128),0)
    def tcopy(s): return pltpu.make_async_copy(dkvt.at[:,pl.ds(al(begin(base_ref,s)//128*128,128),SPAN)],dkvw_hbm.at[s],tsem.at[s])
    def turn(j,c):
        jsl=pl.ds(al(j*128,128),128)
        x=jnp.where(j<groups,dkv[:,jsl],0.0)
        dkvt[:,jsl]=jnp.where(rows<W,x*HEAD**-0.5,x).astype(bf)
        for s in range(L//256):
            @pl.when(begin(base_ref,s)//128+SPAN//128-1==j)
            def _(): tcopy(s).start()
        return c
    lax.fori_loop(0,groups+SPAN//128,turn,0)
    for i in range(max(nq-2,0),nq): ocopy(i).wait()
    for s in range(L//256): tcopy(s).wait()

def back(base,win,datt,p,ot,inv,kct,vct,qkvt,H):
    L=qkvt.shape[1]; W=H*HEAD
    V=pl.BlockSpec(memory_space=pltpu.VMEM); A=pl.BlockSpec(memory_space=pl.ANY); N=pl.BlockSpec(memory_space=pltpu.SMEM)
    S=jax.ShapeDtypeStruct; M=pltpu.VMEM; D=pltpu.SemaphoreType.DMA
    return pl.pallas_call(functools.partial(back_kernel,L,H),
        out_shape=[S((3*W,L),bf),S((L//256,2*W,SPAN),bf)],
        in_specs=[N,N,A,A,A,V,A,A,A],
        out_specs=[A,A],
        scratch_shapes=[M((H,HEAD,L),bf),M((H,HEAD+16,L),bf),M((2*W,L+SPAN),f32),M((2*W,L+SPAN),bf),M((SLOTS,H,QB,KB),bf),M((H,HEAD,QB),f32),
            M((2,3*W,QB),bf),M((2,W,QB),bf),M((2,W,QB),f32),M((2,3*W,QB),bf),
            D((SLOTS,)),D((2,L//KB)),D((3,2)),D((2,)),D((L//256,))],
        compiler_params=pltpu.CompilerParams(vmem_limit_bytes=VMEM))(base,win,datt,p,ot,inv,kct,vct,qkvt)

def placed(base_ref,rank_row,span,own,s):
    r0=begin(base_ref,s)//128*128
    oh=(rank_row==iota((SPAN,256),0)+r0).astype(f32).astype(bf)
    return dot(span,oh,1,0)+own.astype(f32)

def place_kernel(L,W,base_ref,meta_ref,dq_in,dkvw_ref,tok_ref,w_ref,tg_ref,grad_ref,dq_ref):
    dq_ref[...]=dq_in[...]
    def place(s,c):
        ssl=pl.ds(al(s*256,256),256)
        dq_ref[W:3*W,ssl]=placed(base_ref,meta_ref[0:1,ssl],dkvw_ref[s],dq_ref[W:3*W,ssl],s).astype(bf)
        tg_ref[ssl,:]=dot(dq_ref[:,ssl],w_ref[...],0,1).astype(bf)
        return c
    lax.fori_loop(0,L//256,place,0)
    grad_ref[...]=dot(dq_ref[...],tok_ref[...],1,0).T.astype(bf)

def place_all(base,meta,dq,dkvw,tok,w,H):
    L,E=tok.shape; W=H*HEAD
    V=pl.BlockSpec(memory_space=pltpu.VMEM); S=jax.ShapeDtypeStruct
    return pl.pallas_call(functools.partial(place_kernel,L,W),out_shape=[S((L,E),bf),S((E,3*W),bf)],
        in_specs=[pl.BlockSpec(memory_space=pltpu.SMEM)]+[V]*5,out_specs=[V,V],scratch_shapes=[pltpu.VMEM((3*W,L),bf)],
        compiler_params=pltpu.CompilerParams(vmem_limit_bytes=VMEM))(base,meta,dq,dkvw,tok,w)
EPSILON=1e-05
def gelu_parts(h):
    bell=jnp.exp(-0.5*h*h)
    t=1.0/(1.0+(0.3275911*math.sqrt(0.5))*jnp.abs(h))
    tail=0.5*1.061405429
    for c in (-1.453152027,1.421413741,-0.284496736,0.254829592): tail=tail*t+0.5*c
    tail=tail*t*bell
    cdf=jnp.where(h<0.0,tail,1.0-tail)
    return cdf,cdf+h*bell*(1.0/math.sqrt(2.0*math.pi))
def norm(x):
    center=x-jnp.mean(x,-1,keepdims=True)
    inverse=lax.rsqrt(jnp.mean(center*center,-1,keepdims=True)+EPSILON)
    return center*inverse,inverse
def norm_back(e,n,inverse):
    return inverse*(e-jnp.mean(e,-1,keepdims=True)-n*jnp.mean(e*n,-1,keepdims=True))
def middle_kernel(a0_ref,a1_ref,tok_ref,cot_ref,wo_ref,wu_ref,wd_ref,gs_ref,out_ref,r1_ref,da_ref,go_ref,gu_ref,gd_ref,gg_ref):
    @pl.when(pl.program_id(0)==0)
    def _():
        for r in (go_ref,gu_ref,gd_ref,gg_ref): r[...]=jnp.zeros_like(r)
    P2=a0_ref.shape[0]
    att=jnp.concatenate([a0_ref[p] for p in range(P2)]+[a1_ref[p] for p in range(P2)],1)
    g0,g1,b0,b1=[gs_ref[r:r+1,:] for r in range(4)]
    n1,inv1=norm(tok_ref[...].astype(f32)+dot(att,wo_ref[...],1,0))
    first=(n1*g0+b0).astype(bf)
    hidden=dot(first,wu_ref[...],1,0)
    cdf,slope=gelu_parts(hidden)
    act=(hidden*cdf).astype(bf)
    n2,inv2=norm(first.astype(f32)+dot(act,wd_ref[...],1,0))
    out_ref[...]=(n2*g1+b1).astype(bf)
    cot=cot_ref[...].astype(f32)
    r2=norm_back(cot*g1,n2,inv2)
    feed=r2.astype(bf)
    gd_ref[...]+=dot(act,feed,0,0)
    dh=(dot(feed,wd_ref[...],1,1)*slope).astype(bf)
    gu_ref[...]+=dot(first,dh,0,0)
    df=r2+dot(dh,wu_ref[...],1,1)
    r1=norm_back(df*g0,n1,inv1)
    r1_ref[...]=r1
    db=r1.astype(bf)
    go_ref[...]+=dot(att,db,0,0)
    da=dot(db,wo_ref[...],1,1).astype(bf)
    for p in range(2*P2): da_ref[p]=da[:,p*128:(p+1)*128]
    gg_ref[0:1,:]+=jnp.sum(df*n1,0,keepdims=True)
    gg_ref[1:2,:]+=jnp.sum(cot*n2,0,keepdims=True)
    gg_ref[2:3,:]+=jnp.sum(df,0,keepdims=True)
    gg_ref[3:4,:]+=jnp.sum(cot,0,keepdims=True)

def middle(a0,a1,tok,cot,wo,wu,wd,gs):
    P2,N,_=a0.shape; D=tok.shape[1]; F=wu.shape[1]
    T=max(t for t in (256,192,128,64,32,16) if N%t==0)
    tile=pl.BlockSpec((T,D),lambda i:(i,0))
    def pairs(k): return pl.BlockSpec((k,T,128),lambda i:(0,i,0))
    def whole(s): return pl.BlockSpec(s,lambda i:(0,)*len(s))
    return pl.pallas_call(middle_kernel,grid=(N//T,),
        in_specs=[pairs(P2),pairs(P2),tile,tile,whole((D,D)),whole((D,F)),whole((F,D)),whole((8,D))],
        out_specs=[tile,tile,pairs(2*P2),whole((D,D)),whole((D,F)),whole((F,D)),whole((8,D))],
        out_shape=[jax.ShapeDtypeStruct((N,D),bf),jax.ShapeDtypeStruct((N,D),f32),jax.ShapeDtypeStruct((2*P2,N,128),bf),
            jax.ShapeDtypeStruct((D,D),f32),jax.ShapeDtypeStruct((D,F),f32),jax.ShapeDtypeStruct((F,D),f32),jax.ShapeDtypeStruct((8,D),f32)],
        compiler_params=pltpu.CompilerParams(vmem_limit_bytes=60<<20))(a0,a1,tok,cot,wo,wu,wd,gs)
MESH=pl.DeviceIdType.MESH
class Net:
    def __init__(self,Z):
        dp=lax.axis_index("dp"); blk=lax.axis_index("blk")
        self.Z=Z; self.z=dp//2; self.y=dp%2; self.j=blk//2; self.c=blk%2
        self.sent=[]
    def at(self,z=None,y=None,j=None,c=None):
        z=self.z if z is None else z; y=self.y if y is None else y; j=self.j if j is None else j; c=self.c if c is None else c
        return (z*2+y,j*2+c)
    def signal(self):
        barrier=pltpu.get_barrier_semaphore()
        for d in [self.at(j=1-self.j),self.at(y=1-self.y),self.at(c=1-self.c)]+[self.at(z=lax.rem(self.z+k,self.Z)) for k in range(1,self.Z)]:
            pl.semaphore_signal(barrier,inc=1,device_id=d,device_id_type=MESH)
    def wait(self): pl.semaphore_wait(pltpu.get_barrier_semaphore(),2+self.Z)
    def greet(self):
        self.signal()
        self.wait()
    def copy(self,src,dst,ssem,rsem,device):
        return pltpu.make_async_remote_copy(src_ref=src,dst_ref=dst,send_sem=ssem,recv_sem=rsem,device_id=device,device_id_type=MESH)
    def send(self,src,dst,ssem,rsem,device,when=None):
        c=self.copy(src,dst,ssem,rsem,device)
        if when is None: c.start()
        else: pl.when(when)(c.start)
        self.sent.append((c,when))
    def drain(self):
        for c,when in self.sent:
            if when is None: c.wait_send()
            else: pl.when(when)(c.wait_send)

def gather_kernel(Z,block,E,W,rows,tok_hbm,cot_hbm,seg_ref,pad_ref,known_ref,wq_ref,wo_ref,wu_ref,wd_ref,gain_ref,shift_ref,
                  tok_out,bund_out,wmine_out,qkvt_out,base_out,win_out,code_out,meta_out,far_out,
                  tokb,farb,info_ref,infob,pack_ref,wall,bund,wt,qkvt,lsem,qsem,xs,xr,zs,zr,ys,yr,cs,cr,ts,tr,iss,isr):
    net=Net(Z); z,y,j,c=net.z,net.y,net.j,net.c
    NCH=block//rows; D=E
    sib=net.at(c=1-c); xd=net.at(j=1-j); yd=net.at(y=1-y)
    net.signal()
    mine=pltpu.make_async_copy(tok_hbm.at[j],tokb.at[j,c],lsem.at[0]); mine.start()
    far=pltpu.make_async_copy(cot_hbm.at[1-j],farb,lsem.at[3]); far.start()
    at=0
    for ref in (wq_ref,wo_ref,wu_ref,wd_ref):
        n=ref.shape[1]
        pack_ref[:,at:at+n]=ref[...]
        at+=n
    R=gain_ref.shape[1]
    place=(iota((R,128),1)==iota((R,128),0)+R*lax.rem(lax.axis_index("dp")*4+lax.axis_index("blk"),128//R)).astype(f32).astype(bf)
    pack_ref[:,at:]=jnp.concatenate([dot(gain_ref[...],place,1,0),dot(shift_ref[...],place,1,0),jnp.zeros((12,128),f32)],0).astype(bf)
    split=6*W
    wall[z,y,j,c]=pack_ref[:,:split]
    bund[y,j]=pack_ref[:,split:]
    info_ref[...]=seg_ref[...]*4+pad_ref[...]*2+known_ref[...]
    infob[j,c]=info_ref[j]
    net.wait()
    net.send(pack_ref.at[:,:split],wall.at[z,y,j,c],xs.at[0],xr.at[0],xd)
    net.send(pack_ref.at[:,split:],bund.at[y,j],xs.at[1],xr.at[1],xd)
    net.send(info_ref.at[1-j],infob.at[j,c],iss.at[0],isr.at[0],xd)
    net.send(info_ref.at[j],infob.at[j,c],iss.at[1],isr.at[1],sib)
    def chunk(k): return pl.ds(k*rows if type(k) is int else al(k*rows,rows),rows)
    for k in range(NCH):
        net.send(tok_hbm.at[1-j,chunk(k)],tokb.at[j,c,chunk(k)],ts.at[0,k],tr.at[0,k],xd)
        net.send(tok_hbm.at[j,chunk(k)],tokb.at[j,c,chunk(k)],ts.at[1,k],tr.at[1,k],sib)
    def piece(o,y_): return wall.at[o,y_,:,c]
    def landed(ref,sem): pltpu.make_async_copy(ref,ref,sem).wait()
    def pass_on(o):
        net.send(piece(o,y),piece(o,y),ys.at[o],yr.at[o],yd)
        net.send(piece(o,y),piece(o,y),cs.at[0,o],cr.at[0,o],sib)
    far.wait()
    far=pltpu.make_async_copy(farb,far_out,lsem.at[3]); far.start()
    landed(wall.at[z,y,1-j,c],xr.at[0])
    for k in range(1,Z):
        net.send(piece(z,y),piece(z,y),zs.at[k],zr.at[k],net.at(z=lax.rem(z+k,Z)))
    pass_on(z)
    landed(bund.at[y,1-j],xr.at[1])
    net.send(bund.at[y],bund.at[y],ys.at[Z],yr.at[Z],yd)
    for k in range(1,Z):
        o=lax.rem(z+Z-k,Z)
        landed(piece(o,y),zr.at[k])
        pass_on(o)
    for k in range(Z):
        o=lax.rem(z+Z-k,Z)
        landed(piece(o,1-y),yr.at[o])
        net.send(piece(o,1-y),piece(o,1-y),cs.at[1,o],cr.at[1,o],sib)
    for o in range(Z):
        for q in range(2): landed(wall.at[o,y if q==0 else 1-y,:,1-c],cr.at[q,o])
    landed(bund.at[1-y],yr.at[Z])
    outb=pltpu.make_async_copy(bund,bund_out,lsem.at[1]); outb.start()
    def qcopy(g):
        col=pl.ds(al(g*rows,rows),rows)
        return pltpu.make_async_copy(qkvt.at[:,col],qkvt_out.at[:,col],qsem.at[g])
    def project(jj,cc,come=None,onward=False):
        def body(k,carry):
            ref=tokb.at[jj,cc,chunk(k)]
            if come is not None: landed(ref,tr.at[come,k])
            if onward: net.copy(ref,ref,ts.at[2,k],tr.at[2,k],sib).start()
            g=(jj*2+cc)*NCH+k
            r=dot(wt[...],ref[...],1,1)
            qkvt[:,pl.ds(al(g*rows,rows),rows)]=r.astype(bf)
            qcopy(g).start()
            return carry
        lax.fori_loop(0,NCH,body,0)
    parts=[]
    for t in range(3):
        cols=pl.ds(al(t*2*W+c*W,W),W)
        part=wall[:,:,:,:,:,cols].reshape(D,W)
        wt[t*W:(t+1)*W,:]=part.T
        parts.append(part)
    wmine_out[...]=jnp.concatenate(parts,1)
    mine.wait()
    project(j,c)
    project(j,1-c,1)
    landed(infob.at[1-j,c],isr.at[0])
    net.send(infob.at[1-j,c],infob.at[1-j,c],iss.at[2],isr.at[2],sib)
    project(1-j,c,0,True)
    landed(infob.at[j,1-c],isr.at[1])
    landed(infob.at[1-j,1-c],isr.at[2])
    base_out[...],win_out[...],code_out[...],meta_out[...]=flags(jnp.concatenate([infob[0,0],infob[0,1],infob[1,0],infob[1,1]],1))
    project(1-j,1-c,2)
    outt=pltpu.make_async_copy(tokb,tok_out,lsem.at[2]); outt.start()
    net.drain()
    for k in range(NCH):
        ref=tokb.at[1-j,c,chunk(k)]
        net.copy(ref,ref,ts.at[2,k],tr.at[2,k],sib).wait_send()
    lax.fori_loop(0,4*NCH,lambda g,c:(qcopy(g).wait(),c)[1],0)
    outb.wait(); outt.wait(); far.wait()

def gather(tok,cot,seg,pad,known,wq,wo,wu,wd,gain,shift,Z,W):
    _,block,E=tok.shape; R=wq.shape[0]; C=6*W+wo.shape[1]+wu.shape[1]+wd.shape[1]+128
    rows=256; NCH=block//rows; L=4*block
    V=pl.BlockSpec(memory_space=pltpu.VMEM); A=pl.BlockSpec(memory_space=pl.ANY)
    S=jax.ShapeDtypeStruct; M=pltpu.VMEM; D=pltpu.SemaphoreType.DMA; I=jnp.int32
    return pl.pallas_call(functools.partial(gather_kernel,Z,block,E,W,rows),
        out_shape=[S((2,2,block,E),bf),S((2,2,R,C-6*W),bf),S((E,3*W),bf),S((3*W,L),bf),S((16,128),I),S((32,128),I),S((CODE,L),bf),S((8,L),I),S((block,E),bf)],
        in_specs=[A,A]+[V]*9,out_specs=[A,A,V,A,V,V,V,V,A],
        scratch_shapes=[M((2,2,block,E),bf),M((block,E),bf),M((2,1,block),I),M((2,2,1,block),I),M((R,C),bf),M((Z,2,2,2,R,6*W),bf),M((2,2,R,C-6*W),bf),M((3*W,E),bf),M((3*W,L),bf),
            D((4,)),D((4*NCH,)),D((2,)),D((2,)),D((Z,)),D((Z,)),D((Z+1,)),D((Z+1,)),D((2,Z)),D((2,Z)),D((3,NCH)),D((3,NCH)),D((3,)),D((3,))],
        compiler_params=pltpu.CompilerParams(collective_id=0,has_side_effects=True,vmem_limit_bytes=VMEM))(tok,cot,seg,pad,known,wq,wo,wu,wd,gain,shift)
def middle_net_kernel(Z,block,E,F,W,T,att_hbm,tok_hbm,cot_hbm,cotx_hbm,*rest):
    bunds=rest[:Z]; near_out,far_out,r1_out,datt_out=rest[Z:Z+4]; parts=rest[Z+4]
    (go_ref,gu_ref,gd_ref,gg_ref,gt_ref,aown,aget,tok,cot,wall,lay,r1,da,lsem,wsem,osem,asend,aget_sem,dsend,dget,bsend,bget)=rest[Z+5:]
    net=Net(Z); z,y,j,c=net.z,net.y,net.j,net.c
    NCH=block//T; n=2*NCH; P2=att_hbm.shape[0]; G=2
    sib=net.at(c=1-c)
    def place(t):
        jj=jnp.where(t<NCH,1-j,j)
        return jj,pl.ds(al(lax.rem(t,NCH)*T,T),T)
    def where(t): return pl.ds(al((jnp.where(t<NCH,1-j,j)*2+c)*block+lax.rem(t,NCH)*T,T),T)
    def load(t):
        jj,rows=place(t)
        return [pltpu.make_async_copy(att_hbm.at[:,jj,c,rows],aown.at[t],lsem.at[0,t]),pltpu.make_async_copy(tok_hbm.at[jj,c,rows],tok.at[t],lsem.at[1,t])]
    def load_cot(t,near):
        rows=place(t)[1]
        return pltpu.make_async_copy((cot_hbm.at[j,rows] if near else cotx_hbm.at[rows]),cot.at[t],lsem.at[2,t])
    cols=[(0,E),(E,F),(E+F,E),(2*E+F,128)]
    loadw=[pltpu.make_async_copy(bunds[k],wall.at[lax.rem(z+Z-k,Z),:,:,c],wsem.at[k]) for k in range(Z)]
    for x in loadw: x.start()
    def start(t,near):
        for x in load(t): x.start()
        load_cot(t,near).start()
    for t in range(n): start(t,t>=NCH)
    barrier=pltpu.get_barrier_semaphore()
    pl.semaphore_signal(barrier,inc=1,device_id=sib,device_id_type=MESH)
    pl.semaphore_wait(barrier,1)
    def ship(t):
        jj,rows=place(t)
        return net.copy(att_hbm.at[:,jj,1-c,rows],aget.at[t],asend.at[t],aget_sem.at[t],sib)
    ship(0).start()
    weights=[net.copy(bunds[k],wall.at[lax.rem(z+Z-k,Z),:,:,c],bsend.at[k],bget.at[k],sib) for k in range(Z)]
    for x in weights: x.start()
    for t in range(1,n): ship(t).start()
    for x in loadw: x.wait()
    for k in range(Z):
        ref=wall.at[lax.rem(z+Z-k,Z),:,:,1-c]
        pltpu.make_async_copy(ref,ref,bget.at[k]).wait()
    def whole(a,b): return wall[:,:,:,:,:,a:a+b].reshape(E,b)
    gs=wall[:,:,:,:,:,cols[3][0]:].reshape(E//16,16,128).astype(f32)
    gsr=jnp.concatenate([jnp.sum(gs[q*8:(q+1)*8],0) for q in range(E//128)],1)
    g0,g1,b0,b1=[gsr[r:r+1,:] for r in range(4)]
    for r in (go_ref,gu_ref,gd_ref,gg_ref): r[...]=jnp.zeros_like(r)
    def out_near(t): return pltpu.make_async_copy(lay.at[t],near_out.at[place(t)[1]],osem.at[0,t])
    def out_far(t): return pltpu.make_async_copy(lay.at[t],far_out.at[place(t)[1]],osem.at[0,t])
    def out_r1(t):
        jj,rows=place(t)
        return pltpu.make_async_copy(r1.at[t],r1_out.at[jj,rows],osem.at[1,t])
    def out_da(t):
        return pltpu.make_async_copy(da.at[0,t],datt_out.at[:,where(t)],osem.at[2,t])
    def ship_da(t):
        return net.copy(da.at[1,t],datt_out.at[:,where(t)],dsend.at[t],dget.at[t],sib)
    def tiles(u,carry):
        ts=[G*u+g for g in range(G)]
        def each(f,*lists): return [f(*v) for v in zip(*lists)]
        for t in ts:
            for x in load(t): x.wait()
            pltpu.make_async_copy(cotx_hbm.at[place(t)[1]],cot.at[t],lsem.at[2,t]).wait()
            ship(t).wait_recv()
        def whole_att(t):
            mine=[aown[t,p] for p in range(P2)]; his=[aget[t,p] for p in range(P2)]
            return jnp.where(c==0,jnp.concatenate(mine+his,1),jnp.concatenate(his+mine,1))
        wo=whole(*cols[0]); wu=whole(*cols[1]); wd=whole(*cols[2])
        att=each(whole_att,ts)
        branch=each(lambda a:dot(a,wo,1,0),att)
        n1,inv1=zip(*each(lambda t,b:norm(tok[t].astype(f32)+b),ts,branch))
        first=each(lambda n:(n*g0+b0).astype(bf),n1)
        hidden=each(lambda a:dot(a,wu,1,0),first)
        cdf,slope=zip(*each(gelu_parts,hidden))
        act=each(lambda h,p:(h*p).astype(bf),hidden,cdf)
        fed=each(lambda a:dot(a,wd,1,0),act)
        n2,inv2=zip(*each(lambda a,b:norm(a.astype(f32)+b),first,fed))
        ct=each(lambda t:cot[t].astype(f32),ts)
        r2=each(lambda x,n,i:norm_back(x*g1,n,i),ct,n2,inv2)
        feed=each(lambda x:x.astype(bf),r2)
        dact=each(lambda x:dot(x,wd,1,1),feed)
        for t,n in zip(ts,n2): lay[t]=(n*g1+b1).astype(bf)
        both=lambda v:jnp.concatenate(v,0)
        gd_ref[...]+=dot(both(act),both(feed),0,0)
        dh=each(lambda x,s:(x*s).astype(bf),dact,slope)
        df=each(lambda x,h:x+dot(h,wu,1,1),r2,dh)
        gu_ref[...]+=dot(both(first),both(dh),0,0)
        dr=each(lambda x,n,i:norm_back(x*g0,n,i),df,n1,inv1)
        db=each(lambda x:x.astype(bf),dr)
        d=each(lambda x:dot(wo,x,1,1).astype(bf),db)
        go_ref[...]+=dot(both(att),both(db),0,0)
        for t,x,e in zip(ts,dr,d):
            r1[t]=x.astype(r1.dtype)
            da[0,t]=jnp.where(c==0,e[:W],e[W:])
            da[1,t]=jnp.where(c==0,e[W:],e[:W])
        down=lambda v:sum(jnp.sum(x,0,keepdims=True) for x in v)
        gg_ref[0:1,:]+=down(each(lambda x,n:x*n,df,n1))
        gg_ref[1:2,:]+=down(each(lambda x,n:x*n,ct,n2))
        gg_ref[2:3,:]+=down(df)
        gg_ref[3:4,:]+=down(ct)
        for t in ts:
            @pl.when(t<NCH)
            def _(): out_far(t).start()
            @pl.when(t>=NCH)
            def _(): out_near(t).start()
            out_r1(t).start(); out_da(t).start(); ship_da(t).start()
        return carry
    lax.fori_loop(0,n//G,tiles,0)
    ggt=jnp.concatenate([gg_ref[...],jnp.zeros((120,E),f32)],0).T
    gt_ref[...]=ggt
    R=E//(2*Z)
    at=0
    for ref in (go_ref,gu_ref,gd_ref,gt_ref):
        parts[:,:,at:at+ref.shape[1]]=ref[...].astype(bf).reshape(2*Z,R,ref.shape[1])
        at+=ref.shape[1]
    for x in weights: x.wait_send()
    for t in range(n):
        ship(t).wait_send(); out_r1(t).wait(); out_da(t).wait(); ship_da(t).wait()
        (out_far if t<NCH else out_near)(t).wait()

def middle_net(att,tok,cot,cotx,bunds,Z,W,F):
    P2,_,_,block,_=att.shape; E=tok.shape[-1]; C=bunds[0].shape[-1]
    T=256; NCH=block//T; n=2*NCH
    V=pl.BlockSpec(memory_space=pltpu.VMEM); A=pl.BlockSpec(memory_space=pl.ANY)
    S=jax.ShapeDtypeStruct; M=pltpu.VMEM; D=pltpu.SemaphoreType.DMA
    return pl.pallas_call(functools.partial(middle_net_kernel,Z,block,E,F,W,T),
        out_shape=[S((block,E),bf),S((block,E),bf),S((2,block,E),bf),S((W,4*block),bf)]+[S((2*Z,E//(2*Z),C),bf)],
        in_specs=[A]*(4+Z),out_specs=[A,A,A,A,V],
        scratch_shapes=[M((E,E),f32),M((E,F),f32),M((F,E),f32),M((8,E),f32),M((E,128),f32),
            M((n,P2,T,128),bf),M((n,P2,T,128),bf),M((n,T,E),bf),M((n,T,E),bf),M((Z,2,2,2,16,C),bf),M((n,T,E),bf),M((n,T,E),bf),M((2,n,W,T),bf),
            D((3,n)),D((Z,)),D((3,n)),D((n,)),D((n,)),D((n,)),D((n,)),D((Z,)),D((Z,))],
        compiler_params=pltpu.CompilerParams(collective_id=2,has_side_effects=True,vmem_limit_bytes=VMEM))(att,tok,cot,cotx,*bunds)
def reduce_kernel(Z,block,E,W,C1,rows,base_ref,meta_ref,dq_hbm,dkvw_hbm,tok_hbm,w_hbm,r1_hbm,parts_hbm,tok_out,grad_out,
     dq,dkvw,tok,w,r1,parts,own,tgf,tgr,tgs,ob,s0,r0,g0,s1,r1b,su,ru,fin,sx,rx,se,re,sxe,rxe,
     lsem,nsem,osem,ts,tr,xs,xr,cs,cr,ys,yr,us,ur,fs,fr):
    net=Net(Z); z,y,j,c=net.z,net.y,net.j,net.c
    NCH=block//rows; half=2*block
    sib=net.at(c=1-c); xd=net.at(j=1-j); yd=net.at(y=1-y)
    def side(jj): return pl.ds(al(jj*half,128),half)
    def spans(jj): return pl.ds(jj*2*NCH,2*NCH)
    def need(cc,k):
        at=((1-j)*2+cc)*NCH+k; cols=pl.ds(al(at*rows,rows),rows)
        return [pltpu.make_async_copy(dkvw_hbm.at[at],dkvw.at[at],nsem.at[0,cc,k]),pltpu.make_async_copy(dq_hbm.at[:,cols],dq.at[:,cols],nsem.at[1,cc,k])]
    loads=[pltpu.make_async_copy(a,b,lsem.at[k]) for k,(a,b) in enumerate(((w_hbm,w),(r1_hbm,r1),(parts_hbm,parts),
        (dq_hbm.at[:,side(j)],dq.at[:,side(j)]),(tok_hbm,tok),(dkvw_hbm.at[spans(j)],dkvw.at[spans(j)])))]
    net.signal()
    for x in need(1-c,0)+loads[:1]+need(c,0): x.start()
    for k in range(1,NCH):
        for x in need(1-c,k)+need(c,k): x.start()
    for x in loads[1:]: x.start()
    def chunk(k): return pl.ds(k*rows,rows)
    def landed(ref,sem): pltpu.make_async_copy(ref,ref,sem).wait()
    def position(jj,cc,k): return pl.ds(al(((jj*2+cc)*NCH+k)*rows,rows),rows)
    def place(jj,cc,k):
        ssl=position(jj,cc,k)
        dq[W:3*W,ssl]=placed(base_ref,meta_ref[0:1,ssl],dkvw[(jj*2+cc)*NCH+k],dq[W:3*W,ssl],(jj*2+cc)*NCH+k).astype(bf)
    def to_tokens(jj,cc,k): return dot(dq[:,position(jj,cc,k)],w[...],0,1)
    def for_sibling(t,k):
        jj=1-j if t==0 else j
        tgf[jj,chunk(k),:]=to_tokens(jj,1-c,k).astype(bf)
        net.send(tgf.at[jj,chunk(k)],tgr.at[jj,chunk(k)],ts.at[t,k],tr.at[t,k],sib)
    def split(x,n): return x.reshape(Z,2,2,2,16,n)
    def core_sum(v,lo,n):
        x=dot(dq[lo:lo+n,:],tok[...],1,0).T.astype(bf)
        x=split(x,n)
        s0[:,:,:,:,lo:lo+n]=jnp.where(c==0,x[:,:,:,1],x[:,:,:,0])
        net.send(s0.at[:,:,:,:,lo:lo+n],r0.at[:,:,:,:,lo:lo+n],cs.at[v],cr.at[v],sib)
        mine=jnp.where(c==0,x[:,:,:,0],x[:,:,:,1])
        for t in range(lo//W,(lo+n)//W):
            part=mine[:,:,:,:,t*W-lo:(t+1)*W-lo]
            @pl.when(c==0)
            def _(): g0[:,:,:,:,2*t*W:(2*t+1)*W]=part
            @pl.when(c==1)
            def _(): g0[:,:,:,:,(2*t+1)*W:(2*t+2)*W]=part
    def core_get(v,lo,n):
        landed(r0.at[:,:,:,:,lo:lo+n],cr.at[v])
        for t in range(lo//W,(lo+n)//W):
            part=r0[:,:,:,:,t*W:(t+1)*W]
            @pl.when(c==0)
            def _(): g0[:,:,:,:,(2*t+1)*W:(2*t+2)*W]=part
            @pl.when(c==1)
            def _(): g0[:,:,:,:,2*t*W:(2*t+1)*W]=part
    cut=[pl.ds(2*t*W,2*W) for t in range(3)]
    def to_y(v):
        s1[:,:,:,cut[v]]=jnp.where(y==0,g0[:,1,:,:,cut[v]],g0[:,0,:,:,cut[v]])
        net.send(s1.at[:,:,:,cut[v]],r1b.at[:,:,:,cut[v]],ys.at[v],yr.at[v],yd)
    def to_z(v):
        landed(r1b.at[:,:,:,cut[v]],yr.at[v])
        for k in range(1,Z):
            o=lax.rem(z+k,Z)
            su[k,:,:,cut[v]]=(g0[o,y,:,:,cut[v]].astype(f32)+r1b[o,:,:,cut[v]].astype(f32)).astype(bf)
            net.send(su.at[k,:,:,cut[v]],ru.at[k,:,:,cut[v]],us.at[v,k],ur.at[v,k],net.at(z=o))
    def to_x(v):
        sum_=g0[z,y,:,:,cut[v]].astype(f32)+r1b[z,:,:,cut[v]].astype(f32)
        for k in range(1,Z):
            landed(ru.at[k,:,:,cut[v]],ur.at[v,k])
            sum_=sum_+ru[k,:,:,cut[v]].astype(f32)
        fin[:,:,cut[v]]=sum_
        sx[:,cut[v]]=jnp.where(j==0,sum_[1],sum_[0]).astype(bf)
        net.send(sx.at[:,cut[v]],rx.at[:,cut[v]],fs.at[v],fr.at[v],xd)
    def total(jj,k): return (own[jj,chunk(k),:]+tgr[jj,chunk(k),:].astype(f32)+r1[jj,chunk(k),:].astype(f32)).astype(bf)
    def far(k):
        landed(tgr.at[1-j,chunk(k)],tr.at[0,k])
        tgs[chunk(k),:]=total(1-j,k)
        net.send(tgs.at[chunk(k)],ob.at[j,chunk(k)],xs.at[k],xr.at[k],xd)
    for k in range(NCH):
        for x in need(1-c,k): x.wait()
        place(1-j,1-c,k)
        if k==0:
            loads[0].wait()
            net.wait()
        for_sibling(0,k)
        for x in need(c,k): x.wait()
        place(1-j,c,k)
        own[1-j,chunk(k),:]=to_tokens(1-j,c,k)
        if k==0: loads[1].wait()
        else: far(k-1)
    for x in loads[2:]: x.wait()
    core_sum(0,0,W)
    far(NCH-1)
    for cc in (1-c,c):
        for k in range(NCH): place(j,cc,k)
    core_get(0,0,W)
    to_y(0)
    core_sum(1,W,W)
    core_sum(2,2*W,W)
    core_get(1,W,W)
    to_y(1)
    early=parts[0].astype(f32)
    for k in range(1,2*Z): early=early+parts[k].astype(f32)
    early=early.reshape(2,2,16,C1)
    early0=jnp.where(c==0,early[:,0],early[:,1])
    se[...]=jnp.where(c==0,early[:,1],early[:,0]).astype(bf)
    net.send(se,re,cs.at[3],cr.at[3],sib)
    core_get(2,2*W,W)
    to_y(2)
    to_z(0)
    for k in range(NCH): for_sibling(1,k)
    to_z(1)
    landed(re,cr.at[3])
    early0=early0+re[...].astype(f32)
    early1=jnp.where(j==0,early0[0],early0[1])
    sxe[...]=jnp.where(j==0,early0[1],early0[0]).astype(bf)
    net.send(sxe,rxe,fs.at[3],fr.at[3],xd)
    to_x(0)
    for k in range(NCH): own[j,chunk(k),:]=to_tokens(j,c,k)
    to_z(2)
    to_x(1)
    for k in range(NCH):
        landed(tgr.at[j,chunk(k)],tr.at[1,k])
        ob[j,chunk(k),:]=total(j,k)
    near=pltpu.make_async_copy(ob.at[j],tok_out.at[j],osem.at[0]); near.start()
    to_x(2)
    landed(rxe,fr.at[3])
    grad_out[:,6*W:]=early1+rxe[...].astype(f32)
    for v in range(3):
        landed(rx.at[:,cut[v]],fr.at[v])
        grad_out[:,cut[v]]=jnp.where(j==0,fin[0,:,cut[v]],fin[1,:,cut[v]])+rx[:,cut[v]].astype(f32)
    last=[pltpu.make_async_copy(ob.at[1-j,chunk(k)],tok_out.at[1-j,chunk(k)],osem.at[1+k]) for k in range(NCH)]
    for k in range(NCH):
        landed(ob.at[1-j,chunk(k)],xr.at[k])
        last[k].start()
    net.drain()
    near.wait()
    for x in last: x.wait()

def reduce(base,meta,dq,dkvw,tok,w,r1,parts,Z,W):
    _,block,E=r1.shape; L=4*block; C1=parts.shape[2]; C=6*W
    rows=256; NCH=block//rows
    V=pl.BlockSpec(memory_space=pltpu.VMEM); A=pl.BlockSpec(memory_space=pl.ANY)
    S=jax.ShapeDtypeStruct; M=pltpu.VMEM; D=pltpu.SemaphoreType.DMA
    return pl.pallas_call(functools.partial(reduce_kernel,Z,block,E,W,C1,rows),
        out_shape=[S((2,block,E),bf),S((16,C+C1),f32)],
        in_specs=[pl.BlockSpec(memory_space=pltpu.SMEM),V,A,A,A,A,A,A],out_specs=[A,V],
        scratch_shapes=[M(dq.shape,bf),M(dkvw.shape,bf),M(tok.shape,bf),M(w.shape,bf),M(r1.shape,bf),M(parts.shape,bf),M((2,block,E),f32),M((2,block,E),bf),M((2,block,E),bf),M((block,E),bf),M((2,block,E),bf),
            M((Z,2,2,16,3*W),bf),M((Z,2,2,16,3*W),bf),M((Z,2,2,16,C),bf),M((Z,2,16,C),bf),M((Z,2,16,C),bf),
            M((Z,2,16,C),bf),M((Z,2,16,C),bf),M((2,16,C),f32),M((16,C),bf),M((16,C),bf),M((2,16,C1),bf),M((2,16,C1),bf),M((16,C1),bf),M((16,C1),bf),
            D((6,)),D((2,2,NCH)),D((1+NCH,)),D((2,NCH)),D((2,NCH)),D((NCH,)),D((NCH,)),D((4,)),D((4,)),D((3,)),D((3,)),D((3,Z)),D((3,Z)),D((4,)),D((4,))],
        compiler_params=pltpu.CompilerParams(collective_id=1,has_side_effects=True,vmem_limit_bytes=VMEM))(base,meta,dq,dkvw,tok,w,r1,parts)

def finish_kernel(W,E,F,near,far,tg_hbm,grads_hbm,lay_out,tg_out,gq,go,gu,gd,gg,gs,lay,tg,grads,small,isem,osem):
    j=lax.axis_index("blk")//2; block=near.shape[0]; n=4; rows=block//n
    gcopy=pltpu.make_async_copy(grads_hbm,grads,isem.at[4*n]); gcopy.start()
    come=[];leave=[]
    for k in range(n):
        r=pl.ds(k*rows,rows)
        for a,b,o in ((near.at[r],lay.at[j,r],lay_out.at[j,r]),(far.at[r],lay.at[1-j,r],lay_out.at[1-j,r]),(tg_hbm.at[0,r],tg.at[0,r],tg_out.at[0,r]),(tg_hbm.at[1,r],tg.at[1,r],tg_out.at[1,r])):
            at=len(come)
            come.append(pltpu.make_async_copy(a,b,isem.at[at])); leave.append(pltpu.make_async_copy(b,o,osem.at[at]))
    for x in come: x.start()
    gcopy.wait()
    at=0
    for k,ref in enumerate((gq,go,gu,gd)):
        width=ref.shape[1]
        leave.append(pltpu.make_async_copy(grads.at[:,at:at+width],ref,osem.at[4*n+k]))
        at+=width
        leave[-1].start()
    t=grads[:,at:].T
    small[0]=t[0:2,:]; small[1]=t[2:4,:]
    for k,ref in enumerate((gg,gs)):
        leave.append(pltpu.make_async_copy(small.at[k],ref,osem.at[4*n+4+k]))
        leave[-1].start()
    for x,o in zip(come,leave):
        x.wait(); o.start()
    for o in leave: o.wait()

def finish(near,far,tg,grads,W,F):
    _,block,E=tg.shape
    A=pl.BlockSpec(memory_space=pl.ANY); S=jax.ShapeDtypeStruct; M=pltpu.VMEM; D=pltpu.SemaphoreType.DMA
    return pl.pallas_call(functools.partial(finish_kernel,W,E,F),
        out_shape=[S(tg.shape,bf),S(tg.shape,bf),S((16,6*W),f32),S((16,E),f32),S((16,F),f32),S((16,E),f32),S((2,16),f32),S((2,16),f32)],
        in_specs=[A]*4,out_specs=[A]*8,scratch_shapes=[M(tg.shape,bf),M(tg.shape,bf),M(grads.shape,f32),M((2,2,16),f32),D((17,)),D((22,))],
        compiler_params=pltpu.CompilerParams(vmem_limit_bytes=VMEM))(near,far,tg,grads)
def shards(tokens,cotangent,segments,padding,known,w_qkv,w_out,w_up,w_down,norm_gains,norm_shifts):
    micro,rows,block,D=tokens.shape
    J=lax.axis_size("blk")//2; dps=lax.axis_size("dp")
    units=micro*rows
    assert units==J
    H=HEADS//2; W=H*HEAD; L=2*J*block; F=w_up.shape[1]
    quick=J==2 and dps%2==0 and w_qkv.shape[0]==16 and block%256==0
    me=lax.axis_index("blk"); chip=me//2; core=me%2
    flat=lambda x:x.reshape((units,)+x.shape[2:])
    if quick:
        Z=dps//2
        cot=flat(cotangent)
        tok,bund,w_mine,qkvt,base,win,codet,meta,far=gather(flat(tokens),cot,*[flat(x)[:,None,:] for x in (segments,padding,known)],w_qkv,w_out,w_up,w_down,norm_gains,norm_shifts,Z,W)
        bunds=[bund]+[lax.ppermute(bund,"dp",[(d,(d//2+k)%Z*2+d%2) for d in range(dps)]) for k in range(1,Z)]
        across=[(b,b^2) for b in range(4)]
        cotx=lax.ppermute(far,"blk",across)
        p,att,ot,inv,kct,vct=attend(base,win,qkvt,codet,meta,H)
        near,far,r1,datt,parts=middle_net(att.reshape(H//2,2,2,block,128),tok,cot,cotx,bunds,Z,W,F)
        parts=lax.all_to_all(parts,"dp",0,0,tiled=True)
        layx=lax.ppermute(far,"blk",across)
        dq,dkvw=back(base,win,datt,p,ot,inv,kct,vct,qkvt,H)
        tg,grads=reduce(base,meta,dq,dkvw,tok.reshape(L,D),w_mine,r1,parts,Z,W)
        out=finish(near,layx,tg,grads,W,F)
        return (out[0].reshape(tokens.shape),out[1].reshape(tokens.shape))+tuple(out[2:])
    def to_chip(s): return [(2*a+c,2*((a+s)%J)+c) for a in range(J) for c in range(2)]
    swap=[(b,b^1) for b in range(2*J)]
    def other(x): return lax.ppermute(x,"blk",swap)
    def scatter_units(x):
        got=[]
        for s in range(J):
            mine=lax.dynamic_index_in_dim(x,(chip+s)%J,0,keepdims=False)
            got.append(mine if s==0 else lax.ppermute(mine,"blk",to_chip(s)))
        return jnp.stack([lax.dynamic_index_in_dim(jnp.stack(got),(chip-j)%J,0,keepdims=False) for j in range(J)])
    def both(mine,his):
        return jnp.stack([jnp.where(core==0,mine,his),jnp.where(core==0,his,mine)],1)
    def part(x,axis,index): return lax.dynamic_index_in_dim(x,index,axis,keepdims=False)
    own_info=scatter_units(flat(segments*4+padding*2+known)); info=both(own_info,other(own_info)).reshape(1,L)
    own_tok=scatter_units(flat(tokens)); all_tok=both(own_tok,other(own_tok)).reshape(L,D)
    own_cot=scatter_units(flat(cotangent)).reshape(L//2,D)
    full_qkv,full_out,full_up,full_down=[lax.all_gather(w,("dp","blk"),axis=0,tiled=True) for w in (w_qkv,w_out,w_up,w_down)]
    gs=lax.all_gather(jnp.concatenate([norm_gains,norm_shifts],0),("dp","blk"),axis=1,tiled=True).astype(f32)
    gs=jnp.concatenate([gs,jnp.zeros_like(gs)],0)
    w_mine=part(full_qkv.reshape(D,3,2,W),2,core).reshape(D,3*W)
    qkvt=jnp.einsum("ld,de->el",all_tok,w_mine,preferred_element_type=f32).astype(bf)
    base,win,codet,meta=flags(info)
    p,att,ot,inv,kct,vct=attend(base,win,qkvt,codet,meta,H)
    att=att.reshape(H//2,J,2,block,128)
    mine=part(att,2,core).reshape(H//2,J*block,128); his=other(part(att,2,1-core)).reshape(H//2,J*block,128)
    a0=jnp.where(core==0,mine,his); a1=jnp.where(core==0,his,mine)
    out,r1,da,go,gu,gd,gg=middle(a0,a1,own_tok.reshape(L//2,D),own_cot,full_out,full_up,full_down,gs)
    da=da.reshape(2,H//2,J,block,128)
    dmine=part(da,0,core); dhis=other(part(da,0,1-core))
    datt=jnp.stack([jnp.where(core==0,dmine,dhis),jnp.where(core==0,dhis,dmine)],2).reshape(H//2,L,128).transpose(0,2,1).reshape(W,L)
    dq,dkvw=back(base,win,datt,p,ot,inv,kct,vct,qkvt,H)
    tg,gq=place_all(base,meta,dq,dkvw,all_tok,w_mine,H)
    tg=tg.reshape(J,2,block,D)
    layer_out=scatter_units(out.reshape(J,block,D)).reshape(tokens.shape)
    own_tg=(part(tg,1,core).astype(f32)+other(part(tg,1,1-core)).astype(f32)+r1.reshape(J,block,D)).astype(bf)
    token_grad=scatter_units(own_tg).reshape(tokens.shape)
    gq=gq.astype(f32).reshape(D,3,1,W)
    gq=jnp.where(core==0,jnp.concatenate([gq,jnp.zeros_like(gq)],2),jnp.concatenate([jnp.zeros_like(gq),gq],2)).reshape(D,6*W)
    grads=lax.psum_scatter(jnp.concatenate([gq,go,gu,gd],1),("dp","blk"),scatter_dimension=0,tiled=True)
    gg=lax.psum_scatter(gg[:4],("dp","blk"),scatter_dimension=1,tiled=True)
    a,b,e=6*W,6*W+D,6*W+D+F
    return (layer_out,token_grad,grads[:,:a],grads[:,a:b],grads[:,b:e],grads[:,e:],gg[:2],gg[2:])

def solution(mesh):
    in_specs = (
        P(None, "dp", "blk", None),
        P(None, "dp", "blk", None),
        P(None, "dp", "blk"),
        P(None, "dp", "blk"),
        P(None, "dp", "blk"),
        P(("dp", "blk"), None),
        P(("dp", "blk"), None),
        P(("dp", "blk"), None),
        P(("dp", "blk"), None),
        P(None, ("dp", "blk")),
        P(None, ("dp", "blk")),
    )
    out_specs = (
        P(None, "dp", "blk", None),
        P(None, "dp", "blk", None),
        P(("dp", "blk"), None),
        P(("dp", "blk"), None),
        P(("dp", "blk"), None),
        P(("dp", "blk"), None),
        P(None, ("dp", "blk")),
        P(None, ("dp", "blk")),
    )
    return jax.shard_map(shards, mesh=mesh, in_specs=in_specs, out_specs=out_specs, check_vma=False)
```
